32 devices in a mesh: replica: 4 (over x, core), fsdp: 8 (over z, y).
Axes of the slice: x: 2, y: 2, z: 4, core: 2. Of those that a mesh axis runs over, the one named last changes fastest.
Arguments:
- tokens: bfloat16 [12288, 1536], P(('replica', 'fsdp')), may hold values from -6 to 6
- seg_ids: int32 [32, 384], P(('replica', 'fsdp')), may hold values from 0 to 11, never falling along the last dimension, each value on 1 to 192 neighbouring positions
- routes: int32 [12288, 4], P(('replica', 'fsdp')), may hold values from 0 to 7, all different within a row; in each aligned block of 384 rows (0 to 383, 384 to 767, ...) at most 288 rows name the same one
- in_proj: bfloat16 [1536, 2048], P('fsdp'), may hold values from -0.15625 to 0.15625
- out_proj: bfloat16 [1536, 1536], P('fsdp'), may hold values from -0.625 to 0.625
- router: bfloat16 [1536, 8], P('fsdp'), may hold values from -0.078125 to 0.078125
- norm_gains: bfloat16 [1536, 2], P('fsdp'), may hold values from 0.5 to 1.5
- expert_in: bfloat16 [1536, 8, 1536], P('fsdp'), may hold values from -0.15625 to 0.15625
- expert_out: bfloat16 [1536, 8, 768], P('fsdp'), may hold values from -0.625 to 0.625
- out_grad: bfloat16 [12288, 1536], P(('replica', 'fsdp')), may hold values from -6 to 6
Outputs:
- mixed: bfloat16 [12288, 1536], P(('replica', 'fsdp'))
- tokens_grad: bfloat16 [12288, 1536], P(('replica', 'fsdp'))
- in_proj_grad: float32 [1536, 2048], P('fsdp')
- out_proj_grad: float32 [1536, 1536], P('fsdp')
- router_grad: float32 [1536, 8], P('fsdp')
- gains_grad: float32 [1536, 2], P('fsdp')
- expert_in_grad: float32 [1536, 8, 1536], P('fsdp')
- expert_out_grad: float32 [1536, 8, 768], P('fsdp')
The draws below stay inside these ranges and needn't reach their ends.
Inputs may be any that keep to these rules, and one draw needn't show every extreme that they name: `routes`: each token names 4 different experts. In the rows of one device no expert is named more than 288 times, a bound that some block reaches. `seg_ids`: along a sequence document numbers never fall; a document covers at most 192 positions.
All inputs are finite; a program needn't handle non-finite values.
Results may differ from the reference program's by a relative error of at most 0.017.
Values may be sent and summed in bfloat16 or wider, within the bound.
A program may use at most 448 MiB of HBM per device.

```python
import math
import jax
import jax.numpy as jnp
import numpy as np
from jax import lax

D = 1536
HQ = 12
KV = 2
HD = 128
F = 768
TOP = 4
E = 8
TOK_DEV = 384
SEQ_LEN = 384
SEQS = 32
TOKENS = 12288
CAP = 288
DOC_MOST = 192
DOC_IDS = 12


def raised(array, rng, source, target, shards_of, factor):
    owner, partner = [(jnp.arange(array.shape[axis_at]) // (array.shape[axis_at] // shards_of)).reshape([-1 if axis == axis_at else 1 for axis in range(array.ndim)]) for axis_at in (source, target)]
    chosen = jax.random.permutation(rng, shards_of)[partner]
    strong = (owner == chosen) | (owner == (partner + shards_of // 2) % shards_of)
    return jnp.where(strong, factor * array, array)


def shard_levels(rng, extent, split, low, top_value):
    gain, own = 1.0, jax.random.fold_in(rng, 6)
    for axis_at, blocks in split:
        draws = jnp.exp(jax.random.uniform(jax.random.fold_in(own, axis_at), (blocks,), jnp.float32, low / len(split), top_value / len(split)))
        gain = gain * jnp.repeat(draws, extent[axis_at] // blocks).reshape([-1 if axis == axis_at else 1 for axis in range(len(extent))])
    return gain


def length_profile(count, total, limit, slope):
    portions = [(1 << 20) // math.isqrt(grade ** slope) + 1 for grade in range(2, count + 1)]
    surplus, holding = total - limit - (count - 1), [1] * (count - 1)
    while surplus > 0:
        movable = [i for i in range(count - 1) if holding[i] < limit]
        whole, left = sum([portions[i] for i in movable]), surplus
        for i in movable:
            extra = min(limit - holding[i], max(1, left * portions[i] // whole), surplus)
            holding[i] = holding[i] + extra
            surplus = surplus - extra
    return np.array([limit] + holding)


def ragged(key, count, total, bound, lean):
    if count == 2:
        one = jax.random.randint(key, (), max(1, total - bound), min(bound, total - 1) + 1)
        return jnp.stack([one, total - one])
    sizes = jnp.asarray(length_profile(count, total, bound, lean), jnp.int32)
    couples = (count - 1) // 2
    giver, taker = sizes[1:1 + 2 * couples:2], sizes[2:2 + 2 * couples:2]
    slack = jnp.minimum(giver - 1, bound - taker)
    shifted = jax.random.randint(jax.random.fold_in(key, 1), (couples,), 0, 1 << 20) % (slack + 1)
    sizes = sizes.at[1:1 + 2 * couples:2].set(giver - shifted).at[2:2 + 2 * couples:2].set(taker + shifted)
    return sizes[jax.random.permutation(jax.random.fold_in(key, 2), count)]


def assign_block(own_key, own, number, rows, amount, top, most, slope):
    order = jax.random.permutation(own_key, amount)
    packed, ordinary = load_shares(amount, rows * top, most, slope, True), load_shares(amount, rows * top, most, slope, False)
    places = jnp.arange(amount)

    def named(sizes, offset_by):
        used = int((sizes > 0).sum())
        fixed = max(1, used // 4)
        shifted = fixed + (places - fixed + offset_by * (used - fixed)) % max(1, amount - fixed)
        return jnp.zeros((amount,), jnp.int32).at[order[jnp.where(places < fixed, places, shifted)]].set(jnp.asarray(sizes, jnp.int32))

    sizes = jnp.where(number % 4 == 0, named(packed, number // 4), named(ordinary, number - number // 4 - 1))
    mixed = jax.random.permutation(jax.random.fold_in(own, 3), amount)
    giver, sink = mixed[0:amount // 2 * 2:2], mixed[1:amount // 2 * 2:2]
    slack = jnp.minimum(sizes[giver] - 1, most - sizes[sink]) // 2
    slack = jnp.where((giver == order[0]) | (sink == order[0]) | (sizes[sink] == 0), 0, jnp.maximum(slack, 0))
    shifted = jax.random.randint(jax.random.fold_in(own, 4), (amount // 2,), 0, 1 << 20) % (slack + 1)
    sizes = sizes.at[giver].add(-shifted).at[sink].add(shifted)
    members = jnp.searchsorted(jnp.cumsum(sizes), jnp.arange(rows * top), side="right").astype(jnp.int32)
    listing = members.reshape(top, rows).T
    listing = listing[jax.random.permutation(jax.random.fold_in(own, 1), rows)]
    offset_by = jax.random.randint(jax.random.fold_in(own, 2), (rows, 1), 0, top)
    return jnp.take_along_axis(listing, (jnp.arange(top)[None, :] + offset_by) % top, axis=1)


def load_shares(amount, total, most, slope, full):
    portions = [(1 << 20) // math.isqrt(grade ** slope) + 1 for grade in range(1, amount + 1)]
    largest = most if full else min(most, max(-(-total // amount), total * portions[0] // sum(portions)))
    least = 1 if total - largest >= amount - 1 else 0
    given, surplus = [largest] + [least] * (amount - 1), total - largest - least * (amount - 1)
    while surplus > 0:
        candidates = [i for i in range(1, amount) if given[i] < largest] or [i for i in range(1, amount) if given[i] < most]
        pool, budget = sum([portions[i] for i in candidates]), surplus
        for i in candidates:
            extra = min(most - given[i], max(1, budget * portions[i] // pool), surplus)
            given[i] = given[i] + extra
            surplus = surplus - extra
    return np.array(given)


def noise(stream_key, shape, scale, most, split=(), kind=jnp.bfloat16):
    values = scale * jax.random.normal(stream_key, shape, jnp.float32)
    if split:
        values = values * shard_levels(stream_key, shape, split, -0.22, 0.18)
    return jnp.clip(values, -most, most).astype(kind)


def gaussian_with(own_key, extent, scale, bound, split, heavy, kind=jnp.bfloat16):
    array = scale * jax.random.normal(own_key, extent, jnp.float32)
    if split:
        array = array * shard_levels(own_key, extent, split, -0.22, 0.18)
    return jnp.clip(raised(array, jax.random.fold_in(own_key, 3), *heavy), -bound, bound).astype(kind)


def setup_inputs(seed: int = 0) -> dict:
    key_of = jax.random.split(jax.random.key(seed), 11)
    tokens = noise(key_of[0], (TOKENS, D), 1.0, 6.0, ((0, 32),))
    seg_ids = jax.vmap(lambda own: jnp.searchsorted(jnp.cumsum(ragged(own, DOC_IDS, SEQ_LEN, DOC_MOST, 1)), jnp.arange(SEQ_LEN), side="right"))(jax.random.split(key_of[1], SEQS)).reshape((SEQS, SEQ_LEN)).astype(jnp.int32)
    routes_keys = jax.random.split(jax.random.fold_in(key_of[2], 1), TOKENS // TOK_DEV)
    routes_turns = jax.random.permutation(jax.random.fold_in(key_of[2], 3), TOKENS // TOK_DEV)
    routes = jax.vmap(lambda own, number: assign_block(jax.random.fold_in(key_of[2], 2), own, number, TOK_DEV, E, TOP, CAP, 2))(routes_keys, routes_turns).reshape((TOKENS, TOP))
    in_proj = noise(key_of[3], (D, HQ * HD + 2 * KV * HD), D ** -0.5, 0.15625, ((0, 8),))
    out_proj = noise(key_of[4], (D, HQ * HD), (HQ * HD // 16) ** -0.5, 0.625, ((0, 8),))
    router = noise(key_of[5], (D, E), (4 * D) ** -0.5, 0.078125, ((0, 8),))
    norm_gains = jnp.clip(1.0 + 0.1 * jax.random.normal(key_of[6], (D, 2), jnp.float32), 0.5, 1.5).astype(jnp.bfloat16)
    expert_in = noise(key_of[7], (D, E, 2 * F), D ** -0.5, 0.15625, ((0, 8),))
    expert_out = noise(key_of[8], (D, E, F), (F // 8) ** -0.5, 0.625, ((0, 8),))
    out_grad = gaussian_with(key_of[9], (TOKENS, D), 1.0, 6.0, ((0, 32),), (0, 1, 32, 2.75))
    return {"tokens": tokens, "seg_ids": seg_ids, "routes": routes, "in_proj": in_proj, "out_proj": out_proj, "router": router, "norm_gains": norm_gains, "expert_in": expert_in, "expert_out": expert_out, "out_grad": out_grad}


@jax.custom_vjp
def low(v):
    return lax.optimization_barrier(v.astype(jnp.bfloat16)).astype(jnp.float32)

@jax.custom_vjp
def low_back(v):
    return v

def low_keep(v):
    return (low(v), None)

def low_pass(kept, grad):
    return (grad,)

def back_keep(v):
    return (v, None)

def back_low(kept, grad):
    return (low(grad),)
low.defvjp(low_keep, low_pass)
low_back.defvjp(back_keep, back_low)
epsilon = 1e-06
rope_base = 1000000.0

def precise_dot(left, right):
    return jnp.dot(left, right, precision=lax.Precision.HIGHEST)

def rms_scale(v):
    return lax.rsqrt(lax.optimization_barrier(jnp.mean(v * v, axis=-1, keepdims=True)) + epsilon)

def tables(length):
    half = HD // 2
    freq = jnp.power(rope_base, -(jnp.arange(half, dtype=jnp.float32) * 2.0 / HD))
    angle = jnp.arange(length, dtype=jnp.float32)[:, None] * freq[None, :]
    return (jnp.cos(angle)[:, None, :], jnp.sin(angle)[:, None, :])

def rotate(v, cosine, sine):
    half = v.shape[-1] // 2
    first = v[..., :half]
    second = v[..., half:]
    return jnp.concatenate([first * cosine - second * sine, second * cosine + first * sine], axis=-1)

def attend(normed, segment, in_w, out_w, cosine, sine):
    length = normed.shape[0]
    group = HQ // KV
    width_q = HQ * HD
    width_k = KV * HD
    proj = low_back(precise_dot(normed, in_w))
    queries = low(rotate(proj[:, :width_q].reshape(length, HQ, HD), cosine, sine)).reshape(length, KV, group, HD)
    keys = low(rotate(proj[:, width_q:width_q + width_k].reshape(length, KV, HD), cosine, sine))
    values = low(proj[:, width_q + width_k:].reshape(length, KV, HD))
    scores = low_back(jnp.einsum('qkgd,tkd->kgqt', queries, keys, precision=lax.Precision.HIGHEST) * HD ** (-0.5))
    place = jnp.arange(length)
    allowed = (place[:, None] >= place[None, :]) & (segment[:, None] == segment[None, :])
    scores = jnp.where(allowed[None, None], scores, -1e+30)
    probs = low(jax.nn.softmax(scores, axis=-1))
    attn = jnp.einsum('kgqt,tkd->qkgd', probs, values, precision=lax.Precision.HIGHEST)
    attn = low_back(low(attn)).reshape(length, width_q)
    return low_back(jnp.einsum('sj,dj->sd', attn, out_w, precision=lax.Precision.HIGHEST))

def layer(block_x, weights, segs, route_ids, cosine, sine):
    in_w, out_w, router_w, gains_w, ein, eout = weights
    scale_one = rms_scale(block_x)
    normed = low(block_x * scale_one * gains_w[:, 0])
    attn_out = jax.vmap(lambda a, b: attend(a, b, in_w, out_w, cosine, sine))(normed, segs)
    first = block_x + attn_out
    flat = first.reshape(-1, D)
    normed_two = low(flat * rms_scale(flat) * gains_w[:, 1])
    logits = low_back(precise_dot(normed_two, router_w))
    onehot = (route_ids[:, :, None] == jnp.arange(E)[None, None, :]).astype(jnp.float32)
    chosen = lax.optimization_barrier(jnp.sum(onehot * logits[:, None, :], axis=-1))
    gates = jax.nn.softmax(chosen, axis=-1)
    weight_table = lax.optimization_barrier(jnp.sum(gates[:, :, None] * onehot, axis=1))
    gate_up = low_back(jnp.einsum('nd,def->nef', normed_two, ein, precision=lax.Precision.HIGHEST))
    hidden = low(jax.nn.silu(gate_up[..., :F]) * gate_up[..., F:])
    expert_y = low_back(low(jnp.einsum('nef,def->ned', hidden, eout, precision=lax.Precision.HIGHEST)))
    result = flat + jnp.einsum('ne,ned->nd', weight_table, expert_y, precision=lax.Precision.HIGHEST)
    return result.reshape(block_x.shape)

def reference(tokens, seg_ids, routes, in_proj, out_proj, router, norm_gains, expert_in, expert_out, out_grad):
    params = tuple((w.astype(jnp.float32) for w in (in_proj, out_proj, router, norm_gains, expert_in, expert_out)))
    cosine, sine = tables(SEQ_LEN)
    per_block = math.gcd(SEQS, max(1, 4096 // SEQ_LEN))
    blocks = SEQS // per_block
    inputs = tokens.astype(jnp.float32).reshape(blocks, per_block, SEQ_LEN, D)
    segments = seg_ids.reshape(blocks, per_block, SEQ_LEN)
    route_blocks = routes.reshape(blocks, per_block * SEQ_LEN, TOP)
    cotangent = out_grad.astype(jnp.float32).reshape(blocks, per_block, SEQ_LEN, D)

    def step(carry, block):
        block_x, block_seg, block_routes, block_cot = block
        result, pull = jax.vjp(lambda xv, *ws: layer(xv, ws, block_seg, block_routes, cosine, sine), block_x, *params)
        grads = pull(block_cot)
        summed = tuple((c + g for c, g in zip(carry, grads[1:])))
        return (summed, (result.astype(jnp.bfloat16), grads[0].astype(jnp.bfloat16)))
    start = tuple((jnp.zeros(p.shape, jnp.float32) for p in params))
    sums, (results, input_grads) = lax.scan(step, start, (inputs, segments, route_blocks, cotangent))
    return (results.reshape(TOKENS, D), input_grads.reshape(TOKENS, D), sums[0], sums[1], sums[2], sums[3], sums[4], sums[5])
```

```python
import functools

import jax
import jax.numpy as jnp
from jax import lax
from jax.experimental import pallas as pl
from jax.experimental.pallas import tpu as pltpu
from jax.sharding import PartitionSpec as P

HQ = 12
KV = 2
HD = 128
GROUP = HQ // KV
WQ = HQ * HD
WK = KV * HD
EXTRA = 128
MIB = 1024 * 1024

epsilon = 1e-06
rope_base = 1000000.0
bf16 = jnp.bfloat16
f32 = jnp.float32


def rms_scale(v):
    return lax.rsqrt(jnp.mean(v * v, axis=-1, keepdims=True) + epsilon)


def tables(length):
    half = HD // 2
    freq = jnp.power(rope_base, -(jnp.arange(half, dtype=f32) * 2.0 / HD))
    angle = jnp.arange(length, dtype=f32)[:, None] * freq[None, :]
    return (jnp.cos(angle)[:, None, :], jnp.sin(angle)[:, None, :])


def rotate(v, cosine, sine):
    half = v.shape[-1] // 2
    first = v[..., :half]
    second = v[..., half:]
    return jnp.concatenate(
        [first * cosine - second * sine, second * cosine + first * sine], axis=-1
    )


def contract_rows(left, right):
    return lax.dot_general(left, right, (((0,), (0,)), ((), ())), preferred_element_type=f32)


def contract_cols(left, right):
    return lax.dot_general(left, right, (((1,), (1,)), ((), ())), preferred_element_type=f32)


def matmul(left, right):
    return lax.dot_general(left, right, (((1,), (0,)), ((), ())), preferred_element_type=f32)


class Links:
    def __init__(self, n_rep, n_fsdp):
        self.n_rep, self.n_fsdp = n_rep, n_fsdp

    def swap(self, value, d_rep, d_fsdp):
        pairs = [
            (r * self.n_fsdp + f, (r ^ d_rep) * self.n_fsdp + (f ^ d_fsdp))
            for r in range(self.n_rep)
            for f in range(self.n_fsdp)
        ]
        return lax.ppermute(value, ("replica", "fsdp"), pairs)


def place_kernel(n_src, rows, *refs):
    out = refs[n_src]
    sem = refs[n_src + 1]
    me_f = lax.axis_index("fsdp")
    me_r = lax.axis_index("replica")
    copies = []
    slot = 0
    for n, (src, layout) in enumerate(zip(refs[:n_src], PIECES)):
        for i, (j, k) in enumerate(layout):
            owner = jnp.bitwise_xor(me_f, j)
            if k is None:
                start, size = owner * (4 * rows), 4 * rows
            else:
                start = owner * (4 * rows) + jnp.bitwise_xor(me_r, k) * rows
                size = rows
            copy = pltpu.make_async_copy(
                src.at[pl.ds(i * rows, size)],
                out.at[pl.ds(pl.multiple_of(start, rows), size)],
                sem.at[slot],
            )
            copy.start()
            copies.append(copy)
            slot += 1
    for copy in copies:
        copy.wait()


PIECES = [
    [(0, None)],
    [(2, 0), (4, 0), (6, 0)],
    [(2, 2), (4, 2), (6, 2)],
    [(2, 1), (4, 1), (6, 1), (2, 3), (4, 3), (6, 3)],
    [(1, 0), (3, 0), (5, 0), (7, 0)],
    [(1, 2), (3, 2), (5, 2), (7, 2)],
    [(1, 1), (3, 1), (5, 1), (7, 1), (1, 3), (3, 3), (5, 3), (7, 3)],
]


def gather_dense(links, shard, me_r):
    rows = shard.shape[0] // 4
    quarter = lax.dynamic_slice_in_dim(shard, me_r * rows, rows, 0)
    z = [links.swap(quarter, 0, j) for j in (2, 4, 6)]
    zs = jnp.concatenate(z, 0)
    ys = links.swap(jnp.concatenate([quarter] + z, 0), 0, 1)
    zx = links.swap(zs, 2, 0)
    yx = links.swap(ys, 2, 0)
    zc = links.swap(jnp.concatenate([zs, zx], 0), 1, 0)
    yc = links.swap(jnp.concatenate([ys, yx], 0), 1, 0)
    pieces = [shard, zs, zx, zc, ys, yx, yc]
    count = sum(len(p) for p in PIECES)
    full = pl.pallas_call(
        functools.partial(place_kernel, len(pieces), rows),
        out_shape=jax.ShapeDtypeStruct((8 * shard.shape[0], shard.shape[1]), shard.dtype),
        in_specs=[pl.BlockSpec(memory_space=pl.ANY)] * len(pieces),
        out_specs=pl.BlockSpec(memory_space=pltpu.VMEM),
        scratch_shapes=[pltpu.SemaphoreType.DMA((count,))],
        compiler_params=pltpu.CompilerParams(vmem_limit_bytes=20 * MIB),
        name="place",
    )(*pieces)
    return full


def expert_kernel(nt, nw, length, width, hidden, rows, expert_of, offset_of, *refs):
    xs, gs, ws = refs[:nt], refs[nt : 2 * nt], refs[2 * nt : 2 * nt + nw]
    refs = refs[2 * nt + nw :]
    mixes, dxs, grads = refs[:nt], refs[nt : 2 * nt], refs[2 * nt : 2 * nt + nw]
    (
        wbuf, xbuf, gbuf, xt, gt_, hidg, dgu, mbuf, dbuf, acc, stage,
        sem_w, sem_x, sem_g, sem_m, sem_d, sem_s,
    ) = refs[2 * nt + nw :]
    cols = 3 * hidden
    step_cols = 256

    def load(k, slot):
        for i in range(nt):

            @pl.when(k == i)
            def _():
                pltpu.make_async_copy(xs[i], xbuf.at[slot], sem_x.at[slot]).start()
                pltpu.make_async_copy(gs[i], gbuf.at[slot], sem_g.at[slot]).start()

    def store(k, slot):
        for i in range(nt):

            @pl.when(k == i)
            def _():
                pltpu.make_async_copy(mbuf.at[slot], mixes[i], sem_m.at[slot]).start()
                pltpu.make_async_copy(dbuf.at[slot], dxs[i], sem_d.at[slot]).start()

    def stored(slot):
        pltpu.make_async_copy(mbuf.at[slot], mixes[0], sem_m.at[slot]).wait()
        pltpu.make_async_copy(dbuf.at[slot], dxs[0], sem_d.at[slot]).wait()

    for j in range(nw):
        pltpu.make_async_copy(
            ws[j], wbuf.at[pl.ds(pl.multiple_of(offset_of(j), 8), rows)], sem_w.at[j]
        ).start()
    load(0, 0)
    expert = expert_of()
    acc[...] = jnp.zeros_like(acc)
    lane = lax.broadcasted_iota(jnp.int32, (length, EXTRA), 1)
    for j in range(nw):
        pltpu.make_async_copy(
            ws[j], wbuf.at[pl.ds(pl.multiple_of(offset_of(j), 8), rows)], sem_w.at[j]
        ).wait()

    def block(k, carry):
        slot = lax.rem(k, 2)

        @pl.when(k + 1 < nt)
        def _():
            load(k + 1, 1 - slot)

        pltpu.make_async_copy(xs[0], xbuf.at[slot], sem_x.at[slot]).wait()
        pltpu.make_async_copy(gs[0], gbuf.at[slot], sem_g.at[slot]).wait()

        @pl.when(k >= 2)
        def _():
            stored(slot)

        extra = xbuf[slot, :, width:].astype(f32)
        mine = (lane == expert) | (lane == expert + 8)
        gate = jnp.sum(jnp.where(mine, extra, 0.0), axis=1, keepdims=True)
        xt[...] = xbuf[slot, :, :width].T
        gt_[...] = gbuf[slot].T

        def first(c, dgate):
            at = pl.multiple_of(c * step_cols, step_cols)
            u = matmul(xbuf[slot, :, :width], wbuf[:, pl.ds(at, step_cols)])
            up = matmul(xbuf[slot, :, :width], wbuf[:, pl.ds(hidden + at, step_cols)])
            back = matmul(gbuf[slot], wbuf[:, pl.ds(2 * hidden + at, step_cols)])
            sig = 1.0 / (1.0 + jnp.exp(-u))
            act = u * sig
            hid = act * up
            hidg[:, pl.ds(at, step_cols)] = (gate * hid).astype(bf16)
            dgate = dgate + jnp.sum(back * hid, axis=1, keepdims=True)
            dhid = gate * back
            dgu[:, pl.ds(at, step_cols)] = (
                dhid * up * sig * (1.0 + u * (1.0 - sig))
            ).astype(bf16)
            dgu[:, pl.ds(hidden + at, step_cols)] = (dhid * act).astype(bf16)
            return dgate

        dgate = lax.fori_loop(
            0, hidden // step_cols, first, jnp.zeros((length, 1), f32)
        )

        def second(c, carry):
            at = pl.multiple_of(c * step_cols, step_cols)
            mbuf[slot, :, pl.ds(at, step_cols)] = contract_cols(
                hidg[...], wbuf[pl.ds(at, step_cols), pl.ds(2 * hidden, hidden)]
            ).astype(bf16)
            dbuf[slot, :, pl.ds(at, step_cols)] = contract_cols(
                dgu[...], wbuf[pl.ds(at, step_cols), pl.ds(0, 2 * hidden)]
            ).astype(bf16)
            return carry

        lax.fori_loop(0, width // step_cols, second, 0)
        high = dgate.astype(bf16).astype(f32)
        low = dgate - high
        dbuf[slot, :, width:] = (
            jnp.where(lane == expert, high, 0.0) + jnp.where(lane == expert + 8, low, 0.0)
        ).astype(bf16)
        store(k, slot)

        def third(c, carry):
            at = pl.multiple_of(c * step_cols, step_cols)
            acc[:, pl.ds(at, step_cols)] += matmul(xt[...], dgu[:, pl.ds(at, step_cols)])
            return carry

        lax.fori_loop(0, 2 * hidden // step_cols, third, 0)

        def fourth(c, carry):
            at = pl.multiple_of(c * step_cols, step_cols)
            acc[:, pl.ds(2 * hidden + at, step_cols)] += matmul(
                gt_[...], hidg[:, pl.ds(at, step_cols)]
            )
            return carry

        lax.fori_loop(0, hidden // step_cols, fourth, 0)
        return carry

    lax.fori_loop(0, nt, block, 0)
    stored(0)
    stored(1)
    for j in range(nw):
        slot = j % 2
        if j >= 2:
            pltpu.make_async_copy(stage.at[slot], grads[j - 2], sem_s.at[slot]).wait()
        stage[slot] = acc[pl.ds(pl.multiple_of(offset_of(j), 8), rows)].astype(bf16)
        pltpu.make_async_copy(stage.at[slot], grads[j], sem_s.at[slot]).start()
    for j in range(max(0, nw - 2), nw):
        pltpu.make_async_copy(stage.at[j % 2], grads[j], sem_s.at[j % 2]).wait()


def run_expert(xs, gs, ws, expert_of, offset_of):
    nt, nw = len(xs), len(ws)
    length, width = gs[0].shape
    rows, cols = ws[0].shape
    hidden = cols // 3
    outs = (
        [jax.ShapeDtypeStruct((length, width), bf16)] * nt
        + [jax.ShapeDtypeStruct((length, width + EXTRA), bf16)] * nt
        + [jax.ShapeDtypeStruct((rows, cols), bf16)] * nw
    )
    any_spec = pl.BlockSpec(memory_space=pl.ANY)
    result = pl.pallas_call(
        functools.partial(
            expert_kernel, nt, nw, length, width, hidden, rows, expert_of, offset_of
        ),
        out_shape=outs,
        in_specs=[any_spec] * (2 * nt + nw),
        out_specs=[any_spec] * len(outs),
        scratch_shapes=[
            pltpu.VMEM((width, cols), bf16),
            pltpu.VMEM((2, length, width + EXTRA), bf16),
            pltpu.VMEM((2, length, width), bf16),
            pltpu.VMEM((width, length), bf16),
            pltpu.VMEM((width, length), bf16),
            pltpu.VMEM((length, hidden), bf16),
            pltpu.VMEM((length, 2 * hidden), bf16),
            pltpu.VMEM((2, length, width), bf16),
            pltpu.VMEM((2, length, width + EXTRA), bf16),
            pltpu.VMEM((width, cols), f32),
            pltpu.VMEM((2, rows, cols), bf16),
            pltpu.SemaphoreType.DMA((nw,)),
            pltpu.SemaphoreType.DMA((2,)),
            pltpu.SemaphoreType.DMA((2,)),
            pltpu.SemaphoreType.DMA((2,)),
            pltpu.SemaphoreType.DMA((2,)),
            pltpu.SemaphoreType.DMA((2,)),
        ],
        compiler_params=pltpu.CompilerParams(vmem_limit_bytes=60 * MIB),
        cost_estimate=pl.CostEstimate(
            flops=6 * nt * length * width * cols,
            bytes_accessed=8 * nt * length * width + 4 * width * cols,
            transcendentals=nt * length * hidden,
        ),
        name="expert",
    )(*xs, *gs, *ws)
    return result[:nt], result[nt : 2 * nt], result[2 * nt :]


class Near:
    group = ((0, 0), (1, 0), (2, 0), (3, 0), (0, 2), (1, 2), (2, 2), (3, 2))

    def __init__(self, n_rep, n_fsdp):
        self.links = Links(n_rep, n_fsdp)
        self.swap = self.links.swap

    def dense(self, shard):
        return gather_dense(self.links, shard, lax.axis_index("replica"))

    def small(self, shard):
        f = lax.axis_index("fsdp")
        got = shard[None]
        for bit in (1, 2, 4):
            other = self.swap(got, 0, bit)
            up = (f & bit) != 0
            got = jnp.concatenate(
                [jnp.where(up, other, got), jnp.where(up, got, other)], axis=0
            )
        return got

    def sum_all(self, value):
        for d in ((1, 0), (0, 1), (2, 0), (0, 2), (0, 4)):
            value = value + self.swap(value, *d)
        return value

    def spread(self, value):
        half = value.shape[0] // 2
        over_x = self.swap(value, 2, 0)
        over_z = self.swap(value, 0, 2)
        far = jnp.concatenate(
            [self.swap(over_z[:half], 2, 0), self.swap(over_x[half:], 0, 2)], axis=0
        )
        near = [value, over_x, over_z, far]
        cores = [self.swap(v, 1, 0) for v in near]
        return [near[0], cores[0], near[1], cores[1], near[2], cores[2], near[3], cores[3]]

    def collect(self, parts):
        sums = [
            (parts[k].astype(f32) + self.swap(parts[k + 1], 1, 0).astype(f32)).astype(bf16)
            for k in (0, 2, 4, 6)
        ]
        cut = sums[0].shape[0] // 2
        a = [s[:cut] for s in sums]
        b = [s[cut:] for s in sums]

        def add(u, v):
            return u.astype(f32) + v.astype(f32)

        a0 = add(a[0], self.swap(a[1], 2, 0))
        a2 = add(a[2], self.swap(a[3], 2, 0)).astype(bf16)
        b0 = add(b[0], self.swap(b[2], 0, 2))
        b1 = add(b[1], self.swap(b[3], 0, 2)).astype(bf16)
        a0 = a0 + self.swap(a2, 0, 2).astype(f32)
        b0 = b0 + self.swap(b1, 2, 0).astype(f32)
        return jnp.concatenate([a0, b0], axis=0)

    def expert_weights(self, expert_in, expert_out):
        r, f = lax.axis_index("replica"), lax.axis_index("fsdp")
        low = (f >> 1) & 1
        mine, other = [
            jnp.concatenate(
                [
                    lax.dynamic_index_in_dim(expert_in, e, 1, keepdims=False),
                    lax.dynamic_index_in_dim(expert_out, e, 1, keepdims=False),
                ],
                axis=1,
            )
            for e in (2 * r + low, 2 * r + 1 - low)
        ]
        blocks = {0: mine}
        blocks[2] = self.swap(other, 0, 2)
        blocks[4] = self.swap(mine, 0, 4)
        blocks[6] = self.swap(other, 0, 6)
        for j in (0, 2, 4, 6):
            blocks[j + 1] = self.swap(blocks[j], 0, 1)
        return [blocks[j] for j in range(8)]

    def experts(self, xs, gs, weights):
        rows = weights[0].shape[0]

        def expert_of():
            return 2 * lax.axis_index("replica") + lax.rem(lax.axis_index("fsdp") // 2, 2)

        def offset_of(j):
            return jnp.bitwise_xor(lax.axis_index("fsdp"), j) * rows

        return run_expert(xs, gs, weights, expert_of, offset_of)

    def expert_sums(self, grads):
        f = lax.axis_index("fsdp")
        r = lax.axis_index("replica")

        def add(u, v):
            return (u.astype(f32) + v.astype(f32)).astype(bf16)

        held = {j: add(grads[j], self.swap(grads[j + 1], 0, 1)) for j in (0, 2, 4, 6)}
        mine = add(held[0], self.swap(held[4], 0, 4))
        other = add(self.swap(held[2], 0, 2), self.swap(held[6], 0, 6))
        low = ((f >> 1) & 1) == 0
        pair = jnp.stack([jnp.where(low, mine, other), jnp.where(low, other, mine)])
        core = (r & 1) == 0
        peer = self.swap(pair, 1, 0)
        four = jnp.concatenate([jnp.where(core, pair, peer), jnp.where(core, peer, pair)])
        side = (r & 2) == 0
        far = self.swap(four, 2, 0)
        return jnp.concatenate([jnp.where(side, four, far), jnp.where(side, far, four)])

    def spread_quad(self, value):
        return [value] + [self.swap(value, k, 0) for k in (1, 2, 3)]

    def trade_quad(self, value):
        r = lax.axis_index("replica")
        width = value.shape[1] // 4
        return [
            (lambda part: part if k == 0 else self.swap(part, k, 0))(
                lax.dynamic_slice_in_dim(value, (r ^ k) * width, width, 1)
            )
            for k in range(4)
        ]

    def dense_sum(self, quarter):
        f = lax.axis_index("fsdp")
        r = lax.axis_index("replica")
        rows = quarter.shape[0] // 8
        blocks = [
            lax.dynamic_slice_in_dim(quarter, (f ^ j) * rows, rows, 0).astype(bf16)
            for j in range(8)
        ]

        def add(u, v):
            return (u.astype(f32) + v.astype(f32)).astype(bf16)

        got = self.swap(jnp.stack([blocks[j + 1] for j in (0, 2, 4, 6)]), 0, 1)
        held = {j: add(blocks[j], got[j // 2]) for j in (0, 2, 4, 6)}
        total = held[0].astype(f32)
        for j in (2, 4, 6):
            total = total + self.swap(held[j], 0, j).astype(f32)
        total = total.astype(bf16)
        core = (r & 1) == 0
        peer = self.swap(total, 1, 0)
        two = jnp.concatenate(
            [jnp.where(core, total, peer), jnp.where(core, peer, total)], axis=1
        )
        side = (r & 2) == 0
        far = self.swap(two, 2, 0)
        return jnp.concatenate([jnp.where(side, two, far), jnp.where(side, far, two)], axis=1)


class Wide:
    def __init__(self, n_rep, n_fsdp):
        self.n_rep, self.n_fsdp = n_rep, n_fsdp

    def dense(self, shard):
        return lax.all_gather(shard, "fsdp", axis=0, tiled=True)

    def small(self, shard):
        return lax.all_gather(shard, "fsdp", axis=0)

    def sum_all(self, value):
        return lax.psum(value, ("replica", "fsdp"))

    def spread(self, value):
        every = lax.all_gather(value, "replica", axis=0)
        return [every[k] for k in range(self.n_rep)]

    def collect(self, parts):
        return lax.psum_scatter(jnp.stack(parts), "replica", scatter_dimension=0).astype(f32)

    def expert_weights(self, expert_in, expert_out):
        r = lax.axis_index("replica")
        per = expert_in.shape[1] // self.n_rep
        out = []
        for i in range(per):
            both = jnp.concatenate(
                [
                    lax.dynamic_index_in_dim(expert_in, per * r + i, 1, keepdims=False),
                    lax.dynamic_index_in_dim(expert_out, per * r + i, 1, keepdims=False),
                ],
                axis=1,
            )
            out.append(lax.all_gather(both, "fsdp", axis=0, tiled=True))
        return out

    def experts(self, xs, gs, weights):
        per = len(weights)
        mixes, dxs, grads = None, None, []
        for i, w in enumerate(weights):

            def expert_of(i=i):
                return per * lax.axis_index("replica") + i

            mix, dx, grad = run_expert(xs, gs, [w], expert_of, lambda j: 0)
            mixes = mix if mixes is None else [a + b for a, b in zip(mixes, mix)]
            dxs = dx if dxs is None else [a + b for a, b in zip(dxs, dx)]
            grads.append(grad[0])
        return mixes, dxs, grads

    def expert_sums(self, grads):
        own = jnp.stack(
            [lax.psum_scatter(g, "fsdp", scatter_dimension=0, tiled=True) for g in grads]
        )
        return lax.all_gather(own, "replica", axis=0, tiled=True)

    def spread_quad(self, value):
        every = lax.all_gather(value, "replica", axis=0)
        return [every[k] for k in range(self.n_rep)]

    def trade_quad(self, value):
        cut = value.reshape(value.shape[0], self.n_rep, -1).transpose(1, 0, 2)
        got = lax.all_to_all(cut, "replica", 0, 0)
        return [got[k] for k in range(self.n_rep)]

    def dense_sum(self, quarter):
        own = lax.psum_scatter(quarter.astype(bf16), "fsdp", scatter_dimension=0, tiled=True)
        return lax.all_gather(own, "replica", axis=1, tiled=True)


def layer(
    net, tokens, seg_ids, routes, in_proj, out_proj, router, norm_gains, expert_in, expert_out,
    out_grad,
):
    length, width = tokens.shape
    experts = router.shape[1]
    hidden = expert_out.shape[2]
    shard = router.shape[0]
    scale = HD ** (-0.5)
    cosine, sine = tables(length)
    segment = seg_ids[0]
    place = jnp.arange(length)
    allowed = ((place[:, None] >= place[None, :]) & (segment[:, None] == segment[None, :]))[
        None, None
    ]
    tiny = jnp.concatenate(
        [router.T, norm_gains.T, jnp.zeros((16 - experts - 2, shard), bf16)], axis=0
    )
    tiny = net.small(tiny).transpose(1, 0, 2).reshape(16, width)
    router_rows = tiny[:experts]
    gain_one = tiny[experts].astype(f32)
    gain_two = tiny[experts + 1].astype(f32)
    proj_in = net.dense(in_proj)
    out_proj, proj_in = lax.optimization_barrier((out_proj, proj_in))
    proj_out = net.dense(out_proj)
    expert_in, expert_out, out_grad_sent, _ = lax.optimization_barrier(
        (expert_in, expert_out, out_grad, proj_out)
    )
    weights = net.expert_weights(expert_in, expert_out)
    gs = net.spread(out_grad_sent)

    inputs = tokens.astype(f32)
    scale_one = rms_scale(inputs)
    unit_one = inputs * scale_one
    normed = (unit_one * gain_one).astype(bf16)
    proj = matmul(normed, proj_in)
    queries = (
        rotate(proj[:, :WQ].reshape(length, HQ, HD), cosine, sine)
        .astype(bf16)
        .reshape(length, KV, GROUP, HD)
    )
    keys = rotate(proj[:, WQ : WQ + WK].reshape(length, KV, HD), cosine, sine).astype(bf16)
    values = proj[:, WQ + WK :].reshape(length, KV, HD).astype(bf16)
    scores = jnp.einsum("qkgd,tkd->kgqt", queries, keys, preferred_element_type=f32) * scale
    masked = jnp.where(allowed, scores, -1e30)
    highest = jnp.max(masked, axis=-1, keepdims=True)
    expo = jnp.exp(masked - highest)
    total = jnp.sum(expo, axis=-1, keepdims=True)
    log_total = highest + jnp.log(total)
    probs_low = (expo / total).astype(bf16)
    attn = jnp.einsum("kgqt,tkd->qkgd", probs_low, values, preferred_element_type=f32)
    attn = attn.astype(bf16).reshape(length, WQ)
    first = inputs + contract_cols(attn, proj_out)
    scale_two = rms_scale(first)
    unit_two = first * scale_two
    normed_two = (unit_two * gain_two).astype(bf16)
    logits = contract_cols(normed_two, router_rows)
    onehot = (routes[:, :, None] == jnp.arange(experts)[None, None, :]).astype(f32)
    chosen = jnp.sum(onehot * logits[:, None, :], axis=-1)
    gates = jax.nn.softmax(chosen, axis=-1)
    table = jnp.sum(gates[:, :, None] * onehot, axis=1)
    high = table.astype(bf16)
    low = (table - high.astype(f32)).astype(bf16)
    payload = jnp.concatenate(
        [normed_two, high, low, jnp.zeros((length, EXTRA - 2 * experts), bf16)], axis=1
    )
    xs = net.spread(payload)
    mixes, dxs, grads = net.experts(xs, gs, weights)
    dx = net.collect(dxs)
    mixed = (first + net.collect(mixes)).astype(bf16)

    grad_out = out_grad.astype(f32)
    dgate_all = dx[:, width : width + experts] + dx[:, width + experts : width + 2 * experts]
    dgate = jnp.sum(onehot * dgate_all[:, None, :], axis=-1)
    dchosen = gates * (dgate - jnp.sum(gates * dgate, axis=-1, keepdims=True))
    dlogits = jnp.sum(dchosen[:, :, None] * onehot, axis=1).astype(bf16)
    dnormed_two = dx[:, :width] + matmul(dlogits, router_rows)
    gain_two_grad = jnp.sum(dnormed_two * unit_two, axis=0)
    dunit_two = dnormed_two * gain_two
    dfirst = grad_out + scale_two * (
        dunit_two - unit_two * jnp.mean(dunit_two * unit_two, axis=-1, keepdims=True)
    )
    dres = dfirst.astype(bf16)
    dattn = matmul(dres, proj_out).astype(bf16).reshape(length, KV, GROUP, HD)
    probs = jnp.exp(masked - log_total)
    probs_again = probs.astype(bf16)
    dprobs = jnp.einsum("qkgd,tkd->kgqt", dattn, values, preferred_element_type=f32)
    dvalues = jnp.einsum("kgqt,qkgd->tkd", probs_again, dattn, preferred_element_type=f32)
    delta = jnp.sum(probs * dprobs, axis=-1, keepdims=True)
    dscores = (probs * (dprobs - delta)).astype(bf16)
    dqueries = jnp.einsum("kgqt,tkd->qkgd", dscores, keys, preferred_element_type=f32) * scale
    dkeys = jnp.einsum("kgqt,qkgd->tkd", dscores, queries, preferred_element_type=f32) * scale
    dqueries = rotate(dqueries.reshape(length, HQ, HD), cosine, -sine).reshape(length, WQ)
    dkeys = rotate(dkeys, cosine, -sine).reshape(length, WK)
    dproj = jnp.concatenate([dqueries, dkeys, dvalues.reshape(length, WK)], axis=1).astype(bf16)
    dnormed = contract_cols(dproj, proj_in)
    gain_one_grad = jnp.sum(dnormed * unit_one, axis=0)
    dunit_one = dnormed * gain_one
    tokens_grad = (
        dfirst
        + scale_one
        * (dunit_one - unit_one * jnp.mean(dunit_one * unit_one, axis=-1, keepdims=True))
    ).astype(bf16)

    expert_sum = net.expert_sums(grads).transpose(1, 0, 2)
    all_normed = jnp.concatenate(net.spread_quad(normed), axis=0)
    part_attn = jnp.concatenate(net.trade_quad(attn), axis=0)
    all_dres = jnp.concatenate(net.spread_quad(dres), axis=0)
    out_proj_grad = net.dense_sum(contract_rows(all_dres, part_attn)).astype(f32)
    part_dproj = jnp.concatenate(net.trade_quad(dproj), axis=0)
    in_proj_grad = net.dense_sum(contract_rows(all_normed, part_dproj)).astype(f32)

    terms = jnp.concatenate(
        [
            contract_rows(dlogits, normed_two),
            gain_one_grad[None],
            gain_two_grad[None],
            jnp.zeros((16 - experts - 2, width), f32),
        ],
        axis=0,
    )
    terms = lax.dynamic_slice_in_dim(
        net.sum_all(terms), lax.axis_index("fsdp") * shard, shard, 1
    ).T
    return (
        mixed,
        tokens_grad,
        in_proj_grad,
        out_proj_grad,
        terms[:, :experts],
        terms[:, experts : experts + 2],
        expert_sum[..., : 2 * hidden].astype(f32),
        expert_sum[..., 2 * hidden :].astype(f32),
    )


def solution(mesh):
    n_rep, n_fsdp = mesh.shape["replica"], mesh.shape["fsdp"]
    net = Near(n_rep, n_fsdp) if (n_rep, n_fsdp) == (4, 8) else Wide(n_rep, n_fsdp)
    both = P(("replica", "fsdp"), None)
    fsdp, deep = P("fsdp", None), P("fsdp", None, None)
    return jax.shard_map(
        functools.partial(layer, net),
        mesh=mesh,
        in_specs=(both, both, both, fsdp, fsdp, fsdp, fsdp, deep, deep, both),
        out_specs=(both, both, fsdp, fsdp, fsdp, fsdp, deep, deep),
        check_vma=False,
    )
```

```python
import functools

import jax
import jax.numpy as jnp
from jax import lax
from jax.experimental import pallas as pl
from jax.experimental.pallas import tpu as pltpu
from jax.sharding import PartitionSpec as P

HQ = 12
KV = 2
HD = 128
GROUP = HQ // KV
WQ = HQ * HD
WK = KV * HD
EXTRA = 128
MIB = 1024 * 1024

epsilon = 1e-06
rope_base = 1000000.0
bf16 = jnp.bfloat16
f32 = jnp.float32


def rms_scale(v):
    return lax.rsqrt(jnp.mean(v * v, axis=-1, keepdims=True) + epsilon)


def tables(length):
    half = HD // 2
    freq = jnp.power(rope_base, -(jnp.arange(half, dtype=f32) * 2.0 / HD))
    angle = jnp.arange(length, dtype=f32)[:, None] * freq[None, :]
    return (jnp.cos(angle)[:, None, :], jnp.sin(angle)[:, None, :])


def rotate(v, cosine, sine):
    half = v.shape[-1] // 2
    first = v[..., :half]
    second = v[..., half:]
    return jnp.concatenate(
        [first * cosine - second * sine, second * cosine + first * sine], axis=-1
    )


def contract_rows(left, right):
    return lax.dot_general(left, right, (((0,), (0,)), ((), ())), preferred_element_type=f32)


def contract_cols(left, right):
    return lax.dot_general(left, right, (((1,), (1,)), ((), ())), preferred_element_type=f32)


def matmul(left, right):
    return lax.dot_general(left, right, (((1,), (0,)), ((), ())), preferred_element_type=f32)


def expert_kernel(nt, nw, length, width, hidden, rows, expert_of, offset_of, *refs):
    xs, gs, ws = refs[:nt], refs[nt : 2 * nt], refs[2 * nt : 2 * nt + nw]
    refs = refs[2 * nt + nw :]
    mixes, dxs, grads = refs[:nt], refs[nt : 2 * nt], refs[2 * nt : 2 * nt + nw]
    (
        wbuf, xbuf, gbuf, xt, gt_, hidg, dgu, mbuf, dbuf, acc, stage,
        sem_w, sem_x, sem_g, sem_m, sem_d, sem_s,
    ) = refs[2 * nt + nw :]
    cols = 3 * hidden
    step_cols = 256

    def load(k, slot):
        for i in range(nt):

            @pl.when(k == i)
            def _():
                pltpu.make_async_copy(xs[i], xbuf.at[slot], sem_x.at[slot]).start()
                pltpu.make_async_copy(gs[i], gbuf.at[slot], sem_g.at[slot]).start()

    def store(k, slot):
        for i in range(nt):

            @pl.when(k == i)
            def _():
                pltpu.make_async_copy(mbuf.at[slot], mixes[i], sem_m.at[slot]).start()
                pltpu.make_async_copy(dbuf.at[slot], dxs[i], sem_d.at[slot]).start()

    def stored(slot):
        pltpu.make_async_copy(mbuf.at[slot], mixes[0], sem_m.at[slot]).wait()
        pltpu.make_async_copy(dbuf.at[slot], dxs[0], sem_d.at[slot]).wait()

    for j in range(nw):
        pltpu.make_async_copy(
            ws[j], wbuf.at[pl.ds(pl.multiple_of(offset_of(j), 8), rows)], sem_w.at[j]
        ).start()
    load(0, 0)
    expert = expert_of()
    acc[...] = jnp.zeros_like(acc)
    lane = lax.broadcasted_iota(jnp.int32, (length, EXTRA), 1)
    for j in range(nw):
        pltpu.make_async_copy(
            ws[j], wbuf.at[pl.ds(pl.multiple_of(offset_of(j), 8), rows)], sem_w.at[j]
        ).wait()

    def block(k, carry):
        slot = lax.rem(k, 2)

        @pl.when(k + 1 < nt)
        def _():
            load(k + 1, 1 - slot)

        pltpu.make_async_copy(xs[0], xbuf.at[slot], sem_x.at[slot]).wait()
        pltpu.make_async_copy(gs[0], gbuf.at[slot], sem_g.at[slot]).wait()

        @pl.when(k >= 2)
        def _():
            stored(slot)

        extra = xbuf[slot, :, width:].astype(f32)
        mine = (lane == expert) | (lane == expert + 8)
        gate = jnp.sum(jnp.where(mine, extra, 0.0), axis=1, keepdims=True)
        xt[...] = xbuf[slot, :, :width].T
        gt_[...] = gbuf[slot].T

        def first(c, dgate):
            at = pl.multiple_of(c * step_cols, step_cols)
            u = matmul(xbuf[slot, :, :width], wbuf[:, pl.ds(at, step_cols)])
            up = matmul(xbuf[slot, :, :width], wbuf[:, pl.ds(hidden + at, step_cols)])
            back = matmul(gbuf[slot], wbuf[:, pl.ds(2 * hidden + at, step_cols)])
            sig = 1.0 / (1.0 + jnp.exp(-u))
            act = u * sig
            hid = act * up
            hidg[:, pl.ds(at, step_cols)] = (gate * hid).astype(bf16)
            dgate = dgate + jnp.sum(back * hid, axis=1, keepdims=True)
            dhid = gate * back
            dgu[:, pl.ds(at, step_cols)] = (
                dhid * up * sig * (1.0 + u * (1.0 - sig))
            ).astype(bf16)
            dgu[:, pl.ds(hidden + at, step_cols)] = (dhid * act).astype(bf16)
            return dgate

        dgate = lax.fori_loop(
            0, hidden // step_cols, first, jnp.zeros((length, 1), f32)
        )

        def second(c, carry):
            at = pl.multiple_of(c * step_cols, step_cols)
            mbuf[slot, :, pl.ds(at, step_cols)] = contract_cols(
                hidg[...], wbuf[pl.ds(at, step_cols), pl.ds(2 * hidden, hidden)]
            ).astype(bf16)
            dbuf[slot, :, pl.ds(at, step_cols)] = contract_cols(
                dgu[...], wbuf[pl.ds(at, step_cols), pl.ds(0, 2 * hidden)]
            ).astype(bf16)
            return carry

        lax.fori_loop(0, width // step_cols, second, 0)
        high = dgate.astype(bf16).astype(f32)
        low = dgate - high
        dbuf[slot, :, width:] = (
            jnp.where(lane == expert, high, 0.0) + jnp.where(lane == expert + 8, low, 0.0)
        ).astype(bf16)
        store(k, slot)

        def third(c, carry):
            at = pl.multiple_of(c * step_cols, step_cols)
            acc[:, pl.ds(at, step_cols)] += matmul(xt[...], dgu[:, pl.ds(at, step_cols)])
            return carry

        lax.fori_loop(0, 2 * hidden // step_cols, third, 0)

        def fourth(c, carry):
            at = pl.multiple_of(c * step_cols, step_cols)
            acc[:, pl.ds(2 * hidden + at, step_cols)] += matmul(
                gt_[...], hidg[:, pl.ds(at, step_cols)]
            )
            return carry

        lax.fori_loop(0, hidden // step_cols, fourth, 0)
        return carry

    lax.fori_loop(0, nt, block, 0)
    stored(0)
    stored(1)
    for j in range(nw):
        slot = j % 2
        if j >= 2:
            pltpu.make_async_copy(stage.at[slot], grads[j - 2], sem_s.at[slot]).wait()
        stage[slot] = acc[pl.ds(pl.multiple_of(offset_of(j), 8), rows)].astype(bf16)
        pltpu.make_async_copy(stage.at[slot], grads[j], sem_s.at[slot]).start()
    for j in range(max(0, nw - 2), nw):
        pltpu.make_async_copy(stage.at[j % 2], grads[j], sem_s.at[j % 2]).wait()


def run_expert(xs, gs, ws, expert_of, offset_of):
    nt, nw = len(xs), len(ws)
    length, width = gs[0].shape
    rows, cols = ws[0].shape
    hidden = cols // 3
    outs = (
        [jax.ShapeDtypeStruct((length, width), bf16)] * nt
        + [jax.ShapeDtypeStruct((length, width + EXTRA), bf16)] * nt
        + [jax.ShapeDtypeStruct((rows, cols), bf16)] * nw
    )
    any_spec = pl.BlockSpec(memory_space=pl.ANY)
    result = pl.pallas_call(
        functools.partial(
            expert_kernel, nt, nw, length, width, hidden, rows, expert_of, offset_of
        ),
        out_shape=outs,
        in_specs=[any_spec] * (2 * nt + nw),
        out_specs=[any_spec] * len(outs),
        scratch_shapes=[
            pltpu.VMEM((width, cols), bf16),
            pltpu.VMEM((2, length, width + EXTRA), bf16),
            pltpu.VMEM((2, length, width), bf16),
            pltpu.VMEM((width, length), bf16),
            pltpu.VMEM((width, length), bf16),
            pltpu.VMEM((length, hidden), bf16),
            pltpu.VMEM((length, 2 * hidden), bf16),
            pltpu.VMEM((2, length, width), bf16),
            pltpu.VMEM((2, length, width + EXTRA), bf16),
            pltpu.VMEM((width, cols), f32),
            pltpu.VMEM((2, rows, cols), bf16),
            pltpu.SemaphoreType.DMA((nw,)),
            pltpu.SemaphoreType.DMA((2,)),
            pltpu.SemaphoreType.DMA((2,)),
            pltpu.SemaphoreType.DMA((2,)),
            pltpu.SemaphoreType.DMA((2,)),
            pltpu.SemaphoreType.DMA((2,)),
        ],
        compiler_params=pltpu.CompilerParams(vmem_limit_bytes=60 * MIB),
        cost_estimate=pl.CostEstimate(
            flops=6 * nt * length * width * cols,
            bytes_accessed=8 * nt * length * width + 4 * width * cols,
            transcendentals=nt * length * hidden,
        ),
        name="expert",
    )(*xs, *gs, *ws)
    return result[:nt], result[nt : 2 * nt], result[2 * nt :]


MESH_ID = pl.DeviceIdType.MESH


def flip(index, bit):
    return index + bit - 2 * bit * lax.rem(index // bit, 2)


def flips(index, mask):
    for bit in (1, 2, 4):
        if mask & bit:
            index = flip(index, bit)
    return index


class Wire:
    def __init__(self, send_sem, recv_sem):
        self.r, self.f = lax.axis_index("replica"), lax.axis_index("fsdp")
        self.send_sem, self.recv_sem = send_sem, recv_sem
        self.used, self.sent = 0, []

    def meet(self, partners):
        barrier = pltpu.get_barrier_semaphore()
        for d_r, d_f in partners:
            pl.semaphore_signal(
                barrier, inc=1, device_id=self.at(d_r, d_f), device_id_type=MESH_ID
            )
        pl.semaphore_wait(barrier, len(partners))

    def at(self, d_r, d_f):
        return (flips(self.r, d_r), flips(self.f, d_f))

    def send(self, src, dst, d_r, d_f):
        copy = pltpu.make_async_remote_copy(
            src_ref=src,
            dst_ref=dst,
            send_sem=self.send_sem.at[self.used],
            recv_sem=self.recv_sem.at[self.used],
            device_id=self.at(d_r, d_f),
            device_id_type=MESH_ID,
        )
        copy.start()
        self.used += 1
        self.sent.append(copy)
        return copy

    def finish(self):
        for copy in self.sent:
            copy.wait_send()


START_SENDS = 2 * 28 + 7 + 8 + 7
PARTNERS = ((1, 0), (2, 0), (0, 1), (0, 2), (0, 4), (0, 6))


def start_kernel(
    in_ref, out_ref, tiny_ref, mine_ref, other_ref, g_ref,
    in_all, out_all, tiny_all, w_all, g_all,
    in_buf, out_buf, w_buf, tiny_buf, local_sem, send_sem, recv_sem,
):
    wire = Wire(send_sem, recv_sem)
    r, f = wire.r, wire.f
    shard = in_ref.shape[0]
    quarter = shard // 4
    local = []
    for n, (src, buf) in enumerate(
        ((in_ref, in_buf), (out_ref, out_buf), (mine_ref, w_buf), (tiny_ref, tiny_buf))
    ):
        copy = pltpu.make_async_copy(src, buf, local_sem.at[n])
        copy.start()
        local.append(copy)
    wire.meet(PARTNERS)

    def rows(j, k):
        at = flips(f, j) * shard + flips(r, k) * quarter
        return pl.ds(pl.multiple_of(at, quarter), quarter)

    def shard_rows(j):
        return pl.ds(pl.multiple_of(flips(f, j) * shard, shard), shard)

    own = pl.ds(pl.multiple_of(r * quarter, quarter), quarter)
    got_t = {}
    for m in (2, 4, 6):
        got_t[m] = wire.send(tiny_ref, tiny_all.at[f], 0, m)
    got_t[1] = wire.send(tiny_ref, tiny_all.at[f], 0, 1)
    got = {}
    for name, src, dst in (("in", in_ref, in_all), ("out", out_ref, out_all)):
        for m in (2, 4, 6):
            got[name, m, 0] = wire.send(src.at[own], dst.at[rows(0, 0)], 0, m)
        got[name, 1, 0] = wire.send(src.at[own], dst.at[rows(0, 0)], 0, 1)
    for copy, (buf, dst) in zip(
        local,
        (
            (in_buf, in_all.at[shard_rows(0)]),
            (out_buf, out_all.at[shard_rows(0)]),
            (w_buf, w_all.at[shard_rows(0)]),
            (tiny_buf, tiny_all.at[f]),
        ),
    ):
        copy.wait()
    stores = []
    for n, (buf, dst) in enumerate(
        (
            (in_buf, in_all.at[shard_rows(0)]),
            (out_buf, out_all.at[shard_rows(0)]),
            (w_buf, w_all.at[shard_rows(0)]),
            (tiny_buf, tiny_all.at[f]),
        )
    ):
        copy = pltpu.make_async_copy(buf, dst, local_sem.at[4 + n])
        copy.start()
        stores.append(copy)

    for m in (2, 4, 6):
        got_t[m].wait_recv()
        at = tiny_all.at[flips(f, m)]
        got_t[m + 1] = wire.send(at, at, 0, 1)

    half = g_ref.shape[0] // 2
    got_g = {}
    got_g[2] = wire.send(g_ref, g_all.at[2], 2, 0)
    got_g[4] = wire.send(g_ref, g_all.at[4], 0, 2)
    got_g[1] = wire.send(g_ref, g_all.at[1], 1, 0)
    got_w = {}
    for m, src in ((2, other_ref), (4, mine_ref), (6, other_ref)):
        got_w[m] = wire.send(src, w_all.at[shard_rows(0)], 0, m)
    got_w[1] = wire.send(mine_ref, w_all.at[shard_rows(0)], 0, 1)

    for name, dst in (("in", in_all), ("out", out_all)):

        def pass_on(j, k, d_r, d_f):
            at = dst.at[rows(j, k)]
            return wire.send(at, at, d_r, d_f)

        for m in (1, 2, 4, 6):
            got[name, m, 0].wait_recv()
            if m != 1:
                got[name, m + 1, 0] = pass_on(m, 0, 0, 1)
            got[name, m, 2] = pass_on(m, 0, 2, 0)
            got[name, m, 1] = pass_on(m, 0, 1, 0)
        for m in (3, 5, 7):
            got[name, m, 0].wait_recv()
            got[name, m, 2] = pass_on(m, 0, 2, 0)
            got[name, m, 1] = pass_on(m, 0, 1, 0)
        for m in (1, 2, 4, 6, 3, 5, 7):
            got[name, m, 2].wait_recv()
            got[name, m, 3] = pass_on(m, 2, 1, 0)

    for m in (2, 4):
        got_g[m].wait_recv()
        got_g[m + 1] = wire.send(g_all.at[m], g_all.at[m + 1], 1, 0)
    low, top = pl.ds(0, half), pl.ds(half, half)
    far = [
        wire.send(g_all.at[4, low], g_all.at[6, low], 2, 0),
        wire.send(g_all.at[2, top], g_all.at[6, top], 0, 2),
    ]
    for m in (2, 4, 6):
        got_w[m].wait_recv()
        at = w_all.at[shard_rows(m)]
        got_w[m + 1] = wire.send(at, at, 0, 1)
    for copy in far:
        copy.wait_recv()
    got_g[7] = wire.send(g_all.at[6], g_all.at[7], 1, 0)

    for m in (1, 3, 5, 7):
        got_t[m].wait_recv()
        got_w[m].wait_recv()
        got_g[m].wait_recv()
    for name in ("in", "out"):
        for m in range(1, 8):
            got[name, m, 1].wait_recv()
            got[name, m, 3].wait_recv()
    for copy in stores:
        copy.wait()
    wire.finish()


def start(in_proj, out_proj, tiny, mine, other, grad, n_fsdp):
    any_spec = pl.BlockSpec(memory_space=pl.ANY)
    shard = in_proj.shape[0]
    whole = n_fsdp * shard
    return pl.pallas_call(
        start_kernel,
        out_shape=[
            jax.ShapeDtypeStruct((whole, in_proj.shape[1]), bf16),
            jax.ShapeDtypeStruct((whole, out_proj.shape[1]), bf16),
            jax.ShapeDtypeStruct((n_fsdp,) + tiny.shape, bf16),
            jax.ShapeDtypeStruct((whole, mine.shape[1]), bf16),
            jax.ShapeDtypeStruct((8,) + grad.shape, bf16),
        ],
        in_specs=[any_spec] * 6,
        out_specs=[any_spec] * 5,
        scratch_shapes=[
            pltpu.VMEM(in_proj.shape, bf16),
            pltpu.VMEM(out_proj.shape, bf16),
            pltpu.VMEM(mine.shape, bf16),
            pltpu.VMEM(tiny.shape, bf16),
            pltpu.SemaphoreType.DMA((8,)),
            pltpu.SemaphoreType.DMA((START_SENDS,)),
            pltpu.SemaphoreType.DMA((START_SENDS,)),
        ],
        compiler_params=pltpu.CompilerParams(
            collective_id=1, has_side_effects=True, vmem_limit_bytes=16 * MIB
        ),
        name="start",
    )(in_proj, out_proj, tiny, mine, other, grad)


ORDER = (0, 1, 2, 3, 6, 7, 5, 4)
GROUP_AT = {1: (1, 0), 2: (2, 0), 4: (0, 2), 6: (2, 2)}


def pick(step, table):
    value = jnp.int32(table[-1])
    for i, item in enumerate(table[:-1]):
        value = jnp.where(step == i, item, value)
    return value


def group_kernel(
    v_ref, g_ref, g_all, w_ref,
    xs, mix_all, dx_own, dx_in, grads,
    wbuf, xbuf, gbuf, xt, gt_, hidg, dgu, mbuf, dbuf, rc, acc, stage,
    sem_w, sem_x, sem_g, sem_m, sem_s, send_sem, recv_sem,
):
    wire = Wire(send_sem, recv_sem)
    r, f = wire.r, wire.f
    length, width = g_ref.shape
    hidden = w_ref.shape[1] // 3
    expert = 2 * r + lax.rem(f // 2, 2)
    half = length // 2
    low, top = pl.ds(0, half), pl.ds(half, half)
    step_cols = 256

    def plan(src, dst, d):
        copy = pltpu.make_async_remote_copy(
            src_ref=src,
            dst_ref=dst,
            send_sem=send_sem.at[wire.used],
            recv_sem=recv_sem.at[wire.used],
            device_id=wire.at(*d),
            device_id_type=MESH_ID,
        )
        wire.used += 1
        wire.sent.append(copy)
        return copy

    tok = {
        1: plan(v_ref, xs.at[1], (1, 0)),
        2: plan(v_ref, xs.at[2], (2, 0)),
        4: plan(v_ref, xs.at[4], (0, 2)),
        3: plan(xs.at[2], xs.at[3], (1, 0)),
        5: plan(xs.at[4], xs.at[5], (1, 0)),
        6: plan(xs.at[4, low], xs.at[6, low], (2, 0)),
        8: plan(xs.at[2, top], xs.at[6, top], (0, 2)),
        7: plan(xs.at[6], xs.at[7], (1, 0)),
    }
    to_core = {k: plan(dbuf.at[k + 1], rc.at[k // 2], (1, 0)) for k in (0, 2, 4, 6)}
    back = {
        k: plan(dbuf.at[k], dx_in.at[k // 2 - 1], GROUP_AT[k]) for k in (2, 4, 6)
    }

    load_w = pltpu.make_async_copy(w_ref, wbuf, sem_w.at[0])
    load_w.start()

    def load(step):
        slot = lax.rem(step, 2)
        k = pick(step, ORDER)

        @pl.when(step == 0)
        def _():
            pltpu.make_async_copy(v_ref, xbuf.at[0], sem_x.at[0]).start()
            pltpu.make_async_copy(g_ref, gbuf.at[0], sem_g.at[0]).start()

        @pl.when(step > 0)
        def _():
            pltpu.make_async_copy(xs.at[k], xbuf.at[slot], sem_x.at[slot]).start()
            pltpu.make_async_copy(g_all.at[k], gbuf.at[slot], sem_g.at[slot]).start()

    load(jnp.int32(0))
    wire.meet(PARTNERS_GROUP)
    for k in (2, 4, 1):
        tok[k].start()
    acc[...] = jnp.zeros_like(acc)
    lane = lax.broadcasted_iota(jnp.int32, (length, EXTRA), 1)
    load_w.wait()

    def total(k):
        to_core[k].wait_recv()
        dbuf[k] = (dbuf[k].astype(f32) + rc[k // 2].astype(f32)).astype(bf16)

    def block(step, carry):
        slot = lax.rem(step, 2)
        k = pick(step, ORDER)
        pltpu.make_async_copy(v_ref, xbuf.at[slot], sem_x.at[slot]).wait()
        pltpu.make_async_copy(g_ref, gbuf.at[slot], sem_g.at[slot]).wait()

        @pl.when(step >= 2)
        def _():
            pltpu.make_async_copy(mbuf.at[slot], mix_all.at[0], sem_m.at[slot]).wait()

        extra = xbuf[slot, :, width:].astype(f32)
        mine = (lane == expert) | (lane == expert + 8)
        gate = jnp.sum(jnp.where(mine, extra, 0.0), axis=1, keepdims=True)
        xt[...] = xbuf[slot, :, :width].T
        gt_[...] = gbuf[slot].T

        def first(c, dgate):
            at = pl.multiple_of(c * step_cols, step_cols)
            u = matmul(xbuf[slot, :, :width], wbuf[:, pl.ds(at, step_cols)])
            up = matmul(xbuf[slot, :, :width], wbuf[:, pl.ds(hidden + at, step_cols)])
            rev = matmul(gbuf[slot], wbuf[:, pl.ds(2 * hidden + at, step_cols)])
            sig = 1.0 / (1.0 + jnp.exp(-u))
            act = u * sig
            hid = act * up
            hidg[:, pl.ds(at, step_cols)] = (gate * hid).astype(bf16)
            dgate = dgate + jnp.sum(rev * hid, axis=1, keepdims=True)
            dhid = gate * rev
            dgu[:, pl.ds(at, step_cols)] = (
                dhid * up * sig * (1.0 + u * (1.0 - sig))
            ).astype(bf16)
            dgu[:, pl.ds(hidden + at, step_cols)] = (dhid * act).astype(bf16)
            return dgate

        dgate = lax.fori_loop(
            0, hidden // step_cols, first, jnp.zeros((length, 1), f32)
        )

        def second(c, carry):
            at = pl.multiple_of(c * step_cols, step_cols)
            dbuf[k, :, pl.ds(at, step_cols)] = contract_cols(
                dgu[...], wbuf[pl.ds(at, step_cols), pl.ds(0, 2 * hidden)]
            ).astype(bf16)
            mbuf[slot, :, pl.ds(at, step_cols)] = contract_cols(
                hidg[...], wbuf[pl.ds(at, step_cols), pl.ds(2 * hidden, hidden)]
            ).astype(bf16)
            return carry

        lax.fori_loop(0, width // step_cols, second, 0)
        high = dgate.astype(bf16).astype(f32)
        rest = dgate - high
        dbuf[k, :, width:] = (
            jnp.where(lane == expert, high, 0.0) + jnp.where(lane == expert + 8, rest, 0.0)
        ).astype(bf16)
        pltpu.make_async_copy(mbuf.at[slot], mix_all.at[k], sem_m.at[slot]).start()

        @pl.when(step == 0)
        def _():
            tok[1].wait_recv()
            load(step + 1)

        @pl.when(step == 1)
        def _():
            to_core[0].start()

        @pl.when(step == 2)
        def _():
            tok[3].wait_recv()
            load(step + 1)

        @pl.when(step == 3)
        def _():
            to_core[2].start()
            total(0)
            tok[6].wait_recv()
            tok[8].wait_recv()
            tok[7].start()
            load(step + 1)

        @pl.when(step == 4)
        def _():
            total(2)
            back[2].start()
            tok[7].wait_recv()
            load(step + 1)

        @pl.when(step == 5)
        def _():
            to_core[6].start()
            tok[5].wait_recv()
            load(step + 1)

        @pl.when(step == 6)
        def _():
            to_core[4].start()
            total(6)
            back[6].start()
            load(step + 1)

        @pl.when(step == 7)
        def _():
            total(4)
            back[4].start()

        def third(c, carry):
            at = pl.multiple_of(c * step_cols, step_cols)
            acc[:, pl.ds(at, step_cols)] += matmul(xt[...], dgu[:, pl.ds(at, step_cols)])
            return carry

        lax.fori_loop(0, 2 * hidden // step_cols, third, 0)

        def fourth(c, carry):
            at = pl.multiple_of(c * step_cols, step_cols)
            acc[:, pl.ds(2 * hidden + at, step_cols)] += matmul(
                gt_[...], hidg[:, pl.ds(at, step_cols)]
            )
            return carry

        lax.fori_loop(0, hidden // step_cols, fourth, 0)

        @pl.when(step == 1)
        def _():
            tok[2].wait_recv()
            tok[8].start()
            tok[3].start()
            load(step + 1)
            tok[4].wait_recv()
            tok[6].start()
            tok[5].start()

        return carry

    lax.fori_loop(0, 8, block, 0)
    keep = pltpu.make_async_copy(dbuf.at[0], dx_own, sem_w.at[0])
    keep.start()
    for slot in (0, 1):
        pltpu.make_async_copy(mbuf.at[slot], mix_all.at[0], sem_m.at[slot]).wait()
    parts = 8
    rows = width // parts

    def out(j, slot):
        return pltpu.make_async_copy(
            stage.at[slot], grads.at[pl.ds(j * rows, rows)], sem_s.at[slot]
        )

    for j in range(parts):
        slot = j % 2
        if j >= 2:
            out(j - 2, slot).wait()
        stage[slot] = acc[j * rows : (j + 1) * rows].astype(bf16)
        out(j, slot).start()
    for j in range(parts - 2, parts):
        out(j, j % 2).wait()
    keep.wait()
    for k in (2, 4, 6):
        back[k].wait_recv()
    wire.finish()


PARTNERS_GROUP = ((1, 0), (2, 0), (0, 2), (2, 2))
GROUP_SENDS = 8 + 4 + 3


def run_group(v, grad, g_all, w):
    length, width = grad.shape
    wide = v.shape[1]
    cols = w.shape[1]
    hidden = cols // 3
    any_spec = pl.BlockSpec(memory_space=pl.ANY)
    return pl.pallas_call(
        group_kernel,
        out_shape=[
            jax.ShapeDtypeStruct((8, length, wide), bf16),
            jax.ShapeDtypeStruct((8, length, width), bf16),
            jax.ShapeDtypeStruct((length, wide), bf16),
            jax.ShapeDtypeStruct((3, length, wide), bf16),
            jax.ShapeDtypeStruct((width, cols), bf16),
        ],
        in_specs=[any_spec] * 4,
        out_specs=[any_spec] * 5,
        scratch_shapes=[
            pltpu.VMEM((width, cols), bf16),
            pltpu.VMEM((2, length, wide), bf16),
            pltpu.VMEM((2, length, width), bf16),
            pltpu.VMEM((width, length), bf16),
            pltpu.VMEM((width, length), bf16),
            pltpu.VMEM((length, hidden), bf16),
            pltpu.VMEM((length, 2 * hidden), bf16),
            pltpu.VMEM((2, length, width), bf16),
            pltpu.VMEM((8, length, wide), bf16),
            pltpu.VMEM((4, length, wide), bf16),
            pltpu.VMEM((width, cols), f32),
            pltpu.VMEM((2, width // 8, cols), bf16),
            pltpu.SemaphoreType.DMA((1,)),
            pltpu.SemaphoreType.DMA((2,)),
            pltpu.SemaphoreType.DMA((2,)),
            pltpu.SemaphoreType.DMA((2,)),
            pltpu.SemaphoreType.DMA((2,)),
            pltpu.SemaphoreType.DMA((GROUP_SENDS,)),
            pltpu.SemaphoreType.DMA((GROUP_SENDS,)),
        ],
        compiler_params=pltpu.CompilerParams(
            collective_id=2, has_side_effects=True, vmem_limit_bytes=60 * MIB
        ),
        cost_estimate=pl.CostEstimate(
            flops=48 * length * width * cols,
            bytes_accessed=64 * length * width + 4 * width * cols,
            transcendentals=8 * length * hidden,
        ),
        name="group",
    )(v, grad, g_all, w)


PARTNERS_END = ((1, 0), (2, 0), (3, 0), (0, 1), (0, 2), (0, 4), (0, 6), (2, 2))
END_SENDS = 4 + 3 + 4 + 6 + 4 + 3 + 3 * 4 + 4 + 3 + 3 + 5 + 8


def end_kernel(
    grads, mix_all, xn, attn, dres, dproj, terms,
    g_out, mix_own, mix_in, d_out, terms_out,
    gl, gy, gz, pair, ml, mrc, xq, aq, rq, pq, wq, wl, wy, wz, own_d, tbuf, tr,
    local_sem, send_sem, recv_sem,
):
    wire = Wire(send_sem, recv_sem)
    r, f = wire.r, wire.f
    shard = gl.shape[1]
    length = xn.shape[0]
    low = lax.rem(f // 2, 2)
    cols_p, cols_a = pq.shape[1], aq.shape[1]
    used = [0]

    def local(src, dst):
        copy = pltpu.make_async_copy(src, dst, local_sem.at[used[0]])
        copy.start()
        used[0] += 1
        return copy

    def shard_rows(j):
        return pl.ds(pl.multiple_of(flips(f, j) * shard, shard), shard)

    def token_rows(k):
        return pl.ds(k * length, length)

    load_g = {j: local(grads.at[shard_rows(j)], gl.at[j // 2]) for j in (0, 2, 4, 6)}
    load_m = {k: local(mix_all.at[k], ml.at[k // 2]) for k in (0, 2, 4, 6)}
    loads = [
        local(xn, xq.at[token_rows(0)]),
        local(dres, rq.at[token_rows(0)]),
        local(
            attn.at[:, pl.ds(pl.multiple_of(r * cols_a, cols_a), cols_a)],
            aq.at[token_rows(0)],
        ),
        local(
            dproj.at[:, pl.ds(pl.multiple_of(r * cols_p, cols_p), cols_p)],
            pq.at[token_rows(0)],
        ),
    ]
    load_t = local(terms, tbuf.at[0])
    wire.meet(PARTNERS_END)

    act = {}
    for k in (1, 2, 3):
        to_p = flips(r, k) * cols_p
        to_a = flips(r, k) * cols_a
        act["p", k] = wire.send(
            dproj.at[:, pl.ds(pl.multiple_of(to_p, cols_p), cols_p)],
            pq.at[token_rows(k)], k, 0,
        )
        act["a", k] = wire.send(
            attn.at[:, pl.ds(pl.multiple_of(to_a, cols_a), cols_a)],
            aq.at[token_rows(k)], k, 0,
        )
    for k in (2, 1):
        act["x", k] = wire.send(xn, xq.at[token_rows(k)], k, 0)
        act["r", k] = wire.send(dres, rq.at[token_rows(k)], k, 0)
    got_y = {
        j: wire.send(grads.at[shard_rows(j + 1)], gy.at[j // 2], 0, 1) for j in (2, 4, 6, 0)
    }
    got_mc = {k: wire.send(mix_all.at[k + 1], mrc.at[k // 2], 1, 0) for k in (2, 4, 6, 0)}

    load_t.wait()

    for n, d in enumerate(((1, 0), (0, 1), (2, 0), (0, 2), (0, 4))):
        copy = wire.send(tbuf.at[n], tr.at[n], *d)
        copy.wait_recv()
        tbuf[n + 1] = tbuf[n] + tr[n]
    keep_t = local(tbuf.at[5], terms_out)

    for k in ("x", "r"):
        act[k, 2].wait_recv()
        buf = xq if k == "x" else rq
        act[k, 3] = wire.send(buf.at[token_rows(2)], buf.at[token_rows(3)], 1, 0)
    for copy in loads:
        copy.wait()
    for k in (1, 2, 3):
        for name in ("p", "a", "r", "x"):
            if (name, k) != ("x", 2) and (name, k) != ("r", 2):
                act[name, k].wait_recv()

    part = 256

    def dense(c, carry):
        at = pl.multiple_of(c * part, part)
        wq[pl.ds(at, part), pl.ds(0, cols_p)] = matmul(
            xq[:, pl.ds(at, part)].T, pq[...]
        ).astype(bf16)
        wq[pl.ds(at, part), pl.ds(cols_p, cols_a)] = matmul(
            rq[:, pl.ds(at, part)].T, aq[...]
        ).astype(bf16)
        return carry

    lax.fori_loop(0, wq.shape[0] // part, dense, 0)
    got_wy = {
        j: wire.send(wq.at[shard_rows(j + 1)], wy.at[j // 2], 0, 1) for j in (2, 4, 6, 0)
    }

    def add(u, v):
        return (u.astype(f32) + v.astype(f32)).astype(bf16)

    got_m = {}
    for k, d in ((2, (2, 0)), (4, (0, 2)), (6, (2, 2))):
        load_m[k].wait()
        got_mc[k].wait_recv()
        ml[k // 2] = add(ml[k // 2], mrc[k // 2])
        got_m[k] = wire.send(ml.at[k // 2], mix_in.at[k // 2 - 1], *d)
    load_m[0].wait()
    got_mc[0].wait_recv()
    ml[0] = add(ml[0], mrc[0])
    keep_m = local(ml.at[0], mix_own)

    got_z = {}
    for j in (2, 4, 6):
        load_g[j].wait()
        got_y[j].wait_recv()
        gl[j // 2] = add(gl[j // 2], gy[j // 2])
        got_z[j] = wire.send(gl.at[j // 2], gz.at[j // 2 - 1], 0, j)
    load_g[0].wait()
    got_y[0].wait_recv()

    got_wz = {}
    for j in (2, 4, 6):
        wl[j // 2] = wq[shard_rows(j)]
        got_wy[j].wait_recv()
        wl[j // 2] = add(wl[j // 2], wy[j // 2])
        got_wz[j] = wire.send(wl.at[j // 2], wz.at[j // 2 - 1], 0, j)
    got_wy[0].wait_recv()
    own = wq[shard_rows(0)].astype(f32) + wy[0].astype(f32)

    got_z[4].wait_recv()
    pair[0] = (
        gl[0].astype(f32) + gy[0].astype(f32) + gz[1].astype(f32)
    ).astype(bf16)
    mine, other = 2 * r + low, 2 * r + 1 - low
    kept = [local(pair.at[0], g_out.at[mine])]
    got_e = {}
    got_e[2, 0] = wire.send(pair.at[0], g_out.at[mine], 2, 0)
    got_e[1, 0] = wire.send(pair.at[0], g_out.at[mine], 1, 0)
    got_z[2].wait_recv()
    got_z[6].wait_recv()
    pair[1] = add(gz[0], gz[2])
    kept.append(local(pair.at[1], g_out.at[other]))
    got_e[2, 1] = wire.send(pair.at[1], g_out.at[other], 2, 0)
    got_e[1, 1] = wire.send(pair.at[1], g_out.at[other], 1, 0)

    for j in (2, 4, 6):
        got_wz[j].wait_recv()
        own = own + wz[j // 2 - 1].astype(f32)
    own_d[...] = own.astype(bf16)
    kept.append(local(own_d, d_out.at[r]))
    got_d = [wire.send(own_d, d_out.at[r], k, 0) for k in (1, 2, 3)]

    far = flips(r, 2)
    for n, e in ((0, 2 * far + low), (1, 2 * far + 1 - low)):
        got_e[2, n].wait_recv()
        got_e[3, n] = wire.send(g_out.at[e], g_out.at[e], 1, 0)
    for k in (1, 3):
        for n in (0, 1):
            got_e[k, n].wait_recv()
    for copy in got_d:
        copy.wait_recv()
    for k in (2, 4, 6):
        got_m[k].wait_recv()
    for copy in kept + [keep_m, keep_t]:
        copy.wait()
    wire.finish()


def run_end(grads, mix_all, xn, attn, dres, dproj, terms):
    length, width = xn.shape
    shard = width // 8
    cols = grads.shape[1]
    cols_p, cols_a = dproj.shape[1] // 4, attn.shape[1] // 4
    dense = cols_p + cols_a
    any_spec = pl.BlockSpec(memory_space=pl.ANY)
    return pl.pallas_call(
        end_kernel,
        out_shape=[
            jax.ShapeDtypeStruct((8, shard, cols), bf16),
            jax.ShapeDtypeStruct((length, width), bf16),
            jax.ShapeDtypeStruct((3, length, width), bf16),
            jax.ShapeDtypeStruct((4, shard, dense), bf16),
            jax.ShapeDtypeStruct(terms.shape, f32),
        ],
        in_specs=[any_spec] * 7,
        out_specs=[any_spec] * 5,
        scratch_shapes=[
            pltpu.VMEM((4, shard, cols), bf16),
            pltpu.VMEM((4, shard, cols), bf16),
            pltpu.VMEM((3, shard, cols), bf16),
            pltpu.VMEM((2, shard, cols), bf16),
            pltpu.VMEM((4, length, width), bf16),
            pltpu.VMEM((4, length, width), bf16),
            pltpu.VMEM((4 * length, width), bf16),
            pltpu.VMEM((4 * length, cols_a), bf16),
            pltpu.VMEM((4 * length, width), bf16),
            pltpu.VMEM((4 * length, cols_p), bf16),
            pltpu.VMEM((width, dense), bf16),
            pltpu.VMEM((4, shard, dense), bf16),
            pltpu.VMEM((4, shard, dense), bf16),
            pltpu.VMEM((3, shard, dense), bf16),
            pltpu.VMEM((shard, dense), bf16),
            pltpu.VMEM((6,) + terms.shape, f32),
            pltpu.VMEM((5,) + terms.shape, f32),
            pltpu.SemaphoreType.DMA((24,)),
            pltpu.SemaphoreType.DMA((END_SENDS,)),
            pltpu.SemaphoreType.DMA((END_SENDS,)),
        ],
        compiler_params=pltpu.CompilerParams(
            collective_id=3, has_side_effects=True, vmem_limit_bytes=60 * MIB
        ),
        name="end",
    )(grads, mix_all, xn, attn, dres, dproj, terms)


class Near:
    def __init__(self, n_rep, n_fsdp):
        self.n_fsdp = n_fsdp

    def start(self, in_proj, out_proj, tiny, expert_in, expert_out, grad):
        r, f = lax.axis_index("replica"), lax.axis_index("fsdp")
        low = (f >> 1) & 1
        mine, other = [
            jnp.concatenate(
                [
                    lax.dynamic_index_in_dim(expert_in, e, 1, keepdims=False),
                    lax.dynamic_index_in_dim(expert_out, e, 1, keepdims=False),
                ],
                axis=1,
            )
            for e in (2 * r + low, 2 * r + 1 - low)
        ]
        pad = jnp.pad(tiny, ((0, 0), (0, -tiny.shape[1] % 128)))
        proj_in, proj_out, tiny_all, weights, gs = start(
            in_proj, out_proj, pad, mine, other, grad, self.n_fsdp
        )
        tiny_all = tiny_all[:, :, : tiny.shape[1]].transpose(1, 0, 2).reshape(16, -1)
        return proj_in, proj_out, tiny_all, (weights, gs, grad)

    def experts(self, payload, held):
        weights, gs, grad = held
        _, mix_all, dx_own, dx_in, grads = run_group(payload, grad, gs, weights)
        dx = dx_own.astype(f32)
        for k in range(3):
            dx = dx + dx_in[k].astype(f32)
        return dx, (mix_all, grads)

    def end(self, held, first, normed, attn, dres, dproj, terms):
        mix_all, grads = held
        expert_sum, mix_own, mix_in, dense, terms = run_end(
            grads, mix_all, normed, attn, dres, dproj, terms
        )
        mixed = first + mix_own.astype(f32)
        for k in range(3):
            mixed = mixed + mix_in[k].astype(f32)
        cut = dproj.shape[1] // 4
        in_grad = dense[:, :, :cut].transpose(1, 0, 2).reshape(dense.shape[1], -1)
        out_grad = dense[:, :, cut:].transpose(1, 0, 2).reshape(dense.shape[1], -1)
        return mixed, in_grad, out_grad, expert_sum.transpose(1, 0, 2), terms


class Wide:
    def __init__(self, n_rep, n_fsdp):
        self.n_rep, self.n_fsdp = n_rep, n_fsdp

    def spread(self, value):
        every = lax.all_gather(value, "replica", axis=0)
        return [every[k] for k in range(self.n_rep)]

    def collect(self, parts):
        return lax.psum_scatter(jnp.stack(parts), "replica", scatter_dimension=0).astype(f32)

    def start(self, in_proj, out_proj, tiny, expert_in, expert_out, grad):
        r = lax.axis_index("replica")
        per = expert_in.shape[1] // self.n_rep
        weights = []
        for i in range(per):
            both = jnp.concatenate(
                [
                    lax.dynamic_index_in_dim(expert_in, per * r + i, 1, keepdims=False),
                    lax.dynamic_index_in_dim(expert_out, per * r + i, 1, keepdims=False),
                ],
                axis=1,
            )
            weights.append(lax.all_gather(both, "fsdp", axis=0, tiled=True))
        return (
            lax.all_gather(in_proj, "fsdp", axis=0, tiled=True),
            lax.all_gather(out_proj, "fsdp", axis=0, tiled=True),
            lax.all_gather(tiny, "fsdp", axis=1, tiled=True),
            (weights, self.spread(grad)),
        )

    def experts(self, payload, held):
        weights, gs = held
        xs = self.spread(payload)
        per = len(weights)
        mixes, dxs, grads = None, None, []
        for i, w in enumerate(weights):

            def expert_of(i=i):
                return per * lax.axis_index("replica") + i

            mix, dx, grad = run_expert(xs, gs, [w], expert_of, lambda j: 0)
            mixes = mix if mixes is None else [a + b for a, b in zip(mixes, mix)]
            dxs = dx if dxs is None else [a + b for a, b in zip(dxs, dx)]
            grads.append(grad[0])
        return self.collect(dxs), (mixes, grads)

    def trade(self, value):
        cut = value.reshape(value.shape[0], self.n_rep, -1).transpose(1, 0, 2)
        got = lax.all_to_all(cut, "replica", 0, 0)
        return got.reshape(-1, got.shape[2])

    def end(self, held, first, normed, attn, dres, dproj, terms):
        mixes, grads = held
        mixed = first + self.collect(mixes)
        own = jnp.stack(
            [lax.psum_scatter(g, "fsdp", scatter_dimension=0, tiled=True) for g in grads]
        )
        expert_sum = lax.all_gather(own, "replica", axis=0, tiled=True).transpose(1, 0, 2)
        dense = []
        for left, right in ((normed, dproj), (dres, attn)):
            left = lax.all_gather(left, "replica", axis=0, tiled=True)
            part = contract_rows(left, self.trade(right)).astype(bf16)
            own = lax.psum_scatter(part, "fsdp", scatter_dimension=0, tiled=True)
            dense.append(lax.all_gather(own, "replica", axis=1, tiled=True))
        return mixed, dense[0], dense[1], expert_sum, lax.psum(terms, ("replica", "fsdp"))


def layer(
    net, tokens, seg_ids, routes, in_proj, out_proj, router, norm_gains, expert_in, expert_out,
    out_grad,
):
    length, width = tokens.shape
    experts = router.shape[1]
    hidden = expert_out.shape[2]
    shard = router.shape[0]
    scale = HD ** (-0.5)
    cosine, sine = tables(length)
    segment = seg_ids[0]
    place = jnp.arange(length)
    allowed = ((place[:, None] >= place[None, :]) & (segment[:, None] == segment[None, :]))[
        None, None
    ]
    tiny = jnp.concatenate(
        [router.T, norm_gains.T, jnp.zeros((16 - experts - 2, shard), bf16)], axis=0
    )
    proj_in, proj_out, tiny, held = net.start(
        in_proj, out_proj, tiny, expert_in, expert_out, out_grad
    )
    router_rows = tiny[:experts]
    gain_one = tiny[experts].astype(f32)
    gain_two = tiny[experts + 1].astype(f32)

    inputs = tokens.astype(f32)
    scale_one = rms_scale(inputs)
    unit_one = inputs * scale_one
    normed = (unit_one * gain_one).astype(bf16)
    proj = matmul(normed, proj_in)
    queries = (
        rotate(proj[:, :WQ].reshape(length, HQ, HD), cosine, sine)
        .astype(bf16)
        .reshape(length, KV, GROUP, HD)
    )
    keys = rotate(proj[:, WQ : WQ + WK].reshape(length, KV, HD), cosine, sine).astype(bf16)
    values = proj[:, WQ + WK :].reshape(length, KV, HD).astype(bf16)
    scores = jnp.einsum("qkgd,tkd->kgqt", queries, keys, preferred_element_type=f32) * scale
    masked = jnp.where(allowed, scores, -1e30)
    highest = jnp.max(masked, axis=-1, keepdims=True)
    expo = jnp.exp(masked - highest)
    total = jnp.sum(expo, axis=-1, keepdims=True)
    log_total = highest + jnp.log(total)
    probs_low = (expo / total).astype(bf16)
    attn = jnp.einsum("kgqt,tkd->qkgd", probs_low, values, preferred_element_type=f32)
    attn = attn.astype(bf16).reshape(length, WQ)
    first = inputs + contract_cols(attn, proj_out)
    scale_two = rms_scale(first)
    unit_two = first * scale_two
    normed_two = (unit_two * gain_two).astype(bf16)
    logits = contract_cols(normed_two, router_rows)
    onehot = (routes[:, :, None] == jnp.arange(experts)[None, None, :]).astype(f32)
    chosen = jnp.sum(onehot * logits[:, None, :], axis=-1)
    gates = jax.nn.softmax(chosen, axis=-1)
    table = jnp.sum(gates[:, :, None] * onehot, axis=1)
    high = table.astype(bf16)
    low = (table - high.astype(f32)).astype(bf16)
    payload = jnp.concatenate(
        [normed_two, high, low, jnp.zeros((length, EXTRA - 2 * experts), bf16)], axis=1
    )
    dx, held = net.experts(payload, held)

    grad_out = out_grad.astype(f32)
    dgate_all = dx[:, width : width + experts] + dx[:, width + experts : width + 2 * experts]
    dgate = jnp.sum(onehot * dgate_all[:, None, :], axis=-1)
    dchosen = gates * (dgate - jnp.sum(gates * dgate, axis=-1, keepdims=True))
    dlogits = jnp.sum(dchosen[:, :, None] * onehot, axis=1).astype(bf16)
    dnormed_two = dx[:, :width] + matmul(dlogits, router_rows)
    gain_two_grad = jnp.sum(dnormed_two * unit_two, axis=0)
    dunit_two = dnormed_two * gain_two
    dfirst = grad_out + scale_two * (
        dunit_two - unit_two * jnp.mean(dunit_two * unit_two, axis=-1, keepdims=True)
    )
    dres = dfirst.astype(bf16)
    dattn = matmul(dres, proj_out).astype(bf16).reshape(length, KV, GROUP, HD)
    probs = jnp.exp(masked - log_total)
    probs_again = probs.astype(bf16)
    dprobs = jnp.einsum("qkgd,tkd->kgqt", dattn, values, preferred_element_type=f32)
    dvalues = jnp.einsum("kgqt,qkgd->tkd", probs_again, dattn, preferred_element_type=f32)
    delta = jnp.sum(probs * dprobs, axis=-1, keepdims=True)
    dscores = (probs * (dprobs - delta)).astype(bf16)
    dqueries = jnp.einsum("kgqt,tkd->qkgd", dscores, keys, preferred_element_type=f32) * scale
    dkeys = jnp.einsum("kgqt,qkgd->tkd", dscores, queries, preferred_element_type=f32) * scale
    dqueries = rotate(dqueries.reshape(length, HQ, HD), cosine, -sine).reshape(length, WQ)
    dkeys = rotate(dkeys, cosine, -sine).reshape(length, WK)
    dproj = jnp.concatenate([dqueries, dkeys, dvalues.reshape(length, WK)], axis=1).astype(bf16)
    dnormed = contract_cols(dproj, proj_in)
    gain_one_grad = jnp.sum(dnormed * unit_one, axis=0)
    dunit_one = dnormed * gain_one
    tokens_grad = (
        dfirst
        + scale_one
        * (dunit_one - unit_one * jnp.mean(dunit_one * unit_one, axis=-1, keepdims=True))
    ).astype(bf16)

    terms = jnp.concatenate(
        [
            contract_rows(dlogits, normed_two),
            gain_one_grad[None],
            gain_two_grad[None],
            jnp.zeros((16 - experts - 2, width), f32),
        ],
        axis=0,
    )
    mixed, in_proj_grad, out_proj_grad, expert_sum, terms = net.end(
        held, first, normed, attn, dres, dproj, terms
    )
    terms = lax.dynamic_slice_in_dim(terms, lax.axis_index("fsdp") * shard, shard, 1).T
    return (
        mixed.astype(bf16),
        tokens_grad,
        in_proj_grad.astype(f32),
        out_proj_grad.astype(f32),
        terms[:, :experts],
        terms[:, experts : experts + 2],
        expert_sum[..., : 2 * hidden].astype(f32),
        expert_sum[..., 2 * hidden :].astype(f32),
    )


def solution(mesh):
    n_rep, n_fsdp = mesh.shape["replica"], mesh.shape["fsdp"]
    net = Near(n_rep, n_fsdp) if (n_rep, n_fsdp) == (4, 8) else Wide(n_rep, n_fsdp)
    both = P(("replica", "fsdp"), None)
    fsdp, deep = P("fsdp", None), P("fsdp", None, None)
    return jax.shard_map(
        functools.partial(layer, net),
        mesh=mesh,
        in_specs=(both, both, both, fsdp, fsdp, fsdp, fsdp, deep, deep, both),
        out_specs=(both, both, fsdp, fsdp, fsdp, fsdp, deep, deep),
        check_vma=False,
    )
```

```python
import functools

import jax
import jax.numpy as jnp
from jax import lax
from jax.experimental import pallas as pl
from jax.experimental.pallas import tpu as pltpu
from jax.sharding import PartitionSpec as P

HQ = 12
KV = 2
HD = 128
GROUP = HQ // KV
WQ = HQ * HD
WK = KV * HD
EXTRA = 128
MIB = 1024 * 1024

epsilon = 1e-06
rope_base = 1000000.0
bf16 = jnp.bfloat16
f32 = jnp.float32


def rms_scale(v):
    return lax.rsqrt(jnp.mean(v * v, axis=-1, keepdims=True) + epsilon)


def tables(length):
    half = HD // 2
    freq = jnp.power(rope_base, -(jnp.arange(half, dtype=f32) * 2.0 / HD))
    angle = jnp.arange(length, dtype=f32)[:, None] * freq[None, :]
    return (jnp.cos(angle)[:, None, :], jnp.sin(angle)[:, None, :])


def rotate(v, cosine, sine):
    half = v.shape[-1] // 2
    first = v[..., :half]
    second = v[..., half:]
    return jnp.concatenate(
        [first * cosine - second * sine, second * cosine + first * sine], axis=-1
    )


def contract_rows(left, right):
    return lax.dot_general(left, right, (((0,), (0,)), ((), ())), preferred_element_type=f32)


def contract_cols(left, right):
    return lax.dot_general(left, right, (((1,), (1,)), ((), ())), preferred_element_type=f32)


def matmul(left, right):
    return lax.dot_general(left, right, (((1,), (0,)), ((), ())), preferred_element_type=f32)


def expert_kernel(nt, nw, length, width, hidden, rows, expert_of, offset_of, *refs):
    xs, gs, ws = refs[:nt], refs[nt : 2 * nt], refs[2 * nt : 2 * nt + nw]
    refs = refs[2 * nt + nw :]
    mixes, dxs, grads = refs[:nt], refs[nt : 2 * nt], refs[2 * nt : 2 * nt + nw]
    (
        wbuf, xbuf, gbuf, xt, gt_, hidg, dgu, mbuf, dbuf, acc, stage,
        sem_w, sem_x, sem_g, sem_m, sem_d, sem_s,
    ) = refs[2 * nt + nw :]
    cols = 3 * hidden
    step_cols = 256

    def load(k, slot):
        for i in range(nt):

            @pl.when(k == i)
            def _():
                pltpu.make_async_copy(xs[i], xbuf.at[slot], sem_x.at[slot]).start()
                pltpu.make_async_copy(gs[i], gbuf.at[slot], sem_g.at[slot]).start()

    def store(k, slot):
        for i in range(nt):

            @pl.when(k == i)
            def _():
                pltpu.make_async_copy(mbuf.at[slot], mixes[i], sem_m.at[slot]).start()
                pltpu.make_async_copy(dbuf.at[slot], dxs[i], sem_d.at[slot]).start()

    def stored(slot):
        pltpu.make_async_copy(mbuf.at[slot], mixes[0], sem_m.at[slot]).wait()
        pltpu.make_async_copy(dbuf.at[slot], dxs[0], sem_d.at[slot]).wait()

    for j in range(nw):
        pltpu.make_async_copy(
            ws[j], wbuf.at[pl.ds(pl.multiple_of(offset_of(j), 8), rows)], sem_w.at[j]
        ).start()
    load(0, 0)
    expert = expert_of()
    acc[...] = jnp.zeros_like(acc)
    lane = lax.broadcasted_iota(jnp.int32, (length, EXTRA), 1)
    for j in range(nw):
        pltpu.make_async_copy(
            ws[j], wbuf.at[pl.ds(pl.multiple_of(offset_of(j), 8), rows)], sem_w.at[j]
        ).wait()

    def block(k, carry):
        slot = lax.rem(k, 2)

        @pl.when(k + 1 < nt)
        def _():
            load(k + 1, 1 - slot)

        pltpu.make_async_copy(xs[0], xbuf.at[slot], sem_x.at[slot]).wait()
        pltpu.make_async_copy(gs[0], gbuf.at[slot], sem_g.at[slot]).wait()

        @pl.when(k >= 2)
        def _():
            stored(slot)

        extra = xbuf[slot, :, width:].astype(f32)
        mine = (lane == expert) | (lane == expert + 8)
        gate = jnp.sum(jnp.where(mine, extra, 0.0), axis=1, keepdims=True)
        xt[...] = xbuf[slot, :, :width].T
        gt_[...] = gbuf[slot].T

        def first(c, dgate):
            at = pl.multiple_of(c * step_cols, step_cols)
            u = matmul(xbuf[slot, :, :width], wbuf[:, pl.ds(at, step_cols)])
            up = matmul(xbuf[slot, :, :width], wbuf[:, pl.ds(hidden + at, step_cols)])
            back = matmul(gbuf[slot], wbuf[:, pl.ds(2 * hidden + at, step_cols)])
            sig = 1.0 / (1.0 + jnp.exp(-u))
            act = u * sig
            hid = act * up
            hidg[:, pl.ds(at, step_cols)] = (gate * hid).astype(bf16)
            dgate = dgate + jnp.sum(back * hid, axis=1, keepdims=True)
            dhid = gate * back
            dgu[:, pl.ds(at, step_cols)] = (
                dhid * up * sig * (1.0 + u * (1.0 - sig))
            ).astype(bf16)
            dgu[:, pl.ds(hidden + at, step_cols)] = (dhid * act).astype(bf16)
            return dgate

        dgate = lax.fori_loop(
            0, hidden // step_cols, first, jnp.zeros((length, 1), f32)
        )

        def second(c, carry):
            at = pl.multiple_of(c * step_cols, step_cols)
            mbuf[slot, :, pl.ds(at, step_cols)] = contract_cols(
                hidg[...], wbuf[pl.ds(at, step_cols), pl.ds(2 * hidden, hidden)]
            ).astype(bf16)
            dbuf[slot, :, pl.ds(at, step_cols)] = contract_cols(
                dgu[...], wbuf[pl.ds(at, step_cols), pl.ds(0, 2 * hidden)]
            ).astype(bf16)
            return carry

        lax.fori_loop(0, width // step_cols, second, 0)
        high = dgate.astype(bf16).astype(f32)
        low = dgate - high
        dbuf[slot, :, width:] = (
            jnp.where(lane == expert, high, 0.0) + jnp.where(lane == expert + 8, low, 0.0)
        ).astype(bf16)
        store(k, slot)

        def third(c, carry):
            at = pl.multiple_of(c * step_cols, step_cols)
            acc[:, pl.ds(at, step_cols)] += matmul(xt[...], dgu[:, pl.ds(at, step_cols)])
            return carry

        lax.fori_loop(0, 2 * hidden // step_cols, third, 0)

        def fourth(c, carry):
            at = pl.multiple_of(c * step_cols, step_cols)
            acc[:, pl.ds(2 * hidden + at, step_cols)] += matmul(
                gt_[...], hidg[:, pl.ds(at, step_cols)]
            )
            return carry

        lax.fori_loop(0, hidden // step_cols, fourth, 0)
        return carry

    lax.fori_loop(0, nt, block, 0)
    stored(0)
    stored(1)
    for j in range(nw):
        slot = j % 2
        if j >= 2:
            pltpu.make_async_copy(stage.at[slot], grads[j - 2], sem_s.at[slot]).wait()
        stage[slot] = acc[pl.ds(pl.multiple_of(offset_of(j), 8), rows)].astype(bf16)
        pltpu.make_async_copy(stage.at[slot], grads[j], sem_s.at[slot]).start()
    for j in range(max(0, nw - 2), nw):
        pltpu.make_async_copy(stage.at[j % 2], grads[j], sem_s.at[j % 2]).wait()


def run_expert(xs, gs, ws, expert_of, offset_of):
    nt, nw = len(xs), len(ws)
    length, width = gs[0].shape
    rows, cols = ws[0].shape
    hidden = cols // 3
    outs = (
        [jax.ShapeDtypeStruct((length, width), bf16)] * nt
        + [jax.ShapeDtypeStruct((length, width + EXTRA), bf16)] * nt
        + [jax.ShapeDtypeStruct((rows, cols), bf16)] * nw
    )
    any_spec = pl.BlockSpec(memory_space=pl.ANY)
    result = pl.pallas_call(
        functools.partial(
            expert_kernel, nt, nw, length, width, hidden, rows, expert_of, offset_of
        ),
        out_shape=outs,
        in_specs=[any_spec] * (2 * nt + nw),
        out_specs=[any_spec] * len(outs),
        scratch_shapes=[
            pltpu.VMEM((width, cols), bf16),
            pltpu.VMEM((2, length, width + EXTRA), bf16),
            pltpu.VMEM((2, length, width), bf16),
            pltpu.VMEM((width, length), bf16),
            pltpu.VMEM((width, length), bf16),
            pltpu.VMEM((length, hidden), bf16),
            pltpu.VMEM((length, 2 * hidden), bf16),
            pltpu.VMEM((2, length, width), bf16),
            pltpu.VMEM((2, length, width + EXTRA), bf16),
            pltpu.VMEM((width, cols), f32),
            pltpu.VMEM((2, rows, cols), bf16),
            pltpu.SemaphoreType.DMA((nw,)),
            pltpu.SemaphoreType.DMA((2,)),
            pltpu.SemaphoreType.DMA((2,)),
            pltpu.SemaphoreType.DMA((2,)),
            pltpu.SemaphoreType.DMA((2,)),
            pltpu.SemaphoreType.DMA((2,)),
        ],
        compiler_params=pltpu.CompilerParams(vmem_limit_bytes=60 * MIB),
        cost_estimate=pl.CostEstimate(
            flops=6 * nt * length * width * cols,
            bytes_accessed=8 * nt * length * width + 4 * width * cols,
            transcendentals=nt * length * hidden,
        ),
        name="expert",
    )(*xs, *gs, *ws)
    return result[:nt], result[nt : 2 * nt], result[2 * nt :]


MESH_ID = pl.DeviceIdType.MESH


def flip(index, bit):
    return index + bit - 2 * bit * lax.rem(index // bit, 2)


def flips(index, mask):
    for bit in (1, 2, 4):
        if mask & bit:
            index = flip(index, bit)
    return index


class Wire:
    def __init__(self, send_sem, recv_sem):
        self.r, self.f = lax.axis_index("replica"), lax.axis_index("fsdp")
        self.send_sem, self.recv_sem = send_sem, recv_sem
        self.used, self.sent = 0, []

    def meet(self, partners):
        barrier = pltpu.get_barrier_semaphore()
        for d_r, d_f in partners:
            pl.semaphore_signal(
                barrier, inc=1, device_id=self.at(d_r, d_f), device_id_type=MESH_ID
            )
        pl.semaphore_wait(barrier, len(partners))

    def at(self, d_r, d_f):
        return (flips(self.r, d_r), flips(self.f, d_f))

    def plan(self, src, dst, d_r, d_f):
        copy = pltpu.make_async_remote_copy(
            src_ref=src,
            dst_ref=dst,
            send_sem=self.send_sem.at[self.used],
            recv_sem=self.recv_sem.at[self.used],
            device_id=self.at(d_r, d_f),
            device_id_type=MESH_ID,
        )
        self.used += 1
        return copy

    def send(self, src, dst, d_r, d_f):
        copy = self.plan(src, dst, d_r, d_f)
        copy.start()
        self.sent.append(copy)
        return copy

    def finish(self, waited=()):
        for copy in self.sent:
            if all(copy is not other for other in waited):
                copy.wait_send()


FRONT_SENDS = 2 * 28 + 7 + 7 + 8 + 8
PARTNERS = ((1, 0), (2, 0), (0, 1), (0, 2), (0, 4), (0, 6))
ROWS = 64


def turn(v, cosine, sine):
    return v * cosine + pltpu.roll(v, HD // 2, 1) * sine


def front_kernel(
    tokens, seg_col, seg_row, routes, cos, sin,
    in_ref, out_ref, tiny_ref, mine_ref, other_ref, g_ref,
    qkv, attn, xn, first, lse, table, tiny_out, v,
    in_all, out_all, w_all, g_all, xs,
    in_v, out_v, tiny_v, rt, bias, w_buf, local_sem, send_sem, recv_sem,
):
    wire = Wire(send_sem, recv_sem)
    r, f = wire.r, wire.f
    shard = in_ref.shape[0]
    quarter = shard // 4
    length, width = tokens.shape
    half = length // 2
    low, top = pl.ds(0, half), pl.ds(half, half)
    experts = 8
    scale = HD ** (-0.5)

    def rows(j, k):
        at = flips(f, j) * shard + flips(r, k) * quarter
        return pl.ds(pl.multiple_of(at, quarter), quarter)

    def shard_rows(j):
        return pl.ds(pl.multiple_of(flips(f, j) * shard, shard), shard)

    def local(n, src, dst):
        copy = pltpu.make_async_copy(src, dst, local_sem.at[n])
        copy.start()
        return copy

    own_in = local(0, in_ref, in_v.at[shard_rows(0)])
    own_out = local(1, out_ref, out_v.at[shard_rows(0)])
    own_tiny = local(2, tiny_ref, tiny_v.at[f])
    own_w = local(3, mine_ref, w_buf)
    wire.meet(PARTNERS)

    own = pl.ds(pl.multiple_of(r * quarter, quarter), quarter)
    land = {"in": in_v, "out": out_v}
    source = {"in": in_ref, "out": out_ref}
    got, got_t, got_w, got_g, got_x = {}, {}, {}, {}, {}

    for m in (2, 4, 6, 1):
        got_t[m] = wire.send(tiny_ref, tiny_v.at[f], 0, m)

    def own_pieces(name):
        for m in (2, 4, 6, 1):
            got[name, m, 0] = wire.send(
                source[name].at[own], land[name].at[rows(0, 0)], 0, m
            )

    def pass_on(name, j, k, d_r, d_f):
        at = land[name].at[rows(j, k)]
        return wire.send(at, at, d_r, d_f)

    def near_pieces(name):
        for m in (1, 2, 4, 6):
            got[name, m, 0].wait_recv()
            if m != 1:
                got[name, m + 1, 0] = pass_on(name, m, 0, 0, 1)
            got[name, m, 2] = pass_on(name, m, 0, 2, 0)
            got[name, m, 1] = pass_on(name, m, 0, 1, 0)

    def far_pieces(name):
        for m in (3, 5, 7):
            got[name, m, 0].wait_recv()
            got[name, m, 2] = pass_on(name, m, 0, 2, 0)
            got[name, m, 1] = pass_on(name, m, 0, 1, 0)

    def side_pieces(name):
        for m in (1, 2, 4, 6, 3, 5, 7):
            got[name, m, 2].wait_recv()
            got[name, m, 3] = pass_on(name, m, 2, 1, 0)

    def all_pieces(name):
        for m in range(1, 8):
            got[name, m, 1].wait_recv()
            got[name, m, 3].wait_recv()

    own_pieces("in")
    own_w.wait()
    kept = [local(4, w_buf, w_all.at[shard_rows(0)])]

    for m in (2, 4, 6):
        got_t[m].wait_recv()
        at = tiny_v.at[flips(f, m)]
        got_t[m + 1] = wire.send(at, at, 0, 1)
    for m in (1, 3, 5, 7):
        got_t[m].wait_recv()
    own_tiny.wait()
    lanes = tiny_v.shape[2]
    rt[...] = jnp.zeros_like(rt)
    for z in range(4):
        both = tiny_v[2 * z].astype(f32) + tiny_v[2 * z + 1].astype(f32)
        tiny_out[:, z * lanes : (z + 1) * lanes] = both
        row = lax.broadcasted_iota(jnp.int32, both.shape, 0)
        rt[0:16, z * lanes : (z + 1) * lanes] = jnp.where(row < experts, both, 0.0).astype(bf16)

    def norm_one(c, carry):
        at = pl.ds(pl.multiple_of(c * ROWS, ROWS), ROWS)
        x = tokens[at, :].astype(f32)
        unit = x * lax.rsqrt(jnp.mean(x * x, axis=-1, keepdims=True) + epsilon)
        xn[at, :] = (unit * tiny_out[experts : experts + 1, :]).astype(bf16)
        return carry

    lax.fori_loop(0, length // ROWS, norm_one, 0)
    spot = lax.broadcasted_iota(jnp.int32, bias.shape, 0)
    keys_at = lax.broadcasted_iota(jnp.int32, bias.shape, 1)
    bias[...] = jnp.where((spot >= keys_at) & (seg_col[...] == seg_row[...]), 0.0, -1e30)

    near_pieces("in")
    own_pieces("out")
    far_pieces("in")
    side_pieces("in")
    near_pieces("out")
    for m, src in ((2, other_ref), (4, mine_ref), (6, other_ref)):
        got_w[m] = wire.send(src, w_all.at[shard_rows(0)], 0, m)
    got_w[1] = wire.send(mine_ref, w_all.at[shard_rows(0)], 0, 1)
    own_in.wait()
    all_pieces("in")

    def project(c, carry):
        at = pl.multiple_of(c * 256, 256)
        t = matmul(xn[...], in_v[:, pl.ds(at, 256)])
        turned = c < 7
        for n in (0, 1):
            part = t[:, n * HD : (n + 1) * HD]
            part = turn(
                part, jnp.where(turned, cos[...], 1.0), jnp.where(turned, sin[...], 0.0)
            )
            qkv[:, pl.ds(at + n * HD, HD)] = part.astype(bf16)
        return carry

    lax.fori_loop(0, 8, project, 0)
    far_pieces("out")
    side_pieces("out")
    got_g[2] = wire.send(g_ref, g_all.at[2], 2, 0)
    got_g[4] = wire.send(g_ref, g_all.at[4], 0, 2)
    got_g[1] = wire.send(g_ref, g_all.at[1], 1, 0)
    lane = lax.broadcasted_iota(jnp.int32, (length, HD), 1)
    lse[...] = jnp.zeros_like(lse)

    def head(h, carry):
        at = pl.ds(pl.multiple_of(h * HD, HD), HD)
        group = h // GROUP
        k_at = pl.ds(pl.multiple_of(WQ + group * HD, HD), HD)
        v_at = pl.ds(pl.multiple_of(WQ + WK + group * HD, HD), HD)
        s = contract_cols(qkv[:, at], qkv[:, k_at]) * scale + bias[...]
        highest = jnp.max(s, axis=-1, keepdims=True)
        expo = jnp.exp(s - highest)
        total = jnp.sum(expo, axis=-1, keepdims=True)
        p = (expo * (1.0 / total)).astype(bf16)
        attn[:, at] = matmul(p, qkv[:, v_at]).astype(bf16)
        lse[...] = jnp.where(lane == h, highest + jnp.log(total), lse[...])
        return carry

    lax.fori_loop(0, HQ, head, 0)
    own_out.wait()
    all_pieces("out")
    kept.append(local(5, in_v, in_all))
    kept.append(local(6, out_v, out_all))

    def add_out(c, carry):
        at = pl.ds(pl.multiple_of(c * 256, 256), 256)
        first[:, at] = tokens[:, at].astype(f32) + contract_cols(attn[...], out_v[at, :])
        return carry

    lax.fori_loop(0, width // 256, add_out, 0)

    def norm_two(c, carry):
        at = pl.ds(pl.multiple_of(c * ROWS, ROWS), ROWS)
        h = first[at, :]
        unit = h * lax.rsqrt(jnp.mean(h * h, axis=-1, keepdims=True) + epsilon)
        v[at, 0:width] = (unit * tiny_out[experts + 1 : experts + 2, :]).astype(bf16)
        return carry

    lax.fori_loop(0, length // ROWS, norm_two, 0)
    logits = contract_cols(v[:, 0:width], rt[...])
    chosen = lane == routes[:, 0:1]
    for j in range(1, routes.shape[1]):
        chosen = chosen | (lane == routes[:, j : j + 1])
    logits = jnp.where(chosen, logits, -1e30)
    expo = jnp.exp(logits - jnp.max(logits, axis=-1, keepdims=True))
    expo = jnp.where(chosen, expo, 0.0)
    gates = expo / jnp.sum(expo, axis=-1, keepdims=True)
    table[...] = gates
    high = gates.astype(bf16).astype(f32)
    v[:, width:] = (high + pltpu.roll(gates - high, experts, 1)).astype(bf16)

    got_x[2] = wire.send(v, xs.at[2], 2, 0)
    got_x[4] = wire.send(v, xs.at[4], 0, 2)
    got_x[1] = wire.send(v, xs.at[1], 1, 0)

    def onward(got_some, buf):
        for m in (2, 4):
            got_some[m].wait_recv()
            got_some[m + 1] = wire.send(buf.at[m], buf.at[m + 1], 1, 0)
        return [
            wire.send(buf.at[4, low], buf.at[6, low], 2, 0),
            wire.send(buf.at[2, top], buf.at[6, top], 0, 2),
        ]

    far_g = onward(got_g, g_all)
    for m in (2, 4, 6):
        got_w[m].wait_recv()
        at = w_all.at[shard_rows(m)]
        got_w[m + 1] = wire.send(at, at, 0, 1)
    far_x = onward(got_x, xs)
    for copy in far_g:
        copy.wait_recv()
    got_g[7] = wire.send(g_all.at[6], g_all.at[7], 1, 0)
    for copy in far_x:
        copy.wait_recv()
    got_x[7] = wire.send(xs.at[6], xs.at[7], 1, 0)
    for m in (1, 3, 5, 7):
        got_w[m].wait_recv()
        got_g[m].wait_recv()
        got_x[m].wait_recv()
    for copy in kept:
        copy.wait()
    wire.finish()


def front(tokens, seg_ids, routes, cos, sin, in_proj, out_proj, tiny, mine, other, grad):
    any_spec = pl.BlockSpec(memory_space=pl.ANY)
    vmem = pl.BlockSpec(memory_space=pltpu.VMEM)
    length, width = tokens.shape
    shard, cols = in_proj.shape
    whole = 8 * shard
    wide = width + EXTRA
    return pl.pallas_call(
        front_kernel,
        out_shape=[
            jax.ShapeDtypeStruct((length, cols), bf16),
            jax.ShapeDtypeStruct((length, WQ), bf16),
            jax.ShapeDtypeStruct((length, width), bf16),
            jax.ShapeDtypeStruct((length, width), f32),
            jax.ShapeDtypeStruct((length, HD), f32),
            jax.ShapeDtypeStruct((length, EXTRA), f32),
            jax.ShapeDtypeStruct((16, width), f32),
            jax.ShapeDtypeStruct((length, wide), bf16),
            jax.ShapeDtypeStruct((whole, cols), bf16),
            jax.ShapeDtypeStruct((whole, out_proj.shape[1]), bf16),
            jax.ShapeDtypeStruct((whole, mine.shape[1]), bf16),
            jax.ShapeDtypeStruct((8,) + grad.shape, bf16),
            jax.ShapeDtypeStruct((8, length, wide), bf16),
        ],
        in_specs=[vmem] * 6 + [any_spec] * 6,
        out_specs=[vmem] * 8 + [any_spec] * 5,
        scratch_shapes=[
            pltpu.VMEM((whole, cols), bf16),
            pltpu.VMEM((whole, out_proj.shape[1]), bf16),
            pltpu.VMEM((8,) + tiny.shape, bf16),
            pltpu.VMEM((EXTRA, width), bf16),
            pltpu.VMEM((length, length), f32),
            pltpu.VMEM(mine.shape, bf16),
            pltpu.SemaphoreType.DMA((8,)),
            pltpu.SemaphoreType.DMA((FRONT_SENDS,)),
            pltpu.SemaphoreType.DMA((FRONT_SENDS,)),
        ],
        compiler_params=pltpu.CompilerParams(
            collective_id=1, has_side_effects=True, vmem_limit_bytes=56 * MIB
        ),
        name="front",
    )(
        tokens, seg_ids.reshape(length, 1), seg_ids, routes, cos, sin,
        in_proj, out_proj, tiny, mine, other, grad,
    )


ORDER = (7, 6, 3, 2, 5, 4, 1, 0)
GROUP_AT = {2: (2, 0), 4: (0, 2), 6: (2, 2)}


def pick(step, table):
    value = jnp.int32(table[-1])
    for i, item in enumerate(table[:-1]):
        value = jnp.where(step == i, item, value)
    return value


def group_kernel(
    v_ref, g_ref, xs, g_all, w_ref, xn, attn,
    mix_sum, dx_own, dx_in, grads, xq, aq,
    wbuf, xbuf, gbuf, xt, gt_, hidg, dgu, deven, dodd, rc, meven, modd, mrc, acc, stage,
    sem_w, sem_x, sem_g, sem_m, sem_s, send_sem, recv_sem,
):
    wire = Wire(send_sem, recv_sem)
    r, f = wire.r, wire.f
    length, width = g_ref.shape
    hidden = w_ref.shape[1] // 3
    cols_a = aq.shape[2]
    expert = 2 * r + lax.rem(f // 2, 2)
    step_cols = 256

    load_w = pltpu.make_async_copy(w_ref, wbuf, sem_w.at[0])
    load_w.start()

    def load(step):
        slot = lax.rem(step, 2)
        k = pick(step, ORDER)

        @pl.when(k == 0)
        def _():
            pltpu.make_async_copy(v_ref, xbuf.at[slot], sem_x.at[slot]).start()
            pltpu.make_async_copy(g_ref, gbuf.at[slot], sem_g.at[slot]).start()

        @pl.when(k > 0)
        def _():
            pltpu.make_async_copy(xs.at[k], xbuf.at[slot], sem_x.at[slot]).start()
            pltpu.make_async_copy(g_all.at[k], gbuf.at[slot], sem_g.at[slot]).start()

    load(jnp.int32(0))
    wire.meet(PARTNERS_GROUP)
    act = {}
    for k in (2, 3, 1):
        to_a = flips(r, k) * cols_a
        act["a", k] = wire.send(
            attn.at[:, pl.ds(pl.multiple_of(to_a, cols_a), cols_a)], aq.at[k], k, 0
        )
    act["x", 2] = wire.send(xn, xq.at[2], 2, 0)
    act["x", 1] = wire.send(xn, xq.at[1], 1, 0)
    act["x", 3] = wire.plan(xq.at[2], xq.at[3], 1, 0)
    to_core = {k: wire.plan(dodd.at[n % 2], rc.at[n], 1, 0) for n, k in enumerate((6, 2, 4, 0))}
    mix_core = {k: wire.plan(modd.at[n % 2], mrc.at[n], 1, 0) for n, k in enumerate((6, 2, 4, 0))}
    back = {k: wire.plan(deven.at[k // 2], dx_in.at[k // 2 - 1], *GROUP_AT[k]) for k in (2, 4, 6)}
    acc[...] = jnp.zeros_like(acc)
    lane = lax.broadcasted_iota(jnp.int32, (length, EXTRA), 1)
    load_w.wait()

    def keep_mix(n, k):
        return pltpu.make_async_copy(meven.at[n % 2], mix_sum.at[k // 2], sem_m.at[n % 2])

    def block(step, carry):
        slot = lax.rem(step, 2)

        @pl.when(step < 7)
        def _():
            load(step + 1)

        pltpu.make_async_copy(v_ref, xbuf.at[slot], sem_x.at[slot]).wait()
        pltpu.make_async_copy(g_ref, gbuf.at[slot], sem_g.at[slot]).wait()
        extra = xbuf[slot, :, width:].astype(f32)
        mine = (lane == expert) | (lane == expert + 8)
        gate = jnp.sum(jnp.where(mine, extra, 0.0), axis=1, keepdims=True)
        xt[...] = xbuf[slot, :, :width].T
        gt_[...] = gbuf[slot].T

        def first(c, dgate):
            at = pl.multiple_of(c * step_cols, step_cols)
            u = matmul(xbuf[slot, :, :width], wbuf[:, pl.ds(at, step_cols)])
            up = matmul(xbuf[slot, :, :width], wbuf[:, pl.ds(hidden + at, step_cols)])
            rev = matmul(gbuf[slot], wbuf[:, pl.ds(2 * hidden + at, step_cols)])
            sig = 1.0 / (1.0 + jnp.exp(-u))
            act = u * sig
            hid = act * up
            hidg[:, pl.ds(at, step_cols)] = (gate * hid).astype(bf16)
            dgate = dgate + jnp.sum(rev * hid, axis=1, keepdims=True)
            dhid = gate * rev
            dgu[:, pl.ds(at, step_cols)] = (
                dhid * up * sig * (1.0 + u * (1.0 - sig))
            ).astype(bf16)
            dgu[:, pl.ds(hidden + at, step_cols)] = (dhid * act).astype(bf16)
            return dgate

        dgate = lax.fori_loop(
            0, hidden // step_cols, first, jnp.zeros((length, 1), f32)
        )
        high = dgate.astype(bf16).astype(f32)
        rest = dgate - high
        tail = (
            jnp.where(lane == expert, high, 0.0) + jnp.where(lane == expert + 8, rest, 0.0)
        ).astype(bf16)

        def out_parts(dst_d, n_d, dst_m, n_m):
            def second(c, carry):
                at = pl.multiple_of(c * step_cols, step_cols)
                dst_d[n_d, :, pl.ds(at, step_cols)] = contract_cols(
                    dgu[...], wbuf[pl.ds(at, step_cols), pl.ds(0, 2 * hidden)]
                ).astype(bf16)
                dst_m[n_m, :, pl.ds(at, step_cols)] = contract_cols(
                    hidg[...], wbuf[pl.ds(at, step_cols), pl.ds(2 * hidden, hidden)]
                ).astype(bf16)
                return carry

            lax.fori_loop(0, width // step_cols, second, 0)
            dst_d[n_d, :, width:] = tail

        pair = step // 2

        @pl.when(slot == 0)
        def _():
            for n, k in enumerate((6, 2, 4, 0)):
                if n >= 2:

                    @pl.when(pair == n)
                    def _():
                        to_core[(6, 2, 4, 0)[n - 2]].wait_send()
                        mix_core[(6, 2, 4, 0)[n - 2]].wait_send()

            out_parts(dodd, lax.rem(pair, 2), modd, lax.rem(pair, 2))
            for n, k in enumerate((6, 2, 4, 0)):

                @pl.when(pair == n)
                def _():
                    to_core[k].start()
                    mix_core[k].start()
                    if n == 2:
                        act["x", 2].wait_recv()
                        act["x", 3].start()

        @pl.when(slot == 1)
        def _():
            for n, k in enumerate((6, 2, 4, 0)):
                if n >= 2:

                    @pl.when(pair == n)
                    def _():
                        keep_mix(n - 2, (6, 2, 4, 0)[n - 2]).wait()

            out_parts(deven, pick(pair, (3, 1, 2, 0)), meven, lax.rem(pair, 2))
            for n, k in enumerate((6, 2, 4, 0)):

                @pl.when(pair == n)
                def _():
                    to_core[k].wait_recv()
                    deven[k // 2] = (
                        deven[k // 2].astype(f32) + rc[n].astype(f32)
                    ).astype(bf16)
                    if k:
                        back[k].start()
                    mix_core[k].wait_recv()
                    meven[n % 2] = (
                        meven[n % 2].astype(f32) + mrc[n].astype(f32)
                    ).astype(bf16)
                    keep_mix(n, k).start()

        def third(c, carry):
            at = pl.multiple_of(c * step_cols, step_cols)
            acc[:, pl.ds(at, step_cols)] += matmul(xt[...], dgu[:, pl.ds(at, step_cols)])
            return carry

        lax.fori_loop(0, 2 * hidden // step_cols, third, 0)

        def fourth(c, carry):
            at = pl.multiple_of(c * step_cols, step_cols)
            acc[:, pl.ds(2 * hidden + at, step_cols)] += matmul(
                gt_[...], hidg[:, pl.ds(at, step_cols)]
            )
            return carry

        lax.fori_loop(0, hidden // step_cols, fourth, 0)
        return carry

    lax.fori_loop(0, 8, block, 0)
    keep = pltpu.make_async_copy(deven.at[0], dx_own, sem_w.at[0])
    keep.start()
    parts = 8
    rows = width // parts

    def out(j, slot):
        return pltpu.make_async_copy(
            stage.at[slot], grads.at[pl.ds(j * rows, rows)], sem_s.at[slot]
        )

    for j in range(parts):
        slot = j % 2
        if j >= 2:
            out(j - 2, slot).wait()
        stage[slot] = acc[j * rows : (j + 1) * rows].astype(bf16)
        out(j, slot).start()
    for j in range(parts - 2, parts):
        out(j, j % 2).wait()
    keep.wait()
    keep_mix(2, 4).wait()
    keep_mix(3, 0).wait()
    for k in (2, 4, 6):
        back[k].wait_recv()
        back[k].wait_send()
    for k in (4, 0):
        to_core[k].wait_send()
        mix_core[k].wait_send()
    act["x", 1].wait_recv()
    act["x", 3].wait_recv()
    act["x", 3].wait_send()
    for k in (1, 2, 3):
        act["a", k].wait_recv()
    wire.finish()


PARTNERS_GROUP = ((1, 0), (2, 0), (3, 0), (0, 2), (2, 2))
GROUP_SENDS = 6 + 8 + 3


def run_group(v, grad, xs, g_all, w, xn, attn):
    length, width = grad.shape
    wide = v.shape[1]
    cols = w.shape[1]
    hidden = cols // 3
    any_spec = pl.BlockSpec(memory_space=pl.ANY)
    return pl.pallas_call(
        group_kernel,
        out_shape=[
            jax.ShapeDtypeStruct((4, length, width), bf16),
            jax.ShapeDtypeStruct((length, wide), bf16),
            jax.ShapeDtypeStruct((3, length, wide), bf16),
            jax.ShapeDtypeStruct((width, cols), bf16),
            jax.ShapeDtypeStruct((4, length, width), bf16),
            jax.ShapeDtypeStruct((4, length, attn.shape[1] // 4), bf16),
        ],
        in_specs=[any_spec] * 7,
        out_specs=[any_spec] * 6,
        scratch_shapes=[
            pltpu.VMEM((width, cols), bf16),
            pltpu.VMEM((2, length, wide), bf16),
            pltpu.VMEM((2, length, width), bf16),
            pltpu.VMEM((width, length), bf16),
            pltpu.VMEM((width, length), bf16),
            pltpu.VMEM((length, hidden), bf16),
            pltpu.VMEM((length, 2 * hidden), bf16),
            pltpu.VMEM((4, length, wide), bf16),
            pltpu.VMEM((2, length, wide), bf16),
            pltpu.VMEM((4, length, wide), bf16),
            pltpu.VMEM((2, length, width), bf16),
            pltpu.VMEM((2, length, width), bf16),
            pltpu.VMEM((4, length, width), bf16),
            pltpu.VMEM((width, cols), f32),
            pltpu.VMEM((2, width // 8, cols), bf16),
            pltpu.SemaphoreType.DMA((1,)),
            pltpu.SemaphoreType.DMA((2,)),
            pltpu.SemaphoreType.DMA((2,)),
            pltpu.SemaphoreType.DMA((2,)),
            pltpu.SemaphoreType.DMA((2,)),
            pltpu.SemaphoreType.DMA((GROUP_SENDS,)),
            pltpu.SemaphoreType.DMA((GROUP_SENDS,)),
        ],
        compiler_params=pltpu.CompilerParams(
            collective_id=2, has_side_effects=True, vmem_limit_bytes=62 * MIB
        ),
        cost_estimate=pl.CostEstimate(
            flops=48 * length * width * cols,
            bytes_accessed=64 * length * width + 4 * width * cols,
            transcendentals=8 * length * hidden,
        ),
        name="group",
    )(v, grad, xs, g_all, w, xn, attn)


PARTNERS_BACK = ((1, 0), (2, 0), (3, 0), (0, 1), (0, 2), (0, 4), (0, 6), (2, 2))
BACK_SENDS = 4 + 3 + 3 + 3 + 2 * 4 + 3 + 2 * 3 + 6 + 3 + 5


def back_kernel(
    dx_own, g_ref, first, table, tiny, v, tokens, qkv, lse, cos, sin, seg_col, seg_row,
    dx_in, grads, mix_sum, attn, xq, aq, xn, in_all, out_all,
    tokens_grad, terms_out,
    g_out, mix_in, d_out,
    in_v, out_v, din_v, gl, gy, gz, act_v, aq_v, pq, wo, wi, wyo, wyi, wzo, wzi, own_d,
    dn, dxn, dl, dattn, dproj, dkv, bias, tbuf, tr,
    local_sem, send_sem, recv_sem,
):
    wire = Wire(send_sem, recv_sem)
    r, f = wire.r, wire.f
    shard = gl.shape[1]
    length, width = tokens.shape
    experts = 8
    low = lax.rem(f // 2, 2)
    cols_p, cols_a = pq.shape[1], aq_v.shape[1]
    scale = HD ** (-0.5)
    used = [0]

    def local(src, dst):
        copy = pltpu.make_async_copy(src, dst, local_sem.at[used[0]])
        copy.start()
        used[0] += 1
        return copy

    def shard_rows(j):
        return pl.ds(pl.multiple_of(flips(f, j) * shard, shard), shard)

    def token_rows(k):
        return pl.ds(k * length, length)

    def part_of(k, cols):
        return pl.ds(pl.multiple_of(flips(r, k) * cols, cols), cols)

    def add(u, w):
        return (u.astype(f32) + w.astype(f32)).astype(bf16)

    load_dx = local(dx_in, din_v)
    load_out = local(out_all, out_v)
    load_g = {j: local(grads.at[shard_rows(j)], gl.at[j // 2]) for j in (2, 6, 4, 0)}
    load_in = local(in_all, in_v)
    load_a = [local(attn.at[:, part_of(0, cols_a)], aq_v.at[token_rows(0)])]
    load_a += [local(aq.at[k], aq_v.at[token_rows(k)]) for k in (1, 2, 3)]
    wire.meet(PARTNERS_BACK)
    got_y, got_m = {}, {}
    for j in (2, 6, 4, 0):
        got_y[j] = wire.send(grads.at[shard_rows(j + 1)], gy.at[j // 2], 0, 1)
    got_m[4] = wire.send(mix_sum.at[2], mix_in.at[1], 0, 2)

    spot = lax.broadcasted_iota(jnp.int32, bias.shape, 0)
    keys_at = lax.broadcasted_iota(jnp.int32, bias.shape, 1)
    bias[...] = jnp.where((spot >= keys_at) & (seg_col[...] == seg_row[...]), 0.0, -1e30)
    tbuf[0] = jnp.zeros_like(tbuf[0])
    load_dx.wait()

    def sum_dx(c, carry):
        at = pl.ds(pl.multiple_of(c * ROWS, ROWS), ROWS)
        d = dx_own[at, :].astype(f32)
        for n in range(3):
            d = d + din_v[n, at, :].astype(f32)
        dn[at, :] = d[:, :width]
        dgate = d[:, width:]
        dgate = dgate + pltpu.roll(dgate, EXTRA - experts, 1)
        gates = table[at, :]
        mean = jnp.sum(gates * dgate, axis=-1, keepdims=True)
        dl[at, :] = (gates * (dgate - mean)).astype(bf16)
        return carry

    lax.fori_loop(0, length // ROWS, sum_dx, 0)
    dlt = dl[...].T[0:16]

    def add_router(c, carry):
        at = pl.ds(pl.multiple_of(c * 256, 256), 256)
        row = lax.broadcasted_iota(jnp.int32, (16, 256), 0)
        router = jnp.where(row < experts, tiny[:, at], 0.0).astype(bf16)
        dn[:, at] = dn[:, at] + matmul(dl[:, 0:16], router)
        tbuf[0, :, at] = matmul(dlt, v[:, at])
        return carry

    lax.fori_loop(0, width // 256, add_router, 0)

    def norm_two(c, gain):
        at = pl.ds(pl.multiple_of(c * ROWS, ROWS), ROWS)
        h = first[at, :]
        r2 = lax.rsqrt(jnp.mean(h * h, axis=-1, keepdims=True) + epsilon)
        unit = h * r2
        d = dn[at, :]
        gain = gain + jnp.sum(d * unit, axis=0, keepdims=True)
        d = d * tiny[experts + 1 : experts + 2, :]
        d = g_ref[at, :].astype(f32) + r2 * (
            d - unit * jnp.mean(d * unit, axis=-1, keepdims=True)
        )
        dn[at, :] = d
        act_v[at, :] = d.astype(bf16)
        return gain

    gain_two = lax.fori_loop(0, length // ROWS, norm_two, jnp.zeros((1, width), f32))
    tbuf[0, experts + 1 : experts + 2, :] = gain_two
    got_r = {}
    got_r[2] = wire.send(act_v.at[token_rows(0)], act_v.at[token_rows(2)], 2, 0)
    got_r[1] = wire.send(act_v.at[token_rows(0)], act_v.at[token_rows(1)], 1, 0)
    load_out.wait()

    def to_attn(c, carry):
        at = pl.ds(pl.multiple_of(c * 256, 256), 256)
        dattn[:, at] = matmul(act_v[0:length, :], out_v[:, at]).astype(bf16)
        return carry

    lax.fori_loop(0, WQ // 256, to_attn, 0)
    lane = lax.broadcasted_iota(jnp.int32, (length, HD), 1)

    def turn_back(w):
        return w * cos[...] - pltpu.roll(w, HD // 2, 1) * sin[...]

    got_z = {}

    def pass_y(j):
        load_g[j].wait()
        got_y[j].wait_recv()
        gl[j // 2] = add(gl[j // 2], gy[j // 2])
        got_z[j] = wire.send(gl.at[j // 2], gz.at[j // 2 - 1], 0, j)

    for group in range(KV):
        k_at = pl.ds(WQ + group * HD, HD)
        v_at = pl.ds(WQ + WK + group * HD, HD)
        dkv[...] = jnp.zeros_like(dkv)

        def head(i, carry):
            h = group * GROUP + i
            at = pl.ds(pl.multiple_of(h * HD, HD), HD)
            s = contract_cols(qkv[:, at], qkv[:, k_at]) * scale + bias[...]
            level = jnp.sum(jnp.where(lane == h, lse[...], 0.0), axis=1, keepdims=True)
            p = jnp.exp(s - level)
            da = dattn[:, at]
            dp = contract_cols(da, qkv[:, v_at])
            delta = jnp.sum(p * dp, axis=-1, keepdims=True)
            ds = (p * (dp - delta)).astype(bf16)
            dkv[1] += contract_rows(p.astype(bf16), da)
            dkv[0] += contract_rows(ds, qkv[:, at])
            dproj[:, at] = turn_back(matmul(ds, qkv[:, k_at]) * scale).astype(bf16)
            return carry

        lax.fori_loop(0, GROUP, head, 0)
        dproj[:, k_at] = turn_back(dkv[0] * scale).astype(bf16)
        dproj[:, v_at] = dkv[1].astype(bf16)
        if group == 0:
            got_r[2].wait_recv()
            got_r[3] = wire.send(act_v.at[token_rows(2)], act_v.at[token_rows(3)], 1, 0)

    keep_p = local(dproj.at[:, part_of(0, cols_p)], pq.at[token_rows(0)])
    got_p = {}
    for k in (2, 3, 1):
        got_p[k] = wire.send(dproj.at[:, part_of(k, cols_p)], pq.at[token_rows(k)], k, 0)
    got_m[2] = wire.send(mix_sum.at[1], mix_in.at[0], 2, 0)
    got_m[6] = wire.send(mix_sum.at[3], mix_in.at[2], 2, 2)

    for copy in load_a:
        copy.wait()
    got_r[1].wait_recv()
    got_r[3].wait_recv()

    def dense_out(c, carry):
        at = pl.ds(pl.multiple_of(c * 256, 256), 256)
        wo[at, :] = matmul(act_v[:, at].T, aq_v[...]).astype(bf16)
        return carry

    lax.fori_loop(0, width // 256, dense_out, 0)
    for copy in (got_r[2], got_r[1], got_r[3]):
        copy.wait_send()
    load_x = [local(xn, act_v.at[token_rows(0)])]
    load_x += [local(xq.at[k], act_v.at[token_rows(k)]) for k in (1, 2, 3)]
    got_wo, got_wi, got_wzo, got_wzi = {}, {}, {}, {}
    for j in (2, 6, 4, 0):
        got_wo[j] = wire.send(wo.at[shard_rows(j + 1)], wyo.at[j // 2], 0, 1)
    pass_y(2)

    keep_p.wait()
    for copy in load_x:
        copy.wait()
    for k in (1, 2, 3):
        got_p[k].wait_recv()

    def dense_in(c, carry):
        at = pl.ds(pl.multiple_of(c * 256, 256), 256)
        wi[at, :] = matmul(act_v[:, at].T, pq[...]).astype(bf16)
        return carry

    lax.fori_loop(0, width // 256, dense_in, 0)
    for j in (2, 6, 4, 0):
        got_wi[j] = wire.send(wi.at[shard_rows(j + 1)], wyi.at[j // 2], 0, 1)
    pass_y(6)

    load_in.wait()

    def to_norm(c, carry):
        at = pl.ds(pl.multiple_of(c * 256, 256), 256)
        dxn[:, at] = contract_cols(dproj[...], in_v[at, :])
        return carry

    lax.fori_loop(0, width // 256, to_norm, 0)

    def norm_one(c, gain):
        at = pl.ds(pl.multiple_of(c * ROWS, ROWS), ROWS)
        x = tokens[at, :].astype(f32)
        r1 = lax.rsqrt(jnp.mean(x * x, axis=-1, keepdims=True) + epsilon)
        unit = x * r1
        d = dxn[at, :]
        gain = gain + jnp.sum(d * unit, axis=0, keepdims=True)
        d = d * tiny[experts : experts + 1, :]
        d = dn[at, :] + r1 * (d - unit * jnp.mean(d * unit, axis=-1, keepdims=True))
        tokens_grad[at, :] = d.astype(bf16)
        return gain

    gain_one = lax.fori_loop(0, length // ROWS, norm_one, jnp.zeros((1, width), f32))
    tbuf[0, experts : experts + 1, :] = gain_one
    pass_y(4)
    for n, d in enumerate(((1, 0), (0, 1), (2, 0), (0, 2), (0, 4))):
        copy = wire.send(tbuf.at[n], tr.at[n], *d)
        copy.wait_recv()
        tbuf[n + 1] = tbuf[n] + tr[n]
    terms_out[...] = tbuf[5]

    for j in (2, 6, 4):
        got_wo[j].wait_recv()
        wyo[j // 2] = add(wo[shard_rows(j), :], wyo[j // 2])
        got_wzo[j] = wire.send(wyo.at[j // 2], wzo.at[j // 2 - 1], 0, j)
    for j in (2, 6, 4):
        got_wi[j].wait_recv()
        wyi[j // 2] = add(wi[shard_rows(j), :], wyi[j // 2])
        got_wzi[j] = wire.send(wyi.at[j // 2], wzi.at[j // 2 - 1], 0, j)

    mine, other = 2 * r + low, 2 * r + 1 - low
    load_g[0].wait()
    got_y[0].wait_recv()
    got_z[4].wait_recv()
    got_z[2].wait_send()
    gl[0] = (gl[0].astype(f32) + gy[0].astype(f32) + gz[1].astype(f32)).astype(bf16)
    kept = [local(gl.at[0], g_out.at[mine])]
    got_e = {}
    got_e[2, 0] = wire.send(gl.at[0], g_out.at[mine], 2, 0)
    got_e[1, 0] = wire.send(gl.at[0], g_out.at[mine], 1, 0)
    got_z[2].wait_recv()
    got_z[6].wait_recv()
    gz[0] = add(gz[0], gz[2])
    kept.append(local(gz.at[0], g_out.at[other]))
    got_e[2, 1] = wire.send(gz.at[0], g_out.at[other], 2, 0)
    got_e[1, 1] = wire.send(gz.at[0], g_out.at[other], 1, 0)

    def own_rows(w, y, z, got_w, got_zs, cols):
        got_w[0].wait_recv()
        total = w[shard_rows(0), :].astype(f32) + y[0].astype(f32)
        for j in (2, 4, 6):
            got_zs[j].wait_recv()
            total = total + z[j // 2 - 1].astype(f32)
        own_d[:, cols] = total.astype(bf16)

    own_rows(wo, wyo, wzo, got_wo, got_wzo, pl.ds(cols_p, cols_a))
    own_rows(wi, wyi, wzi, got_wi, got_wzi, pl.ds(0, cols_p))
    kept.append(local(own_d, d_out.at[r]))
    got_d = [wire.send(own_d, d_out.at[r], k, 0) for k in (2, 3, 1)]

    far = flips(r, 2)
    for n, e in ((0, 2 * far + low), (1, 2 * far + 1 - low)):
        got_e[2, n].wait_recv()
        got_e[3, n] = wire.send(g_out.at[e], g_out.at[e], 1, 0)
    for k in (1, 3):
        for n in (0, 1):
            got_e[k, n].wait_recv()
    for copy in got_d:
        copy.wait_recv()
    for k in (2, 4, 6):
        got_m[k].wait_recv()
    for copy in kept:
        copy.wait()
    wire.finish((got_r[2], got_r[1], got_r[3], got_z[2]))


def run_back(
    dx_own, grad, first, table, tiny, v, tokens, qkv, lse, cos, sin, seg_ids,
    dx_in, grads, mix_sum, attn, xq, aq, xn, in_all, out_all,
):
    any_spec = pl.BlockSpec(memory_space=pl.ANY)
    vmem = pl.BlockSpec(memory_space=pltpu.VMEM)
    length, width = tokens.shape
    shard = width // 8
    cols = grads.shape[1]
    cols_p, cols_a = qkv.shape[1] // 4, attn.shape[1] // 4
    return pl.pallas_call(
        back_kernel,
        out_shape=[
            jax.ShapeDtypeStruct((length, width), bf16),
            jax.ShapeDtypeStruct((16, width), f32),
            jax.ShapeDtypeStruct((8, shard, cols), bf16),
            jax.ShapeDtypeStruct((3, length, width), bf16),
            jax.ShapeDtypeStruct((4, shard, cols_p + cols_a), bf16),
        ],
        in_specs=[vmem] * 13 + [any_spec] * 9,
        out_specs=[vmem] * 2 + [any_spec] * 3,
        scratch_shapes=[
            pltpu.VMEM(in_all.shape, bf16),
            pltpu.VMEM(out_all.shape, bf16),
            pltpu.VMEM(dx_in.shape, bf16),
            pltpu.VMEM((4, shard, cols), bf16),
            pltpu.VMEM((4, shard, cols), bf16),
            pltpu.VMEM((3, shard, cols), bf16),
            pltpu.VMEM((4 * length, width), bf16),
            pltpu.VMEM((4 * length, cols_a), bf16),
            pltpu.VMEM((4 * length, cols_p), bf16),
            pltpu.VMEM((width, cols_a), bf16),
            pltpu.VMEM((width, cols_p), bf16),
            pltpu.VMEM((4, shard, cols_a), bf16),
            pltpu.VMEM((4, shard, cols_p), bf16),
            pltpu.VMEM((3, shard, cols_a), bf16),
            pltpu.VMEM((3, shard, cols_p), bf16),
            pltpu.VMEM((shard, cols_p + cols_a), bf16),
            pltpu.VMEM((length, width), f32),
            pltpu.VMEM((length, width), f32),
            pltpu.VMEM((length, EXTRA), bf16),
            pltpu.VMEM((length, WQ), bf16),
            pltpu.VMEM(qkv.shape, bf16),
            pltpu.VMEM((2, length, HD), f32),
            pltpu.VMEM((length, length), f32),
            pltpu.VMEM((6, 16, width), f32),
            pltpu.VMEM((5, 16, width), f32),
            pltpu.SemaphoreType.DMA((20,)),
            pltpu.SemaphoreType.DMA((BACK_SENDS,)),
            pltpu.SemaphoreType.DMA((BACK_SENDS,)),
        ],
        compiler_params=pltpu.CompilerParams(
            collective_id=3, has_side_effects=True, vmem_limit_bytes=62 * MIB
        ),
        name="back",
    )(
        dx_own, grad, first, table, tiny, v, tokens, qkv, lse, cos, sin,
        seg_ids.reshape(length, 1), seg_ids,
        dx_in, grads, mix_sum, attn, xq, aq, xn, in_all, out_all,
    )


def near_layer(
    tokens, seg_ids, routes, in_proj, out_proj, router, norm_gains, expert_in, expert_out,
    out_grad,
):
    length, width = tokens.shape
    experts = router.shape[1]
    hidden = expert_out.shape[2]
    shard = router.shape[0]
    r, f = lax.axis_index("replica"), lax.axis_index("fsdp")
    cosine, sine = [t[:, 0] for t in tables(length)]
    cos = jnp.concatenate([cosine, cosine], axis=1)
    sin = jnp.concatenate([-sine, sine], axis=1)
    tiny = jnp.concatenate(
        [router.T, norm_gains.T, jnp.zeros((16 - experts - 2, shard), bf16)], axis=0
    )
    none = jnp.zeros_like(tiny)
    tiny = jnp.where(
        f % 2 == 0,
        jnp.concatenate([tiny, none], axis=1),
        jnp.concatenate([none, tiny], axis=1),
    )
    low = (f >> 1) & 1
    mine, other = [
        jnp.concatenate(
            [
                lax.dynamic_index_in_dim(expert_in, e, 1, keepdims=False),
                lax.dynamic_index_in_dim(expert_out, e, 1, keepdims=False),
            ],
            axis=1,
        )
        for e in (2 * r + low, 2 * r + 1 - low)
    ]
    qkv, attn, xn, first, lse, table, small, v, in_all, out_all, w_all, g_all, xs = front(
        tokens, seg_ids, routes, cos, sin, in_proj, out_proj, tiny, mine, other, out_grad
    )
    mix_sum, dx_own, dx_in, grads, xq, aq = run_group(v, out_grad, xs, g_all, w_all, xn, attn)
    tokens_grad, terms, expert_sum, mix_in, dense = run_back(
        dx_own, out_grad, first, table, small, v, tokens, qkv, lse, cos, sin, seg_ids,
        dx_in, grads, mix_sum, attn, xq, aq, xn, in_all, out_all,
    )
    mixed = first + mix_sum[0].astype(f32)
    for k in range(3):
        mixed = mixed + mix_in[k].astype(f32)
    cut = in_proj.shape[1] // 4
    in_grad = dense[:, :, :cut].transpose(1, 0, 2).reshape(shard, -1)
    out_proj_grad = dense[:, :, cut:].transpose(1, 0, 2).reshape(shard, -1)
    expert_sum = expert_sum.transpose(1, 0, 2)
    terms = lax.dynamic_slice_in_dim(terms, f * shard, shard, 1).T
    return (
        mixed.astype(bf16),
        tokens_grad,
        in_grad.astype(f32),
        out_proj_grad.astype(f32),
        terms[:, :experts],
        terms[:, experts : experts + 2],
        expert_sum[..., : 2 * hidden].astype(f32),
        expert_sum[..., 2 * hidden :].astype(f32),
    )


class Wide:
    def __init__(self, n_rep, n_fsdp):
        self.n_rep, self.n_fsdp = n_rep, n_fsdp

    def spread(self, value):
        every = lax.all_gather(value, "replica", axis=0)
        return [every[k] for k in range(self.n_rep)]

    def collect(self, parts):
        return lax.psum_scatter(jnp.stack(parts), "replica", scatter_dimension=0).astype(f32)

    def start(self, in_proj, out_proj, tiny, expert_in, expert_out, grad):
        r = lax.axis_index("replica")
        per = expert_in.shape[1] // self.n_rep
        weights = []
        for i in range(per):
            both = jnp.concatenate(
                [
                    lax.dynamic_index_in_dim(expert_in, per * r + i, 1, keepdims=False),
                    lax.dynamic_index_in_dim(expert_out, per * r + i, 1, keepdims=False),
                ],
                axis=1,
            )
            weights.append(lax.all_gather(both, "fsdp", axis=0, tiled=True))
        return (
            lax.all_gather(in_proj, "fsdp", axis=0, tiled=True),
            lax.all_gather(out_proj, "fsdp", axis=0, tiled=True),
            lax.all_gather(tiny, "fsdp", axis=1, tiled=True),
            (weights, self.spread(grad)),
        )

    def experts(self, payload, held):
        weights, gs = held
        xs = self.spread(payload)
        per = len(weights)
        mixes, dxs, grads = None, None, []
        for i, w in enumerate(weights):

            def expert_of(i=i):
                return per * lax.axis_index("replica") + i

            mix, dx, grad = run_expert(xs, gs, [w], expert_of, lambda j: 0)
            mixes = mix if mixes is None else [a + b for a, b in zip(mixes, mix)]
            dxs = dx if dxs is None else [a + b for a, b in zip(dxs, dx)]
            grads.append(grad[0])
        return self.collect(dxs), (mixes, grads)

    def trade(self, value):
        cut = value.reshape(value.shape[0], self.n_rep, -1).transpose(1, 0, 2)
        got = lax.all_to_all(cut, "replica", 0, 0)
        return got.reshape(-1, got.shape[2])

    def end(self, held, first, normed, attn, dres, dproj, terms):
        mixes, grads = held
        mixed = first + self.collect(mixes)
        own = jnp.stack(
            [lax.psum_scatter(g, "fsdp", scatter_dimension=0, tiled=True) for g in grads]
        )
        expert_sum = lax.all_gather(own, "replica", axis=0, tiled=True).transpose(1, 0, 2)
        dense = []
        for left, right in ((normed, dproj), (dres, attn)):
            left = lax.all_gather(left, "replica", axis=0, tiled=True)
            part = contract_rows(left, self.trade(right)).astype(bf16)
            own = lax.psum_scatter(part, "fsdp", scatter_dimension=0, tiled=True)
            dense.append(lax.all_gather(own, "replica", axis=1, tiled=True))
        return mixed, dense[0], dense[1], expert_sum, lax.psum(terms, ("replica", "fsdp"))


def layer(
    net, tokens, seg_ids, routes, in_proj, out_proj, router, norm_gains, expert_in, expert_out,
    out_grad,
):
    length, width = tokens.shape
    experts = router.shape[1]
    hidden = expert_out.shape[2]
    shard = router.shape[0]
    scale = HD ** (-0.5)
    cosine, sine = tables(length)
    segment = seg_ids[0]
    place = jnp.arange(length)
    allowed = ((place[:, None] >= place[None, :]) & (segment[:, None] == segment[None, :]))[
        None, None
    ]
    tiny = jnp.concatenate(
        [router.T, norm_gains.T, jnp.zeros((16 - experts - 2, shard), bf16)], axis=0
    )
    proj_in, proj_out, tiny, held = net.start(
        in_proj, out_proj, tiny, expert_in, expert_out, out_grad
    )
    router_rows = tiny[:experts]
    gain_one = tiny[experts].astype(f32)
    gain_two = tiny[experts + 1].astype(f32)

    inputs = tokens.astype(f32)
    scale_one = rms_scale(inputs)
    unit_one = inputs * scale_one
    normed = (unit_one * gain_one).astype(bf16)
    proj = matmul(normed, proj_in)
    queries = (
        rotate(proj[:, :WQ].reshape(length, HQ, HD), cosine, sine)
        .astype(bf16)
        .reshape(length, KV, GROUP, HD)
    )
    keys = rotate(proj[:, WQ : WQ + WK].reshape(length, KV, HD), cosine, sine).astype(bf16)
    values = proj[:, WQ + WK :].reshape(length, KV, HD).astype(bf16)
    scores = jnp.einsum("qkgd,tkd->kgqt", queries, keys, preferred_element_type=f32) * scale
    masked = jnp.where(allowed, scores, -1e30)
    highest = jnp.max(masked, axis=-1, keepdims=True)
    expo = jnp.exp(masked - highest)
    total = jnp.sum(expo, axis=-1, keepdims=True)
    log_total = highest + jnp.log(total)
    probs_low = (expo / total).astype(bf16)
    attn = jnp.einsum("kgqt,tkd->qkgd", probs_low, values, preferred_element_type=f32)
    attn = attn.astype(bf16).reshape(length, WQ)
    first = inputs + contract_cols(attn, proj_out)
    scale_two = rms_scale(first)
    unit_two = first * scale_two
    normed_two = (unit_two * gain_two).astype(bf16)
    logits = contract_cols(normed_two, router_rows)
    onehot = (routes[:, :, None] == jnp.arange(experts)[None, None, :]).astype(f32)
    chosen = jnp.sum(onehot * logits[:, None, :], axis=-1)
    gates = jax.nn.softmax(chosen, axis=-1)
    table = jnp.sum(gates[:, :, None] * onehot, axis=1)
    high = table.astype(bf16)
    low = (table - high.astype(f32)).astype(bf16)
    payload = jnp.concatenate(
        [normed_two, high, low, jnp.zeros((length, EXTRA - 2 * experts), bf16)], axis=1
    )
    dx, held = net.experts(payload, held)

    grad_out = out_grad.astype(f32)
    dgate_all = dx[:, width : width + experts] + dx[:, width + experts : width + 2 * experts]
    dgate = jnp.sum(onehot * dgate_all[:, None, :], axis=-1)
    dchosen = gates * (dgate - jnp.sum(gates * dgate, axis=-1, keepdims=True))
    dlogits = jnp.sum(dchosen[:, :, None] * onehot, axis=1).astype(bf16)
    dnormed_two = dx[:, :width] + matmul(dlogits, router_rows)
    gain_two_grad = jnp.sum(dnormed_two * unit_two, axis=0)
    dunit_two = dnormed_two * gain_two
    dfirst = grad_out + scale_two * (
        dunit_two - unit_two * jnp.mean(dunit_two * unit_two, axis=-1, keepdims=True)
    )
    dres = dfirst.astype(bf16)
    dattn = matmul(dres, proj_out).astype(bf16).reshape(length, KV, GROUP, HD)
    probs = jnp.exp(masked - log_total)
    probs_again = probs.astype(bf16)
    dprobs = jnp.einsum("qkgd,tkd->kgqt", dattn, values, preferred_element_type=f32)
    dvalues = jnp.einsum("kgqt,qkgd->tkd", probs_again, dattn, preferred_element_type=f32)
    delta = jnp.sum(probs * dprobs, axis=-1, keepdims=True)
    dscores = (probs * (dprobs - delta)).astype(bf16)
    dqueries = jnp.einsum("kgqt,tkd->qkgd", dscores, keys, preferred_element_type=f32) * scale
    dkeys = jnp.einsum("kgqt,qkgd->tkd", dscores, queries, preferred_element_type=f32) * scale
    dqueries = rotate(dqueries.reshape(length, HQ, HD), cosine, -sine).reshape(length, WQ)
    dkeys = rotate(dkeys, cosine, -sine).reshape(length, WK)
    dproj = jnp.concatenate([dqueries, dkeys, dvalues.reshape(length, WK)], axis=1).astype(bf16)
    dnormed = contract_cols(dproj, proj_in)
    gain_one_grad = jnp.sum(dnormed * unit_one, axis=0)
    dunit_one = dnormed * gain_one
    tokens_grad = (
        dfirst
        + scale_one
        * (dunit_one - unit_one * jnp.mean(dunit_one * unit_one, axis=-1, keepdims=True))
    ).astype(bf16)

    terms = jnp.concatenate(
        [
            contract_rows(dlogits, normed_two),
            gain_one_grad[None],
            gain_two_grad[None],
            jnp.zeros((16 - experts - 2, width), f32),
        ],
        axis=0,
    )
    mixed, in_proj_grad, out_proj_grad, expert_sum, terms = net.end(
        held, first, normed, attn, dres, dproj, terms
    )
    terms = lax.dynamic_slice_in_dim(terms, lax.axis_index("fsdp") * shard, shard, 1).T
    return (
        mixed.astype(bf16),
        tokens_grad,
        in_proj_grad.astype(f32),
        out_proj_grad.astype(f32),
        terms[:, :experts],
        terms[:, experts : experts + 2],
        expert_sum[..., : 2 * hidden].astype(f32),
        expert_sum[..., 2 * hidden :].astype(f32),
    )


def solution(mesh):
    n_rep, n_fsdp = mesh.shape["replica"], mesh.shape["fsdp"]
    if (n_rep, n_fsdp) == (4, 8):
        body = near_layer
    else:
        body = functools.partial(layer, Wide(n_rep, n_fsdp))
    both = P(("replica", "fsdp"), None)
    fsdp, deep = P("fsdp", None), P("fsdp", None, None)
    return jax.shard_map(
        body,
        mesh=mesh,
        in_specs=(both, both, both, fsdp, fsdp, fsdp, fsdp, deep, deep, both),
        out_specs=(both, both, fsdp, fsdp, fsdp, fsdp, deep, deep),
        check_vma=False,
    )
```

```python
import functools

import jax
import jax.numpy as jnp
from jax import lax
from jax.experimental import pallas as pl
from jax.experimental.pallas import tpu as pltpu
from jax.sharding import PartitionSpec as P

HQ = 12
KV = 2
HD = 128
GROUP = HQ // KV
WQ = HQ * HD
WK = KV * HD
EXTRA = 128
MIB = 1024 * 1024

epsilon = 1e-06
rope_base = 1000000.0
bf16 = jnp.bfloat16
f32 = jnp.float32


def rms_scale(v):
    return lax.rsqrt(jnp.mean(v * v, axis=-1, keepdims=True) + epsilon)


def tables(length):
    half = HD // 2
    freq = jnp.power(rope_base, -(jnp.arange(half, dtype=f32) * 2.0 / HD))
    angle = jnp.arange(length, dtype=f32)[:, None] * freq[None, :]
    return (jnp.cos(angle)[:, None, :], jnp.sin(angle)[:, None, :])


def rotate(v, cosine, sine):
    half = v.shape[-1] // 2
    first = v[..., :half]
    second = v[..., half:]
    return jnp.concatenate(
        [first * cosine - second * sine, second * cosine + first * sine], axis=-1
    )


def contract_rows(left, right):
    return lax.dot_general(left, right, (((0,), (0,)), ((), ())), preferred_element_type=f32)


def contract_cols(left, right):
    return lax.dot_general(left, right, (((1,), (1,)), ((), ())), preferred_element_type=f32)


def matmul(left, right):
    return lax.dot_general(left, right, (((1,), (0,)), ((), ())), preferred_element_type=f32)


def expert_kernel(nt, nw, length, width, hidden, rows, expert_of, offset_of, *refs):
    xs, gs, ws = refs[:nt], refs[nt : 2 * nt], refs[2 * nt : 2 * nt + nw]
    refs = refs[2 * nt + nw :]
    mixes, dxs, grads = refs[:nt], refs[nt : 2 * nt], refs[2 * nt : 2 * nt + nw]
    (
        wbuf, xbuf, gbuf, xt, gt_, hidg, dgu, mbuf, dbuf, acc, stage,
        sem_w, sem_x, sem_g, sem_m, sem_d, sem_s,
    ) = refs[2 * nt + nw :]
    cols = 3 * hidden
    step_cols = 256

    def load(k, slot):
        for i in range(nt):

            @pl.when(k == i)
            def _():
                pltpu.make_async_copy(xs[i], xbuf.at[slot], sem_x.at[slot]).start()
                pltpu.make_async_copy(gs[i], gbuf.at[slot], sem_g.at[slot]).start()

    def store(k, slot):
        for i in range(nt):

            @pl.when(k == i)
            def _():
                pltpu.make_async_copy(mbuf.at[slot], mixes[i], sem_m.at[slot]).start()
                pltpu.make_async_copy(dbuf.at[slot], dxs[i], sem_d.at[slot]).start()

    def stored(slot):
        pltpu.make_async_copy(mbuf.at[slot], mixes[0], sem_m.at[slot]).wait()
        pltpu.make_async_copy(dbuf.at[slot], dxs[0], sem_d.at[slot]).wait()

    for j in range(nw):
        pltpu.make_async_copy(
            ws[j], wbuf.at[pl.ds(pl.multiple_of(offset_of(j), 8), rows)], sem_w.at[j]
        ).start()
    load(0, 0)
    expert = expert_of()
    acc[...] = jnp.zeros_like(acc)
    lane = lax.broadcasted_iota(jnp.int32, (length, EXTRA), 1)
    for j in range(nw):
        pltpu.make_async_copy(
            ws[j], wbuf.at[pl.ds(pl.multiple_of(offset_of(j), 8), rows)], sem_w.at[j]
        ).wait()

    def block(k, carry):
        slot = lax.rem(k, 2)

        @pl.when(k + 1 < nt)
        def _():
            load(k + 1, 1 - slot)

        pltpu.make_async_copy(xs[0], xbuf.at[slot], sem_x.at[slot]).wait()
        pltpu.make_async_copy(gs[0], gbuf.at[slot], sem_g.at[slot]).wait()

        @pl.when(k >= 2)
        def _():
            stored(slot)

        extra = xbuf[slot, :, width:].astype(f32)
        mine = (lane == expert) | (lane == expert + 8)
        gate = jnp.sum(jnp.where(mine, extra, 0.0), axis=1, keepdims=True)
        xt[...] = xbuf[slot, :, :width].T
        gt_[...] = gbuf[slot].T

        def first(c, dgate):
            at = pl.multiple_of(c * step_cols, step_cols)
            u = matmul(xbuf[slot, :, :width], wbuf[:, pl.ds(at, step_cols)])
            up = matmul(xbuf[slot, :, :width], wbuf[:, pl.ds(hidden + at, step_cols)])
            back = matmul(gbuf[slot], wbuf[:, pl.ds(2 * hidden + at, step_cols)])
            sig = 1.0 / (1.0 + jnp.exp(-u))
            act = u * sig
            hid = act * up
            hidg[:, pl.ds(at, step_cols)] = (gate * hid).astype(bf16)
            dgate = dgate + jnp.sum(back * hid, axis=1, keepdims=True)
            dhid = gate * back
            dgu[:, pl.ds(at, step_cols)] = (
                dhid * up * sig * (1.0 + u * (1.0 - sig))
            ).astype(bf16)
            dgu[:, pl.ds(hidden + at, step_cols)] = (dhid * act).astype(bf16)
            return dgate

        dgate = lax.fori_loop(
            0, hidden // step_cols, first, jnp.zeros((length, 1), f32)
        )

        def second(c, carry):
            at = pl.multiple_of(c * step_cols, step_cols)
            mbuf[slot, :, pl.ds(at, step_cols)] = contract_cols(
                hidg[...], wbuf[pl.ds(at, step_cols), pl.ds(2 * hidden, hidden)]
            ).astype(bf16)
            dbuf[slot, :, pl.ds(at, step_cols)] = contract_cols(
                dgu[...], wbuf[pl.ds(at, step_cols), pl.ds(0, 2 * hidden)]
            ).astype(bf16)
            return carry

        lax.fori_loop(0, width // step_cols, second, 0)
        high = dgate.astype(bf16).astype(f32)
        low = dgate - high
        dbuf[slot, :, width:] = (
            jnp.where(lane == expert, high, 0.0) + jnp.where(lane == expert + 8, low, 0.0)
        ).astype(bf16)
        store(k, slot)

        def third(c, carry):
            at = pl.multiple_of(c * step_cols, step_cols)
            acc[:, pl.ds(at, step_cols)] += matmul(xt[...], dgu[:, pl.ds(at, step_cols)])
            return carry

        lax.fori_loop(0, 2 * hidden // step_cols, third, 0)

        def fourth(c, carry):
            at = pl.multiple_of(c * step_cols, step_cols)
            acc[:, pl.ds(2 * hidden + at, step_cols)] += matmul(
                gt_[...], hidg[:, pl.ds(at, step_cols)]
            )
            return carry

        lax.fori_loop(0, hidden // step_cols, fourth, 0)
        return carry

    lax.fori_loop(0, nt, block, 0)
    stored(0)
    stored(1)
    for j in range(nw):
        slot = j % 2
        if j >= 2:
            pltpu.make_async_copy(stage.at[slot], grads[j - 2], sem_s.at[slot]).wait()
        stage[slot] = acc[pl.ds(pl.multiple_of(offset_of(j), 8), rows)].astype(bf16)
        pltpu.make_async_copy(stage.at[slot], grads[j], sem_s.at[slot]).start()
    for j in range(max(0, nw - 2), nw):
        pltpu.make_async_copy(stage.at[j % 2], grads[j], sem_s.at[j % 2]).wait()


def run_expert(xs, gs, ws, expert_of, offset_of):
    nt, nw = len(xs), len(ws)
    length, width = gs[0].shape
    rows, cols = ws[0].shape
    hidden = cols // 3
    outs = (
        [jax.ShapeDtypeStruct((length, width), bf16)] * nt
        + [jax.ShapeDtypeStruct((length, width + EXTRA), bf16)] * nt
        + [jax.ShapeDtypeStruct((rows, cols), bf16)] * nw
    )
    any_spec = pl.BlockSpec(memory_space=pl.ANY)
    result = pl.pallas_call(
        functools.partial(
            expert_kernel, nt, nw, length, width, hidden, rows, expert_of, offset_of
        ),
        out_shape=outs,
        in_specs=[any_spec] * (2 * nt + nw),
        out_specs=[any_spec] * len(outs),
        scratch_shapes=[
            pltpu.VMEM((width, cols), bf16),
            pltpu.VMEM((2, length, width + EXTRA), bf16),
            pltpu.VMEM((2, length, width), bf16),
            pltpu.VMEM((width, length), bf16),
            pltpu.VMEM((width, length), bf16),
            pltpu.VMEM((length, hidden), bf16),
            pltpu.VMEM((length, 2 * hidden), bf16),
            pltpu.VMEM((2, length, width), bf16),
            pltpu.VMEM((2, length, width + EXTRA), bf16),
            pltpu.VMEM((width, cols), f32),
            pltpu.VMEM((2, rows, cols), bf16),
            pltpu.SemaphoreType.DMA((nw,)),
            pltpu.SemaphoreType.DMA((2,)),
            pltpu.SemaphoreType.DMA((2,)),
            pltpu.SemaphoreType.DMA((2,)),
            pltpu.SemaphoreType.DMA((2,)),
            pltpu.SemaphoreType.DMA((2,)),
        ],
        compiler_params=pltpu.CompilerParams(vmem_limit_bytes=60 * MIB),
        cost_estimate=pl.CostEstimate(
            flops=6 * nt * length * width * cols,
            bytes_accessed=8 * nt * length * width + 4 * width * cols,
            transcendentals=nt * length * hidden,
        ),
        name="expert",
    )(*xs, *gs, *ws)
    return result[:nt], result[nt : 2 * nt], result[2 * nt :]


MESH_ID = pl.DeviceIdType.MESH


def flip(index, bit):
    return index + bit - 2 * bit * lax.rem(index // bit, 2)


def flips(index, mask):
    for bit in (1, 2, 4):
        if mask & bit:
            index = flip(index, bit)
    return index


class Wire:
    def __init__(self, send_sem, recv_sem):
        self.r, self.f = lax.axis_index("replica"), lax.axis_index("fsdp")
        self.send_sem, self.recv_sem = send_sem, recv_sem
        self.used, self.sent = 0, []

    def meet(self, partners):
        barrier = pltpu.get_barrier_semaphore()
        for d_r, d_f in partners:
            pl.semaphore_signal(
                barrier, inc=1, device_id=self.at(d_r, d_f), device_id_type=MESH_ID
            )
        pl.semaphore_wait(barrier, len(partners))

    def at(self, d_r, d_f):
        return (flips(self.r, d_r), flips(self.f, d_f))

    def plan(self, src, dst, d_r, d_f):
        copy = pltpu.make_async_remote_copy(
            src_ref=src,
            dst_ref=dst,
            send_sem=self.send_sem.at[self.used],
            recv_sem=self.recv_sem.at[self.used],
            device_id=self.at(d_r, d_f),
            device_id_type=MESH_ID,
        )
        self.used += 1
        assert self.used <= self.send_sem.shape[0]
        return copy

    def send(self, src, dst, d_r, d_f):
        copy = self.plan(src, dst, d_r, d_f)
        copy.start()
        self.sent.append(copy)
        return copy

    def finish(self, waited=()):
        for copy in self.sent:
            if all(copy is not other for other in waited):
                copy.wait_send()


CUTS = 2
FRONT_SENDS = 2 * 28 + 7 + 7 * CUTS + 4 + 3
PARTNERS = ((1, 0), (2, 0), (0, 1), (0, 2), (0, 4), (0, 6))
ROWS = 64


def turn(v, cosine, sine):
    return v * cosine + pltpu.roll(v, HD // 2, 1) * sine


def front_kernel(
    tokens, seg_col, seg_row, routes, cos, sin,
    in_ref, out_ref, tiny_ref, mine_ref, other_ref, g_ref,
    qkv, attn, xn, first, lse, table, tiny_out, v,
    in_all, out_all, w_all, g_all, xs,
    in_v, out_v, tiny_v, rt, bias, w_buf, local_sem, send_sem, recv_sem,
):
    wire = Wire(send_sem, recv_sem)
    r, f = wire.r, wire.f
    shard = in_ref.shape[0]
    quarter = shard // 4
    length, width = tokens.shape
    experts = 8
    scale = HD ** (-0.5)

    def rows(j, k):
        at = flips(f, j) * shard + flips(r, k) * quarter
        return pl.ds(pl.multiple_of(at, quarter), quarter)

    def shard_rows(j):
        return pl.ds(pl.multiple_of(flips(f, j) * shard, shard), shard)

    def local(n, src, dst):
        copy = pltpu.make_async_copy(src, dst, local_sem.at[n])
        copy.start()
        return copy

    own_in = local(0, in_ref, in_v.at[shard_rows(0)])
    own_out = local(1, out_ref, out_v.at[shard_rows(0)])
    own_tiny = local(2, tiny_ref, tiny_v.at[f])
    own_w = local(3, mine_ref, w_buf)
    wire.meet(PARTNERS)

    own = pl.ds(pl.multiple_of(r * quarter, quarter), quarter)
    land = {"in": in_v, "out": out_v}
    source = {"in": in_ref, "out": out_ref}
    got, got_t, got_w, got_g, got_x = {}, {}, {}, {}, {}

    for m in (2, 4, 6, 1):
        got_t[m] = wire.send(tiny_ref, tiny_v.at[f], 0, m)

    def own_pieces(name):
        for m in (2, 4, 6, 1):
            got[name, m, 0] = wire.send(
                source[name].at[own], land[name].at[rows(0, 0)], 0, m
            )

    def pass_on(name, j, k, d_r, d_f):
        at = land[name].at[rows(j, k)]
        return wire.send(at, at, d_r, d_f)

    def near_pieces(name):
        for m in (1, 2, 4, 6):
            got[name, m, 0].wait_recv()
            if m != 1:
                got[name, m + 1, 0] = pass_on(name, m, 0, 0, 1)
            got[name, m, 2] = pass_on(name, m, 0, 2, 0)
            got[name, m, 1] = pass_on(name, m, 0, 1, 0)

    def far_pieces(name):
        for m in (3, 5, 7):
            got[name, m, 0].wait_recv()
            got[name, m, 2] = pass_on(name, m, 0, 2, 0)
            got[name, m, 1] = pass_on(name, m, 0, 1, 0)

    def side_pieces(name):
        for m in (1, 2, 4, 6, 3, 5, 7):
            got[name, m, 2].wait_recv()
            got[name, m, 3] = pass_on(name, m, 2, 1, 0)

    def all_pieces(name):
        for m in range(1, 8):
            got[name, m, 1].wait_recv()
            got[name, m, 3].wait_recv()

    own_pieces("in")
    own_pieces("out")
    own_w.wait()
    kept = [local(4, w_buf, w_all.at[shard_rows(0)])]

    for m in (2, 4, 6):
        got_t[m].wait_recv()
        at = tiny_v.at[flips(f, m)]
        got_t[m + 1] = wire.send(at, at, 0, 1)
    for m in (1, 3, 5, 7):
        got_t[m].wait_recv()
    own_tiny.wait()
    lanes = tiny_v.shape[2]
    rt[...] = jnp.zeros_like(rt)
    for z in range(4):
        both = tiny_v[2 * z].astype(f32) + tiny_v[2 * z + 1].astype(f32)
        tiny_out[:, z * lanes : (z + 1) * lanes] = both
        row = lax.broadcasted_iota(jnp.int32, both.shape, 0)
        rt[0:16, z * lanes : (z + 1) * lanes] = jnp.where(row < experts, both, 0.0).astype(bf16)

    def norm_one(c, carry):
        at = pl.ds(pl.multiple_of(c * ROWS, ROWS), ROWS)
        x = tokens[at, :].astype(f32)
        unit = x * lax.rsqrt(jnp.mean(x * x, axis=-1, keepdims=True) + epsilon)
        xn[at, :] = (unit * tiny_out[experts : experts + 1, :]).astype(bf16)
        return carry

    lax.fori_loop(0, length // ROWS, norm_one, 0)
    spot = lax.broadcasted_iota(jnp.int32, bias.shape, 0)
    keys_at = lax.broadcasted_iota(jnp.int32, bias.shape, 1)
    bias[...] = jnp.where((spot >= keys_at) & (seg_col[...] == seg_row[...]), 0.0, -1e30)

    cut = shard // CUTS

    def send_w(n, src, d_f):
        at = pl.ds(n * cut, cut)
        to = pl.ds(pl.multiple_of(f * shard + n * cut, cut), cut)
        return wire.send(src.at[at], w_all.at[to], 0, d_f)

    def pass_w(n, m):
        got_w[m, n].wait_recv()
        at = w_all.at[pl.ds(pl.multiple_of(flips(f, m) * shard + n * cut, cut), cut)]
        got_w[m + 1, n] = wire.send(at, at, 0, 1)

    near_pieces("in")
    for n in range(CUTS):
        for m, src in ((2, other_ref), (4, mine_ref), (6, other_ref)):
            got_w[m, n] = send_w(n, src, m)
    got_g[4] = wire.send(g_ref, g_all.at[4], 0, 2)
    got_g[1] = wire.send(g_ref, g_all.at[1], 1, 0)
    far_pieces("in")
    near_pieces("out")
    far_pieces("out")
    for n in range(CUTS):
        got_w[1, n] = send_w(n, mine_ref, 1)
    got_g[2] = wire.send(g_ref, g_all.at[2], 2, 0)
    side_pieces("in")
    own_in.wait()
    all_pieces("in")

    def project(c, carry):
        at = pl.multiple_of(c * 256, 256)
        t = matmul(xn[...], in_v[:, pl.ds(at, 256)])
        turned = c < 7
        for n in (0, 1):
            part = t[:, n * HD : (n + 1) * HD]
            part = turn(
                part, jnp.where(turned, cos[...], 1.0), jnp.where(turned, sin[...], 0.0)
            )
            qkv[:, pl.ds(at + n * HD, HD)] = part.astype(bf16)
        return carry

    lax.fori_loop(0, 8, project, 0)
    pass_w(0, 2)
    lane = lax.broadcasted_iota(jnp.int32, (length, HD), 1)
    lse[...] = jnp.zeros_like(lse)

    def head(h, carry):
        at = pl.ds(pl.multiple_of(h * HD, HD), HD)
        group = h // GROUP
        k_at = pl.ds(pl.multiple_of(WQ + group * HD, HD), HD)
        v_at = pl.ds(pl.multiple_of(WQ + WK + group * HD, HD), HD)
        s = contract_cols(qkv[:, at], qkv[:, k_at]) * scale + bias[...]
        highest = jnp.max(s, axis=-1, keepdims=True)
        expo = jnp.exp(s - highest)
        total = jnp.sum(expo, axis=-1, keepdims=True)
        p = (expo * (1.0 / total)).astype(bf16)
        attn[:, at] = matmul(p, qkv[:, v_at]).astype(bf16)
        lse[...] = jnp.where(lane == h, highest + jnp.log(total), lse[...])
        return carry

    lax.fori_loop(0, HQ // 2, head, 0)
    side_pieces("out")
    pass_w(0, 4)
    lax.fori_loop(HQ // 2, HQ, head, 0)
    pass_w(0, 6)
    own_out.wait()
    all_pieces("out")
    kept.append(local(5, in_v, in_all))
    kept.append(local(6, out_v, out_all))

    def add_out(c, carry):
        at = pl.ds(pl.multiple_of(c * 256, 256), 256)
        first[:, at] = tokens[:, at].astype(f32) + contract_cols(attn[...], out_v[at, :])
        return carry

    lax.fori_loop(0, width // 256, add_out, 0)

    def norm_two(c, carry):
        at = pl.ds(pl.multiple_of(c * ROWS, ROWS), ROWS)
        h = first[at, :]
        unit = h * lax.rsqrt(jnp.mean(h * h, axis=-1, keepdims=True) + epsilon)
        v[at, 0:width] = (unit * tiny_out[experts + 1 : experts + 2, :]).astype(bf16)
        return carry

    lax.fori_loop(0, length // ROWS, norm_two, 0)
    logits = contract_cols(v[:, 0:width], rt[...])
    chosen = lane == routes[:, 0:1]
    for j in range(1, routes.shape[1]):
        chosen = chosen | (lane == routes[:, j : j + 1])
    logits = jnp.where(chosen, logits, -1e30)
    expo = jnp.exp(logits - jnp.max(logits, axis=-1, keepdims=True))
    expo = jnp.where(chosen, expo, 0.0)
    gates = expo / jnp.sum(expo, axis=-1, keepdims=True)
    table[...] = gates
    high = gates.astype(bf16).astype(f32)
    v[:, width:] = (high + pltpu.roll(gates - high, experts, 1)).astype(bf16)

    got_x[2] = wire.send(v, xs.at[2], 2, 0)
    got_x[1] = wire.send(v, xs.at[1], 1, 0)
    for n in range(1, CUTS):
        for m in (2, 4, 6):
            pass_w(n, m)
    got_g[2].wait_recv()
    got_g[3] = wire.send(g_all.at[2], g_all.at[3], 1, 0)
    got_x[2].wait_recv()
    got_x[3] = wire.send(xs.at[2], xs.at[3], 1, 0)
    for n in range(CUTS):
        for m in (1, 3, 5, 7):
            got_w[m, n].wait_recv()
    for m in (1, 3, 4):
        got_g[m].wait_recv()
    for m in (1, 3):
        got_x[m].wait_recv()
    for copy in kept:
        copy.wait()
    wire.finish()


def front(tokens, seg_ids, routes, cos, sin, in_proj, out_proj, tiny, mine, other, grad):
    any_spec = pl.BlockSpec(memory_space=pl.ANY)
    vmem = pl.BlockSpec(memory_space=pltpu.VMEM)
    length, width = tokens.shape
    shard, cols = in_proj.shape
    whole = 8 * shard
    wide = width + EXTRA
    return pl.pallas_call(
        front_kernel,
        out_shape=[
            jax.ShapeDtypeStruct((length, cols), bf16),
            jax.ShapeDtypeStruct((length, WQ), bf16),
            jax.ShapeDtypeStruct((length, width), bf16),
            jax.ShapeDtypeStruct((length, width), f32),
            jax.ShapeDtypeStruct((length, HD), f32),
            jax.ShapeDtypeStruct((length, EXTRA), f32),
            jax.ShapeDtypeStruct((16, width), f32),
            jax.ShapeDtypeStruct((length, wide), bf16),
            jax.ShapeDtypeStruct((whole, cols), bf16),
            jax.ShapeDtypeStruct((whole, out_proj.shape[1]), bf16),
            jax.ShapeDtypeStruct((whole, mine.shape[1]), bf16),
            jax.ShapeDtypeStruct((5,) + grad.shape, bf16),
            jax.ShapeDtypeStruct((4, length, wide), bf16),
        ],
        in_specs=[vmem] * 6 + [any_spec] * 6,
        out_specs=[vmem] * 8 + [any_spec] * 5,
        scratch_shapes=[
            pltpu.VMEM((whole, cols), bf16),
            pltpu.VMEM((whole, out_proj.shape[1]), bf16),
            pltpu.VMEM((8,) + tiny.shape, bf16),
            pltpu.VMEM((EXTRA, width), bf16),
            pltpu.VMEM((length, length), f32),
            pltpu.VMEM(mine.shape, bf16),
            pltpu.SemaphoreType.DMA((8,)),
            pltpu.SemaphoreType.DMA((FRONT_SENDS,)),
            pltpu.SemaphoreType.DMA((FRONT_SENDS,)),
        ],
        compiler_params=pltpu.CompilerParams(
            collective_id=1, has_side_effects=True, vmem_limit_bytes=56 * MIB
        ),
        name="front",
    )(
        tokens, seg_ids.reshape(length, 1), seg_ids, routes, cos, sin,
        in_proj, out_proj, tiny, mine, other, grad,
    )


ORDER = (3, 2, 4, 5, 7, 6, 1, 0)
GROUP_AT = {2: (2, 0), 4: (0, 2), 6: (2, 2)}


def pick(step, table):
    value = jnp.int32(table[-1])
    for i, item in enumerate(table[:-1]):
        value = jnp.where(step == i, item, value)
    return value


def group_kernel(
    v_ref, g_ref, xs, g_all, w_ref, xn,
    mix_sum, dx_own, dx_in, grads, xq, x_late, g_late,
    wbuf, xbuf, gbuf, xt, gt_, hidg, dgu, deven, dodd, rc, meven, modd, mrc, acc, stage,
    sem_w, sem_x, sem_g, sem_m, sem_s, send_sem, recv_sem,
):
    wire = Wire(send_sem, recv_sem)
    r, f = wire.r, wire.f
    length, width = g_ref.shape
    hidden = w_ref.shape[1] // 3
    half = length // 2
    low, top = pl.ds(0, half), pl.ds(half, half)
    expert = 2 * r + lax.rem(f // 2, 2)
    step_cols = 256

    load_w = pltpu.make_async_copy(w_ref, wbuf, sem_w.at[0])
    load_w.start()

    def load(step):
        slot = lax.rem(step, 2)
        k = pick(step, ORDER)

        @pl.when(k == 0)
        def _():
            pltpu.make_async_copy(v_ref, xbuf.at[slot], sem_x.at[slot]).start()
            pltpu.make_async_copy(g_ref, gbuf.at[slot], sem_g.at[slot]).start()

        for table, src_x, src_g in (
            ((1, 2, 3), xs, g_all), ((4,), x_late, g_all), ((5, 6, 7), x_late, g_late)
        ):

            @pl.when((k >= table[0]) & (k <= table[-1]))
            def _():
                pltpu.make_async_copy(src_x.at[k], xbuf.at[slot], sem_x.at[slot]).start()
                pltpu.make_async_copy(src_g.at[k], gbuf.at[slot], sem_g.at[slot]).start()

    load(jnp.int32(0))
    wire.meet(PARTNERS_GROUP)
    late_x = {4: wire.send(v_ref, x_late.at[4], 0, 2)}
    far = [
        wire.send(g_all.at[4, low], g_late.at[6, low], 2, 0),
        wire.send(xs.at[2, top], x_late.at[6, top], 0, 2),
        wire.send(g_all.at[2, top], g_late.at[6, top], 0, 2),
    ]
    late_g = {5: wire.send(g_all.at[4], g_late.at[5], 1, 0)}
    act = {2: wire.send(xn, xq.at[2], 2, 0), 1: wire.send(xn, xq.at[1], 1, 0)}
    act[3] = wire.plan(xq.at[2], xq.at[3], 1, 0)
    far.append(wire.plan(x_late.at[4, low], x_late.at[6, low], 2, 0))
    late_x[5] = wire.plan(x_late.at[4], x_late.at[5], 1, 0)
    late_x[7] = wire.plan(x_late.at[6], x_late.at[7], 1, 0)
    late_g[7] = wire.plan(g_late.at[6], g_late.at[7], 1, 0)
    slots = {2: 0, 4: 1, 6: 2, 0: 3}
    to_core = {k: wire.plan(dodd.at[n % 2], rc.at[n], 1, 0) for k, n in slots.items()}
    mix_core = {k: wire.plan(modd.at[n % 2], mrc.at[n], 1, 0) for k, n in slots.items()}
    back = {k: wire.plan(deven.at[k // 2], dx_in.at[k // 2 - 1], *GROUP_AT[k]) for k in (2, 4, 6)}
    acc[...] = jnp.zeros_like(acc)
    lane = lax.broadcasted_iota(jnp.int32, (length, EXTRA), 1)
    load_w.wait()

    def keep_mix(k):
        n = slots[k] % 2
        return pltpu.make_async_copy(meven.at[n], mix_sum.at[k // 2], sem_m.at[n])

    def send_core(k):
        to_core[k].start()
        mix_core[k].start()

    def sent_core(k):
        to_core[k].wait_send()
        mix_core[k].wait_send()

    def complete(k):
        n = slots[k]
        to_core[k].wait_recv()
        deven[k // 2] = (deven[k // 2].astype(f32) + rc[n].astype(f32)).astype(bf16)
        if k in (4, 6):
            back[k].start()
        mix_core[k].wait_recv()
        meven[n % 2] = (meven[n % 2].astype(f32) + mrc[n].astype(f32)).astype(bf16)
        keep_mix(k).start()

    def block(step, carry):
        slot = lax.rem(step, 2)

        @pl.when((step == 0) | (step >= 4) & (step < 7))
        def _():
            load(step + 1)

        pltpu.make_async_copy(v_ref, xbuf.at[slot], sem_x.at[slot]).wait()
        pltpu.make_async_copy(g_ref, gbuf.at[slot], sem_g.at[slot]).wait()
        extra = xbuf[slot, :, width:].astype(f32)
        mine = (lane == expert) | (lane == expert + 8)
        gate = jnp.sum(jnp.where(mine, extra, 0.0), axis=1, keepdims=True)
        xt[...] = xbuf[slot, :, :width].T
        gt_[...] = gbuf[slot].T

        def first(c, dgate):
            at = pl.multiple_of(c * step_cols, step_cols)
            u = matmul(xbuf[slot, :, :width], wbuf[:, pl.ds(at, step_cols)])
            up = matmul(xbuf[slot, :, :width], wbuf[:, pl.ds(hidden + at, step_cols)])
            rev = matmul(gbuf[slot], wbuf[:, pl.ds(2 * hidden + at, step_cols)])
            sig = 1.0 / (1.0 + jnp.exp(-u))
            act = u * sig
            hid = act * up
            hidg[:, pl.ds(at, step_cols)] = (gate * hid).astype(bf16)
            dgate = dgate + jnp.sum(rev * hid, axis=1, keepdims=True)
            dhid = gate * rev
            dgu[:, pl.ds(at, step_cols)] = (
                dhid * up * sig * (1.0 + u * (1.0 - sig))
            ).astype(bf16)
            dgu[:, pl.ds(hidden + at, step_cols)] = (dhid * act).astype(bf16)
            return dgate

        dgate = lax.fori_loop(
            0, hidden // step_cols, first, jnp.zeros((length, 1), f32)
        )
        high = dgate.astype(bf16).astype(f32)
        rest = dgate - high
        tail = (
            jnp.where(lane == expert, high, 0.0) + jnp.where(lane == expert + 8, rest, 0.0)
        ).astype(bf16)

        def out_parts(dst_d, n_d, dst_m, n_m):
            def second(c, carry):
                at = pl.multiple_of(c * step_cols, step_cols)
                dst_d[n_d, :, pl.ds(at, step_cols)] = contract_cols(
                    dgu[...], wbuf[pl.ds(at, step_cols), pl.ds(0, 2 * hidden)]
                ).astype(bf16)
                dst_m[n_m, :, pl.ds(at, step_cols)] = contract_cols(
                    hidg[...], wbuf[pl.ds(at, step_cols), pl.ds(2 * hidden, hidden)]
                ).astype(bf16)
                return carry

            lax.fori_loop(0, width // step_cols, second, 0)
            dst_d[n_d, :, width:] = tail

        slot_two = pick(step, (0, 0, 1, 1, 0, 0, 1, 1))
        k = pick(step, ORDER)

        @pl.when(step == 4)
        def _():
            sent_core(2)

        @pl.when(step == 6)
        def _():
            sent_core(4)

        @pl.when(step == 5)
        def _():
            keep_mix(2).wait()

        @pl.when(step == 7)
        def _():
            keep_mix(4).wait()

        @pl.when(lax.rem(k, 2) == 1)
        def _():
            out_parts(dodd, slot_two, modd, slot_two)

        @pl.when(lax.rem(k, 2) == 0)
        def _():
            out_parts(deven, k // 2, meven, slot_two)

        def come_5():
            late_x[5].wait_recv()
            late_g[5].wait_recv()
            load(step + 1)

        def come_6():
            for copy in far:
                copy.wait_recv()
            late_x[7].start()
            late_g[7].start()
            act[2].wait_recv()
            act[3].start()

        for at_step, todo in (
            (0, (lambda: send_core(2),)),
            (1, (lambda: complete(2),)),
            (2, (come_5,)),
            (3, (lambda: send_core(4), come_6)),
            (4, (lambda: complete(4), lambda: send_core(6))),
            (5, (lambda: complete(6),)),
            (6, (lambda: send_core(0),)),
            (7, (lambda: complete(0),)),
        ):

            @pl.when(step == at_step)
            def _():
                for do in todo:
                    do()

        def third(c, carry):
            at = pl.multiple_of(c * step_cols, step_cols)
            acc[:, pl.ds(at, step_cols)] += matmul(xt[...], dgu[:, pl.ds(at, step_cols)])
            return carry

        lax.fori_loop(0, 2 * hidden // step_cols, third, 0)

        def fourth(c, carry):
            at = pl.multiple_of(c * step_cols, step_cols)
            acc[:, pl.ds(2 * hidden + at, step_cols)] += matmul(
                gt_[...], hidg[:, pl.ds(at, step_cols)]
            )
            return carry

        lax.fori_loop(0, hidden // step_cols, fourth, 0)

        @pl.when(step == 1)
        def _():
            late_x[4].wait_recv()
            late_x[5].start()
            far[3].start()
            back[2].start()
            load(step + 1)

        @pl.when(step == 3)
        def _():
            late_x[7].wait_recv()
            late_g[7].wait_recv()
            load(step + 1)

        return carry

    lax.fori_loop(0, 8, block, 0)
    keep = pltpu.make_async_copy(deven.at[0], dx_own, sem_w.at[0])
    keep.start()
    parts = 8
    rows = width // parts

    def out(j, slot):
        return pltpu.make_async_copy(
            stage.at[slot], grads.at[pl.ds(j * rows, rows)], sem_s.at[slot]
        )

    for j in range(parts):
        slot = j % 2
        if j >= 2:
            out(j - 2, slot).wait()
        stage[slot] = acc[j * rows : (j + 1) * rows].astype(bf16)
        out(j, slot).start()
    for j in range(parts - 2, parts):
        out(j, j % 2).wait()
    keep.wait()
    keep_mix(6).wait()
    keep_mix(0).wait()
    for k in (2, 4, 6):
        back[k].wait_recv()
        back[k].wait_send()
    sent_core(6)
    sent_core(0)
    act[1].wait_recv()
    act[3].wait_recv()
    for copy in (act[3], far[3], late_x[5], late_x[7], late_g[7]):
        copy.wait_send()
    wire.finish()


PARTNERS_GROUP = ((1, 0), (2, 0), (0, 2), (2, 2))
GROUP_SENDS = 12 + 8 + 3


def run_group(v, grad, xs, g_all, w, xn):
    length, width = grad.shape
    wide = v.shape[1]
    cols = w.shape[1]
    hidden = cols // 3
    any_spec = pl.BlockSpec(memory_space=pl.ANY)
    return pl.pallas_call(
        group_kernel,
        out_shape=[
            jax.ShapeDtypeStruct((4, length, width), bf16),
            jax.ShapeDtypeStruct((length, wide), bf16),
            jax.ShapeDtypeStruct((3, length, wide), bf16),
            jax.ShapeDtypeStruct((width, cols), bf16),
            jax.ShapeDtypeStruct((4, length, width), bf16),
            jax.ShapeDtypeStruct((8, length, wide), bf16),
            jax.ShapeDtypeStruct((8, length, width), bf16),
        ],
        in_specs=[any_spec] * 6,
        out_specs=[any_spec] * 7,
        scratch_shapes=[
            pltpu.VMEM((width, cols), bf16),
            pltpu.VMEM((2, length, wide), bf16),
            pltpu.VMEM((2, length, width), bf16),
            pltpu.VMEM((width, length), bf16),
            pltpu.VMEM((width, length), bf16),
            pltpu.VMEM((length, hidden), bf16),
            pltpu.VMEM((length, 2 * hidden), bf16),
            pltpu.VMEM((4, length, wide), bf16),
            pltpu.VMEM((2, length, wide), bf16),
            pltpu.VMEM((4, length, wide), bf16),
            pltpu.VMEM((2, length, width), bf16),
            pltpu.VMEM((2, length, width), bf16),
            pltpu.VMEM((4, length, width), bf16),
            pltpu.VMEM((width, cols), f32),
            pltpu.VMEM((2, width // 8, cols), bf16),
            pltpu.SemaphoreType.DMA((1,)),
            pltpu.SemaphoreType.DMA((2,)),
            pltpu.SemaphoreType.DMA((2,)),
            pltpu.SemaphoreType.DMA((2,)),
            pltpu.SemaphoreType.DMA((2,)),
            pltpu.SemaphoreType.DMA((GROUP_SENDS,)),
            pltpu.SemaphoreType.DMA((GROUP_SENDS,)),
        ],
        compiler_params=pltpu.CompilerParams(
            collective_id=2, has_side_effects=True, vmem_limit_bytes=62 * MIB
        ),
        cost_estimate=pl.CostEstimate(
            flops=48 * length * width * cols,
            bytes_accessed=64 * length * width + 4 * width * cols,
            transcendentals=8 * length * hidden,
        ),
        name="group",
    )(v, grad, xs, g_all, w, xn)


PARTNERS_BACK = ((1, 0), (2, 0), (3, 0), (0, 1), (0, 2), (0, 4), (0, 6))
TERMS = 16
BACK_SENDS = 4 + 3 + 3 + 2 + 3 + 2 * 4 + 2 * 3 + 1 + 6 + 3


def back_kernel(
    dx_own, g_ref, first, table, tiny, v, tokens, qkv, lse, cos, sin, seg_col, seg_row,
    dx_in, grads, mix_sum, attn, xq, xn, in_all, out_all,
    tokens_grad,
    g_out, mix_in, d_out,
    in_v, out_v, mix_v, gl, gy, gz, act_v, aq_v, pq, wo, wi, wyo, wyi, wzo, wzi, wxo, own_d,
    dn, dxn, dl, dattn, dproj, dkv, bias, tbuf,
    local_sem, send_sem, recv_sem,
):
    wire = Wire(send_sem, recv_sem)
    r, f = wire.r, wire.f
    shard = gl.shape[1]
    length, width = tokens.shape
    experts = 8
    low = lax.rem(f // 2, 2)
    cols_p, cols_a = pq.shape[1], aq_v.shape[1]
    scale = HD ** (-0.5)
    used = [0]

    def local(src, dst):
        copy = pltpu.make_async_copy(src, dst, local_sem.at[used[0]])
        copy.start()
        used[0] += 1
        return copy

    def shard_rows(j):
        return pl.ds(pl.multiple_of(flips(f, j) * shard, shard), shard)

    def token_rows(k):
        return pl.ds(k * length, length)

    def part_of(k, cols):
        return pl.ds(pl.multiple_of(flips(r, k) * cols, cols), cols)

    def add(u, w):
        return (u.astype(f32) + w.astype(f32)).astype(bf16)

    half = lax.rem(r, 2)
    side = r // 2

    def half_of(index):
        return pl.ds(pl.multiple_of(index * cols_a, cols_a), cols_a)

    load_dx = [
        local(dx_in.at[n], in_v.at[token_rows(n), pl.ds(0, dx_in.shape[2])]) for n in range(3)
    ]
    load_out = local(out_all, out_v)
    load_g = {j: local(grads.at[shard_rows(j)], gl.at[j // 2]) for j in (4, 0, 2, 6)}
    load_a = local(attn.at[:, half_of(half)], aq_v.at[token_rows(0)])
    load_mix = local(mix_sum.at[2], mix_v.at[0])
    wire.meet(PARTNERS_BACK)
    got_y, got_m = {}, {}
    for j in (4, 0, 2, 6):
        got_y[j] = wire.send(grads.at[shard_rows(j + 1)], gy.at[j // 2], 0, 1)
    got_a = wire.send(attn.at[:, half_of(1 - half)], aq_v.at[token_rows(1)], 1, 0)
    got_m[2] = wire.send(mix_sum.at[1], mix_in.at[0], 2, 0)
    got_m[6] = wire.send(mix_sum.at[3], mix_v.at[1], 2, 0)

    spot = lax.broadcasted_iota(jnp.int32, bias.shape, 0)
    keys_at = lax.broadcasted_iota(jnp.int32, bias.shape, 1)
    bias[...] = jnp.where((spot >= keys_at) & (seg_col[...] == seg_row[...]), 0.0, -1e30)
    tbuf[...] = jnp.zeros_like(tbuf)
    for copy in load_dx:
        copy.wait()

    def sum_dx(c, carry):
        at = pl.ds(pl.multiple_of(c * ROWS, ROWS), ROWS)
        d = dx_own[at, :].astype(f32)
        for n in range(3):
            here = pl.ds(pl.multiple_of(n * length + c * ROWS, ROWS), ROWS)
            d = d + in_v[here, 0 : dx_own.shape[1]].astype(f32)
        dn[at, :] = d[:, :width]
        dgate = d[:, width:]
        dgate = dgate + pltpu.roll(dgate, EXTRA - experts, 1)
        gates = table[at, :]
        mean = jnp.sum(gates * dgate, axis=-1, keepdims=True)
        dl[at, :] = (gates * (dgate - mean)).astype(bf16)
        return carry

    lax.fori_loop(0, length // ROWS, sum_dx, 0)
    load_in = local(in_all, in_v)
    dlt = dl[...].T[0:16]

    def add_router(c, carry):
        at = pl.ds(pl.multiple_of(c * 256, 256), 256)
        row = lax.broadcasted_iota(jnp.int32, (16, 256), 0)
        router = jnp.where(row < experts, tiny[:, at], 0.0).astype(bf16)
        dn[:, at] = dn[:, at] + matmul(dl[:, 0:16], router)
        tbuf[:, at] = matmul(dlt, v[:, at])
        return carry

    lax.fori_loop(0, width // 256, add_router, 0)

    def norm_two(c, gain):
        at = pl.ds(pl.multiple_of(c * ROWS, ROWS), ROWS)
        h = first[at, :]
        r2 = lax.rsqrt(jnp.mean(h * h, axis=-1, keepdims=True) + epsilon)
        unit = h * r2
        d = dn[at, :]
        gain = gain + jnp.sum(d * unit, axis=0, keepdims=True)
        d = d * tiny[experts + 1 : experts + 2, :]
        d = g_ref[at, :].astype(f32) + r2 * (
            d - unit * jnp.mean(d * unit, axis=-1, keepdims=True)
        )
        dn[at, :] = d
        act_v[at, :] = d.astype(bf16)
        return gain

    gain_two = lax.fori_loop(0, length // ROWS, norm_two, jnp.zeros((1, width), f32))
    tbuf[experts + 1 : experts + 2, :] = gain_two
    got_r = wire.send(act_v.at[token_rows(0)], act_v.at[token_rows(1)], 1, 0)
    load_out.wait()

    def to_attn(c, carry):
        at = pl.ds(pl.multiple_of(c * 256, 256), 256)
        dattn[:, at] = matmul(act_v[0:length, :], out_v[:, at]).astype(bf16)
        return carry

    lax.fori_loop(0, WQ // 256, to_attn, 0)
    lane = lax.broadcasted_iota(jnp.int32, (length, HD), 1)

    def turn_back(w):
        return w * cos[...] - pltpu.roll(w, HD // 2, 1) * sin[...]

    got_z = {}

    def pass_y(j):
        load_g[j].wait()
        got_y[j].wait_recv()
        gl[j // 2] = add(gl[j // 2], gy[j // 2])
        got_z[j] = wire.send(gl.at[j // 2], gz.at[j // 2 - 1], 0, j)

    pass_y(4)
    for group in range(KV):
        k_at = pl.ds(WQ + group * HD, HD)
        v_at = pl.ds(WQ + WK + group * HD, HD)
        dkv[...] = jnp.zeros_like(dkv)

        def head(i, carry):
            h = group * GROUP + i
            at = pl.ds(pl.multiple_of(h * HD, HD), HD)
            s = contract_cols(qkv[:, at], qkv[:, k_at]) * scale + bias[...]
            level = jnp.sum(jnp.where(lane == h, lse[...], 0.0), axis=1, keepdims=True)
            p = jnp.exp(s - level)
            da = dattn[:, at]
            dp = contract_cols(da, qkv[:, v_at])
            delta = jnp.sum(p * dp, axis=-1, keepdims=True)
            ds = (p * (dp - delta)).astype(bf16)
            dkv[1] += contract_rows(p.astype(bf16), da)
            dkv[0] += contract_rows(ds, qkv[:, at])
            dproj[:, at] = turn_back(matmul(ds, qkv[:, k_at]) * scale).astype(bf16)
            return carry

        lax.fori_loop(0, GROUP, head, 0)
        dproj[:, k_at] = turn_back(dkv[0] * scale).astype(bf16)
        dproj[:, v_at] = dkv[1].astype(bf16)

    keep_p = local(dproj.at[:, part_of(0, cols_p)], pq.at[token_rows(0)])
    got_p = {}
    for k in (2, 3, 1):
        got_p[k] = wire.send(dproj.at[:, part_of(k, cols_p)], pq.at[token_rows(k)], k, 0)

    load_a.wait()
    got_a.wait_recv()
    got_r.wait_recv()

    def dense_out(c, carry):
        at = pl.ds(pl.multiple_of(c * 256, 256), 256)
        wo[at, :] = matmul(act_v[0 : 2 * length, at].T, aq_v[...]).astype(bf16)
        return carry

    lax.fori_loop(0, width // 256, dense_out, 0)
    got_r.wait_send()
    load_x = [local(xn, act_v.at[token_rows(0)])]
    load_x += [local(xq.at[k], act_v.at[token_rows(k)]) for k in (1, 2, 3)]
    got_wo, got_wi, got_wzo, got_wzi = {}, {}, {}, {}
    for j in (2, 6, 4, 0):
        got_wo[j] = wire.send(wo.at[shard_rows(j + 1)], wyo.at[j // 2], 0, 1)

    load_in.wait()

    def to_norm(c, carry):
        at = pl.ds(pl.multiple_of(c * 256, 256), 256)
        dxn[:, at] = contract_cols(dproj[...], in_v[at, :])
        return carry

    lax.fori_loop(0, width // 256, to_norm, 0)

    def norm_one(c, gain):
        at = pl.ds(pl.multiple_of(c * ROWS, ROWS), ROWS)
        x = tokens[at, :].astype(f32)
        r1 = lax.rsqrt(jnp.mean(x * x, axis=-1, keepdims=True) + epsilon)
        unit = x * r1
        d = dxn[at, :]
        gain = gain + jnp.sum(d * unit, axis=0, keepdims=True)
        d = d * tiny[experts : experts + 1, :]
        d = dn[at, :] + r1 * (d - unit * jnp.mean(d * unit, axis=-1, keepdims=True))
        tokens_grad[at, :] = d.astype(bf16)
        return gain

    gain_one = lax.fori_loop(0, length // ROWS, norm_one, jnp.zeros((1, width), f32))
    tbuf[experts : experts + 1, :] = gain_one
    load_mix.wait()
    got_m[6].wait_recv()
    mix_v[0] = add(mix_v[0], mix_v[1])
    got_m[4] = wire.send(mix_v.at[0], mix_in.at[1], 0, 2)
    pass_y(2)

    mine, other = 2 * r + low, 2 * r + 1 - low
    load_g[0].wait()
    got_y[0].wait_recv()
    got_z[4].wait_recv()
    gl[0] = (gl[0].astype(f32) + gy[0].astype(f32) + gz[1].astype(f32)).astype(bf16)
    kept = [local(gl.at[0], g_out.at[mine])]
    got_e = {}

    keep_p.wait()
    for copy in load_x:
        copy.wait()
    for k in (1, 2, 3):
        got_p[k].wait_recv()
    got_e[2, 0] = wire.send(gl.at[0], g_out.at[mine], 2, 0)
    got_e[1, 0] = wire.send(gl.at[0], g_out.at[mine], 1, 0)

    tall = shard + TERMS

    def tall_rows(j):
        return pl.ds(pl.multiple_of(flips(f, j) * tall, TERMS), tall)

    for z in range(4):
        lanes = slice(2 * z * shard, 2 * (z + 1) * shard)
        both = matmul(act_v[:, lanes].T, pq[...]).astype(bf16)
        for y in (0, 1):
            top = (2 * z + y) * tall
            wi[top : top + shard, :] = both[y * shard : (y + 1) * shard]
            wi[top + shard : top + tall, :] = jnp.zeros((TERMS, cols_p), bf16)
            wi[top + shard : top + tall, 0 : 2 * shard] = tbuf[:, lanes].astype(bf16)
    for j in (2, 6, 4, 0):
        got_wi[j] = wire.send(wi.at[tall_rows(j + 1)], wyi.at[j // 2], 0, 1)
    pass_y(6)

    for j in (2, 6, 4):
        got_wo[j].wait_recv()
        wyo[j // 2] = add(wo[shard_rows(j), :], wyo[j // 2])
        got_wzo[j] = wire.send(wyo.at[j // 2], wzo.at[j // 2 - 1], 0, j)
    for j in (2, 6, 4):
        got_wi[j].wait_recv()
        wyi[j // 2] = add(wi[tall_rows(j), :], wyi[j // 2])
        got_wzi[j] = wire.send(wyi.at[j // 2], wzi.at[j // 2 - 1], 0, j)

    got_z[2].wait_recv()
    got_z[6].wait_recv()
    gz[0] = add(gz[0], gz[2])
    kept.append(local(gz.at[0], g_out.at[other]))
    got_e[2, 1] = wire.send(gz.at[0], g_out.at[other], 2, 0)
    got_e[1, 1] = wire.send(gz.at[0], g_out.at[other], 1, 0)

    def own_rows(w, rows, y, z, got_w, got_zs):
        got_w[0].wait_recv()
        total = w[rows, :].astype(f32) + y[0].astype(f32)
        for j in (2, 4, 6):
            got_zs[j].wait_recv()
            total = total + z[j // 2 - 1].astype(f32)
        return total

    wxo[0] = own_rows(wo, shard_rows(0), wyo, wzo, got_wo, got_wzo).astype(bf16)
    quarter = cols_a // 2

    def quarter_of(index):
        return pl.ds(pl.multiple_of(index * quarter, quarter), quarter)

    got_x = wire.send(
        wxo.at[0, :, quarter_of(1 - side)], wxo.at[1, :, pl.ds(0, quarter)], 2, 0
    )
    own_d[:, 0:cols_p] = own_rows(wi, tall_rows(0), wyi, wzi, got_wi, got_wzi).astype(bf16)
    got_x.wait_recv()
    own_d[shard:, cols_p:] = jnp.zeros((TERMS, quarter), bf16)
    own_d[0:shard, cols_p:] = add(wxo[0, :, quarter_of(side)], wxo[1, :, 0:quarter])
    kept.append(local(own_d, d_out.at[r]))
    got_d = [wire.send(own_d, d_out.at[r], k, 0) for k in (2, 3, 1)]

    far = flips(r, 2)
    for n, e in ((0, 2 * far + low), (1, 2 * far + 1 - low)):
        got_e[2, n].wait_recv()
        got_e[3, n] = wire.send(g_out.at[e], g_out.at[e], 1, 0)
    for k in (1, 3):
        for n in (0, 1):
            got_e[k, n].wait_recv()
    for copy in got_d:
        copy.wait_recv()
    for k in (2, 4):
        got_m[k].wait_recv()
    for copy in kept:
        copy.wait()
    wire.finish((got_r,))


def run_back(
    dx_own, grad, first, table, tiny, v, tokens, qkv, lse, cos, sin, seg_ids,
    dx_in, grads, mix_sum, attn, xq, xn, in_all, out_all,
):
    any_spec = pl.BlockSpec(memory_space=pl.ANY)
    vmem = pl.BlockSpec(memory_space=pltpu.VMEM)
    length, width = tokens.shape
    shard = width // 8
    cols = grads.shape[1]
    cols_p, cols_a = qkv.shape[1] // 4, attn.shape[1] // 2
    return pl.pallas_call(
        back_kernel,
        out_shape=[
            jax.ShapeDtypeStruct((length, width), bf16),
            jax.ShapeDtypeStruct((8, shard, cols), bf16),
            jax.ShapeDtypeStruct((2, length, width), bf16),
            jax.ShapeDtypeStruct((4, shard + TERMS, cols_p + cols_a // 2), bf16),
        ],
        in_specs=[vmem] * 13 + [any_spec] * 8,
        out_specs=[vmem] + [any_spec] * 3,
        scratch_shapes=[
            pltpu.VMEM(in_all.shape, bf16),
            pltpu.VMEM(out_all.shape, bf16),
            pltpu.VMEM((2, length, width), bf16),
            pltpu.VMEM((4, shard, cols), bf16),
            pltpu.VMEM((4, shard, cols), bf16),
            pltpu.VMEM((3, shard, cols), bf16),
            pltpu.VMEM((4 * length, width), bf16),
            pltpu.VMEM((2 * length, cols_a), bf16),
            pltpu.VMEM((4 * length, cols_p), bf16),
            pltpu.VMEM((width, cols_a), bf16),
            pltpu.VMEM((width + 8 * TERMS, cols_p), bf16),
            pltpu.VMEM((4, shard, cols_a), bf16),
            pltpu.VMEM((4, shard + TERMS, cols_p), bf16),
            pltpu.VMEM((3, shard, cols_a), bf16),
            pltpu.VMEM((3, shard + TERMS, cols_p), bf16),
            pltpu.VMEM((2, shard, cols_a), bf16),
            pltpu.VMEM((shard + TERMS, cols_p + cols_a // 2), bf16),
            pltpu.VMEM((length, width), f32),
            pltpu.VMEM((length, width), f32),
            pltpu.VMEM((length, EXTRA), bf16),
            pltpu.VMEM((length, WQ), bf16),
            pltpu.VMEM(qkv.shape, bf16),
            pltpu.VMEM((2, length, HD), f32),
            pltpu.VMEM((length, length), f32),
            pltpu.VMEM((TERMS, width), f32),
            pltpu.SemaphoreType.DMA((20,)),
            pltpu.SemaphoreType.DMA((BACK_SENDS,)),
            pltpu.SemaphoreType.DMA((BACK_SENDS,)),
        ],
        compiler_params=pltpu.CompilerParams(
            collective_id=3, has_side_effects=True, vmem_limit_bytes=62 * MIB
        ),
        name="back",
    )(
        dx_own, grad, first, table, tiny, v, tokens, qkv, lse, cos, sin,
        seg_ids.reshape(length, 1), seg_ids,
        dx_in, grads, mix_sum, attn, xq, xn, in_all, out_all,
    )


def near_layer(
    tokens, seg_ids, routes, in_proj, out_proj, router, norm_gains, expert_in, expert_out,
    out_grad,
):
    length, width = tokens.shape
    experts = router.shape[1]
    hidden = expert_out.shape[2]
    shard = router.shape[0]
    r, f = lax.axis_index("replica"), lax.axis_index("fsdp")
    cosine, sine = [t[:, 0] for t in tables(length)]
    cos = jnp.concatenate([cosine, cosine], axis=1)
    sin = jnp.concatenate([-sine, sine], axis=1)
    tiny = jnp.concatenate(
        [router.T, norm_gains.T, jnp.zeros((16 - experts - 2, shard), bf16)], axis=0
    )
    none = jnp.zeros_like(tiny)
    tiny = jnp.where(
        f % 2 == 0,
        jnp.concatenate([tiny, none], axis=1),
        jnp.concatenate([none, tiny], axis=1),
    )
    low = (f >> 1) & 1
    mine, other = [
        jnp.concatenate(
            [
                lax.dynamic_index_in_dim(expert_in, e, 1, keepdims=False),
                lax.dynamic_index_in_dim(expert_out, e, 1, keepdims=False),
            ],
            axis=1,
        )
        for e in (2 * r + low, 2 * r + 1 - low)
    ]
    qkv, attn, xn, first, lse, table, small, v, in_all, out_all, w_all, g_all, xs = front(
        tokens, seg_ids, routes, cos, sin, in_proj, out_proj, tiny, mine, other, out_grad
    )
    mix_sum, dx_own, dx_in, grads, xq, _, _ = run_group(v, out_grad, xs, g_all, w_all, xn)
    tokens_grad, expert_sum, mix_in, dense = run_back(
        dx_own, out_grad, first, table, small, v, tokens, qkv, lse, cos, sin, seg_ids,
        dx_in, grads, mix_sum, attn, xq, xn, in_all, out_all,
    )
    mixed = first + mix_sum[0].astype(f32)
    for k in range(2):
        mixed = mixed + mix_in[k].astype(f32)
    cut = in_proj.shape[1] // 4
    in_grad = dense[:, :shard, :cut].transpose(1, 0, 2).reshape(shard, -1)
    out_proj_grad = jnp.concatenate([dense[k, :shard, cut:] for k in (0, 2, 1, 3)], axis=1)
    expert_sum = expert_sum.transpose(1, 0, 2)
    terms = jnp.sum(dense[:, shard:, :cut].astype(f32), axis=0)
    terms = jnp.where(f % 2 == 0, terms[:, :shard], terms[:, shard : 2 * shard]).T
    return (
        mixed.astype(bf16),
        tokens_grad,
        in_grad.astype(f32),
        out_proj_grad.astype(f32),
        terms[:, :experts],
        terms[:, experts : experts + 2],
        expert_sum[..., : 2 * hidden].astype(f32),
        expert_sum[..., 2 * hidden :].astype(f32),
    )


class Wide:
    def __init__(self, n_rep, n_fsdp):
        self.n_rep, self.n_fsdp = n_rep, n_fsdp

    def spread(self, value):
        every = lax.all_gather(value, "replica", axis=0)
        return [every[k] for k in range(self.n_rep)]

    def collect(self, parts):
        return lax.psum_scatter(jnp.stack(parts), "replica", scatter_dimension=0).astype(f32)

    def start(self, in_proj, out_proj, tiny, expert_in, expert_out, grad):
        r = lax.axis_index("replica")
        per = expert_in.shape[1] // self.n_rep
        weights = []
        for i in range(per):
            both = jnp.concatenate(
                [
                    lax.dynamic_index_in_dim(expert_in, per * r + i, 1, keepdims=False),
                    lax.dynamic_index_in_dim(expert_out, per * r + i, 1, keepdims=False),
                ],
                axis=1,
            )
            weights.append(lax.all_gather(both, "fsdp", axis=0, tiled=True))
        return (
            lax.all_gather(in_proj, "fsdp", axis=0, tiled=True),
            lax.all_gather(out_proj, "fsdp", axis=0, tiled=True),
            lax.all_gather(tiny, "fsdp", axis=1, tiled=True),
            (weights, self.spread(grad)),
        )

    def experts(self, payload, held):
        weights, gs = held
        xs = self.spread(payload)
        per = len(weights)
        mixes, dxs, grads = None, None, []
        for i, w in enumerate(weights):

            def expert_of(i=i):
                return per * lax.axis_index("replica") + i

            mix, dx, grad = run_expert(xs, gs, [w], expert_of, lambda j: 0)
            mixes = mix if mixes is None else [a + b for a, b in zip(mixes, mix)]
            dxs = dx if dxs is None else [a + b for a, b in zip(dxs, dx)]
            grads.append(grad[0])
        return self.collect(dxs), (mixes, grads)

    def trade(self, value):
        cut = value.reshape(value.shape[0], self.n_rep, -1).transpose(1, 0, 2)
        got = lax.all_to_all(cut, "replica", 0, 0)
        return got.reshape(-1, got.shape[2])

    def end(self, held, first, normed, attn, dres, dproj, terms):
        mixes, grads = held
        mixed = first + self.collect(mixes)
        own = jnp.stack(
            [lax.psum_scatter(g, "fsdp", scatter_dimension=0, tiled=True) for g in grads]
        )
        expert_sum = lax.all_gather(own, "replica", axis=0, tiled=True).transpose(1, 0, 2)
        dense = []
        for left, right in ((normed, dproj), (dres, attn)):
            left = lax.all_gather(left, "replica", axis=0, tiled=True)
            part = contract_rows(left, self.trade(right)).astype(bf16)
            own = lax.psum_scatter(part, "fsdp", scatter_dimension=0, tiled=True)
            dense.append(lax.all_gather(own, "replica", axis=1, tiled=True))
        return mixed, dense[0], dense[1], expert_sum, lax.psum(terms, ("replica", "fsdp"))


def layer(
    net, tokens, seg_ids, routes, in_proj, out_proj, router, norm_gains, expert_in, expert_out,
    out_grad,
):
    length, width = tokens.shape
    experts = router.shape[1]
    hidden = expert_out.shape[2]
    shard = router.shape[0]
    scale = HD ** (-0.5)
    cosine, sine = tables(length)
    segment = seg_ids[0]
    place = jnp.arange(length)
    allowed = ((place[:, None] >= place[None, :]) & (segment[:, None] == segment[None, :]))[
        None, None
    ]
    tiny = jnp.concatenate(
        [router.T, norm_gains.T, jnp.zeros((16 - experts - 2, shard), bf16)], axis=0
    )
    proj_in, proj_out, tiny, held = net.start(
        in_proj, out_proj, tiny, expert_in, expert_out, out_grad
    )
    router_rows = tiny[:experts]
    gain_one = tiny[experts].astype(f32)
    gain_two = tiny[experts + 1].astype(f32)

    inputs = tokens.astype(f32)
    scale_one = rms_scale(inputs)
    unit_one = inputs * scale_one
    normed = (unit_one * gain_one).astype(bf16)
    proj = matmul(normed, proj_in)
    queries = (
        rotate(proj[:, :WQ].reshape(length, HQ, HD), cosine, sine)
        .astype(bf16)
        .reshape(length, KV, GROUP, HD)
    )
    keys = rotate(proj[:, WQ : WQ + WK].reshape(length, KV, HD), cosine, sine).astype(bf16)
    values = proj[:, WQ + WK :].reshape(length, KV, HD).astype(bf16)
    scores = jnp.einsum("qkgd,tkd->kgqt", queries, keys, preferred_element_type=f32) * scale
    masked = jnp.where(allowed, scores, -1e30)
    highest = jnp.max(masked, axis=-1, keepdims=True)
    expo = jnp.exp(masked - highest)
    total = jnp.sum(expo, axis=-1, keepdims=True)
    log_total = highest + jnp.log(total)
    probs_low = (expo / total).astype(bf16)
    attn = jnp.einsum("kgqt,tkd->qkgd", probs_low, values, preferred_element_type=f32)
    attn = attn.astype(bf16).reshape(length, WQ)
    first = inputs + contract_cols(attn, proj_out)
    scale_two = rms_scale(first)
    unit_two = first * scale_two
    normed_two = (unit_two * gain_two).astype(bf16)
    logits = contract_cols(normed_two, router_rows)
    onehot = (routes[:, :, None] == jnp.arange(experts)[None, None, :]).astype(f32)
    chosen = jnp.sum(onehot * logits[:, None, :], axis=-1)
    gates = jax.nn.softmax(chosen, axis=-1)
    table = jnp.sum(gates[:, :, None] * onehot, axis=1)
    high = table.astype(bf16)
    low = (table - high.astype(f32)).astype(bf16)
    payload = jnp.concatenate(
        [normed_two, high, low, jnp.zeros((length, EXTRA - 2 * experts), bf16)], axis=1
    )
    dx, held = net.experts(payload, held)

    grad_out = out_grad.astype(f32)
    dgate_all = dx[:, width : width + experts] + dx[:, width + experts : width + 2 * experts]
    dgate = jnp.sum(onehot * dgate_all[:, None, :], axis=-1)
    dchosen = gates * (dgate - jnp.sum(gates * dgate, axis=-1, keepdims=True))
    dlogits = jnp.sum(dchosen[:, :, None] * onehot, axis=1).astype(bf16)
    dnormed_two = dx[:, :width] + matmul(dlogits, router_rows)
    gain_two_grad = jnp.sum(dnormed_two * unit_two, axis=0)
    dunit_two = dnormed_two * gain_two
    dfirst = grad_out + scale_two * (
        dunit_two - unit_two * jnp.mean(dunit_two * unit_two, axis=-1, keepdims=True)
    )
    dres = dfirst.astype(bf16)
    dattn = matmul(dres, proj_out).astype(bf16).reshape(length, KV, GROUP, HD)
    probs = jnp.exp(masked - log_total)
    probs_again = probs.astype(bf16)
    dprobs = jnp.einsum("qkgd,tkd->kgqt", dattn, values, preferred_element_type=f32)
    dvalues = jnp.einsum("kgqt,qkgd->tkd", probs_again, dattn, preferred_element_type=f32)
    delta = jnp.sum(probs * dprobs, axis=-1, keepdims=True)
    dscores = (probs * (dprobs - delta)).astype(bf16)
    dqueries = jnp.einsum("kgqt,tkd->qkgd", dscores, keys, preferred_element_type=f32) * scale
    dkeys = jnp.einsum("kgqt,qkgd->tkd", dscores, queries, preferred_element_type=f32) * scale
    dqueries = rotate(dqueries.reshape(length, HQ, HD), cosine, -sine).reshape(length, WQ)
    dkeys = rotate(dkeys, cosine, -sine).reshape(length, WK)
    dproj = jnp.concatenate([dqueries, dkeys, dvalues.reshape(length, WK)], axis=1).astype(bf16)
    dnormed = contract_cols(dproj, proj_in)
    gain_one_grad = jnp.sum(dnormed * unit_one, axis=0)
    dunit_one = dnormed * gain_one
    tokens_grad = (
        dfirst
        + scale_one
        * (dunit_one - unit_one * jnp.mean(dunit_one * unit_one, axis=-1, keepdims=True))
    ).astype(bf16)

    terms = jnp.concatenate(
        [
            contract_rows(dlogits, normed_two),
            gain_one_grad[None],
            gain_two_grad[None],
            jnp.zeros((16 - experts - 2, width), f32),
        ],
        axis=0,
    )
    mixed, in_proj_grad, out_proj_grad, expert_sum, terms = net.end(
        held, first, normed, attn, dres, dproj, terms
    )
    terms = lax.dynamic_slice_in_dim(terms, lax.axis_index("fsdp") * shard, shard, 1).T
    return (
        mixed.astype(bf16),
        tokens_grad,
        in_proj_grad.astype(f32),
        out_proj_grad.astype(f32),
        terms[:, :experts],
        terms[:, experts : experts + 2],
        expert_sum[..., : 2 * hidden].astype(f32),
        expert_sum[..., 2 * hidden :].astype(f32),
    )


def solution(mesh):
    n_rep, n_fsdp = mesh.shape["replica"], mesh.shape["fsdp"]
    if (n_rep, n_fsdp) == (4, 8):
        body = near_layer
    else:
        body = functools.partial(layer, Wide(n_rep, n_fsdp))
    both = P(("replica", "fsdp"), None)
    fsdp, deep = P("fsdp", None), P("fsdp", None, None)
    return jax.shard_map(
        body,
        mesh=mesh,
        in_specs=(both, both, both, fsdp, fsdp, fsdp, fsdp, deep, deep, both),
        out_specs=(both, both, fsdp, fsdp, fsdp, fsdp, deep, deep),
        check_vma=False,
    )
```

```python
import functools

import jax
import jax.numpy as jnp
from jax import lax
from jax.experimental import pallas as pl
from jax.experimental.pallas import tpu as pltpu
from jax.sharding import PartitionSpec as P

HQ = 12
KV = 2
HD = 128
GROUP = HQ // KV
WQ = HQ * HD
WK = KV * HD
EXTRA = 128
MIB = 1024 * 1024

epsilon = 1e-06
rope_base = 1000000.0
bf16 = jnp.bfloat16
f32 = jnp.float32


def rms_scale(v):
    return lax.rsqrt(jnp.mean(v * v, axis=-1, keepdims=True) + epsilon)


def tables(length):
    half = HD // 2
    freq = jnp.power(rope_base, -(jnp.arange(half, dtype=f32) * 2.0 / HD))
    angle = jnp.arange(length, dtype=f32)[:, None] * freq[None, :]
    return (jnp.cos(angle)[:, None, :], jnp.sin(angle)[:, None, :])


def rotate(v, cosine, sine):
    half = v.shape[-1] // 2
    first = v[..., :half]
    second = v[..., half:]
    return jnp.concatenate(
        [first * cosine - second * sine, second * cosine + first * sine], axis=-1
    )


def contract_rows(left, right):
    return lax.dot_general(left, right, (((0,), (0,)), ((), ())), preferred_element_type=f32)


def contract_cols(left, right):
    return lax.dot_general(left, right, (((1,), (1,)), ((), ())), preferred_element_type=f32)


def matmul(left, right):
    return lax.dot_general(left, right, (((1,), (0,)), ((), ())), preferred_element_type=f32)


def expert_kernel(nt, nw, length, width, hidden, rows, expert_of, offset_of, *refs):
    xs, gs, ws = refs[:nt], refs[nt : 2 * nt], refs[2 * nt : 2 * nt + nw]
    refs = refs[2 * nt + nw :]
    mixes, dxs, grads = refs[:nt], refs[nt : 2 * nt], refs[2 * nt : 2 * nt + nw]
    (
        wbuf, xbuf, gbuf, xt, gt_, hidg, dgu, mbuf, dbuf, acc, stage,
        sem_w, sem_x, sem_g, sem_m, sem_d, sem_s,
    ) = refs[2 * nt + nw :]
    cols = 3 * hidden
    step_cols = 256

    def load(k, slot):
        for i in range(nt):

            @pl.when(k == i)
            def _():
                pltpu.make_async_copy(xs[i], xbuf.at[slot], sem_x.at[slot]).start()
                pltpu.make_async_copy(gs[i], gbuf.at[slot], sem_g.at[slot]).start()

    def store(k, slot):
        for i in range(nt):

            @pl.when(k == i)
            def _():
                pltpu.make_async_copy(mbuf.at[slot], mixes[i], sem_m.at[slot]).start()
                pltpu.make_async_copy(dbuf.at[slot], dxs[i], sem_d.at[slot]).start()

    def stored(slot):
        pltpu.make_async_copy(mbuf.at[slot], mixes[0], sem_m.at[slot]).wait()
        pltpu.make_async_copy(dbuf.at[slot], dxs[0], sem_d.at[slot]).wait()

    for j in range(nw):
        pltpu.make_async_copy(
            ws[j], wbuf.at[pl.ds(pl.multiple_of(offset_of(j), 8), rows)], sem_w.at[j]
        ).start()
    load(0, 0)
    expert = expert_of()
    acc[...] = jnp.zeros_like(acc)
    lane = lax.broadcasted_iota(jnp.int32, (length, EXTRA), 1)
    for j in range(nw):
        pltpu.make_async_copy(
            ws[j], wbuf.at[pl.ds(pl.multiple_of(offset_of(j), 8), rows)], sem_w.at[j]
        ).wait()

    def block(k, carry):
        slot = lax.rem(k, 2)

        @pl.when(k + 1 < nt)
        def _():
            load(k + 1, 1 - slot)

        pltpu.make_async_copy(xs[0], xbuf.at[slot], sem_x.at[slot]).wait()
        pltpu.make_async_copy(gs[0], gbuf.at[slot], sem_g.at[slot]).wait()

        @pl.when(k >= 2)
        def _():
            stored(slot)

        extra = xbuf[slot, :, width:].astype(f32)
        mine = (lane == expert) | (lane == expert + 8)
        gate = jnp.sum(jnp.where(mine, extra, 0.0), axis=1, keepdims=True)
        xt[...] = xbuf[slot, :, :width].T
        gt_[...] = gbuf[slot].T

        def first(c, dgate):
            at = pl.multiple_of(c * step_cols, step_cols)
            u = matmul(xbuf[slot, :, :width], wbuf[:, pl.ds(at, step_cols)])
            up = matmul(xbuf[slot, :, :width], wbuf[:, pl.ds(hidden + at, step_cols)])
            back = matmul(gbuf[slot], wbuf[:, pl.ds(2 * hidden + at, step_cols)])
            sig = 1.0 / (1.0 + jnp.exp(-u))
            act = u * sig
            hid = act * up
            hidg[:, pl.ds(at, step_cols)] = (gate * hid).astype(bf16)
            dgate = dgate + jnp.sum(back * hid, axis=1, keepdims=True)
            dhid = gate * back
            dgu[:, pl.ds(at, step_cols)] = (
                dhid * up * sig * (1.0 + u * (1.0 - sig))
            ).astype(bf16)
            dgu[:, pl.ds(hidden + at, step_cols)] = (dhid * act).astype(bf16)
            return dgate

        dgate = lax.fori_loop(
            0, hidden // step_cols, first, jnp.zeros((length, 1), f32)
        )

        def second(c, carry):
            at = pl.multiple_of(c * step_cols, step_cols)
            mbuf[slot, :, pl.ds(at, step_cols)] = contract_cols(
                hidg[...], wbuf[pl.ds(at, step_cols), pl.ds(2 * hidden, hidden)]
            ).astype(bf16)
            dbuf[slot, :, pl.ds(at, step_cols)] = contract_cols(
                dgu[...], wbuf[pl.ds(at, step_cols), pl.ds(0, 2 * hidden)]
            ).astype(bf16)
            return carry

        lax.fori_loop(0, width // step_cols, second, 0)
        high = dgate.astype(bf16).astype(f32)
        low = dgate - high
        dbuf[slot, :, width:] = (
            jnp.where(lane == expert, high, 0.0) + jnp.where(lane == expert + 8, low, 0.0)
        ).astype(bf16)
        store(k, slot)

        def third(c, carry):
            at = pl.multiple_of(c * step_cols, step_cols)
            acc[:, pl.ds(at, step_cols)] += matmul(xt[...], dgu[:, pl.ds(at, step_cols)])
            return carry

        lax.fori_loop(0, 2 * hidden // step_cols, third, 0)

        def fourth(c, carry):
            at = pl.multiple_of(c * step_cols, step_cols)
            acc[:, pl.ds(2 * hidden + at, step_cols)] += matmul(
                gt_[...], hidg[:, pl.ds(at, step_cols)]
            )
            return carry

        lax.fori_loop(0, hidden // step_cols, fourth, 0)
        return carry

    lax.fori_loop(0, nt, block, 0)
    stored(0)
    stored(1)
    for j in range(nw):
        slot = j % 2
        if j >= 2:
            pltpu.make_async_copy(stage.at[slot], grads[j - 2], sem_s.at[slot]).wait()
        stage[slot] = acc[pl.ds(pl.multiple_of(offset_of(j), 8), rows)].astype(bf16)
        pltpu.make_async_copy(stage.at[slot], grads[j], sem_s.at[slot]).start()
    for j in range(max(0, nw - 2), nw):
        pltpu.make_async_copy(stage.at[j % 2], grads[j], sem_s.at[j % 2]).wait()


def run_expert(xs, gs, ws, expert_of, offset_of):
    nt, nw = len(xs), len(ws)
    length, width = gs[0].shape
    rows, cols = ws[0].shape
    hidden = cols // 3
    outs = (
        [jax.ShapeDtypeStruct((length, width), bf16)] * nt
        + [jax.ShapeDtypeStruct((length, width + EXTRA), bf16)] * nt
        + [jax.ShapeDtypeStruct((rows, cols), bf16)] * nw
    )
    any_spec = pl.BlockSpec(memory_space=pl.ANY)
    result = pl.pallas_call(
        functools.partial(
            expert_kernel, nt, nw, length, width, hidden, rows, expert_of, offset_of
        ),
        out_shape=outs,
        in_specs=[any_spec] * (2 * nt + nw),
        out_specs=[any_spec] * len(outs),
        scratch_shapes=[
            pltpu.VMEM((width, cols), bf16),
            pltpu.VMEM((2, length, width + EXTRA), bf16),
            pltpu.VMEM((2, length, width), bf16),
            pltpu.VMEM((width, length), bf16),
            pltpu.VMEM((width, length), bf16),
            pltpu.VMEM((length, hidden), bf16),
            pltpu.VMEM((length, 2 * hidden), bf16),
            pltpu.VMEM((2, length, width), bf16),
            pltpu.VMEM((2, length, width + EXTRA), bf16),
            pltpu.VMEM((width, cols), f32),
            pltpu.VMEM((2, rows, cols), bf16),
            pltpu.SemaphoreType.DMA((nw,)),
            pltpu.SemaphoreType.DMA((2,)),
            pltpu.SemaphoreType.DMA((2,)),
            pltpu.SemaphoreType.DMA((2,)),
            pltpu.SemaphoreType.DMA((2,)),
            pltpu.SemaphoreType.DMA((2,)),
        ],
        compiler_params=pltpu.CompilerParams(vmem_limit_bytes=60 * MIB),
        cost_estimate=pl.CostEstimate(
            flops=6 * nt * length * width * cols,
            bytes_accessed=8 * nt * length * width + 4 * width * cols,
            transcendentals=nt * length * hidden,
        ),
        name="expert",
    )(*xs, *gs, *ws)
    return result[:nt], result[nt : 2 * nt], result[2 * nt :]


MESH_ID = pl.DeviceIdType.MESH


def flip(index, bit):
    return index + bit - 2 * bit * lax.rem(index // bit, 2)


def flips(index, mask):
    for bit in (1, 2, 4):
        if mask & bit:
            index = flip(index, bit)
    return index


class Wire:
    def __init__(self, send_sem, recv_sem):
        self.r, self.f = lax.axis_index("replica"), lax.axis_index("fsdp")
        self.send_sem, self.recv_sem = send_sem, recv_sem
        self.used, self.sent = 0, []

    def meet(self, partners):
        barrier = pltpu.get_barrier_semaphore()
        for d_r, d_f in partners:
            pl.semaphore_signal(
                barrier, inc=1, device_id=self.at(d_r, d_f), device_id_type=MESH_ID
            )
        pl.semaphore_wait(barrier, len(partners))

    def at(self, d_r, d_f):
        return (flips(self.r, d_r), flips(self.f, d_f))

    def plan(self, src, dst, d_r, d_f):
        copy = pltpu.make_async_remote_copy(
            src_ref=src,
            dst_ref=dst,
            send_sem=self.send_sem.at[self.used],
            recv_sem=self.recv_sem.at[self.used],
            device_id=self.at(d_r, d_f),
            device_id_type=MESH_ID,
        )
        self.used += 1
        assert self.used <= self.send_sem.shape[0]
        return copy

    def send(self, src, dst, d_r, d_f):
        copy = self.plan(src, dst, d_r, d_f)
        copy.start()
        self.sent.append(copy)
        return copy

    def finish(self, waited=()):
        for copy in self.sent:
            if all(copy is not other for other in waited):
                copy.wait_send()


CUTS = 4
FRONT_SENDS = 2 * 28 + 7 + 7 * CUTS + 4 + 3
PARTNERS = ((1, 0), (2, 0), (0, 1), (0, 2), (0, 4), (0, 6))
ROWS = 64


def turn(v, cosine, sine):
    return v * cosine + pltpu.roll(v, HD // 2, 1) * sine


def front_kernel(
    tokens, seg_col, seg_row, routes, cos, sin,
    in_ref, out_ref, tiny_ref, mine_ref, other_ref, g_ref,
    qkv, attn, xn, first, lse, table, tiny_out, v,
    in_all, out_all, w_all, g_all, xs,
    in_v, out_v, tiny_v, rt, bias, w_buf, local_sem, send_sem, recv_sem,
):
    wire = Wire(send_sem, recv_sem)
    r, f = wire.r, wire.f
    shard = in_ref.shape[0]
    quarter = shard // 4
    length, width = tokens.shape
    experts = 8
    scale = HD ** (-0.5)

    def rows(j, k):
        at = flips(f, j) * shard + flips(r, k) * quarter
        return pl.ds(pl.multiple_of(at, quarter), quarter)

    def shard_rows(j):
        return pl.ds(pl.multiple_of(flips(f, j) * shard, shard), shard)

    def local(n, src, dst):
        copy = pltpu.make_async_copy(src, dst, local_sem.at[n])
        copy.start()
        return copy

    own_in = local(0, in_ref, in_v.at[shard_rows(0)])
    own_out = local(1, out_ref, out_v.at[shard_rows(0)])
    own_tiny = local(2, tiny_ref, tiny_v.at[f])
    own_w = local(3, mine_ref, w_buf)
    wire.meet(PARTNERS)

    own = pl.ds(pl.multiple_of(r * quarter, quarter), quarter)
    land = {"in": in_v, "out": out_v}
    source = {"in": in_ref, "out": out_ref}
    got, got_t, got_w, got_g, got_x = {}, {}, {}, {}, {}

    for m in (2, 4, 6, 1):
        got_t[m] = wire.send(tiny_ref, tiny_v.at[f], 0, m)

    def own_pieces(name):
        for m in (2, 4, 6, 1):
            got[name, m, 0] = wire.send(
                source[name].at[own], land[name].at[rows(0, 0)], 0, m
            )

    def pass_on(name, j, k, d_r, d_f):
        at = land[name].at[rows(j, k)]
        return wire.send(at, at, d_r, d_f)

    def near_pieces(name):
        for m in (1, 2, 4, 6):
            got[name, m, 0].wait_recv()
            if m != 1:
                got[name, m + 1, 0] = pass_on(name, m, 0, 0, 1)
            got[name, m, 2] = pass_on(name, m, 0, 2, 0)
            got[name, m, 1] = pass_on(name, m, 0, 1, 0)

    def far_pieces(name):
        for m in (3, 5, 7):
            got[name, m, 0].wait_recv()
            got[name, m, 2] = pass_on(name, m, 0, 2, 0)
            got[name, m, 1] = pass_on(name, m, 0, 1, 0)

    def side_pieces(name):
        for m in (1, 2, 4, 6, 3, 5, 7):
            got[name, m, 2].wait_recv()
            got[name, m, 3] = pass_on(name, m, 2, 1, 0)

    def all_pieces(name):
        for m in range(1, 8):
            got[name, m, 1].wait_recv()
            got[name, m, 3].wait_recv()

    own_pieces("in")
    own_pieces("out")
    own_w.wait()
    kept = [local(4, w_buf, w_all.at[shard_rows(0)])]

    for m in (2, 4, 6):
        got_t[m].wait_recv()
        at = tiny_v.at[flips(f, m)]
        got_t[m + 1] = wire.send(at, at, 0, 1)
    for m in (1, 3, 5, 7):
        got_t[m].wait_recv()
    own_tiny.wait()
    lanes = tiny_v.shape[2]
    rt[...] = jnp.zeros_like(rt)
    for z in range(4):
        both = tiny_v[2 * z].astype(f32) + tiny_v[2 * z + 1].astype(f32)
        tiny_out[:, z * lanes : (z + 1) * lanes] = both
        row = lax.broadcasted_iota(jnp.int32, both.shape, 0)
        rt[0:16, z * lanes : (z + 1) * lanes] = jnp.where(row < experts, both, 0.0).astype(bf16)

    def norm_one(c, carry):
        at = pl.ds(pl.multiple_of(c * ROWS, ROWS), ROWS)
        x = tokens[at, :].astype(f32)
        unit = x * lax.rsqrt(jnp.mean(x * x, axis=-1, keepdims=True) + epsilon)
        xn[at, :] = (unit * tiny_out[experts : experts + 1, :]).astype(bf16)
        return carry

    lax.fori_loop(0, length // ROWS, norm_one, 0)
    spot = lax.broadcasted_iota(jnp.int32, bias.shape, 0)
    keys_at = lax.broadcasted_iota(jnp.int32, bias.shape, 1)
    bias[...] = jnp.where((spot >= keys_at) & (seg_col[...] == seg_row[...]), 0.0, -1e30)

    cut = shard // CUTS

    def send_w(n, src, d_f):
        at = pl.ds(n * cut, cut)
        to = pl.ds(pl.multiple_of(f * shard + n * cut, cut), cut)
        return wire.send(src.at[at], w_all.at[to], 0, d_f)

    def pass_w(n, m):
        got_w[m, n].wait_recv()
        at = w_all.at[pl.ds(pl.multiple_of(flips(f, m) * shard + n * cut, cut), cut)]
        got_w[m + 1, n] = wire.send(at, at, 0, 1)

    near_pieces("in")
    for n in range(CUTS):
        for m, src in ((2, other_ref), (4, mine_ref), (6, other_ref)):
            got_w[m, n] = send_w(n, src, m)
    got_g[4] = wire.send(g_ref, g_all.at[4], 0, 2)
    got_g[1] = wire.send(g_ref, g_all.at[1], 1, 0)
    far_pieces("in")
    near_pieces("out")
    far_pieces("out")
    for n in range(CUTS):
        got_w[1, n] = send_w(n, mine_ref, 1)
    got_g[2] = wire.send(g_ref, g_all.at[2], 2, 0)
    side_pieces("in")
    own_in.wait()
    all_pieces("in")

    def project(c, carry):
        at = pl.multiple_of(c * 256, 256)
        t = matmul(xn[...], in_v[:, pl.ds(at, 256)])
        turned = c < 7
        for n in (0, 1):
            part = t[:, n * HD : (n + 1) * HD]
            part = turn(
                part, jnp.where(turned, cos[...], 1.0), jnp.where(turned, sin[...], 0.0)
            )
            qkv[:, pl.ds(at + n * HD, HD)] = part.astype(bf16)
        return carry

    lax.fori_loop(0, 8, project, 0)
    pass_w(0, 2)
    pass_w(0, 4)
    lane = lax.broadcasted_iota(jnp.int32, (length, HD), 1)
    lse[...] = jnp.zeros_like(lse)

    def head(h, carry):
        at = pl.ds(pl.multiple_of(h * HD, HD), HD)
        group = h // GROUP
        k_at = pl.ds(pl.multiple_of(WQ + group * HD, HD), HD)
        v_at = pl.ds(pl.multiple_of(WQ + WK + group * HD, HD), HD)
        s = contract_cols(qkv[:, at], qkv[:, k_at]) * scale + bias[...]
        highest = jnp.max(s, axis=-1, keepdims=True)
        expo = jnp.exp(s - highest)
        total = jnp.sum(expo, axis=-1, keepdims=True)
        p = (expo * (1.0 / total)).astype(bf16)
        attn[:, at] = matmul(p, qkv[:, v_at]).astype(bf16)
        lse[...] = jnp.where(lane == h, highest + jnp.log(total), lse[...])
        return carry

    lax.fori_loop(0, HQ // 2, head, 0)
    side_pieces("out")
    pass_w(0, 6)
    pass_w(1, 2)
    lax.fori_loop(HQ // 2, HQ, head, 0)
    pass_w(1, 4)
    pass_w(1, 6)
    own_out.wait()
    all_pieces("out")
    kept.append(local(5, in_v, in_all))
    kept.append(local(6, out_v, out_all))

    def add_out(c, carry):
        at = pl.ds(pl.multiple_of(c * 256, 256), 256)
        first[:, at] = tokens[:, at].astype(f32) + contract_cols(attn[...], out_v[at, :])
        return carry

    lax.fori_loop(0, width // 256, add_out, 0)

    def norm_two(c, carry):
        at = pl.ds(pl.multiple_of(c * ROWS, ROWS), ROWS)
        h = first[at, :]
        unit = h * lax.rsqrt(jnp.mean(h * h, axis=-1, keepdims=True) + epsilon)
        v[at, 0:width] = (unit * tiny_out[experts + 1 : experts + 2, :]).astype(bf16)
        return carry

    lax.fori_loop(0, length // ROWS, norm_two, 0)
    logits = contract_cols(v[:, 0:width], rt[...])
    chosen = lane == routes[:, 0:1]
    for j in range(1, routes.shape[1]):
        chosen = chosen | (lane == routes[:, j : j + 1])
    logits = jnp.where(chosen, logits, -1e30)
    expo = jnp.exp(logits - jnp.max(logits, axis=-1, keepdims=True))
    expo = jnp.where(chosen, expo, 0.0)
    gates = expo / jnp.sum(expo, axis=-1, keepdims=True)
    table[...] = gates
    high = gates.astype(bf16).astype(f32)
    v[:, width:] = (high + pltpu.roll(gates - high, experts, 1)).astype(bf16)

    got_x[2] = wire.send(v, xs.at[2], 2, 0)
    got_x[1] = wire.send(v, xs.at[1], 1, 0)
    for n in range(2, CUTS):
        for m in (2, 4, 6):
            pass_w(n, m)
    got_g[2].wait_recv()
    got_g[3] = wire.send(g_all.at[2], g_all.at[3], 1, 0)
    got_x[2].wait_recv()
    got_x[3] = wire.send(xs.at[2], xs.at[3], 1, 0)
    for n in range(CUTS):
        for m in (1, 3, 5, 7):
            got_w[m, n].wait_recv()
    for m in (1, 3, 4):
        got_g[m].wait_recv()
    for m in (1, 3):
        got_x[m].wait_recv()
    for copy in kept:
        copy.wait()
    wire.finish()


def front(tokens, seg_ids, routes, cos, sin, in_proj, out_proj, tiny, mine, other, grad):
    any_spec = pl.BlockSpec(memory_space=pl.ANY)
    vmem = pl.BlockSpec(memory_space=pltpu.VMEM)
    length, width = tokens.shape
    shard, cols = in_proj.shape
    whole = 8 * shard
    wide = width + EXTRA
    return pl.pallas_call(
        front_kernel,
        out_shape=[
            jax.ShapeDtypeStruct((length, cols), bf16),
            jax.ShapeDtypeStruct((length, WQ), bf16),
            jax.ShapeDtypeStruct((length, width), bf16),
            jax.ShapeDtypeStruct((length, width), f32),
            jax.ShapeDtypeStruct((length, HD), f32),
            jax.ShapeDtypeStruct((length, EXTRA), f32),
            jax.ShapeDtypeStruct((16, width), f32),
            jax.ShapeDtypeStruct((length, wide), bf16),
            jax.ShapeDtypeStruct((whole, cols), bf16),
            jax.ShapeDtypeStruct((whole, out_proj.shape[1]), bf16),
            jax.ShapeDtypeStruct((whole, mine.shape[1]), bf16),
            jax.ShapeDtypeStruct((5,) + grad.shape, bf16),
            jax.ShapeDtypeStruct((4, length, wide), bf16),
        ],
        in_specs=[vmem] * 6 + [any_spec] * 6,
        out_specs=[vmem] * 8 + [any_spec] * 5,
        scratch_shapes=[
            pltpu.VMEM((whole, cols), bf16),
            pltpu.VMEM((whole, out_proj.shape[1]), bf16),
            pltpu.VMEM((8,) + tiny.shape, bf16),
            pltpu.VMEM((EXTRA, width), bf16),
            pltpu.VMEM((length, length), f32),
            pltpu.VMEM(mine.shape, bf16),
            pltpu.SemaphoreType.DMA((8,)),
            pltpu.SemaphoreType.DMA((FRONT_SENDS,)),
            pltpu.SemaphoreType.DMA((FRONT_SENDS,)),
        ],
        compiler_params=pltpu.CompilerParams(
            collective_id=1, has_side_effects=True, vmem_limit_bytes=56 * MIB
        ),
        name="front",
    )(
        tokens, seg_ids.reshape(length, 1), seg_ids, routes, cos, sin,
        in_proj, out_proj, tiny, mine, other, grad,
    )


ORDER = (3, 2, 4, 5, 7, 6, 1, 0)
UNROLL = True
WIDE_COLS = 256
GROUP_AT = {2: (2, 0), 4: (0, 2), 6: (2, 2)}


def pick(step, table):
    value = jnp.int32(table[-1])
    for i, item in enumerate(table[:-1]):
        value = jnp.where(step == i, item, value)
    return value


def group_kernel(
    v_ref, g_ref, xs, g_all, w_ref,
    mix_sum, dx_own, dx_in, grads, x_late, g_late,
    wbuf, xbuf, gbuf, xt, gt_, hidg, dgu, deven, dodd, rc, meven, modd, mrc, acc, stage,
    sem_w, sem_x, sem_g, sem_m, sem_s, send_sem, recv_sem,
):
    wire = Wire(send_sem, recv_sem)
    r, f = wire.r, wire.f
    length, width = g_ref.shape
    hidden = w_ref.shape[1] // 3
    half = length // 2
    low, top = pl.ds(0, half), pl.ds(half, half)
    expert = 2 * r + lax.rem(f // 2, 2)
    step_cols = 256

    load_w = pltpu.make_async_copy(w_ref, wbuf, sem_w.at[0])
    load_w.start()

    def load(step):
        slot = lax.rem(step, 2)
        k = pick(step, ORDER)

        @pl.when(k == 0)
        def _():
            pltpu.make_async_copy(v_ref, xbuf.at[slot], sem_x.at[slot]).start()
            pltpu.make_async_copy(g_ref, gbuf.at[slot], sem_g.at[slot]).start()

        for table, src_x, src_g in (
            ((1, 2, 3), xs, g_all), ((4,), x_late, g_all), ((5, 6, 7), x_late, g_late)
        ):

            @pl.when((k >= table[0]) & (k <= table[-1]))
            def _():
                pltpu.make_async_copy(src_x.at[k], xbuf.at[slot], sem_x.at[slot]).start()
                pltpu.make_async_copy(src_g.at[k], gbuf.at[slot], sem_g.at[slot]).start()

    load(jnp.int32(0))
    wire.meet(PARTNERS_GROUP)
    late_x = {4: wire.send(v_ref, x_late.at[4], 0, 2)}
    far = [
        wire.send(g_all.at[4], g_late.at[6], 2, 0),
        wire.send(xs.at[2, top], x_late.at[6, top], 0, 2),
    ]
    late_g = {5: wire.send(g_all.at[4], g_late.at[5], 1, 0)}
    far.append(wire.plan(x_late.at[4, low], x_late.at[6, low], 2, 0))
    late_x[5] = wire.plan(x_late.at[4], x_late.at[5], 1, 0)
    late_x[7] = wire.plan(x_late.at[6], x_late.at[7], 1, 0)
    late_g[7] = wire.plan(g_late.at[6], g_late.at[7], 1, 0)
    slots = {2: 0, 4: 1, 6: 2, 0: 3}
    to_core = {k: wire.plan(dodd.at[n % 2], rc.at[n], 1, 0) for k, n in slots.items()}
    mix_core = {k: wire.plan(modd.at[n % 2], mrc.at[n], 1, 0) for k, n in slots.items()}
    back = {k: wire.plan(deven.at[k // 2], dx_in.at[k // 2 - 1], *GROUP_AT[k]) for k in (2, 4, 6)}
    acc[...] = jnp.zeros_like(acc)
    lane = lax.broadcasted_iota(jnp.int32, (length, EXTRA), 1)
    load_w.wait()

    def keep_mix(k):
        n = slots[k] % 2
        return pltpu.make_async_copy(meven.at[n], mix_sum.at[k // 2], sem_m.at[n])

    def send_core(k):
        to_core[k].start()
        mix_core[k].start()

    def sent_core(k):
        to_core[k].wait_send()
        mix_core[k].wait_send()

    def complete(k):
        n = slots[k]
        to_core[k].wait_recv()
        deven[k // 2] = (deven[k // 2].astype(f32) + rc[n].astype(f32)).astype(bf16)
        if k in (4, 6):
            back[k].start()
        mix_core[k].wait_recv()
        meven[n % 2] = (meven[n % 2].astype(f32) + mrc[n].astype(f32)).astype(bf16)
        keep_mix(k).start()

    def block(step, carry):
        slot = lax.rem(step, 2)

        @pl.when((step == 0) | (step >= 4) & (step < 7))
        def _():
            load(step + 1)

        pltpu.make_async_copy(v_ref, xbuf.at[slot], sem_x.at[slot]).wait()
        pltpu.make_async_copy(g_ref, gbuf.at[slot], sem_g.at[slot]).wait()
        extra = xbuf[slot, :, width:].astype(f32)
        mine = (lane == expert) | (lane == expert + 8)
        gate = jnp.sum(jnp.where(mine, extra, 0.0), axis=1, keepdims=True)
        here = pl.ds(pl.multiple_of(slot * length, length), length)
        xt[:, here] = xbuf[slot, :, :width].T
        gt_[:, here] = gbuf[slot].T

        def first(c, dgate):
            at = pl.multiple_of(c * step_cols, step_cols)
            u = matmul(xbuf[slot, :, :width], wbuf[:, pl.ds(at, step_cols)])
            up = matmul(xbuf[slot, :, :width], wbuf[:, pl.ds(hidden + at, step_cols)])
            rev = matmul(gbuf[slot], wbuf[:, pl.ds(2 * hidden + at, step_cols)])
            sig = 1.0 / (1.0 + jnp.exp(-u))
            act = u * sig
            hid = act * up
            hidg[here, pl.ds(at, step_cols)] = (gate * hid).astype(bf16)
            dgate = dgate + jnp.sum(rev * hid, axis=1, keepdims=True)
            dhid = gate * rev
            dgu[here, pl.ds(at, step_cols)] = (
                dhid * up * sig * (1.0 + u * (1.0 - sig))
            ).astype(bf16)
            dgu[here, pl.ds(hidden + at, step_cols)] = (dhid * act).astype(bf16)
            return dgate

        dgate = lax.fori_loop(
            0, hidden // step_cols, first, jnp.zeros((length, 1), f32), unroll=UNROLL
        )
        high = dgate.astype(bf16).astype(f32)
        rest = dgate - high
        tail = (
            jnp.where(lane == expert, high, 0.0) + jnp.where(lane == expert + 8, rest, 0.0)
        ).astype(bf16)

        def out_parts(dst_d, n_d, dst_m, n_m):
            def second(c, carry):
                at = pl.multiple_of(c * step_cols, step_cols)
                dst_d[n_d, :, pl.ds(at, step_cols)] = contract_cols(
                    dgu[here, :], wbuf[pl.ds(at, step_cols), pl.ds(0, 2 * hidden)]
                ).astype(bf16)
                dst_m[n_m, :, pl.ds(at, step_cols)] = contract_cols(
                    hidg[here, :], wbuf[pl.ds(at, step_cols), pl.ds(2 * hidden, hidden)]
                ).astype(bf16)
                return carry

            lax.fori_loop(0, width // step_cols, second, 0, unroll=UNROLL)
            dst_d[n_d, :, width:] = tail

        slot_two = pick(step, (0, 0, 1, 1, 0, 0, 1, 1))
        k = pick(step, ORDER)

        @pl.when(step == 4)
        def _():
            sent_core(2)

        @pl.when(step == 6)
        def _():
            sent_core(4)

        @pl.when(step == 5)
        def _():
            keep_mix(2).wait()

        @pl.when(step == 7)
        def _():
            keep_mix(4).wait()

        @pl.when(lax.rem(k, 2) == 1)
        def _():
            out_parts(dodd, slot_two, modd, slot_two)

        @pl.when(lax.rem(k, 2) == 0)
        def _():
            out_parts(deven, k // 2, meven, slot_two)

        def come_5():
            late_x[5].wait_recv()
            late_g[5].wait_recv()
            load(step + 1)

        def come_6():
            for copy in far:
                copy.wait_recv()
            late_x[7].start()
            late_g[7].start()

        for at_step, todo in (
            (0, (lambda: send_core(2),)),
            (1, (lambda: complete(2),)),
            (2, (come_5,)),
            (3, (lambda: send_core(4), come_6)),
            (4, (lambda: complete(4), lambda: send_core(6))),
            (5, (lambda: complete(6),)),
            (6, (lambda: send_core(0),)),
            (7, (lambda: complete(0),)),
        ):

            @pl.when(step == at_step)
            def _():
                for do in todo:
                    do()

        @pl.when(slot == 1)
        def _():
            def third(c, carry):
                at = pl.multiple_of(c * WIDE_COLS, WIDE_COLS)
                acc[:, pl.ds(at, WIDE_COLS)] += matmul(xt[...], dgu[:, pl.ds(at, WIDE_COLS)])
                return carry

            lax.fori_loop(0, 2 * hidden // WIDE_COLS, third, 0, unroll=UNROLL)

            def fourth(c, carry):
                at = pl.multiple_of(c * WIDE_COLS, WIDE_COLS)
                acc[:, pl.ds(2 * hidden + at, WIDE_COLS)] += matmul(
                    gt_[...], hidg[:, pl.ds(at, WIDE_COLS)]
                )
                return carry

            lax.fori_loop(0, hidden // WIDE_COLS, fourth, 0, unroll=UNROLL)

        @pl.when(step == 1)
        def _():
            late_x[4].wait_recv()
            late_x[5].start()
            far[2].start()
            back[2].start()
            load(step + 1)

        @pl.when(step == 3)
        def _():
            late_x[7].wait_recv()
            late_g[7].wait_recv()
            load(step + 1)

        return carry

    lax.fori_loop(0, 8, block, 0)
    keep = pltpu.make_async_copy(deven.at[0], dx_own, sem_w.at[0])
    keep.start()
    parts = 8
    rows = width // parts

    def out(j, slot):
        return pltpu.make_async_copy(
            stage.at[slot], grads.at[pl.ds(j * rows, rows)], sem_s.at[slot]
        )

    for j in range(parts):
        slot = j % 2
        if j >= 2:
            out(j - 2, slot).wait()
        stage[slot] = acc[j * rows : (j + 1) * rows].astype(bf16)
        out(j, slot).start()
    for j in range(parts - 2, parts):
        out(j, j % 2).wait()
    keep.wait()
    keep_mix(6).wait()
    keep_mix(0).wait()
    for k in (2, 4, 6):
        back[k].wait_recv()
        back[k].wait_send()
    sent_core(6)
    sent_core(0)
    for copy in (far[2], late_x[5], late_x[7], late_g[7]):
        copy.wait_send()
    wire.finish()


PARTNERS_GROUP = ((1, 0), (2, 0), (0, 2), (2, 2))
GROUP_SENDS = 8 + 8 + 3


def run_group(v, grad, xs, g_all, w):
    length, width = grad.shape
    wide = v.shape[1]
    cols = w.shape[1]
    hidden = cols // 3
    any_spec = pl.BlockSpec(memory_space=pl.ANY)
    return pl.pallas_call(
        group_kernel,
        out_shape=[
            jax.ShapeDtypeStruct((4, length, width), bf16),
            jax.ShapeDtypeStruct((length, wide), bf16),
            jax.ShapeDtypeStruct((3, length, wide), bf16),
            jax.ShapeDtypeStruct((width, cols), bf16),
            jax.ShapeDtypeStruct((8, length, wide), bf16),
            jax.ShapeDtypeStruct((8, length, width), bf16),
        ],
        in_specs=[any_spec] * 5,
        out_specs=[any_spec] * 6,
        scratch_shapes=[
            pltpu.VMEM((width, cols), bf16),
            pltpu.VMEM((2, length, wide), bf16),
            pltpu.VMEM((2, length, width), bf16),
            pltpu.VMEM((width, 2 * length), bf16),
            pltpu.VMEM((width, 2 * length), bf16),
            pltpu.VMEM((2 * length, hidden), bf16),
            pltpu.VMEM((2 * length, 2 * hidden), bf16),
            pltpu.VMEM((4, length, wide), bf16),
            pltpu.VMEM((2, length, wide), bf16),
            pltpu.VMEM((4, length, wide), bf16),
            pltpu.VMEM((2, length, width), bf16),
            pltpu.VMEM((2, length, width), bf16),
            pltpu.VMEM((4, length, width), bf16),
            pltpu.VMEM((width, cols), f32),
            pltpu.VMEM((2, width // 8, cols), bf16),
            pltpu.SemaphoreType.DMA((1,)),
            pltpu.SemaphoreType.DMA((2,)),
            pltpu.SemaphoreType.DMA((2,)),
            pltpu.SemaphoreType.DMA((2,)),
            pltpu.SemaphoreType.DMA((2,)),
            pltpu.SemaphoreType.DMA((GROUP_SENDS,)),
            pltpu.SemaphoreType.DMA((GROUP_SENDS,)),
        ],
        compiler_params=pltpu.CompilerParams(
            collective_id=2, has_side_effects=True, vmem_limit_bytes=62 * MIB
        ),
        cost_estimate=pl.CostEstimate(
            flops=48 * length * width * cols,
            bytes_accessed=64 * length * width + 4 * width * cols,
            transcendentals=8 * length * hidden,
        ),
        name="group",
    )(v, grad, xs, g_all, w)


PARTNERS_BACK = ((1, 0), (2, 0), (3, 0), (0, 1), (0, 2), (0, 4), (0, 6))
TERMS = 16
BACK_SENDS = 3 + 8 + 6 + 3 + 2 + 3 + 2 * 4 + 2 * 3 + 1 + 6 + 3


def back_kernel(
    dx_own, g_ref, first, table, tiny, v, tokens, qkv, lse, cos, sin, seg_col, seg_row,
    dx_in, grads, mix_sum, attn, xn, in_all, out_all,
    tokens_grad,
    g_out, mix_in, d_out, xn_core,
    in_v, out_v, mix_v, gl, gy, gz, act_v, aq_v, pq, wo, wi, wyo, wyi, wzo, wzi, wxo, own_d,
    dn, dxn, dl, dattn, dproj, dkv, bias, tbuf,
    local_sem, send_sem, recv_sem,
):
    wire = Wire(send_sem, recv_sem)
    r, f = wire.r, wire.f
    shard = gl.shape[1]
    length, width = tokens.shape
    experts = 8
    low = lax.rem(f // 2, 2)
    cols_p, cols_a = pq.shape[1], aq_v.shape[1]
    scale = HD ** (-0.5)
    used = [0]

    def local(src, dst):
        copy = pltpu.make_async_copy(src, dst, local_sem.at[used[0]])
        copy.start()
        used[0] += 1
        return copy

    def shard_rows(j):
        return pl.ds(pl.multiple_of(flips(f, j) * shard, shard), shard)

    def token_rows(k):
        return pl.ds(k * length, length)

    def part_of(k, cols):
        return pl.ds(pl.multiple_of(flips(r, k) * cols, cols), cols)

    def add(u, w):
        return (u.astype(f32) + w.astype(f32)).astype(bf16)

    half = lax.rem(r, 2)
    side = r // 2

    def half_of(index):
        return pl.ds(pl.multiple_of(index * cols_a, cols_a), cols_a)

    load_dx = [
        local(dx_in.at[n], in_v.at[token_rows(n), pl.ds(0, dx_in.shape[2])]) for n in range(3)
    ]
    load_out = local(out_all, out_v)
    load_g = {j: local(grads.at[shard_rows(j)], gl.at[j // 2]) for j in (4, 6, 2, 0)}
    load_a = local(attn.at[:, half_of(half)], aq_v.at[token_rows(0)])
    load_mix = local(mix_sum.at[2], mix_v.at[0])
    wire.meet(PARTNERS_BACK)
    got_y, got_m = {}, {}
    cut = shard // 2
    for j in (4, 6, 2, 0):
        for n in (0, 1):
            at = pl.ds(pl.multiple_of(flips(f, j + 1) * shard + n * cut, cut), cut)
            got_y[j, n] = wire.send(grads.at[at], gy.at[j // 2, pl.ds(n * cut, cut)], 0, 1)
    got_a = wire.send(attn.at[:, half_of(1 - half)], aq_v.at[token_rows(1)], 1, 0)
    got_m[6] = wire.send(mix_sum.at[3], mix_v.at[1], 2, 0)
    got_n = {2: wire.send(xn, act_v.at[token_rows(2)], 2, 0), 1: wire.send(xn, xn_core, 1, 0)}

    spot = lax.broadcasted_iota(jnp.int32, bias.shape, 0)
    keys_at = lax.broadcasted_iota(jnp.int32, bias.shape, 1)
    bias[...] = jnp.where((spot >= keys_at) & (seg_col[...] == seg_row[...]), 0.0, -1e30)
    tbuf[...] = jnp.zeros_like(tbuf)
    for copy in load_dx:
        copy.wait()

    def sum_dx(c, carry):
        at = pl.ds(pl.multiple_of(c * ROWS, ROWS), ROWS)
        d = dx_own[at, :].astype(f32)
        for n in range(3):
            here = pl.ds(pl.multiple_of(n * length + c * ROWS, ROWS), ROWS)
            d = d + in_v[here, 0 : dx_own.shape[1]].astype(f32)
        dn[at, :] = d[:, :width]
        dgate = d[:, width:]
        dgate = dgate + pltpu.roll(dgate, EXTRA - experts, 1)
        gates = table[at, :]
        mean = jnp.sum(gates * dgate, axis=-1, keepdims=True)
        dl[at, :] = (gates * (dgate - mean)).astype(bf16)
        return carry

    lax.fori_loop(0, length // ROWS, sum_dx, 0)
    load_in = local(in_all, in_v)
    dlt = dl[...].T[0:16]

    def add_router(c, carry):
        at = pl.ds(pl.multiple_of(c * 256, 256), 256)
        row = lax.broadcasted_iota(jnp.int32, (16, 256), 0)
        router = jnp.where(row < experts, tiny[:, at], 0.0).astype(bf16)
        dn[:, at] = dn[:, at] + matmul(dl[:, 0:16], router)
        tbuf[:, at] = matmul(dlt, v[:, at])
        return carry

    lax.fori_loop(0, width // 256, add_router, 0)

    def norm_two(c, gain):
        at = pl.ds(pl.multiple_of(c * ROWS, ROWS), ROWS)
        h = first[at, :]
        r2 = lax.rsqrt(jnp.mean(h * h, axis=-1, keepdims=True) + epsilon)
        unit = h * r2
        d = dn[at, :]
        gain = gain + jnp.sum(d * unit, axis=0, keepdims=True)
        d = d * tiny[experts + 1 : experts + 2, :]
        d = g_ref[at, :].astype(f32) + r2 * (
            d - unit * jnp.mean(d * unit, axis=-1, keepdims=True)
        )
        dn[at, :] = d
        act_v[at, :] = d.astype(bf16)
        return gain

    gain_two = lax.fori_loop(0, length // ROWS, norm_two, jnp.zeros((1, width), f32))
    tbuf[experts + 1 : experts + 2, :] = gain_two
    got_r = wire.send(act_v.at[token_rows(0)], act_v.at[token_rows(1)], 1, 0)
    got_z = {}

    def pass_y(j, n):
        if n == 0:
            load_g[j].wait()
        got_y[j, n].wait_recv()
        at = pl.ds(n * cut, cut)
        gl[j // 2, at] = add(gl[j // 2, at], gy[j // 2, at])
        got_z[j, n] = wire.send(gl.at[j // 2, at], gz.at[j // 2 - 1, at], 0, j)

    def came(got_some, j):
        for n in (0, 1):
            got_some[j, n].wait_recv()

    load_out.wait()

    def to_attn(c, carry):
        at = pl.ds(pl.multiple_of(c * 256, 256), 256)
        dattn[:, at] = matmul(act_v[0:length, :], out_v[:, at]).astype(bf16)
        return carry

    lax.fori_loop(0, WQ // 256, to_attn, 0)
    pass_y(4, 0)
    lane = lax.broadcasted_iota(jnp.int32, (length, HD), 1)

    def turn_back(w):
        return w * cos[...] - pltpu.roll(w, HD // 2, 1) * sin[...]

    for group in range(KV):
        k_at = pl.ds(WQ + group * HD, HD)
        v_at = pl.ds(WQ + WK + group * HD, HD)
        dkv[...] = jnp.zeros_like(dkv)

        def head(i, carry):
            h = group * GROUP + i
            at = pl.ds(pl.multiple_of(h * HD, HD), HD)
            s = contract_cols(qkv[:, at], qkv[:, k_at]) * scale + bias[...]
            level = jnp.sum(jnp.where(lane == h, lse[...], 0.0), axis=1, keepdims=True)
            p = jnp.exp(s - level)
            da = dattn[:, at]
            dp = contract_cols(da, qkv[:, v_at])
            delta = jnp.sum(p * dp, axis=-1, keepdims=True)
            ds = (p * (dp - delta)).astype(bf16)
            dkv[1] += contract_rows(p.astype(bf16), da)
            dkv[0] += contract_rows(ds, qkv[:, at])
            dproj[:, at] = turn_back(matmul(ds, qkv[:, k_at]) * scale).astype(bf16)
            return carry

        lax.fori_loop(0, GROUP, head, 0)
        if group == 0:
            pass_y(4, 1)
            load_mix.wait()
            got_m[6].wait_recv()
            mix_v[0] = add(mix_v[0], mix_v[1])
            got_m[4] = wire.send(mix_v.at[0], mix_in.at[1], 0, 2)
        dproj[:, k_at] = turn_back(dkv[0] * scale).astype(bf16)
        dproj[:, v_at] = dkv[1].astype(bf16)

    keep_p = local(dproj.at[:, part_of(0, cols_p)], pq.at[token_rows(0)])
    got_p = {}
    for k in (2, 3, 1):
        got_p[k] = wire.send(dproj.at[:, part_of(k, cols_p)], pq.at[token_rows(k)], k, 0)

    got_m[2] = wire.send(mix_sum.at[1], mix_in.at[0], 2, 0)
    pass_y(6, 0)

    load_a.wait()
    got_a.wait_recv()
    got_r.wait_recv()

    def dense_out(c, carry):
        at = pl.ds(pl.multiple_of(c * 256, 256), 256)
        wo[at, :] = matmul(act_v[0 : 2 * length, at].T, aq_v[...]).astype(bf16)
        return carry

    lax.fori_loop(0, width // 256, dense_out, 0)
    got_r.wait_send()
    load_x = [local(xn, act_v.at[token_rows(0)])]
    got_n[1].wait_recv()
    load_x.append(local(xn_core, act_v.at[token_rows(1)]))
    got_wo, got_wi, got_wzo, got_wzi = {}, {}, {}, {}
    for j in (4, 6, 2, 0):
        got_wo[j] = wire.send(wo.at[shard_rows(j + 1)], wyo.at[j // 2], 0, 1)

    pass_y(6, 1)

    load_in.wait()

    def to_norm(c, carry):
        at = pl.ds(pl.multiple_of(c * 256, 256), 256)
        dxn[:, at] = contract_cols(dproj[...], in_v[at, :])
        return carry

    lax.fori_loop(0, width // 256, to_norm, 0)

    def norm_one(c, gain):
        at = pl.ds(pl.multiple_of(c * ROWS, ROWS), ROWS)
        x = tokens[at, :].astype(f32)
        r1 = lax.rsqrt(jnp.mean(x * x, axis=-1, keepdims=True) + epsilon)
        unit = x * r1
        d = dxn[at, :]
        gain = gain + jnp.sum(d * unit, axis=0, keepdims=True)
        d = d * tiny[experts : experts + 1, :]
        d = dn[at, :] + r1 * (d - unit * jnp.mean(d * unit, axis=-1, keepdims=True))
        tokens_grad[at, :] = d.astype(bf16)
        return gain

    gain_one = lax.fori_loop(0, length // ROWS, norm_one, jnp.zeros((1, width), f32))
    tbuf[experts : experts + 1, :] = gain_one

    pass_y(2, 0)
    pass_y(2, 1)
    mine, other = 2 * r + low, 2 * r + 1 - low
    load_g[0].wait()
    came(got_y, 0)
    came(got_z, 4)
    gl[0] = (gl[0].astype(f32) + gy[0].astype(f32) + gz[1].astype(f32)).astype(bf16)
    kept = [local(gl.at[0], g_out.at[mine])]
    got_e = {}

    got_n[2].wait_recv()
    got_n[3] = wire.send(act_v.at[token_rows(2)], act_v.at[token_rows(3)], 1, 0)
    keep_p.wait()
    for copy in load_x:
        copy.wait()
    for k in (1, 2, 3):
        got_p[k].wait_recv()
    got_n[3].wait_recv()
    got_e[2, 0] = wire.send(gl.at[0], g_out.at[mine], 2, 0)
    got_e[1, 0] = wire.send(gl.at[0], g_out.at[mine], 1, 0)

    tall = shard + TERMS

    def tall_rows(j):
        return pl.ds(pl.multiple_of(flips(f, j) * tall, TERMS), tall)

    for z in range(4):
        lanes = slice(2 * z * shard, 2 * (z + 1) * shard)
        both = matmul(act_v[:, lanes].T, pq[...]).astype(bf16)
        for y in (0, 1):
            top = (2 * z + y) * tall
            wi[top : top + shard, :] = both[y * shard : (y + 1) * shard]
            wi[top + shard : top + tall, :] = jnp.zeros((TERMS, cols_p), bf16)
            wi[top + shard : top + tall, 0 : 2 * shard] = tbuf[:, lanes].astype(bf16)
    for j in (4, 6, 2, 0):
        got_wi[j] = wire.send(wi.at[tall_rows(j + 1)], wyi.at[j // 2], 0, 1)
    for j in (4, 6, 2):
        got_wo[j].wait_recv()
        wyo[j // 2] = add(wo[shard_rows(j), :], wyo[j // 2])
        got_wzo[j] = wire.send(wyo.at[j // 2], wzo.at[j // 2 - 1], 0, j)

    came(got_z, 2)
    came(got_z, 6)
    gz[0] = add(gz[0], gz[2])
    kept.append(local(gz.at[0], g_out.at[other]))
    got_e[2, 1] = wire.send(gz.at[0], g_out.at[other], 2, 0)
    got_e[1, 1] = wire.send(gz.at[0], g_out.at[other], 1, 0)

    for j in (4, 6, 2):
        got_wi[j].wait_recv()
        wyi[j // 2] = add(wi[tall_rows(j), :], wyi[j // 2])
        got_wzi[j] = wire.send(wyi.at[j // 2], wzi.at[j // 2 - 1], 0, j)

    def own_rows(w, rows, y, z, got_w, got_zs):
        got_w[0].wait_recv()
        total = w[rows, :].astype(f32) + y[0].astype(f32)
        for j in (2, 4, 6):
            got_zs[j].wait_recv()
            total = total + z[j // 2 - 1].astype(f32)
        return total

    wxo[0] = own_rows(wo, shard_rows(0), wyo, wzo, got_wo, got_wzo).astype(bf16)
    quarter = cols_a // 2

    def quarter_of(index):
        return pl.ds(pl.multiple_of(index * quarter, quarter), quarter)

    got_x = wire.send(
        wxo.at[0, :, quarter_of(1 - side)], wxo.at[1, :, pl.ds(0, quarter)], 2, 0
    )
    own_d[:, 0:cols_p] = own_rows(wi, tall_rows(0), wyi, wzi, got_wi, got_wzi).astype(bf16)
    got_x.wait_recv()
    own_d[shard:, cols_p:] = jnp.zeros((TERMS, quarter), bf16)
    own_d[0:shard, cols_p:] = add(wxo[0, :, quarter_of(side)], wxo[1, :, 0:quarter])
    kept.append(local(own_d, d_out.at[r]))
    got_d = [wire.send(own_d, d_out.at[r], k, 0) for k in (2, 1)]

    far = flips(r, 2)
    for n, e in ((0, 2 * far + low), (1, 2 * far + 1 - low)):
        got_e[2, n].wait_recv()
        got_e[3, n] = wire.send(g_out.at[e], g_out.at[e], 1, 0)
    got_d[0].wait_recv()
    got_d.append(wire.send(d_out.at[far], d_out.at[far], 1, 0))
    for k in (1, 3):
        for n in (0, 1):
            got_e[k, n].wait_recv()
    for copy in got_d[1:]:
        copy.wait_recv()
    for k in (2, 4):
        got_m[k].wait_recv()
    for copy in kept:
        copy.wait()
    wire.finish((got_r,))


def run_back(
    dx_own, grad, first, table, tiny, v, tokens, qkv, lse, cos, sin, seg_ids,
    dx_in, grads, mix_sum, attn, xn, in_all, out_all,
):
    any_spec = pl.BlockSpec(memory_space=pl.ANY)
    vmem = pl.BlockSpec(memory_space=pltpu.VMEM)
    length, width = tokens.shape
    shard = width // 8
    cols = grads.shape[1]
    cols_p, cols_a = qkv.shape[1] // 4, attn.shape[1] // 2
    return pl.pallas_call(
        back_kernel,
        out_shape=[
            jax.ShapeDtypeStruct((length, width), bf16),
            jax.ShapeDtypeStruct((8, shard, cols), bf16),
            jax.ShapeDtypeStruct((2, length, width), bf16),
            jax.ShapeDtypeStruct((4, shard + TERMS, cols_p + cols_a // 2), bf16),
            jax.ShapeDtypeStruct((length, width), bf16),
        ],
        in_specs=[vmem] * 13 + [any_spec] * 7,
        out_specs=[vmem] + [any_spec] * 4,
        scratch_shapes=[
            pltpu.VMEM(in_all.shape, bf16),
            pltpu.VMEM(out_all.shape, bf16),
            pltpu.VMEM((2, length, width), bf16),
            pltpu.VMEM((4, shard, cols), bf16),
            pltpu.VMEM((4, shard, cols), bf16),
            pltpu.VMEM((3, shard, cols), bf16),
            pltpu.VMEM((4 * length, width), bf16),
            pltpu.VMEM((2 * length, cols_a), bf16),
            pltpu.VMEM((4 * length, cols_p), bf16),
            pltpu.VMEM((width, cols_a), bf16),
            pltpu.VMEM((width + 8 * TERMS, cols_p), bf16),
            pltpu.VMEM((4, shard, cols_a), bf16),
            pltpu.VMEM((4, shard + TERMS, cols_p), bf16),
            pltpu.VMEM((3, shard, cols_a), bf16),
            pltpu.VMEM((3, shard + TERMS, cols_p), bf16),
            pltpu.VMEM((2, shard, cols_a), bf16),
            pltpu.VMEM((shard + TERMS, cols_p + cols_a // 2), bf16),
            pltpu.VMEM((length, width), f32),
            pltpu.VMEM((length, width), f32),
            pltpu.VMEM((length, EXTRA), bf16),
            pltpu.VMEM((length, WQ), bf16),
            pltpu.VMEM(qkv.shape, bf16),
            pltpu.VMEM((2, length, HD), f32),
            pltpu.VMEM((length, length), f32),
            pltpu.VMEM((TERMS, width), f32),
            pltpu.SemaphoreType.DMA((20,)),
            pltpu.SemaphoreType.DMA((BACK_SENDS,)),
            pltpu.SemaphoreType.DMA((BACK_SENDS,)),
        ],
        compiler_params=pltpu.CompilerParams(
            collective_id=3, has_side_effects=True, vmem_limit_bytes=62 * MIB
        ),
        name="back",
    )(
        dx_own, grad, first, table, tiny, v, tokens, qkv, lse, cos, sin,
        seg_ids.reshape(length, 1), seg_ids,
        dx_in, grads, mix_sum, attn, xn, in_all, out_all,
    )


def finish_kernel(sums, dense, first, own, parts, e_in, e_out, in_grad, out_grad, mixed):
    split = e_in.shape[2]
    for c in range(0, sums.shape[2], 128):
        part = jnp.swapaxes(sums[:, :, c : c + 128].astype(f32), 0, 1)
        if c < split:
            e_in[:, :, c : c + 128] = part
        else:
            e_out[:, :, c - split : c - split + 128] = part
    cut = in_grad.shape[1] // 4
    quarter = out_grad.shape[1] // 4
    for r in range(4):
        in_grad[:, r * cut : (r + 1) * cut] = dense[r, :, :cut].astype(f32)
        place = 2 * (r % 2) + r // 2
        out_grad[:, place * quarter : (place + 1) * quarter] = dense[r, :, cut:].astype(f32)
    total = first[...] + own[0].astype(f32)
    for n in range(parts.shape[0]):
        total = total + parts[n].astype(f32)
    mixed[...] = total.astype(bf16)


def run_finish(expert_sum, dense, first, mix_sum, mix_in, hidden):
    n_experts, shard, cols = expert_sum.shape
    length, width = first.shape
    steps = 6
    rows, tokens = shard // steps, length // steps
    cut = dense.shape[2] - width // 4
    return pl.pallas_call(
        finish_kernel,
        grid=(steps,),
        out_shape=[
            jax.ShapeDtypeStruct((shard, n_experts, 2 * hidden), f32),
            jax.ShapeDtypeStruct((shard, n_experts, hidden), f32),
            jax.ShapeDtypeStruct((shard, 4 * cut), f32),
            jax.ShapeDtypeStruct((shard, width), f32),
            jax.ShapeDtypeStruct((length, width), bf16),
        ],
        in_specs=[
            pl.BlockSpec((n_experts, rows, cols), lambda i: (0, i, 0)),
            pl.BlockSpec((4, rows, dense.shape[2]), lambda i: (0, i, 0)),
            pl.BlockSpec((tokens, width), lambda i: (i, 0)),
            pl.BlockSpec((1, tokens, width), lambda i: (0, i, 0)),
            pl.BlockSpec((mix_in.shape[0], tokens, width), lambda i: (0, i, 0)),
        ],
        out_specs=[
            pl.BlockSpec((rows, n_experts, 2 * hidden), lambda i: (i, 0, 0)),
            pl.BlockSpec((rows, n_experts, hidden), lambda i: (i, 0, 0)),
            pl.BlockSpec((rows, 4 * cut), lambda i: (i, 0)),
            pl.BlockSpec((rows, width), lambda i: (i, 0)),
            pl.BlockSpec((tokens, width), lambda i: (i, 0)),
        ],
        compiler_params=pltpu.CompilerParams(vmem_limit_bytes=48 * MIB),
        name="finish",
    )(expert_sum, dense, first, mix_sum, mix_in)


def near_layer(
    tokens, seg_ids, routes, in_proj, out_proj, router, norm_gains, expert_in, expert_out,
    out_grad,
):
    length, width = tokens.shape
    experts = router.shape[1]
    hidden = expert_out.shape[2]
    shard = router.shape[0]
    r, f = lax.axis_index("replica"), lax.axis_index("fsdp")
    cosine, sine = [t[:, 0] for t in tables(length)]
    cos = jnp.concatenate([cosine, cosine], axis=1)
    sin = jnp.concatenate([-sine, sine], axis=1)
    tiny = jnp.concatenate(
        [router.T, norm_gains.T, jnp.zeros((16 - experts - 2, shard), bf16)], axis=0
    )
    none = jnp.zeros_like(tiny)
    tiny = jnp.where(
        f % 2 == 0,
        jnp.concatenate([tiny, none], axis=1),
        jnp.concatenate([none, tiny], axis=1),
    )
    low = (f >> 1) & 1
    mine, other = [
        jnp.concatenate(
            [
                lax.dynamic_index_in_dim(expert_in, e, 1, keepdims=False),
                lax.dynamic_index_in_dim(expert_out, e, 1, keepdims=False),
            ],
            axis=1,
        )
        for e in (2 * r + low, 2 * r + 1 - low)
    ]
    qkv, attn, xn, first, lse, table, small, v, in_all, out_all, w_all, g_all, xs = front(
        tokens, seg_ids, routes, cos, sin, in_proj, out_proj, tiny, mine, other, out_grad
    )
    mix_sum, dx_own, dx_in, grads, _, _ = run_group(v, out_grad, xs, g_all, w_all)
    tokens_grad, expert_sum, mix_in, dense, _ = run_back(
        dx_own, out_grad, first, table, small, v, tokens, qkv, lse, cos, sin, seg_ids,
        dx_in, grads, mix_sum, attn, xn, in_all, out_all,
    )
    e_in, e_out, in_grad, out_proj_grad, mixed = run_finish(
        expert_sum, dense, first, mix_sum, mix_in, hidden
    )
    terms = jnp.sum(dense[:, shard:, : 2 * shard].astype(f32), axis=0)
    terms = jnp.where(f % 2 == 0, terms[:, :shard], terms[:, shard:]).T
    return (
        mixed,
        tokens_grad,
        in_grad,
        out_proj_grad,
        terms[:, :experts],
        terms[:, experts : experts + 2],
        e_in,
        e_out,
    )


class Wide:
    def __init__(self, n_rep, n_fsdp):
        self.n_rep, self.n_fsdp = n_rep, n_fsdp

    def spread(self, value):
        every = lax.all_gather(value, "replica", axis=0)
        return [every[k] for k in range(self.n_rep)]

    def collect(self, parts):
        return lax.psum_scatter(jnp.stack(parts), "replica", scatter_dimension=0).astype(f32)

    def start(self, in_proj, out_proj, tiny, expert_in, expert_out, grad):
        r = lax.axis_index("replica")
        per = expert_in.shape[1] // self.n_rep
        weights = []
        for i in range(per):
            both = jnp.concatenate(
                [
                    lax.dynamic_index_in_dim(expert_in, per * r + i, 1, keepdims=False),
                    lax.dynamic_index_in_dim(expert_out, per * r + i, 1, keepdims=False),
                ],
                axis=1,
            )
            weights.append(lax.all_gather(both, "fsdp", axis=0, tiled=True))
        return (
            lax.all_gather(in_proj, "fsdp", axis=0, tiled=True),
            lax.all_gather(out_proj, "fsdp", axis=0, tiled=True),
            lax.all_gather(tiny, "fsdp", axis=1, tiled=True),
            (weights, self.spread(grad)),
        )

    def experts(self, payload, held):
        weights, gs = held
        xs = self.spread(payload)
        per = len(weights)
        mixes, dxs, grads = None, None, []
        for i, w in enumerate(weights):

            def expert_of(i=i):
                return per * lax.axis_index("replica") + i

            mix, dx, grad = run_expert(xs, gs, [w], expert_of, lambda j: 0)
            mixes = mix if mixes is None else [a + b for a, b in zip(mixes, mix)]
            dxs = dx if dxs is None else [a + b for a, b in zip(dxs, dx)]
            grads.append(grad[0])
        return self.collect(dxs), (mixes, grads)

    def trade(self, value):
        cut = value.reshape(value.shape[0], self.n_rep, -1).transpose(1, 0, 2)
        got = lax.all_to_all(cut, "replica", 0, 0)
        return got.reshape(-1, got.shape[2])

    def end(self, held, first, normed, attn, dres, dproj, terms):
        mixes, grads = held
        mixed = first + self.collect(mixes)
        own = jnp.stack(
            [lax.psum_scatter(g, "fsdp", scatter_dimension=0, tiled=True) for g in grads]
        )
        expert_sum = lax.all_gather(own, "replica", axis=0, tiled=True).transpose(1, 0, 2)
        dense = []
        for left, right in ((normed, dproj), (dres, attn)):
            left = lax.all_gather(left, "replica", axis=0, tiled=True)
            part = contract_rows(left, self.trade(right)).astype(bf16)
            own = lax.psum_scatter(part, "fsdp", scatter_dimension=0, tiled=True)
            dense.append(lax.all_gather(own, "replica", axis=1, tiled=True))
        return mixed, dense[0], dense[1], expert_sum, lax.psum(terms, ("replica", "fsdp"))


def layer(
    net, tokens, seg_ids, routes, in_proj, out_proj, router, norm_gains, expert_in, expert_out,
    out_grad,
):
    length, width = tokens.shape
    experts = router.shape[1]
    hidden = expert_out.shape[2]
    shard = router.shape[0]
    scale = HD ** (-0.5)
    cosine, sine = tables(length)
    segment = seg_ids[0]
    place = jnp.arange(length)
    allowed = ((place[:, None] >= place[None, :]) & (segment[:, None] == segment[None, :]))[
        None, None
    ]
    tiny = jnp.concatenate(
        [router.T, norm_gains.T, jnp.zeros((16 - experts - 2, shard), bf16)], axis=0
    )
    proj_in, proj_out, tiny, held = net.start(
        in_proj, out_proj, tiny, expert_in, expert_out, out_grad
    )
    router_rows = tiny[:experts]
    gain_one = tiny[experts].astype(f32)
    gain_two = tiny[experts + 1].astype(f32)

    inputs = tokens.astype(f32)
    scale_one = rms_scale(inputs)
    unit_one = inputs * scale_one
    normed = (unit_one * gain_one).astype(bf16)
    proj = matmul(normed, proj_in)
    queries = (
        rotate(proj[:, :WQ].reshape(length, HQ, HD), cosine, sine)
        .astype(bf16)
        .reshape(length, KV, GROUP, HD)
    )
    keys = rotate(proj[:, WQ : WQ + WK].reshape(length, KV, HD), cosine, sine).astype(bf16)
    values = proj[:, WQ + WK :].reshape(length, KV, HD).astype(bf16)
    scores = jnp.einsum("qkgd,tkd->kgqt", queries, keys, preferred_element_type=f32) * scale
    masked = jnp.where(allowed, scores, -1e30)
    highest = jnp.max(masked, axis=-1, keepdims=True)
    expo = jnp.exp(masked - highest)
    total = jnp.sum(expo, axis=-1, keepdims=True)
    log_total = highest + jnp.log(total)
    probs_low = (expo / total).astype(bf16)
    attn = jnp.einsum("kgqt,tkd->qkgd", probs_low, values, preferred_element_type=f32)
    attn = attn.astype(bf16).reshape(length, WQ)
    first = inputs + contract_cols(attn, proj_out)
    scale_two = rms_scale(first)
    unit_two = first * scale_two
    normed_two = (unit_two * gain_two).astype(bf16)
    logits = contract_cols(normed_two, router_rows)
    onehot = (routes[:, :, None] == jnp.arange(experts)[None, None, :]).astype(f32)
    chosen = jnp.sum(onehot * logits[:, None, :], axis=-1)
    gates = jax.nn.softmax(chosen, axis=-1)
    table = jnp.sum(gates[:, :, None] * onehot, axis=1)
    high = table.astype(bf16)
    low = (table - high.astype(f32)).astype(bf16)
    payload = jnp.concatenate(
        [normed_two, high, low, jnp.zeros((length, EXTRA - 2 * experts), bf16)], axis=1
    )
    dx, held = net.experts(payload, held)

    grad_out = out_grad.astype(f32)
    dgate_all = dx[:, width : width + experts] + dx[:, width + experts : width + 2 * experts]
    dgate = jnp.sum(onehot * dgate_all[:, None, :], axis=-1)
    dchosen = gates * (dgate - jnp.sum(gates * dgate, axis=-1, keepdims=True))
    dlogits = jnp.sum(dchosen[:, :, None] * onehot, axis=1).astype(bf16)
    dnormed_two = dx[:, :width] + matmul(dlogits, router_rows)
    gain_two_grad = jnp.sum(dnormed_two * unit_two, axis=0)
    dunit_two = dnormed_two * gain_two
    dfirst = grad_out + scale_two * (
        dunit_two - unit_two * jnp.mean(dunit_two * unit_two, axis=-1, keepdims=True)
    )
    dres = dfirst.astype(bf16)
    dattn = matmul(dres, proj_out).astype(bf16).reshape(length, KV, GROUP, HD)
    probs = jnp.exp(masked - log_total)
    probs_again = probs.astype(bf16)
    dprobs = jnp.einsum("qkgd,tkd->kgqt", dattn, values, preferred_element_type=f32)
    dvalues = jnp.einsum("kgqt,qkgd->tkd", probs_again, dattn, preferred_element_type=f32)
    delta = jnp.sum(probs * dprobs, axis=-1, keepdims=True)
    dscores = (probs * (dprobs - delta)).astype(bf16)
    dqueries = jnp.einsum("kgqt,tkd->qkgd", dscores, keys, preferred_element_type=f32) * scale
    dkeys = jnp.einsum("kgqt,qkgd->tkd", dscores, queries, preferred_element_type=f32) * scale
    dqueries = rotate(dqueries.reshape(length, HQ, HD), cosine, -sine).reshape(length, WQ)
    dkeys = rotate(dkeys, cosine, -sine).reshape(length, WK)
    dproj = jnp.concatenate([dqueries, dkeys, dvalues.reshape(length, WK)], axis=1).astype(bf16)
    dnormed = contract_cols(dproj, proj_in)
    gain_one_grad = jnp.sum(dnormed * unit_one, axis=0)
    dunit_one = dnormed * gain_one
    tokens_grad = (
        dfirst
        + scale_one
        * (dunit_one - unit_one * jnp.mean(dunit_one * unit_one, axis=-1, keepdims=True))
    ).astype(bf16)

    terms = jnp.concatenate(
        [
            contract_rows(dlogits, normed_two),
            gain_one_grad[None],
            gain_two_grad[None],
            jnp.zeros((16 - experts - 2, width), f32),
        ],
        axis=0,
    )
    mixed, in_proj_grad, out_proj_grad, expert_sum, terms = net.end(
        held, first, normed, attn, dres, dproj, terms
    )
    terms = lax.dynamic_slice_in_dim(terms, lax.axis_index("fsdp") * shard, shard, 1).T
    return (
        mixed.astype(bf16),
        tokens_grad,
        in_proj_grad.astype(f32),
        out_proj_grad.astype(f32),
        terms[:, :experts],
        terms[:, experts : experts + 2],
        expert_sum[..., : 2 * hidden].astype(f32),
        expert_sum[..., 2 * hidden :].astype(f32),
    )


def solution(mesh):
    n_rep, n_fsdp = mesh.shape["replica"], mesh.shape["fsdp"]
    if (n_rep, n_fsdp) == (4, 8):
        body = near_layer
    else:
        body = functools.partial(layer, Wide(n_rep, n_fsdp))
    both = P(("replica", "fsdp"), None)
    fsdp, deep = P("fsdp", None), P("fsdp", None, None)
    return jax.shard_map(
        body,
        mesh=mesh,
        in_specs=(both, both, both, fsdp, fsdp, fsdp, fsdp, deep, deep, both),
        out_specs=(both, both, fsdp, fsdp, fsdp, fsdp, deep, deep),
        check_vma=False,
    )
```

```python
import functools

import jax
import jax.numpy as jnp
from jax import lax
from jax.experimental import pallas as pl
from jax.experimental.pallas import tpu as pltpu
from jax.sharding import PartitionSpec as P

HQ = 12
KV = 2
HD = 128
GROUP = HQ // KV
WQ = HQ * HD
WK = KV * HD
EXTRA = 128
MIB = 1024 * 1024

epsilon = 1e-06
rope_base = 1000000.0
bf16 = jnp.bfloat16
f32 = jnp.float32


def rms_scale(v):
    return lax.rsqrt(jnp.mean(v * v, axis=-1, keepdims=True) + epsilon)


def tables(length):
    half = HD // 2
    freq = jnp.power(rope_base, -(jnp.arange(half, dtype=f32) * 2.0 / HD))
    angle = jnp.arange(length, dtype=f32)[:, None] * freq[None, :]
    return (jnp.cos(angle)[:, None, :], jnp.sin(angle)[:, None, :])


def rotate(v, cosine, sine):
    half = v.shape[-1] // 2
    first = v[..., :half]
    second = v[..., half:]
    return jnp.concatenate(
        [first * cosine - second * sine, second * cosine + first * sine], axis=-1
    )


def contract_rows(left, right):
    return lax.dot_general(left, right, (((0,), (0,)), ((), ())), preferred_element_type=f32)


def contract_cols(left, right):
    return lax.dot_general(left, right, (((1,), (1,)), ((), ())), preferred_element_type=f32)


def matmul(left, right):
    return lax.dot_general(left, right, (((1,), (0,)), ((), ())), preferred_element_type=f32)


def expert_kernel(nt, nw, length, width, hidden, rows, expert_of, offset_of, *refs):
    xs, gs, ws = refs[:nt], refs[nt : 2 * nt], refs[2 * nt : 2 * nt + nw]
    refs = refs[2 * nt + nw :]
    mixes, dxs, grads = refs[:nt], refs[nt : 2 * nt], refs[2 * nt : 2 * nt + nw]
    (
        wbuf, xbuf, gbuf, xt, gt_, hidg, dgu, mbuf, dbuf, acc, stage,
        sem_w, sem_x, sem_g, sem_m, sem_d, sem_s,
    ) = refs[2 * nt + nw :]
    cols = 3 * hidden
    step_cols = 256

    def load(k, slot):
        for i in range(nt):

            @pl.when(k == i)
            def _():
                pltpu.make_async_copy(xs[i], xbuf.at[slot], sem_x.at[slot]).start()
                pltpu.make_async_copy(gs[i], gbuf.at[slot], sem_g.at[slot]).start()

    def store(k, slot):
        for i in range(nt):

            @pl.when(k == i)
            def _():
                pltpu.make_async_copy(mbuf.at[slot], mixes[i], sem_m.at[slot]).start()
                pltpu.make_async_copy(dbuf.at[slot], dxs[i], sem_d.at[slot]).start()

    def stored(slot):
        pltpu.make_async_copy(mbuf.at[slot], mixes[0], sem_m.at[slot]).wait()
        pltpu.make_async_copy(dbuf.at[slot], dxs[0], sem_d.at[slot]).wait()

    for j in range(nw):
        pltpu.make_async_copy(
            ws[j], wbuf.at[pl.ds(pl.multiple_of(offset_of(j), 8), rows)], sem_w.at[j]
        ).start()
    load(0, 0)
    expert = expert_of()
    acc[...] = jnp.zeros_like(acc)
    lane = lax.broadcasted_iota(jnp.int32, (length, EXTRA), 1)
    for j in range(nw):
        pltpu.make_async_copy(
            ws[j], wbuf.at[pl.ds(pl.multiple_of(offset_of(j), 8), rows)], sem_w.at[j]
        ).wait()

    def block(k, carry):
        slot = lax.rem(k, 2)

        @pl.when(k + 1 < nt)
        def _():
            load(k + 1, 1 - slot)

        pltpu.make_async_copy(xs[0], xbuf.at[slot], sem_x.at[slot]).wait()
        pltpu.make_async_copy(gs[0], gbuf.at[slot], sem_g.at[slot]).wait()

        @pl.when(k >= 2)
        def _():
            stored(slot)

        extra = xbuf[slot, :, width:].astype(f32)
        mine = (lane == expert) | (lane == expert + 8)
        gate = jnp.sum(jnp.where(mine, extra, 0.0), axis=1, keepdims=True)
        xt[...] = xbuf[slot, :, :width].T
        gt_[...] = gbuf[slot].T

        def first(c, dgate):
            at = pl.multiple_of(c * step_cols, step_cols)
            u = matmul(xbuf[slot, :, :width], wbuf[:, pl.ds(at, step_cols)])
            up = matmul(xbuf[slot, :, :width], wbuf[:, pl.ds(hidden + at, step_cols)])
            back = matmul(gbuf[slot], wbuf[:, pl.ds(2 * hidden + at, step_cols)])
            sig = 1.0 / (1.0 + jnp.exp(-u))
            act = u * sig
            hid = act * up
            hidg[:, pl.ds(at, step_cols)] = (gate * hid).astype(bf16)
            dgate = dgate + jnp.sum(back * hid, axis=1, keepdims=True)
            dhid = gate * back
            dgu[:, pl.ds(at, step_cols)] = (
                dhid * up * sig * (1.0 + u * (1.0 - sig))
            ).astype(bf16)
            dgu[:, pl.ds(hidden + at, step_cols)] = (dhid * act).astype(bf16)
            return dgate

        dgate = lax.fori_loop(
            0, hidden // step_cols, first, jnp.zeros((length, 1), f32)
        )

        def second(c, carry):
            at = pl.multiple_of(c * step_cols, step_cols)
            mbuf[slot, :, pl.ds(at, step_cols)] = contract_cols(
                hidg[...], wbuf[pl.ds(at, step_cols), pl.ds(2 * hidden, hidden)]
            ).astype(bf16)
            dbuf[slot, :, pl.ds(at, step_cols)] = contract_cols(
                dgu[...], wbuf[pl.ds(at, step_cols), pl.ds(0, 2 * hidden)]
            ).astype(bf16)
            return carry

        lax.fori_loop(0, width // step_cols, second, 0)
        high = dgate.astype(bf16).astype(f32)
        low = dgate - high
        dbuf[slot, :, width:] = (
            jnp.where(lane == expert, high, 0.0) + jnp.where(lane == expert + 8, low, 0.0)
        ).astype(bf16)
        store(k, slot)

        def third(c, carry):
            at = pl.multiple_of(c * step_cols, step_cols)
            acc[:, pl.ds(at, step_cols)] += matmul(xt[...], dgu[:, pl.ds(at, step_cols)])
            return carry

        lax.fori_loop(0, 2 * hidden // step_cols, third, 0)

        def fourth(c, carry):
            at = pl.multiple_of(c * step_cols, step_cols)
            acc[:, pl.ds(2 * hidden + at, step_cols)] += matmul(
                gt_[...], hidg[:, pl.ds(at, step_cols)]
            )
            return carry

        lax.fori_loop(0, hidden // step_cols, fourth, 0)
        return carry

    lax.fori_loop(0, nt, block, 0)
    stored(0)
    stored(1)
    for j in range(nw):
        slot = j % 2
        if j >= 2:
            pltpu.make_async_copy(stage.at[slot], grads[j - 2], sem_s.at[slot]).wait()
        stage[slot] = acc[pl.ds(pl.multiple_of(offset_of(j), 8), rows)].astype(bf16)
        pltpu.make_async_copy(stage.at[slot], grads[j], sem_s.at[slot]).start()
    for j in range(max(0, nw - 2), nw):
        pltpu.make_async_copy(stage.at[j % 2], grads[j], sem_s.at[j % 2]).wait()


def run_expert(xs, gs, ws, expert_of, offset_of):
    nt, nw = len(xs), len(ws)
    length, width = gs[0].shape
    rows, cols = ws[0].shape
    hidden = cols // 3
    outs = (
        [jax.ShapeDtypeStruct((length, width), bf16)] * nt
        + [jax.ShapeDtypeStruct((length, width + EXTRA), bf16)] * nt
        + [jax.ShapeDtypeStruct((rows, cols), bf16)] * nw
    )
    any_spec = pl.BlockSpec(memory_space=pl.ANY)
    result = pl.pallas_call(
        functools.partial(
            expert_kernel, nt, nw, length, width, hidden, rows, expert_of, offset_of
        ),
        out_shape=outs,
        in_specs=[any_spec] * (2 * nt + nw),
        out_specs=[any_spec] * len(outs),
        scratch_shapes=[
            pltpu.VMEM((width, cols), bf16),
            pltpu.VMEM((2, length, width + EXTRA), bf16),
            pltpu.VMEM((2, length, width), bf16),
            pltpu.VMEM((width, length), bf16),
            pltpu.VMEM((width, length), bf16),
            pltpu.VMEM((length, hidden), bf16),
            pltpu.VMEM((length, 2 * hidden), bf16),
            pltpu.VMEM((2, length, width), bf16),
            pltpu.VMEM((2, length, width + EXTRA), bf16),
            pltpu.VMEM((width, cols), f32),
            pltpu.VMEM((2, rows, cols), bf16),
            pltpu.SemaphoreType.DMA((nw,)),
            pltpu.SemaphoreType.DMA((2,)),
            pltpu.SemaphoreType.DMA((2,)),
            pltpu.SemaphoreType.DMA((2,)),
            pltpu.SemaphoreType.DMA((2,)),
            pltpu.SemaphoreType.DMA((2,)),
        ],
        compiler_params=pltpu.CompilerParams(vmem_limit_bytes=60 * MIB),
        cost_estimate=pl.CostEstimate(
            flops=6 * nt * length * width * cols,
            bytes_accessed=8 * nt * length * width + 4 * width * cols,
            transcendentals=nt * length * hidden,
        ),
        name="expert",
    )(*xs, *gs, *ws)
    return result[:nt], result[nt : 2 * nt], result[2 * nt :]


MESH_ID = pl.DeviceIdType.MESH


def flip(index, bit):
    return index + bit - 2 * bit * lax.rem(index // bit, 2)


def flips(index, mask):
    for bit in (1, 2, 4):
        if mask & bit:
            index = flip(index, bit)
    return index


class Wire:
    def __init__(self, send_sem, recv_sem):
        self.r, self.f = lax.axis_index("replica"), lax.axis_index("fsdp")
        self.send_sem, self.recv_sem = send_sem, recv_sem
        self.used, self.sent = 0, []

    def meet(self, partners):
        barrier = pltpu.get_barrier_semaphore()
        for d_r, d_f in partners:
            pl.semaphore_signal(
                barrier, inc=1, device_id=self.at(d_r, d_f), device_id_type=MESH_ID
            )
        pl.semaphore_wait(barrier, len(partners))

    def at(self, d_r, d_f):
        return (flips(self.r, d_r), flips(self.f, d_f))

    def plan(self, src, dst, d_r, d_f):
        copy = pltpu.make_async_remote_copy(
            src_ref=src,
            dst_ref=dst,
            send_sem=self.send_sem.at[self.used],
            recv_sem=self.recv_sem.at[self.used],
            device_id=self.at(d_r, d_f),
            device_id_type=MESH_ID,
        )
        self.used += 1
        assert self.used <= self.send_sem.shape[0]
        return copy

    def send(self, src, dst, d_r, d_f):
        copy = self.plan(src, dst, d_r, d_f)
        copy.start()
        self.sent.append(copy)
        return copy

    def finish(self, waited=()):
        for copy in self.sent:
            if all(copy is not other for other in waited):
                copy.wait_send()


CUTS = 4
FRONT_SENDS = 2 * 28 + 7 + 7 * CUTS + 4 + 3
PARTNERS = ((1, 0), (2, 0), (0, 1), (0, 2), (0, 4), (0, 6))
ROWS = 64


def turn(v, cosine, sine):
    return v * cosine + pltpu.roll(v, HD // 2, 1) * sine


def front_kernel(
    tokens, seg_col, seg_row, routes, cos, sin,
    in_ref, out_ref, tiny_ref, mine_ref, other_ref, g_ref,
    qkv, attn, xn, first, lse, table, tiny_out, v,
    in_all, out_all, w_all, g_all, xs,
    in_v, out_v, tiny_v, rt, bias, w_buf, local_sem, send_sem, recv_sem,
):
    wire = Wire(send_sem, recv_sem)
    r, f = wire.r, wire.f
    shard = in_ref.shape[0]
    quarter = shard // 4
    length, width = tokens.shape
    experts = 8
    scale = HD ** (-0.5)

    def rows(j, k):
        at = flips(f, j) * shard + flips(r, k) * quarter
        return pl.ds(pl.multiple_of(at, quarter), quarter)

    def shard_rows(j):
        return pl.ds(pl.multiple_of(flips(f, j) * shard, shard), shard)

    def local(n, src, dst):
        copy = pltpu.make_async_copy(src, dst, local_sem.at[n])
        copy.start()
        return copy

    own_in = local(0, in_ref, in_v.at[shard_rows(0)])
    own_out = local(1, out_ref, out_v.at[shard_rows(0)])
    own_tiny = local(2, tiny_ref, tiny_v.at[f])
    own_w = local(3, mine_ref, w_buf)
    wire.meet(PARTNERS)

    own = pl.ds(pl.multiple_of(r * quarter, quarter), quarter)
    land = {"in": in_v, "out": out_v}
    source = {"in": in_ref, "out": out_ref}
    got, got_t, got_w, got_g, got_x = {}, {}, {}, {}, {}

    for m in (2, 4, 6, 1):
        got_t[m] = wire.send(tiny_ref, tiny_v.at[f], 0, m)

    def own_pieces(name):
        for m in (2, 4, 6, 1):
            got[name, m, 0] = wire.send(
                source[name].at[own], land[name].at[rows(0, 0)], 0, m
            )

    def pass_on(name, j, k, d_r, d_f):
        at = land[name].at[rows(j, k)]
        return wire.send(at, at, d_r, d_f)

    def near_pieces(name):
        for m in (1, 2, 4, 6):
            got[name, m, 0].wait_recv()
            if m != 1:
                got[name, m + 1, 0] = pass_on(name, m, 0, 0, 1)
            got[name, m, 2] = pass_on(name, m, 0, 2, 0)
            got[name, m, 1] = pass_on(name, m, 0, 1, 0)

    def far_pieces(name):
        for m in (3, 5, 7):
            got[name, m, 0].wait_recv()
            got[name, m, 2] = pass_on(name, m, 0, 2, 0)
            got[name, m, 1] = pass_on(name, m, 0, 1, 0)

    def side_pieces(name):
        for m in (1, 2, 4, 6, 3, 5, 7):
            got[name, m, 2].wait_recv()
            got[name, m, 3] = pass_on(name, m, 2, 1, 0)

    def all_pieces(name):
        for m in range(1, 8):
            got[name, m, 1].wait_recv()
            got[name, m, 3].wait_recv()

    own_pieces("in")
    own_pieces("out")
    own_w.wait()
    kept = [local(4, w_buf, w_all.at[shard_rows(0)])]

    for m in (2, 4, 6):
        got_t[m].wait_recv()
        at = tiny_v.at[flips(f, m)]
        got_t[m + 1] = wire.send(at, at, 0, 1)
    for m in (1, 3, 5, 7):
        got_t[m].wait_recv()
    own_tiny.wait()
    lanes = tiny_v.shape[2]
    rt[...] = jnp.zeros_like(rt)
    for z in range(4):
        both = tiny_v[2 * z].astype(f32) + tiny_v[2 * z + 1].astype(f32)
        tiny_out[:, z * lanes : (z + 1) * lanes] = both
        row = lax.broadcasted_iota(jnp.int32, both.shape, 0)
        rt[0:16, z * lanes : (z + 1) * lanes] = jnp.where(row < experts, both, 0.0).astype(bf16)

    def norm_one(c, carry):
        at = pl.ds(pl.multiple_of(c * ROWS, ROWS), ROWS)
        x = tokens[at, :].astype(f32)
        unit = x * lax.rsqrt(jnp.mean(x * x, axis=-1, keepdims=True) + epsilon)
        xn[at, :] = (unit * tiny_out[experts : experts + 1, :]).astype(bf16)
        return carry

    lax.fori_loop(0, length // ROWS, norm_one, 0)
    spot = lax.broadcasted_iota(jnp.int32, bias.shape, 0)
    keys_at = lax.broadcasted_iota(jnp.int32, bias.shape, 1)
    bias[...] = jnp.where((spot >= keys_at) & (seg_col[...] == seg_row[...]), 0.0, -1e30)

    cut = shard // CUTS

    def send_w(n, src, d_f):
        at = pl.ds(n * cut, cut)
        to = pl.ds(pl.multiple_of(f * shard + n * cut, cut), cut)
        return wire.send(src.at[at], w_all.at[to], 0, d_f)

    def pass_w(n, m):
        got_w[m, n].wait_recv()
        at = w_all.at[pl.ds(pl.multiple_of(flips(f, m) * shard + n * cut, cut), cut)]
        got_w[m + 1, n] = wire.send(at, at, 0, 1)

    near_pieces("in")
    for n in range(CUTS):
        for m, src in ((2, other_ref), (4, mine_ref), (6, other_ref)):
            got_w[m, n] = send_w(n, src, m)
    got_g[4] = wire.send(g_ref, g_all.at[4], 0, 2)
    got_g[1] = wire.send(g_ref, g_all.at[1], 1, 0)
    far_pieces("in")
    near_pieces("out")
    far_pieces("out")
    for n in range(CUTS):
        got_w[1, n] = send_w(n, mine_ref, 1)
    got_g[2] = wire.send(g_ref, g_all.at[2], 2, 0)
    side_pieces("in")
    own_in.wait()
    all_pieces("in")

    def project(c, carry):
        at = pl.multiple_of(c * 256, 256)
        t = matmul(xn[...], in_v[:, pl.ds(at, 256)])
        turned = c < 7
        for n in (0, 1):
            part = t[:, n * HD : (n + 1) * HD]
            part = turn(
                part, jnp.where(turned, cos[...], 1.0), jnp.where(turned, sin[...], 0.0)
            )
            qkv[:, pl.ds(at + n * HD, HD)] = part.astype(bf16)
        return carry

    lax.fori_loop(0, 8, project, 0)
    pass_w(0, 2)
    pass_w(0, 4)
    lane = lax.broadcasted_iota(jnp.int32, (length, HD), 1)
    lse[...] = jnp.zeros_like(lse)

    def head(h, carry):
        at = pl.ds(pl.multiple_of(h * HD, HD), HD)
        group = h // GROUP
        k_at = pl.ds(pl.multiple_of(WQ + group * HD, HD), HD)
        v_at = pl.ds(pl.multiple_of(WQ + WK + group * HD, HD), HD)
        s = contract_cols(qkv[:, at], qkv[:, k_at]) * scale + bias[...]
        highest = jnp.max(s, axis=-1, keepdims=True)
        expo = jnp.exp(s - highest)
        total = jnp.sum(expo, axis=-1, keepdims=True)
        p = (expo * (1.0 / total)).astype(bf16)
        attn[:, at] = matmul(p, qkv[:, v_at]).astype(bf16)
        lse[...] = jnp.where(lane == h, highest + jnp.log(total), lse[...])
        return carry

    lax.fori_loop(0, HQ // 2, head, 0)
    side_pieces("out")
    pass_w(0, 6)
    pass_w(1, 2)
    lax.fori_loop(HQ // 2, HQ, head, 0)
    pass_w(1, 4)
    pass_w(1, 6)
    own_out.wait()
    all_pieces("out")
    kept.append(local(5, in_v, in_all))
    kept.append(local(6, out_v, out_all))

    def add_out(c, carry):
        at = pl.ds(pl.multiple_of(c * 256, 256), 256)
        first[:, at] = tokens[:, at].astype(f32) + contract_cols(attn[...], out_v[at, :])
        return carry

    lax.fori_loop(0, width // 256, add_out, 0)

    def norm_two(c, carry):
        at = pl.ds(pl.multiple_of(c * ROWS, ROWS), ROWS)
        h = first[at, :]
        unit = h * lax.rsqrt(jnp.mean(h * h, axis=-1, keepdims=True) + epsilon)
        v[at, 0:width] = (unit * tiny_out[experts + 1 : experts + 2, :]).astype(bf16)
        return carry

    lax.fori_loop(0, length // ROWS, norm_two, 0)
    logits = contract_cols(v[:, 0:width], rt[...])
    chosen = lane == routes[:, 0:1]
    for j in range(1, routes.shape[1]):
        chosen = chosen | (lane == routes[:, j : j + 1])
    logits = jnp.where(chosen, logits, -1e30)
    expo = jnp.exp(logits - jnp.max(logits, axis=-1, keepdims=True))
    expo = jnp.where(chosen, expo, 0.0)
    gates = expo / jnp.sum(expo, axis=-1, keepdims=True)
    table[...] = gates
    high = gates.astype(bf16).astype(f32)
    v[:, width:] = (high + pltpu.roll(gates - high, experts, 1)).astype(bf16)

    got_x[2] = wire.send(v, xs.at[2], 2, 0)
    got_x[1] = wire.send(v, xs.at[1], 1, 0)
    for n in range(2, CUTS):
        for m in (2, 4, 6):
            pass_w(n, m)
    got_g[2].wait_recv()
    got_g[3] = wire.send(g_all.at[2], g_all.at[3], 1, 0)
    got_x[2].wait_recv()
    got_x[3] = wire.send(xs.at[2], xs.at[3], 1, 0)
    for n in range(CUTS):
        for m in (1, 3, 5, 7):
            got_w[m, n].wait_recv()
    for m in (1, 3, 4):
        got_g[m].wait_recv()
    for m in (1, 3):
        got_x[m].wait_recv()
    for copy in kept:
        copy.wait()
    wire.finish()


def front(tokens, seg_ids, routes, cos, sin, in_proj, out_proj, tiny, mine, other, grad):
    any_spec = pl.BlockSpec(memory_space=pl.ANY)
    vmem = pl.BlockSpec(memory_space=pltpu.VMEM)
    length, width = tokens.shape
    shard, cols = in_proj.shape
    whole = 8 * shard
    wide = width + EXTRA
    return pl.pallas_call(
        front_kernel,
        out_shape=[
            jax.ShapeDtypeStruct((length, cols), bf16),
            jax.ShapeDtypeStruct((length, WQ), bf16),
            jax.ShapeDtypeStruct((length, width), bf16),
            jax.ShapeDtypeStruct((length, width), f32),
            jax.ShapeDtypeStruct((length, HD), f32),
            jax.ShapeDtypeStruct((length, EXTRA), f32),
            jax.ShapeDtypeStruct((16, width), f32),
            jax.ShapeDtypeStruct((length, wide), bf16),
            jax.ShapeDtypeStruct((whole, cols), bf16),
            jax.ShapeDtypeStruct((whole, out_proj.shape[1]), bf16),
            jax.ShapeDtypeStruct((whole, mine.shape[1]), bf16),
            jax.ShapeDtypeStruct((5,) + grad.shape, bf16),
            jax.ShapeDtypeStruct((4, length, wide), bf16),
        ],
        in_specs=[vmem] * 6 + [any_spec] * 6,
        out_specs=[vmem] * 8 + [any_spec] * 5,
        scratch_shapes=[
            pltpu.VMEM((whole, cols), bf16),
            pltpu.VMEM((whole, out_proj.shape[1]), bf16),
            pltpu.VMEM((8,) + tiny.shape, bf16),
            pltpu.VMEM((EXTRA, width), bf16),
            pltpu.VMEM((length, length), f32),
            pltpu.VMEM(mine.shape, bf16),
            pltpu.SemaphoreType.DMA((8,)),
            pltpu.SemaphoreType.DMA((FRONT_SENDS,)),
            pltpu.SemaphoreType.DMA((FRONT_SENDS,)),
        ],
        compiler_params=pltpu.CompilerParams(
            collective_id=1, has_side_effects=True, vmem_limit_bytes=56 * MIB
        ),
        name="front",
    )(
        tokens, seg_ids.reshape(length, 1), seg_ids, routes, cos, sin,
        in_proj, out_proj, tiny, mine, other, grad,
    )


ORDER = (3, 2, 4, 5, 7, 6, 1, 0)
UNROLL = True
WIDE_COLS = 256
GROUP_AT = {2: (2, 0), 4: (0, 2), 6: (2, 2)}


def pick(step, table):
    value = jnp.int32(table[-1])
    for i, item in enumerate(table[:-1]):
        value = jnp.where(step == i, item, value)
    return value


def group_kernel(
    v_ref, g_ref, xs, g_all, w_ref,
    mix_sum, dx_own, dx_in, grads, x_late, g_late,
    wbuf, xbuf, gbuf, xt, gt_, hidg, dgu, deven, dodd, rc, meven, modd, mrc, acc, stage,
    sem_w, sem_x, sem_g, sem_m, sem_s, send_sem, recv_sem,
):
    wire = Wire(send_sem, recv_sem)
    r, f = wire.r, wire.f
    length, width = g_ref.shape
    hidden = w_ref.shape[1] // 3
    half = length // 2
    low, top = pl.ds(0, half), pl.ds(half, half)
    expert = 2 * r + lax.rem(f // 2, 2)
    step_cols = 256

    load_w = pltpu.make_async_copy(w_ref, wbuf, sem_w.at[0])
    load_w.start()

    def load(step):
        slot = lax.rem(step, 2)
        k = pick(step, ORDER)

        @pl.when(k == 0)
        def _():
            pltpu.make_async_copy(v_ref, xbuf.at[slot], sem_x.at[slot]).start()
            pltpu.make_async_copy(g_ref, gbuf.at[slot], sem_g.at[slot]).start()

        for table, src_x, src_g in (
            ((1, 2, 3), xs, g_all), ((4,), x_late, g_all), ((5, 6, 7), x_late, g_late)
        ):

            @pl.when((k >= table[0]) & (k <= table[-1]))
            def _():
                pltpu.make_async_copy(src_x.at[k], xbuf.at[slot], sem_x.at[slot]).start()
                pltpu.make_async_copy(src_g.at[k], gbuf.at[slot], sem_g.at[slot]).start()

    load(jnp.int32(0))
    wire.meet(PARTNERS_GROUP)
    late_x = {4: wire.send(v_ref, x_late.at[4], 0, 2)}
    far = [
        wire.send(g_all.at[4], g_late.at[6], 2, 0),
        wire.send(xs.at[2, top], x_late.at[6, top], 0, 2),
    ]
    late_g = {5: wire.send(g_all.at[4], g_late.at[5], 1, 0)}
    far.append(wire.plan(x_late.at[4, low], x_late.at[6, low], 2, 0))
    late_x[5] = wire.plan(x_late.at[4], x_late.at[5], 1, 0)
    late_x[7] = wire.plan(x_late.at[6], x_late.at[7], 1, 0)
    late_g[7] = wire.plan(g_late.at[6], g_late.at[7], 1, 0)
    slots = {2: 0, 4: 1, 6: 2, 0: 3}
    to_core = {k: wire.plan(dodd.at[n % 2], rc.at[n], 1, 0) for k, n in slots.items()}
    mix_core = {k: wire.plan(modd.at[n % 2], mrc.at[n], 1, 0) for k, n in slots.items()}
    back = {k: wire.plan(deven.at[k // 2], dx_in.at[k // 2 - 1], *GROUP_AT[k]) for k in (2, 4, 6)}
    acc[...] = jnp.zeros_like(acc)
    lane = lax.broadcasted_iota(jnp.int32, (length, EXTRA), 1)
    load_w.wait()

    def keep_mix(k):
        n = slots[k] % 2
        return pltpu.make_async_copy(meven.at[n], mix_sum.at[k // 2], sem_m.at[n])

    def send_core(k):
        to_core[k].start()
        mix_core[k].start()

    def sent_core(k):
        to_core[k].wait_send()
        mix_core[k].wait_send()

    def complete(k):
        n = slots[k]
        to_core[k].wait_recv()
        deven[k // 2] = (deven[k // 2].astype(f32) + rc[n].astype(f32)).astype(bf16)
        if k in (4, 6):
            back[k].start()
        mix_core[k].wait_recv()
        meven[n % 2] = (meven[n % 2].astype(f32) + mrc[n].astype(f32)).astype(bf16)
        keep_mix(k).start()

    def block(step, carry):
        slot = lax.rem(step, 2)

        @pl.when((step == 0) | (step >= 4) & (step < 7))
        def _():
            load(step + 1)

        pltpu.make_async_copy(v_ref, xbuf.at[slot], sem_x.at[slot]).wait()
        pltpu.make_async_copy(g_ref, gbuf.at[slot], sem_g.at[slot]).wait()
        extra = xbuf[slot, :, width:].astype(f32)
        mine = (lane == expert) | (lane == expert + 8)
        gate = jnp.sum(jnp.where(mine, extra, 0.0), axis=1, keepdims=True)
        here = pl.ds(pl.multiple_of(slot * length, length), length)
        xt[:, here] = xbuf[slot, :, :width].T
        gt_[:, here] = gbuf[slot].T

        def first(c, dgate):
            at = pl.multiple_of(c * step_cols, step_cols)
            u = matmul(xbuf[slot, :, :width], wbuf[:, pl.ds(at, step_cols)])
            up = matmul(xbuf[slot, :, :width], wbuf[:, pl.ds(hidden + at, step_cols)])
            rev = matmul(gbuf[slot], wbuf[:, pl.ds(2 * hidden + at, step_cols)])
            sig = 1.0 / (1.0 + jnp.exp(-u))
            act = u * sig
            hid = act * up
            hidg[here, pl.ds(at, step_cols)] = (gate * hid).astype(bf16)
            dgate = dgate + jnp.sum(rev * hid, axis=1, keepdims=True)
            dhid = gate * rev
            dgu[here, pl.ds(at, step_cols)] = (
                dhid * up * sig * (1.0 + u * (1.0 - sig))
            ).astype(bf16)
            dgu[here, pl.ds(hidden + at, step_cols)] = (dhid * act).astype(bf16)
            return dgate

        dgate = lax.fori_loop(
            0, hidden // step_cols, first, jnp.zeros((length, 1), f32), unroll=UNROLL
        )
        high = dgate.astype(bf16).astype(f32)
        rest = dgate - high
        tail = (
            jnp.where(lane == expert, high, 0.0) + jnp.where(lane == expert + 8, rest, 0.0)
        ).astype(bf16)

        def out_parts(dst_d, n_d, dst_m, n_m):
            def second(c, carry):
                at = pl.multiple_of(c * step_cols, step_cols)
                dst_d[n_d, :, pl.ds(at, step_cols)] = contract_cols(
                    dgu[here, :], wbuf[pl.ds(at, step_cols), pl.ds(0, 2 * hidden)]
                ).astype(bf16)
                dst_m[n_m, :, pl.ds(at, step_cols)] = contract_cols(
                    hidg[here, :], wbuf[pl.ds(at, step_cols), pl.ds(2 * hidden, hidden)]
                ).astype(bf16)
                return carry

            lax.fori_loop(0, width // step_cols, second, 0, unroll=UNROLL)
            dst_d[n_d, :, width:] = tail

        slot_two = pick(step, (0, 0, 1, 1, 0, 0, 1, 1))
        k = pick(step, ORDER)

        @pl.when(step == 4)
        def _():
            sent_core(2)

        @pl.when(step == 6)
        def _():
            sent_core(4)

        @pl.when(step == 5)
        def _():
            keep_mix(2).wait()

        @pl.when(step == 7)
        def _():
            keep_mix(4).wait()

        @pl.when(lax.rem(k, 2) == 1)
        def _():
            out_parts(dodd, slot_two, modd, slot_two)

        @pl.when(lax.rem(k, 2) == 0)
        def _():
            out_parts(deven, k // 2, meven, slot_two)

        def come_5():
            late_x[5].wait_recv()
            late_g[5].wait_recv()
            load(step + 1)

        def come_6():
            for copy in far:
                copy.wait_recv()
            late_x[7].start()
            late_g[7].start()

        for at_step, todo in (
            (0, (lambda: send_core(2),)),
            (1, (lambda: complete(2),)),
            (2, (come_5,)),
            (3, (lambda: send_core(4), come_6)),
            (4, (lambda: complete(4), lambda: send_core(6))),
            (5, (lambda: complete(6),)),
            (6, (lambda: send_core(0),)),
            (7, (lambda: complete(0),)),
        ):

            @pl.when(step == at_step)
            def _():
                for do in todo:
                    do()

        @pl.when(slot == 1)
        def _():
            def third(c, carry):
                at = pl.multiple_of(c * WIDE_COLS, WIDE_COLS)
                acc[:, pl.ds(at, WIDE_COLS)] += matmul(xt[...], dgu[:, pl.ds(at, WIDE_COLS)])
                return carry

            lax.fori_loop(0, 2 * hidden // WIDE_COLS, third, 0, unroll=UNROLL)

            def fourth(c, carry):
                at = pl.multiple_of(c * WIDE_COLS, WIDE_COLS)
                acc[:, pl.ds(2 * hidden + at, WIDE_COLS)] += matmul(
                    gt_[...], hidg[:, pl.ds(at, WIDE_COLS)]
                )
                return carry

            lax.fori_loop(0, hidden // WIDE_COLS, fourth, 0, unroll=UNROLL)

        @pl.when(step == 1)
        def _():
            late_x[4].wait_recv()
            late_x[5].start()
            far[2].start()
            back[2].start()
            load(step + 1)

        @pl.when(step == 3)
        def _():
            late_x[7].wait_recv()
            late_g[7].wait_recv()
            load(step + 1)

        return carry

    lax.fori_loop(0, 8, block, 0)
    keep = pltpu.make_async_copy(deven.at[0], dx_own, sem_w.at[0])
    keep.start()
    parts = 8
    rows = width // parts

    def out(j, slot):
        return pltpu.make_async_copy(
            stage.at[slot], grads.at[pl.ds(j * rows, rows)], sem_s.at[slot]
        )

    for j in range(parts):
        slot = j % 2
        if j >= 2:
            out(j - 2, slot).wait()
        stage[slot] = acc[j * rows : (j + 1) * rows].astype(bf16)
        out(j, slot).start()
    for j in range(parts - 2, parts):
        out(j, j % 2).wait()
    keep.wait()
    keep_mix(6).wait()
    keep_mix(0).wait()
    for k in (2, 4, 6):
        back[k].wait_recv()
        back[k].wait_send()
    sent_core(6)
    sent_core(0)
    for copy in (far[2], late_x[5], late_x[7], late_g[7]):
        copy.wait_send()
    wire.finish()


PARTNERS_GROUP = ((1, 0), (2, 0), (0, 2), (2, 2))
GROUP_SENDS = 8 + 8 + 3


def run_group(v, grad, xs, g_all, w):
    length, width = grad.shape
    wide = v.shape[1]
    cols = w.shape[1]
    hidden = cols // 3
    any_spec = pl.BlockSpec(memory_space=pl.ANY)
    return pl.pallas_call(
        group_kernel,
        out_shape=[
            jax.ShapeDtypeStruct((4, length, width), bf16),
            jax.ShapeDtypeStruct((length, wide), bf16),
            jax.ShapeDtypeStruct((3, length, wide), bf16),
            jax.ShapeDtypeStruct((width, cols), bf16),
            jax.ShapeDtypeStruct((8, length, wide), bf16),
            jax.ShapeDtypeStruct((8, length, width), bf16),
        ],
        in_specs=[any_spec] * 5,
        out_specs=[any_spec] * 6,
        scratch_shapes=[
            pltpu.VMEM((width, cols), bf16),
            pltpu.VMEM((2, length, wide), bf16),
            pltpu.VMEM((2, length, width), bf16),
            pltpu.VMEM((width, 2 * length), bf16),
            pltpu.VMEM((width, 2 * length), bf16),
            pltpu.VMEM((2 * length, hidden), bf16),
            pltpu.VMEM((2 * length, 2 * hidden), bf16),
            pltpu.VMEM((4, length, wide), bf16),
            pltpu.VMEM((2, length, wide), bf16),
            pltpu.VMEM((4, length, wide), bf16),
            pltpu.VMEM((2, length, width), bf16),
            pltpu.VMEM((2, length, width), bf16),
            pltpu.VMEM((4, length, width), bf16),
            pltpu.VMEM((width, cols), f32),
            pltpu.VMEM((2, width // 8, cols), bf16),
            pltpu.SemaphoreType.DMA((1,)),
            pltpu.SemaphoreType.DMA((2,)),
            pltpu.SemaphoreType.DMA((2,)),
            pltpu.SemaphoreType.DMA((2,)),
            pltpu.SemaphoreType.DMA((2,)),
            pltpu.SemaphoreType.DMA((GROUP_SENDS,)),
            pltpu.SemaphoreType.DMA((GROUP_SENDS,)),
        ],
        compiler_params=pltpu.CompilerParams(
            collective_id=2, has_side_effects=True, vmem_limit_bytes=62 * MIB
        ),
        cost_estimate=pl.CostEstimate(
            flops=48 * length * width * cols,
            bytes_accessed=64 * length * width + 4 * width * cols,
            transcendentals=8 * length * hidden,
        ),
        name="group",
    )(v, grad, xs, g_all, w)


PARTNERS_BACK = ((1, 0), (2, 0), (3, 0), (0, 1), (0, 2), (0, 4), (0, 6))
TERMS = 16
BACK_SENDS = 3 + 8 + 6 + 3 + 2 + 3 + 2 * 4 + 2 * 3 + 1 + 6 + 6


def back_kernel(
    dx_own, g_ref, first, table, tiny, v, tokens, qkv, lse, cos, sin, seg_col, seg_row,
    dx_in, grads, mix_sum, attn, xn, in_all, out_all,
    tokens_grad,
    g_out, mix_in, d_out, xn_core,
    in_v, out_v, mix_v, gl, gy, gz, act_v, aq_v, pq, wo, wi, wyo, wyi, wzo, wzi, wxo, own_d,
    dn, dxn, dl, dattn, dproj, dkv, bias, tbuf,
    local_sem, send_sem, recv_sem,
):
    wire = Wire(send_sem, recv_sem)
    r, f = wire.r, wire.f
    shard = gl.shape[1]
    length, width = tokens.shape
    experts = 8
    low = lax.rem(f // 2, 2)
    cols_p, cols_a = pq.shape[1], aq_v.shape[1]
    scale = HD ** (-0.5)
    used = [0]

    def local(src, dst):
        copy = pltpu.make_async_copy(src, dst, local_sem.at[used[0]])
        copy.start()
        used[0] += 1
        return copy

    def shard_rows(j):
        return pl.ds(pl.multiple_of(flips(f, j) * shard, shard), shard)

    def token_rows(k):
        return pl.ds(k * length, length)

    def part_of(k, cols):
        return pl.ds(pl.multiple_of(flips(r, k) * cols, cols), cols)

    def add(u, w):
        return (u.astype(f32) + w.astype(f32)).astype(bf16)

    half = lax.rem(r, 2)
    side = r // 2

    def half_of(index):
        return pl.ds(pl.multiple_of(index * cols_a, cols_a), cols_a)

    load_dx = [
        local(dx_in.at[n], in_v.at[token_rows(n), pl.ds(0, dx_in.shape[2])]) for n in range(3)
    ]
    load_out = local(out_all, out_v)
    load_g = {j: local(grads.at[shard_rows(j)], gl.at[j // 2]) for j in (4, 6, 2, 0)}
    load_a = local(attn.at[:, half_of(half)], aq_v.at[token_rows(0)])
    load_mix = local(mix_sum.at[2], mix_v.at[0])
    wire.meet(PARTNERS_BACK)
    got_y, got_m = {}, {}
    place_z = f // 2
    inner = (place_z == 1) | (place_z == 2)
    cut = shard // 2
    got_z = {}
    for j in (4, 6, 2, 0):
        for n in (0, 1):
            at = pl.ds(pl.multiple_of(flips(f, j + 1) * shard + n * cut, cut), cut)
            got_y[j, n] = wire.plan(grads.at[at], gy.at[j // 2, pl.ds(n * cut, cut)], 0, 1)
            wire.sent.append(got_y[j, n])
            if j:
                at = pl.ds(n * cut, cut)
                got_z[j, n] = wire.plan(gl.at[j // 2, at], gz.at[j // 2 - 1, at], 0, j)
                wire.sent.append(got_z[j, n])

    def by_place(do, outer_j, inner_j, n):
        @pl.when(inner)
        def _():
            do(inner_j, n)

        @pl.when(jnp.logical_not(inner))
        def _():
            do(outer_j, n)

    def send_y(j, n):
        got_y[j, n].start()

    for outer_j, inner_j in ((4, 2), (6, 4), (2, 6)):
        for n in (0, 1):
            by_place(send_y, outer_j, inner_j, n)
    for n in (0, 1):
        send_y(0, n)
    got_a = wire.send(attn.at[:, half_of(1 - half)], aq_v.at[token_rows(1)], 1, 0)
    got_m[6] = wire.send(mix_sum.at[3], mix_v.at[1], 2, 0)
    got_n = {2: wire.send(xn, act_v.at[token_rows(2)], 2, 0), 1: wire.send(xn, xn_core, 1, 0)}

    spot = lax.broadcasted_iota(jnp.int32, bias.shape, 0)
    keys_at = lax.broadcasted_iota(jnp.int32, bias.shape, 1)
    bias[...] = jnp.where((spot >= keys_at) & (seg_col[...] == seg_row[...]), 0.0, -1e30)
    tbuf[...] = jnp.zeros_like(tbuf)
    for copy in load_dx:
        copy.wait()

    def sum_dx(c, carry):
        at = pl.ds(pl.multiple_of(c * ROWS, ROWS), ROWS)
        d = dx_own[at, :].astype(f32)
        for n in range(3):
            here = pl.ds(pl.multiple_of(n * length + c * ROWS, ROWS), ROWS)
            d = d + in_v[here, 0 : dx_own.shape[1]].astype(f32)
        dn[at, :] = d[:, :width]
        dgate = d[:, width:]
        dgate = dgate + pltpu.roll(dgate, EXTRA - experts, 1)
        gates = table[at, :]
        mean = jnp.sum(gates * dgate, axis=-1, keepdims=True)
        dl[at, :] = (gates * (dgate - mean)).astype(bf16)
        return carry

    lax.fori_loop(0, length // ROWS, sum_dx, 0)
    load_in = local(in_all, in_v)
    dlt = dl[...].T[0:16]

    def add_router(c, carry):
        at = pl.ds(pl.multiple_of(c * 256, 256), 256)
        row = lax.broadcasted_iota(jnp.int32, (16, 256), 0)
        router = jnp.where(row < experts, tiny[:, at], 0.0).astype(bf16)
        dn[:, at] = dn[:, at] + matmul(dl[:, 0:16], router)
        tbuf[:, at] = matmul(dlt, v[:, at])
        return carry

    lax.fori_loop(0, width // 256, add_router, 0)

    def norm_two(c, gain):
        at = pl.ds(pl.multiple_of(c * ROWS, ROWS), ROWS)
        h = first[at, :]
        r2 = lax.rsqrt(jnp.mean(h * h, axis=-1, keepdims=True) + epsilon)
        unit = h * r2
        d = dn[at, :]
        gain = gain + jnp.sum(d * unit, axis=0, keepdims=True)
        d = d * tiny[experts + 1 : experts + 2, :]
        d = g_ref[at, :].astype(f32) + r2 * (
            d - unit * jnp.mean(d * unit, axis=-1, keepdims=True)
        )
        dn[at, :] = d
        act_v[at, :] = d.astype(bf16)
        return gain

    gain_two = lax.fori_loop(0, length // ROWS, norm_two, jnp.zeros((1, width), f32))
    tbuf[experts + 1 : experts + 2, :] = gain_two
    got_r = wire.send(act_v.at[token_rows(0)], act_v.at[token_rows(1)], 1, 0)
    def pass_y(j, n):
        if n == 0:
            load_g[j].wait()
        got_y[j, n].wait_recv()
        at = pl.ds(n * cut, cut)
        gl[j // 2, at] = add(gl[j // 2, at], gy[j // 2, at])
        got_z[j, n].start()

    def came(got_some, j):
        for n in (0, 1):
            got_some[j, n].wait_recv()

    load_out.wait()

    def to_attn(c, carry):
        at = pl.ds(pl.multiple_of(c * 256, 256), 256)
        dattn[:, at] = matmul(act_v[0:length, :], out_v[:, at]).astype(bf16)
        return carry

    lax.fori_loop(0, WQ // 256, to_attn, 0)
    by_place(pass_y, 4, 2, 0)
    lane = lax.broadcasted_iota(jnp.int32, (length, HD), 1)

    def turn_back(w):
        return w * cos[...] - pltpu.roll(w, HD // 2, 1) * sin[...]

    for group in range(KV):
        k_at = pl.ds(WQ + group * HD, HD)
        v_at = pl.ds(WQ + WK + group * HD, HD)
        dkv[...] = jnp.zeros_like(dkv)

        def head(i, carry):
            h = group * GROUP + i
            at = pl.ds(pl.multiple_of(h * HD, HD), HD)
            s = contract_cols(qkv[:, at], qkv[:, k_at]) * scale + bias[...]
            level = jnp.sum(jnp.where(lane == h, lse[...], 0.0), axis=1, keepdims=True)
            p = jnp.exp(s - level)
            da = dattn[:, at]
            dp = contract_cols(da, qkv[:, v_at])
            delta = jnp.sum(p * dp, axis=-1, keepdims=True)
            ds = (p * (dp - delta)).astype(bf16)
            dkv[1] += contract_rows(p.astype(bf16), da)
            dkv[0] += contract_rows(ds, qkv[:, at])
            dproj[:, at] = turn_back(matmul(ds, qkv[:, k_at]) * scale).astype(bf16)
            return carry

        lax.fori_loop(0, GROUP, head, 0)
        if group == 0:
            by_place(pass_y, 4, 2, 1)
            load_mix.wait()
            got_m[6].wait_recv()
            mix_v[0] = add(mix_v[0], mix_v[1])
            got_m[4] = wire.send(mix_v.at[0], mix_in.at[1], 0, 2)
        dproj[:, k_at] = turn_back(dkv[0] * scale).astype(bf16)
        dproj[:, v_at] = dkv[1].astype(bf16)

    keep_p = local(dproj.at[:, part_of(0, cols_p)], pq.at[token_rows(0)])
    got_p = {}
    for k in (2, 3, 1):
        got_p[k] = wire.send(dproj.at[:, part_of(k, cols_p)], pq.at[token_rows(k)], k, 0)

    got_m[2] = wire.send(mix_sum.at[1], mix_in.at[0], 2, 0)
    by_place(pass_y, 6, 4, 0)

    load_a.wait()
    got_a.wait_recv()
    got_r.wait_recv()

    def dense_out(c, carry):
        at = pl.ds(pl.multiple_of(c * 256, 256), 256)
        wo[at, :] = matmul(act_v[0 : 2 * length, at].T, aq_v[...]).astype(bf16)
        return carry

    lax.fori_loop(0, width // 256, dense_out, 0)
    got_r.wait_send()
    load_x = [local(xn, act_v.at[token_rows(0)])]
    got_n[1].wait_recv()
    load_x.append(local(xn_core, act_v.at[token_rows(1)]))
    got_wo, got_wi, got_wzo, got_wzi = {}, {}, {}, {}
    for j in (4, 6, 2, 0):
        got_wo[j] = wire.send(wo.at[shard_rows(j + 1)], wyo.at[j // 2], 0, 1)

    by_place(pass_y, 6, 4, 1)

    load_in.wait()

    def to_norm(c, carry):
        at = pl.ds(pl.multiple_of(c * 256, 256), 256)
        dxn[:, at] = contract_cols(dproj[...], in_v[at, :])
        return carry

    lax.fori_loop(0, width // 256, to_norm, 0)

    def norm_one(c, gain):
        at = pl.ds(pl.multiple_of(c * ROWS, ROWS), ROWS)
        x = tokens[at, :].astype(f32)
        r1 = lax.rsqrt(jnp.mean(x * x, axis=-1, keepdims=True) + epsilon)
        unit = x * r1
        d = dxn[at, :]
        gain = gain + jnp.sum(d * unit, axis=0, keepdims=True)
        d = d * tiny[experts : experts + 1, :]
        d = dn[at, :] + r1 * (d - unit * jnp.mean(d * unit, axis=-1, keepdims=True))
        tokens_grad[at, :] = d.astype(bf16)
        return gain

    gain_one = lax.fori_loop(0, length // ROWS, norm_one, jnp.zeros((1, width), f32))
    tbuf[experts : experts + 1, :] = gain_one

    by_place(pass_y, 2, 6, 0)
    by_place(pass_y, 2, 6, 1)
    mine, other = 2 * r + low, 2 * r + 1 - low
    load_g[0].wait()
    came(got_y, 0)
    came(got_z, 4)
    gl[0] = (gl[0].astype(f32) + gy[0].astype(f32) + gz[1].astype(f32)).astype(bf16)
    kept = [local(gl.at[0], g_out.at[mine])]
    got_e = {}

    got_n[2].wait_recv()
    got_n[3] = wire.send(act_v.at[token_rows(2)], act_v.at[token_rows(3)], 1, 0)
    keep_p.wait()
    for copy in load_x:
        copy.wait()
    for k in (1, 2, 3):
        got_p[k].wait_recv()
    got_n[3].wait_recv()
    got_e[2, 0] = wire.send(gl.at[0], g_out.at[mine], 2, 0)
    got_e[1, 0] = wire.send(gl.at[0], g_out.at[mine], 1, 0)

    tall = shard + TERMS

    def tall_rows(j):
        return pl.ds(pl.multiple_of(flips(f, j) * tall, TERMS), tall)

    for z in range(4):
        lanes = slice(2 * z * shard, 2 * (z + 1) * shard)
        both = matmul(act_v[:, lanes].T, pq[...]).astype(bf16)
        for y in (0, 1):
            top = (2 * z + y) * tall
            wi[top : top + shard, :] = both[y * shard : (y + 1) * shard]
            wi[top + shard : top + tall, :] = jnp.zeros((TERMS, cols_p), bf16)
            wi[top + shard : top + tall, 0 : 2 * shard] = tbuf[:, lanes].astype(bf16)
    for j in (4, 6, 2, 0):
        got_wi[j] = wire.send(wi.at[tall_rows(j + 1)], wyi.at[j // 2], 0, 1)
    for j in (4, 6, 2):
        got_wo[j].wait_recv()
        wyo[j // 2] = add(wo[shard_rows(j), :], wyo[j // 2])
        got_wzo[j] = wire.send(wyo.at[j // 2], wzo.at[j // 2 - 1], 0, j)

    came(got_z, 2)
    came(got_z, 6)
    gz[0] = add(gz[0], gz[2])
    kept.append(local(gz.at[0], g_out.at[other]))
    got_e[2, 1] = wire.send(gz.at[0], g_out.at[other], 2, 0)
    got_e[1, 1] = wire.send(gz.at[0], g_out.at[other], 1, 0)

    for j in (4, 6, 2):
        got_wi[j].wait_recv()
        wyi[j // 2] = add(wi[tall_rows(j), :], wyi[j // 2])
        got_wzi[j] = wire.send(wyi.at[j // 2], wzi.at[j // 2 - 1], 0, j)

    def own_rows(w, rows, y, z, got_w, got_zs):
        got_w[0].wait_recv()
        total = w[rows, :].astype(f32) + y[0].astype(f32)
        for j in (2, 4, 6):
            got_zs[j].wait_recv()
            total = total + z[j // 2 - 1].astype(f32)
        return total

    wxo[0] = own_rows(wo, shard_rows(0), wyo, wzo, got_wo, got_wzo).astype(bf16)
    quarter = cols_a // 2

    def quarter_of(index):
        return pl.ds(pl.multiple_of(index * quarter, quarter), quarter)

    got_x = wire.send(
        wxo.at[0, :, quarter_of(1 - side)], wxo.at[1, :, pl.ds(0, quarter)], 2, 0
    )
    got_x.wait_recv()
    own_d[shard:, cols_p:] = jnp.zeros((TERMS, quarter), bf16)
    own_d[0:shard, cols_p:] = add(wxo[0, :, quarter_of(side)], wxo[1, :, 0:quarter])
    got_d = {}

    def send_d(n, columns):
        kept.append(local(own_d.at[:, columns], d_out.at[r, :, columns]))
        for k in (2, 1):
            got_d[k, n] = wire.send(own_d.at[:, columns], d_out.at[r, :, columns], k, 0)

    parts_d = (pl.ds(cols_p, quarter), pl.ds(0, cols_p))
    send_d(0, parts_d[0])
    own_d[:, 0:cols_p] = own_rows(wi, tall_rows(0), wyi, wzi, got_wi, got_wzi).astype(bf16)
    send_d(1, parts_d[1])

    far = flips(r, 2)
    for n, e in ((0, 2 * far + low), (1, 2 * far + 1 - low)):
        got_e[2, n].wait_recv()
        got_e[3, n] = wire.send(g_out.at[e], g_out.at[e], 1, 0)
    for n, columns in enumerate(parts_d):
        got_d[2, n].wait_recv()
        at = d_out.at[far, :, columns]
        got_d[3, n] = wire.send(at, at, 1, 0)
    for k in (1, 3):
        for n in (0, 1):
            got_e[k, n].wait_recv()
    for k in (1, 3):
        for n in (0, 1):
            got_d[k, n].wait_recv()
    for k in (2, 4):
        got_m[k].wait_recv()
    for copy in kept:
        copy.wait()
    wire.finish((got_r,))


def run_back(
    dx_own, grad, first, table, tiny, v, tokens, qkv, lse, cos, sin, seg_ids,
    dx_in, grads, mix_sum, attn, xn, in_all, out_all,
):
    any_spec = pl.BlockSpec(memory_space=pl.ANY)
    vmem = pl.BlockSpec(memory_space=pltpu.VMEM)
    length, width = tokens.shape
    shard = width // 8
    cols = grads.shape[1]
    cols_p, cols_a = qkv.shape[1] // 4, attn.shape[1] // 2
    return pl.pallas_call(
        back_kernel,
        out_shape=[
            jax.ShapeDtypeStruct((length, width), bf16),
            jax.ShapeDtypeStruct((8, shard, cols), bf16),
            jax.ShapeDtypeStruct((2, length, width), bf16),
            jax.ShapeDtypeStruct((4, shard + TERMS, cols_p + cols_a // 2), bf16),
            jax.ShapeDtypeStruct((length, width), bf16),
        ],
        in_specs=[vmem] * 13 + [any_spec] * 7,
        out_specs=[vmem] + [any_spec] * 4,
        scratch_shapes=[
            pltpu.VMEM(in_all.shape, bf16),
            pltpu.VMEM(out_all.shape, bf16),
            pltpu.VMEM((2, length, width), bf16),
            pltpu.VMEM((4, shard, cols), bf16),
            pltpu.VMEM((4, shard, cols), bf16),
            pltpu.VMEM((3, shard, cols), bf16),
            pltpu.VMEM((4 * length, width), bf16),
            pltpu.VMEM((2 * length, cols_a), bf16),
            pltpu.VMEM((4 * length, cols_p), bf16),
            pltpu.VMEM((width, cols_a), bf16),
            pltpu.VMEM((width + 8 * TERMS, cols_p), bf16),
            pltpu.VMEM((4, shard, cols_a), bf16),
            pltpu.VMEM((4, shard + TERMS, cols_p), bf16),
            pltpu.VMEM((3, shard, cols_a), bf16),
            pltpu.VMEM((3, shard + TERMS, cols_p), bf16),
            pltpu.VMEM((2, shard, cols_a), bf16),
            pltpu.VMEM((shard + TERMS, cols_p + cols_a // 2), bf16),
            pltpu.VMEM((length, width), f32),
            pltpu.VMEM((length, width), f32),
            pltpu.VMEM((length, EXTRA), bf16),
            pltpu.VMEM((length, WQ), bf16),
            pltpu.VMEM(qkv.shape, bf16),
            pltpu.VMEM((2, length, HD), f32),
            pltpu.VMEM((length, length), f32),
            pltpu.VMEM((TERMS, width), f32),
            pltpu.SemaphoreType.DMA((20,)),
            pltpu.SemaphoreType.DMA((BACK_SENDS,)),
            pltpu.SemaphoreType.DMA((BACK_SENDS,)),
        ],
        compiler_params=pltpu.CompilerParams(
            collective_id=3, has_side_effects=True, vmem_limit_bytes=62 * MIB
        ),
        name="back",
    )(
        dx_own, grad, first, table, tiny, v, tokens, qkv, lse, cos, sin,
        seg_ids.reshape(length, 1), seg_ids,
        dx_in, grads, mix_sum, attn, xn, in_all, out_all,
    )


def finish_kernel(sums, dense, first, own, parts, e_in, e_out, in_grad, out_grad, mixed):
    split = e_in.shape[2]
    for c in range(0, sums.shape[2], 128):
        part = jnp.swapaxes(sums[:, :, c : c + 128].astype(f32), 0, 1)
        if c < split:
            e_in[:, :, c : c + 128] = part
        else:
            e_out[:, :, c - split : c - split + 128] = part
    cut = in_grad.shape[1] // 4
    quarter = out_grad.shape[1] // 4
    for r in range(4):
        in_grad[:, r * cut : (r + 1) * cut] = dense[r, :, :cut].astype(f32)
        place = 2 * (r % 2) + r // 2
        out_grad[:, place * quarter : (place + 1) * quarter] = dense[r, :, cut:].astype(f32)
    total = first[...] + own[0].astype(f32)
    for n in range(parts.shape[0]):
        total = total + parts[n].astype(f32)
    mixed[...] = total.astype(bf16)


def run_finish(expert_sum, dense, first, mix_sum, mix_in, hidden):
    n_experts, shard, cols = expert_sum.shape
    length, width = first.shape
    steps = 6
    rows, tokens = shard // steps, length // steps
    cut = dense.shape[2] - width // 4
    return pl.pallas_call(
        finish_kernel,
        grid=(steps,),
        out_shape=[
            jax.ShapeDtypeStruct((shard, n_experts, 2 * hidden), f32),
            jax.ShapeDtypeStruct((shard, n_experts, hidden), f32),
            jax.ShapeDtypeStruct((shard, 4 * cut), f32),
            jax.ShapeDtypeStruct((shard, width), f32),
            jax.ShapeDtypeStruct((length, width), bf16),
        ],
        in_specs=[
            pl.BlockSpec((n_experts, rows, cols), lambda i: (0, i, 0)),
            pl.BlockSpec((4, rows, dense.shape[2]), lambda i: (0, i, 0)),
            pl.BlockSpec((tokens, width), lambda i: (i, 0)),
            pl.BlockSpec((1, tokens, width), lambda i: (0, i, 0)),
            pl.BlockSpec((mix_in.shape[0], tokens, width), lambda i: (0, i, 0)),
        ],
        out_specs=[
            pl.BlockSpec((rows, n_experts, 2 * hidden), lambda i: (i, 0, 0)),
            pl.BlockSpec((rows, n_experts, hidden), lambda i: (i, 0, 0)),
            pl.BlockSpec((rows, 4 * cut), lambda i: (i, 0)),
            pl.BlockSpec((rows, width), lambda i: (i, 0)),
            pl.BlockSpec((tokens, width), lambda i: (i, 0)),
        ],
        compiler_params=pltpu.CompilerParams(vmem_limit_bytes=48 * MIB),
        name="finish",
    )(expert_sum, dense, first, mix_sum, mix_in)


def near_layer(
    tokens, seg_ids, routes, in_proj, out_proj, router, norm_gains, expert_in, expert_out,
    out_grad,
):
    length, width = tokens.shape
    experts = router.shape[1]
    hidden = expert_out.shape[2]
    shard = router.shape[0]
    r, f = lax.axis_index("replica"), lax.axis_index("fsdp")
    cosine, sine = [t[:, 0] for t in tables(length)]
    cos = jnp.concatenate([cosine, cosine], axis=1)
    sin = jnp.concatenate([-sine, sine], axis=1)
    tiny = jnp.concatenate(
        [router.T, norm_gains.T, jnp.zeros((16 - experts - 2, shard), bf16)], axis=0
    )
    none = jnp.zeros_like(tiny)
    tiny = jnp.where(
        f % 2 == 0,
        jnp.concatenate([tiny, none], axis=1),
        jnp.concatenate([none, tiny], axis=1),
    )
    low = (f >> 1) & 1
    mine, other = [
        jnp.concatenate(
            [
                lax.dynamic_index_in_dim(expert_in, e, 1, keepdims=False),
                lax.dynamic_index_in_dim(expert_out, e, 1, keepdims=False),
            ],
            axis=1,
        )
        for e in (2 * r + low, 2 * r + 1 - low)
    ]
    qkv, attn, xn, first, lse, table, small, v, in_all, out_all, w_all, g_all, xs = front(
        tokens, seg_ids, routes, cos, sin, in_proj, out_proj, tiny, mine, other, out_grad
    )
    mix_sum, dx_own, dx_in, grads, _, _ = run_group(v, out_grad, xs, g_all, w_all)
    tokens_grad, expert_sum, mix_in, dense, _ = run_back(
        dx_own, out_grad, first, table, small, v, tokens, qkv, lse, cos, sin, seg_ids,
        dx_in, grads, mix_sum, attn, xn, in_all, out_all,
    )
    e_in, e_out, in_grad, out_proj_grad, mixed = run_finish(
        expert_sum, dense, first, mix_sum, mix_in, hidden
    )
    terms = jnp.sum(dense[:, shard:, : 2 * shard].astype(f32), axis=0)
    terms = jnp.where(f % 2 == 0, terms[:, :shard], terms[:, shard:]).T
    return (
        mixed,
        tokens_grad,
        in_grad,
        out_proj_grad,
        terms[:, :experts],
        terms[:, experts : experts + 2],
        e_in,
        e_out,
    )


class Wide:
    def __init__(self, n_rep, n_fsdp):
        self.n_rep, self.n_fsdp = n_rep, n_fsdp

    def spread(self, value):
        every = lax.all_gather(value, "replica", axis=0)
        return [every[k] for k in range(self.n_rep)]

    def collect(self, parts):
        return lax.psum_scatter(jnp.stack(parts), "replica", scatter_dimension=0).astype(f32)

    def start(self, in_proj, out_proj, tiny, expert_in, expert_out, grad):
        r = lax.axis_index("replica")
        per = expert_in.shape[1] // self.n_rep
        weights = []
        for i in range(per):
            both = jnp.concatenate(
                [
                    lax.dynamic_index_in_dim(expert_in, per * r + i, 1, keepdims=False),
                    lax.dynamic_index_in_dim(expert_out, per * r + i, 1, keepdims=False),
                ],
                axis=1,
            )
            weights.append(lax.all_gather(both, "fsdp", axis=0, tiled=True))
        return (
            lax.all_gather(in_proj, "fsdp", axis=0, tiled=True),
            lax.all_gather(out_proj, "fsdp", axis=0, tiled=True),
            lax.all_gather(tiny, "fsdp", axis=1, tiled=True),
            (weights, self.spread(grad)),
        )

    def experts(self, payload, held):
        weights, gs = held
        xs = self.spread(payload)
        per = len(weights)
        mixes, dxs, grads = None, None, []
        for i, w in enumerate(weights):

            def expert_of(i=i):
                return per * lax.axis_index("replica") + i

            mix, dx, grad = run_expert(xs, gs, [w], expert_of, lambda j: 0)
            mixes = mix if mixes is None else [a + b for a, b in zip(mixes, mix)]
            dxs = dx if dxs is None else [a + b for a, b in zip(dxs, dx)]
            grads.append(grad[0])
        return self.collect(dxs), (mixes, grads)

    def trade(self, value):
        cut = value.reshape(value.shape[0], self.n_rep, -1).transpose(1, 0, 2)
        got = lax.all_to_all(cut, "replica", 0, 0)
        return got.reshape(-1, got.shape[2])

    def end(self, held, first, normed, attn, dres, dproj, terms):
        mixes, grads = held
        mixed = first + self.collect(mixes)
        own = jnp.stack(
            [lax.psum_scatter(g, "fsdp", scatter_dimension=0, tiled=True) for g in grads]
        )
        expert_sum = lax.all_gather(own, "replica", axis=0, tiled=True).transpose(1, 0, 2)
        dense = []
        for left, right in ((normed, dproj), (dres, attn)):
            left = lax.all_gather(left, "replica", axis=0, tiled=True)
            part = contract_rows(left, self.trade(right)).astype(bf16)
            own = lax.psum_scatter(part, "fsdp", scatter_dimension=0, tiled=True)
            dense.append(lax.all_gather(own, "replica", axis=1, tiled=True))
        return mixed, dense[0], dense[1], expert_sum, lax.psum(terms, ("replica", "fsdp"))


def layer(
    net, tokens, seg_ids, routes, in_proj, out_proj, router, norm_gains, expert_in, expert_out,
    out_grad,
):
    length, width = tokens.shape
    experts = router.shape[1]
    hidden = expert_out.shape[2]
    shard = router.shape[0]
    scale = HD ** (-0.5)
    cosine, sine = tables(length)
    segment = seg_ids[0]
    place = jnp.arange(length)
    allowed = ((place[:, None] >= place[None, :]) & (segment[:, None] == segment[None, :]))[
        None, None
    ]
    tiny = jnp.concatenate(
        [router.T, norm_gains.T, jnp.zeros((16 - experts - 2, shard), bf16)], axis=0
    )
    proj_in, proj_out, tiny, held = net.start(
        in_proj, out_proj, tiny, expert_in, expert_out, out_grad
    )
    router_rows = tiny[:experts]
    gain_one = tiny[experts].astype(f32)
    gain_two = tiny[experts + 1].astype(f32)

    inputs = tokens.astype(f32)
    scale_one = rms_scale(inputs)
    unit_one = inputs * scale_one
    normed = (unit_one * gain_one).astype(bf16)
    proj = matmul(normed, proj_in)
    queries = (
        rotate(proj[:, :WQ].reshape(length, HQ, HD), cosine, sine)
        .astype(bf16)
        .reshape(length, KV, GROUP, HD)
    )
    keys = rotate(proj[:, WQ : WQ + WK].reshape(length, KV, HD), cosine, sine).astype(bf16)
    values = proj[:, WQ + WK :].reshape(length, KV, HD).astype(bf16)
    scores = jnp.einsum("qkgd,tkd->kgqt", queries, keys, preferred_element_type=f32) * scale
    masked = jnp.where(allowed, scores, -1e30)
    highest = jnp.max(masked, axis=-1, keepdims=True)
    expo = jnp.exp(masked - highest)
    total = jnp.sum(expo, axis=-1, keepdims=True)
    log_total = highest + jnp.log(total)
    probs_low = (expo / total).astype(bf16)
    attn = jnp.einsum("kgqt,tkd->qkgd", probs_low, values, preferred_element_type=f32)
    attn = attn.astype(bf16).reshape(length, WQ)
    first = inputs + contract_cols(attn, proj_out)
    scale_two = rms_scale(first)
    unit_two = first * scale_two
    normed_two = (unit_two * gain_two).astype(bf16)
    logits = contract_cols(normed_two, router_rows)
    onehot = (routes[:, :, None] == jnp.arange(experts)[None, None, :]).astype(f32)
    chosen = jnp.sum(onehot * logits[:, None, :], axis=-1)
    gates = jax.nn.softmax(chosen, axis=-1)
    table = jnp.sum(gates[:, :, None] * onehot, axis=1)
    high = table.astype(bf16)
    low = (table - high.astype(f32)).astype(bf16)
    payload = jnp.concatenate(
        [normed_two, high, low, jnp.zeros((length, EXTRA - 2 * experts), bf16)], axis=1
    )
    dx, held = net.experts(payload, held)

    grad_out = out_grad.astype(f32)
    dgate_all = dx[:, width : width + experts] + dx[:, width + experts : width + 2 * experts]
    dgate = jnp.sum(onehot * dgate_all[:, None, :], axis=-1)
    dchosen = gates * (dgate - jnp.sum(gates * dgate, axis=-1, keepdims=True))
    dlogits = jnp.sum(dchosen[:, :, None] * onehot, axis=1).astype(bf16)
    dnormed_two = dx[:, :width] + matmul(dlogits, router_rows)
    gain_two_grad = jnp.sum(dnormed_two * unit_two, axis=0)
    dunit_two = dnormed_two * gain_two
    dfirst = grad_out + scale_two * (
        dunit_two - unit_two * jnp.mean(dunit_two * unit_two, axis=-1, keepdims=True)
    )
    dres = dfirst.astype(bf16)
    dattn = matmul(dres, proj_out).astype(bf16).reshape(length, KV, GROUP, HD)
    probs = jnp.exp(masked - log_total)
    probs_again = probs.astype(bf16)
    dprobs = jnp.einsum("qkgd,tkd->kgqt", dattn, values, preferred_element_type=f32)
    dvalues = jnp.einsum("kgqt,qkgd->tkd", probs_again, dattn, preferred_element_type=f32)
    delta = jnp.sum(probs * dprobs, axis=-1, keepdims=True)
    dscores = (probs * (dprobs - delta)).astype(bf16)
    dqueries = jnp.einsum("kgqt,tkd->qkgd", dscores, keys, preferred_element_type=f32) * scale
    dkeys = jnp.einsum("kgqt,qkgd->tkd", dscores, queries, preferred_element_type=f32) * scale
    dqueries = rotate(dqueries.reshape(length, HQ, HD), cosine, -sine).reshape(length, WQ)
    dkeys = rotate(dkeys, cosine, -sine).reshape(length, WK)
    dproj = jnp.concatenate([dqueries, dkeys, dvalues.reshape(length, WK)], axis=1).astype(bf16)
    dnormed = contract_cols(dproj, proj_in)
    gain_one_grad = jnp.sum(dnormed * unit_one, axis=0)
    dunit_one = dnormed * gain_one
    tokens_grad = (
        dfirst
        + scale_one
        * (dunit_one - unit_one * jnp.mean(dunit_one * unit_one, axis=-1, keepdims=True))
    ).astype(bf16)

    terms = jnp.concatenate(
        [
            contract_rows(dlogits, normed_two),
            gain_one_grad[None],
            gain_two_grad[None],
            jnp.zeros((16 - experts - 2, width), f32),
        ],
        axis=0,
    )
    mixed, in_proj_grad, out_proj_grad, expert_sum, terms = net.end(
        held, first, normed, attn, dres, dproj, terms
    )
    terms = lax.dynamic_slice_in_dim(terms, lax.axis_index("fsdp") * shard, shard, 1).T
    return (
        mixed.astype(bf16),
        tokens_grad,
        in_proj_grad.astype(f32),
        out_proj_grad.astype(f32),
        terms[:, :experts],
        terms[:, experts : experts + 2],
        expert_sum[..., : 2 * hidden].astype(f32),
        expert_sum[..., 2 * hidden :].astype(f32),
    )


def solution(mesh):
    n_rep, n_fsdp = mesh.shape["replica"], mesh.shape["fsdp"]
    if (n_rep, n_fsdp) == (4, 8):
        body = near_layer
    else:
        body = functools.partial(layer, Wide(n_rep, n_fsdp))
    both = P(("replica", "fsdp"), None)
    fsdp, deep = P("fsdp", None), P("fsdp", None, None)
    return jax.shard_map(
        body,
        mesh=mesh,
        in_specs=(both, both, both, fsdp, fsdp, fsdp, fsdp, deep, deep, both),
        out_specs=(both, both, fsdp, fsdp, fsdp, fsdp, deep, deep),
        check_vma=False,
    )
```

```python
import functools

import jax
import jax.numpy as jnp
from jax import lax
from jax.experimental import pallas as pl
from jax.experimental.pallas import tpu as pltpu
from jax.sharding import PartitionSpec as P

HQ = 12
KV = 2
HD = 128
GROUP = HQ // KV
WQ = HQ * HD
WK = KV * HD
EXTRA = 128
MIB = 1024 * 1024

epsilon = 1e-06
rope_base = 1000000.0
bf16 = jnp.bfloat16
f32 = jnp.float32


def rms_scale(v):
    return lax.rsqrt(jnp.mean(v * v, axis=-1, keepdims=True) + epsilon)


def tables(length):
    half = HD // 2
    freq = jnp.power(rope_base, -(jnp.arange(half, dtype=f32) * 2.0 / HD))
    angle = jnp.arange(length, dtype=f32)[:, None] * freq[None, :]
    return (jnp.cos(angle)[:, None, :], jnp.sin(angle)[:, None, :])


def rotate(v, cosine, sine):
    half = v.shape[-1] // 2
    first = v[..., :half]
    second = v[..., half:]
    return jnp.concatenate(
        [first * cosine - second * sine, second * cosine + first * sine], axis=-1
    )


def contract_rows(left, right):
    return lax.dot_general(left, right, (((0,), (0,)), ((), ())), preferred_element_type=f32)


def contract_cols(left, right):
    return lax.dot_general(left, right, (((1,), (1,)), ((), ())), preferred_element_type=f32)


def matmul(left, right):
    return lax.dot_general(left, right, (((1,), (0,)), ((), ())), preferred_element_type=f32)


def expert_kernel(nt, nw, length, width, hidden, rows, expert_of, offset_of, *refs):
    xs, gs, ws = refs[:nt], refs[nt : 2 * nt], refs[2 * nt : 2 * nt + nw]
    refs = refs[2 * nt + nw :]
    mixes, dxs, grads = refs[:nt], refs[nt : 2 * nt], refs[2 * nt : 2 * nt + nw]
    (
        wbuf, xbuf, gbuf, xt, gt_, hidg, dgu, mbuf, dbuf, acc, stage,
        sem_w, sem_x, sem_g, sem_m, sem_d, sem_s,
    ) = refs[2 * nt + nw :]
    cols = 3 * hidden
    step_cols = 256

    def load(k, slot):
        for i in range(nt):

            @pl.when(k == i)
            def _():
                pltpu.make_async_copy(xs[i], xbuf.at[slot], sem_x.at[slot]).start()
                pltpu.make_async_copy(gs[i], gbuf.at[slot], sem_g.at[slot]).start()

    def store(k, slot):
        for i in range(nt):

            @pl.when(k == i)
            def _():
                pltpu.make_async_copy(mbuf.at[slot], mixes[i], sem_m.at[slot]).start()
                pltpu.make_async_copy(dbuf.at[slot], dxs[i], sem_d.at[slot]).start()

    def stored(slot):
        pltpu.make_async_copy(mbuf.at[slot], mixes[0], sem_m.at[slot]).wait()
        pltpu.make_async_copy(dbuf.at[slot], dxs[0], sem_d.at[slot]).wait()

    for j in range(nw):
        pltpu.make_async_copy(
            ws[j], wbuf.at[pl.ds(pl.multiple_of(offset_of(j), 8), rows)], sem_w.at[j]
        ).start()
    load(0, 0)
    expert = expert_of()
    acc[...] = jnp.zeros_like(acc)
    lane = lax.broadcasted_iota(jnp.int32, (length, EXTRA), 1)
    for j in range(nw):
        pltpu.make_async_copy(
            ws[j], wbuf.at[pl.ds(pl.multiple_of(offset_of(j), 8), rows)], sem_w.at[j]
        ).wait()

    def block(k, carry):
        slot = lax.rem(k, 2)

        @pl.when(k + 1 < nt)
        def _():
            load(k + 1, 1 - slot)

        pltpu.make_async_copy(xs[0], xbuf.at[slot], sem_x.at[slot]).wait()
        pltpu.make_async_copy(gs[0], gbuf.at[slot], sem_g.at[slot]).wait()

        @pl.when(k >= 2)
        def _():
            stored(slot)

        extra = xbuf[slot, :, width:].astype(f32)
        mine = (lane == expert) | (lane == expert + 8)
        gate = jnp.sum(jnp.where(mine, extra, 0.0), axis=1, keepdims=True)
        xt[...] = xbuf[slot, :, :width].T
        gt_[...] = gbuf[slot].T

        def first(c, dgate):
            at = pl.multiple_of(c * step_cols, step_cols)
            u = matmul(xbuf[slot, :, :width], wbuf[:, pl.ds(at, step_cols)])
            up = matmul(xbuf[slot, :, :width], wbuf[:, pl.ds(hidden + at, step_cols)])
            back = matmul(gbuf[slot], wbuf[:, pl.ds(2 * hidden + at, step_cols)])
            sig = 1.0 / (1.0 + jnp.exp(-u))
            act = u * sig
            hid = act * up
            hidg[:, pl.ds(at, step_cols)] = (gate * hid).astype(bf16)
            dgate = dgate + jnp.sum(back * hid, axis=1, keepdims=True)
            dhid = gate * back
            dgu[:, pl.ds(at, step_cols)] = (
                dhid * up * sig * (1.0 + u * (1.0 - sig))
            ).astype(bf16)
            dgu[:, pl.ds(hidden + at, step_cols)] = (dhid * act).astype(bf16)
            return dgate

        dgate = lax.fori_loop(
            0, hidden // step_cols, first, jnp.zeros((length, 1), f32)
        )

        def second(c, carry):
            at = pl.multiple_of(c * step_cols, step_cols)
            mbuf[slot, :, pl.ds(at, step_cols)] = contract_cols(
                hidg[...], wbuf[pl.ds(at, step_cols), pl.ds(2 * hidden, hidden)]
            ).astype(bf16)
            dbuf[slot, :, pl.ds(at, step_cols)] = contract_cols(
                dgu[...], wbuf[pl.ds(at, step_cols), pl.ds(0, 2 * hidden)]
            ).astype(bf16)
            return carry

        lax.fori_loop(0, width // step_cols, second, 0)
        high = dgate.astype(bf16).astype(f32)
        low = dgate - high
        dbuf[slot, :, width:] = (
            jnp.where(lane == expert, high, 0.0) + jnp.where(lane == expert + 8, low, 0.0)
        ).astype(bf16)
        store(k, slot)

        def third(c, carry):
            at = pl.multiple_of(c * step_cols, step_cols)
            acc[:, pl.ds(at, step_cols)] += matmul(xt[...], dgu[:, pl.ds(at, step_cols)])
            return carry

        lax.fori_loop(0, 2 * hidden // step_cols, third, 0)

        def fourth(c, carry):
            at = pl.multiple_of(c * step_cols, step_cols)
            acc[:, pl.ds(2 * hidden + at, step_cols)] += matmul(
                gt_[...], hidg[:, pl.ds(at, step_cols)]
            )
            return carry

        lax.fori_loop(0, hidden // step_cols, fourth, 0)
        return carry

    lax.fori_loop(0, nt, block, 0)
    stored(0)
    stored(1)
    for j in range(nw):
        slot = j % 2
        if j >= 2:
            pltpu.make_async_copy(stage.at[slot], grads[j - 2], sem_s.at[slot]).wait()
        stage[slot] = acc[pl.ds(pl.multiple_of(offset_of(j), 8), rows)].astype(bf16)
        pltpu.make_async_copy(stage.at[slot], grads[j], sem_s.at[slot]).start()
    for j in range(max(0, nw - 2), nw):
        pltpu.make_async_copy(stage.at[j % 2], grads[j], sem_s.at[j % 2]).wait()


def run_expert(xs, gs, ws, expert_of, offset_of):
    nt, nw = len(xs), len(ws)
    length, width = gs[0].shape
    rows, cols = ws[0].shape
    hidden = cols // 3
    outs = (
        [jax.ShapeDtypeStruct((length, width), bf16)] * nt
        + [jax.ShapeDtypeStruct((length, width + EXTRA), bf16)] * nt
        + [jax.ShapeDtypeStruct((rows, cols), bf16)] * nw
    )
    any_spec = pl.BlockSpec(memory_space=pl.ANY)
    result = pl.pallas_call(
        functools.partial(
            expert_kernel, nt, nw, length, width, hidden, rows, expert_of, offset_of
        ),
        out_shape=outs,
        in_specs=[any_spec] * (2 * nt + nw),
        out_specs=[any_spec] * len(outs),
        scratch_shapes=[
            pltpu.VMEM((width, cols), bf16),
            pltpu.VMEM((2, length, width + EXTRA), bf16),
            pltpu.VMEM((2, length, width), bf16),
            pltpu.VMEM((width, length), bf16),
            pltpu.VMEM((width, length), bf16),
            pltpu.VMEM((length, hidden), bf16),
            pltpu.VMEM((length, 2 * hidden), bf16),
            pltpu.VMEM((2, length, width), bf16),
            pltpu.VMEM((2, length, width + EXTRA), bf16),
            pltpu.VMEM((width, cols), f32),
            pltpu.VMEM((2, rows, cols), bf16),
            pltpu.SemaphoreType.DMA((nw,)),
            pltpu.SemaphoreType.DMA((2,)),
            pltpu.SemaphoreType.DMA((2,)),
            pltpu.SemaphoreType.DMA((2,)),
            pltpu.SemaphoreType.DMA((2,)),
            pltpu.SemaphoreType.DMA((2,)),
        ],
        compiler_params=pltpu.CompilerParams(vmem_limit_bytes=60 * MIB),
        cost_estimate=pl.CostEstimate(
            flops=6 * nt * length * width * cols,
            bytes_accessed=8 * nt * length * width + 4 * width * cols,
            transcendentals=nt * length * hidden,
        ),
        name="expert",
    )(*xs, *gs, *ws)
    return result[:nt], result[nt : 2 * nt], result[2 * nt :]


MESH_ID = pl.DeviceIdType.MESH


def flip(index, bit):
    return index + bit - 2 * bit * lax.rem(index // bit, 2)


def flips(index, mask):
    for bit in (1, 2, 4):
        if mask & bit:
            index = flip(index, bit)
    return index


class Wire:
    def __init__(self, send_sem, recv_sem):
        self.r, self.f = lax.axis_index("replica"), lax.axis_index("fsdp")
        self.send_sem, self.recv_sem = send_sem, recv_sem
        self.used, self.sent = 0, []

    def meet(self, partners):
        barrier = pltpu.get_barrier_semaphore()
        for d_r, d_f in partners:
            pl.semaphore_signal(
                barrier, inc=1, device_id=self.at(d_r, d_f), device_id_type=MESH_ID
            )
        pl.semaphore_wait(barrier, len(partners))

    def at(self, d_r, d_f):
        return (flips(self.r, d_r), flips(self.f, d_f))

    def plan(self, src, dst, d_r, d_f):
        copy = pltpu.make_async_remote_copy(
            src_ref=src,
            dst_ref=dst,
            send_sem=self.send_sem.at[self.used],
            recv_sem=self.recv_sem.at[self.used],
            device_id=self.at(d_r, d_f),
            device_id_type=MESH_ID,
        )
        self.used += 1
        assert self.used <= self.send_sem.shape[0]
        return copy

    def send(self, src, dst, d_r, d_f):
        copy = self.plan(src, dst, d_r, d_f)
        copy.start()
        self.sent.append(copy)
        return copy

    def finish(self, waited=()):
        for copy in self.sent:
            if all(copy is not other for other in waited):
                copy.wait_send()


CUTS = 4
FRONT_SENDS = 2 * 28 + 7 + 7 * CUTS + 4 + 3
PARTNERS = ((1, 0), (2, 0), (0, 1), (0, 2), (0, 4), (0, 6))
ROWS = 64


def as_columns(rows):
    rows = rows.astype(f32)
    rest = jnp.zeros((128 - rows.shape[0], rows.shape[1]), f32)
    return jnp.concatenate([rows, rest], axis=0).T


def turn(v, cosine, sine):
    return v * cosine + pltpu.roll(v, HD // 2, 1) * sine


def front_kernel(
    tokens, seg_row, routes, cos, sin,
    in_ref, out_ref, tiny_ref, e_in_ref, e_out_ref, g_ref,
    qkv, attn, xn, first, lse, table, tiny_out, v,
    in_all, out_all, w_all, g_all, xs,
    in_v, out_v, tiny_v, rt, bias, e_in, e_out, e_part, mine_ref, other_ref,
    local_sem, send_sem, recv_sem,
):
    wire = Wire(send_sem, recv_sem)
    r, f = wire.r, wire.f
    shard = in_ref.shape[0]
    quarter = shard // 4
    length, width = tokens.shape
    experts = 8
    scale = HD ** (-0.5)

    def rows(j, k):
        at = flips(f, j) * shard + flips(r, k) * quarter
        return pl.ds(pl.multiple_of(at, quarter), quarter)

    def shard_rows(j):
        return pl.ds(pl.multiple_of(flips(f, j) * shard, shard), shard)

    def local(n, src, dst):
        copy = pltpu.make_async_copy(src, dst, local_sem.at[n])
        copy.start()
        return copy

    own_in = local(0, in_ref, in_v.at[shard_rows(0)])
    own_out = local(1, out_ref, out_v.at[shard_rows(0)])
    own_tiny = local(2, tiny_ref, tiny_v.at[f])
    own_w = (local(3, e_in_ref, e_in), local(7, e_out_ref, e_out))
    wire.meet(PARTNERS)

    own = pl.ds(pl.multiple_of(r * quarter, quarter), quarter)
    land = {"in": in_v, "out": out_v}
    source = {"in": in_ref, "out": out_ref}
    got, got_t, got_w, got_g, got_x = {}, {}, {}, {}, {}

    for m in (2, 4, 6, 1):
        got_t[m] = wire.send(tiny_ref, tiny_v.at[f], 0, m)

    def own_pieces(name):
        for m in (2, 4, 6, 1):
            got[name, m, 0] = wire.send(
                source[name].at[own], land[name].at[rows(0, 0)], 0, m
            )

    def pass_on(name, j, k, d_r, d_f):
        at = land[name].at[rows(j, k)]
        return wire.send(at, at, d_r, d_f)

    def near_pieces(name):
        for m in (1, 2, 4, 6):
            got[name, m, 0].wait_recv()
            if m != 1:
                got[name, m + 1, 0] = pass_on(name, m, 0, 0, 1)
            got[name, m, 2] = pass_on(name, m, 0, 2, 0)
            got[name, m, 1] = pass_on(name, m, 0, 1, 0)

    def far_pieces(name):
        for m in (3, 5, 7):
            got[name, m, 0].wait_recv()
            got[name, m, 2] = pass_on(name, m, 0, 2, 0)
            got[name, m, 1] = pass_on(name, m, 0, 1, 0)

    def side_pieces(name):
        for m in (1, 2, 4, 6, 3, 5, 7):
            got[name, m, 2].wait_recv()
            got[name, m, 3] = pass_on(name, m, 2, 1, 0)

    def all_pieces(name):
        for m in range(1, 8):
            got[name, m, 1].wait_recv()
            got[name, m, 3].wait_recv()

    own_pieces("in")
    own_pieces("out")

    for m in (2, 4, 6):
        got_t[m].wait_recv()
        at = tiny_v.at[flips(f, m)]
        got_t[m + 1] = wire.send(at, at, 0, 1)
    for m in (1, 3, 5, 7):
        got_t[m].wait_recv()
    own_tiny.wait()
    lanes = tiny_v.shape[2]
    rt[...] = jnp.zeros_like(rt)
    for z in range(4):
        both = tiny_v[2 * z].astype(f32) + tiny_v[2 * z + 1].astype(f32)
        tiny_out[:, z * lanes : (z + 1) * lanes] = both
        row = lax.broadcasted_iota(jnp.int32, both.shape, 0)
        rt[0:16, z * lanes : (z + 1) * lanes] = jnp.where(row < experts, both, 0.0).astype(bf16)

    def norm_one(c, carry):
        at = pl.ds(pl.multiple_of(c * ROWS, ROWS), ROWS)
        x = tokens[at, :].astype(f32)
        unit = x * lax.rsqrt(jnp.mean(x * x, axis=-1, keepdims=True) + epsilon)
        xn[at, :] = (unit * tiny_out[experts : experts + 1, :]).astype(bf16)
        return carry

    lax.fori_loop(0, length // ROWS, norm_one, 0)
    spot = lax.broadcasted_iota(jnp.int32, bias.shape, 0)
    keys_at = lax.broadcasted_iota(jnp.int32, bias.shape, 1)
    seg_col = as_columns(seg_row[...])[:, 0:1].astype(jnp.int32)
    bias[...] = jnp.where((spot >= keys_at) & (seg_col == seg_row[...]), 0.0, -1e30)

    for copy in own_w:
        copy.wait()
    plane = lax.rem(f // 2, 2)
    split = e_in.shape[2]
    for c in range(0, mine_ref.shape[1], 128):
        part = e_in[:, :, c : c + 128] if c < split else e_out[:, :, c - split : c - split + 128]
        e_part[...] = jnp.swapaxes(part.astype(f32), 0, 1)
        mine_ref[:, c : c + 128] = e_part[2 * r + plane].astype(bf16)
        other_ref[:, c : c + 128] = e_part[2 * r + 1 - plane].astype(bf16)
    kept = [local(4, mine_ref, w_all.at[shard_rows(0)])]
    cut = shard // CUTS

    def send_w(n, src, d_f):
        at = pl.ds(n * cut, cut)
        to = pl.ds(pl.multiple_of(f * shard + n * cut, cut), cut)
        return wire.send(src.at[at], w_all.at[to], 0, d_f)

    def pass_w(n, m):
        got_w[m, n].wait_recv()
        at = w_all.at[pl.ds(pl.multiple_of(flips(f, m) * shard + n * cut, cut), cut)]
        got_w[m + 1, n] = wire.send(at, at, 0, 1)

    near_pieces("in")
    for n in range(CUTS):
        for m, src in ((2, other_ref), (4, mine_ref), (6, other_ref)):
            got_w[m, n] = send_w(n, src, m)
    got_g[4] = wire.send(g_ref, g_all.at[4], 0, 2)
    got_g[1] = wire.send(g_ref, g_all.at[1], 1, 0)
    far_pieces("in")
    near_pieces("out")
    far_pieces("out")
    for n in range(CUTS):
        got_w[1, n] = send_w(n, mine_ref, 1)
    got_g[2] = wire.send(g_ref, g_all.at[2], 2, 0)
    side_pieces("in")
    own_in.wait()
    all_pieces("in")

    def project(c, carry):
        at = pl.multiple_of(c * 256, 256)
        t = matmul(xn[...], in_v[:, pl.ds(at, 256)])
        turned = c < 7
        for n in (0, 1):
            part = t[:, n * HD : (n + 1) * HD]
            part = turn(
                part, jnp.where(turned, cos[...], 1.0), jnp.where(turned, sin[...], 0.0)
            )
            qkv[:, pl.ds(at + n * HD, HD)] = part.astype(bf16)
        return carry

    lax.fori_loop(0, 8, project, 0)
    pass_w(0, 2)
    pass_w(0, 4)
    lane = lax.broadcasted_iota(jnp.int32, (length, HD), 1)
    lse[...] = jnp.zeros_like(lse)

    def head(h, carry):
        at = pl.ds(pl.multiple_of(h * HD, HD), HD)
        group = h // GROUP
        k_at = pl.ds(pl.multiple_of(WQ + group * HD, HD), HD)
        v_at = pl.ds(pl.multiple_of(WQ + WK + group * HD, HD), HD)
        s = contract_cols(qkv[:, at], qkv[:, k_at]) * scale + bias[...]
        highest = jnp.max(s, axis=-1, keepdims=True)
        expo = jnp.exp(s - highest)
        total = jnp.sum(expo, axis=-1, keepdims=True)
        p = (expo * (1.0 / total)).astype(bf16)
        attn[:, at] = matmul(p, qkv[:, v_at]).astype(bf16)
        lse[...] = jnp.where(lane == h, highest + jnp.log(total), lse[...])
        return carry

    lax.fori_loop(0, HQ // 2, head, 0)
    side_pieces("out")
    pass_w(0, 6)
    pass_w(1, 2)
    lax.fori_loop(HQ // 2, HQ, head, 0)
    pass_w(1, 4)
    pass_w(1, 6)
    own_out.wait()
    all_pieces("out")
    kept.append(local(5, in_v, in_all))
    kept.append(local(6, out_v, out_all))

    def add_out(c, carry):
        at = pl.ds(pl.multiple_of(c * 256, 256), 256)
        first[:, at] = tokens[:, at].astype(f32) + contract_cols(attn[...], out_v[at, :])
        return carry

    lax.fori_loop(0, width // 256, add_out, 0)

    def norm_two(c, carry):
        at = pl.ds(pl.multiple_of(c * ROWS, ROWS), ROWS)
        h = first[at, :]
        unit = h * lax.rsqrt(jnp.mean(h * h, axis=-1, keepdims=True) + epsilon)
        v[at, 0:width] = (unit * tiny_out[experts + 1 : experts + 2, :]).astype(bf16)
        return carry

    lax.fori_loop(0, length // ROWS, norm_two, 0)
    logits = contract_cols(v[:, 0:width], rt[...])
    named = as_columns(routes[...]).astype(jnp.int32)
    chosen = lane == named[:, 0:1]
    for j in range(1, routes.shape[0]):
        chosen = chosen | (lane == named[:, j : j + 1])
    logits = jnp.where(chosen, logits, -1e30)
    expo = jnp.exp(logits - jnp.max(logits, axis=-1, keepdims=True))
    expo = jnp.where(chosen, expo, 0.0)
    gates = expo / jnp.sum(expo, axis=-1, keepdims=True)
    table[...] = gates
    high = gates.astype(bf16).astype(f32)
    v[:, width:] = (high + pltpu.roll(gates - high, experts, 1)).astype(bf16)

    got_x[2] = wire.send(v, xs.at[2], 2, 0)
    got_x[1] = wire.send(v, xs.at[1], 1, 0)
    for n in range(2, CUTS):
        for m in (2, 4, 6):
            pass_w(n, m)
    got_g[2].wait_recv()
    got_g[3] = wire.send(g_all.at[2], g_all.at[3], 1, 0)
    got_x[2].wait_recv()
    got_x[3] = wire.send(xs.at[2], xs.at[3], 1, 0)
    for n in range(CUTS):
        for m in (1, 3, 5, 7):
            got_w[m, n].wait_recv()
    for m in (1, 3, 4):
        got_g[m].wait_recv()
    for m in (1, 3):
        got_x[m].wait_recv()
    for copy in kept:
        copy.wait()
    wire.finish()


def front(
    tokens, seg_ids, routes, cos, sin, in_proj, out_proj, tiny, expert_in, expert_out, grad
):
    any_spec = pl.BlockSpec(memory_space=pl.ANY)
    vmem = pl.BlockSpec(memory_space=pltpu.VMEM)
    length, width = tokens.shape
    shard, cols = in_proj.shape
    whole = 8 * shard
    wide = width + EXTRA
    e_cols = expert_in.shape[2] + expert_out.shape[2]
    return pl.pallas_call(
        front_kernel,
        out_shape=[
            jax.ShapeDtypeStruct((length, cols), bf16),
            jax.ShapeDtypeStruct((length, WQ), bf16),
            jax.ShapeDtypeStruct((length, width), bf16),
            jax.ShapeDtypeStruct((length, width), f32),
            jax.ShapeDtypeStruct((length, HD), f32),
            jax.ShapeDtypeStruct((length, EXTRA), f32),
            jax.ShapeDtypeStruct((16, width), f32),
            jax.ShapeDtypeStruct((length, wide), bf16),
            jax.ShapeDtypeStruct((whole, cols), bf16),
            jax.ShapeDtypeStruct((whole, out_proj.shape[1]), bf16),
            jax.ShapeDtypeStruct((whole, e_cols), bf16),
            jax.ShapeDtypeStruct((5,) + grad.shape, bf16),
            jax.ShapeDtypeStruct((4, length, wide), bf16),
        ],
        in_specs=[vmem] * 5 + [any_spec] * 6,
        out_specs=[vmem] * 8 + [any_spec] * 5,
        scratch_shapes=[
            pltpu.VMEM((whole, cols), bf16),
            pltpu.VMEM((whole, out_proj.shape[1]), bf16),
            pltpu.VMEM((8,) + tiny.shape, bf16),
            pltpu.VMEM((EXTRA, width), bf16),
            pltpu.VMEM((length, length), f32),
            pltpu.VMEM(expert_in.shape, bf16),
            pltpu.VMEM(expert_out.shape, bf16),
            pltpu.VMEM((expert_in.shape[1], shard, 128), f32),
            pltpu.VMEM((shard, e_cols), bf16),
            pltpu.VMEM((shard, e_cols), bf16),
            pltpu.SemaphoreType.DMA((8,)),
            pltpu.SemaphoreType.DMA((FRONT_SENDS,)),
            pltpu.SemaphoreType.DMA((FRONT_SENDS,)),
        ],
        compiler_params=pltpu.CompilerParams(
            collective_id=1, has_side_effects=True, vmem_limit_bytes=56 * MIB
        ),
        name="front",
    )(
        tokens, seg_ids, routes.T, cos, sin,
        in_proj, out_proj, tiny, expert_in, expert_out, grad,
    )


ORDER = (3, 2, 4, 5, 7, 6, 1, 0)
UNROLL = True
WIDE_COLS = 256
GROUP_AT = {2: (2, 0), 4: (0, 2), 6: (2, 2)}


def pick(step, table):
    value = jnp.int32(table[-1])
    for i, item in enumerate(table[:-1]):
        value = jnp.where(step == i, item, value)
    return value


def group_kernel(
    v_ref, g_ref, xs, g_all, w_ref,
    mix_sum, dx_own, dx_in, grads, x_late, g_late,
    wbuf, xbuf, gbuf, xt, gt_, hidg, dgu, deven, dodd, rc, meven, modd, mrc, acc, stage,
    sem_w, sem_x, sem_g, sem_m, sem_s, send_sem, recv_sem,
):
    wire = Wire(send_sem, recv_sem)
    r, f = wire.r, wire.f
    length, width = g_ref.shape
    hidden = w_ref.shape[1] // 3
    half = length // 2
    low, top = pl.ds(0, half), pl.ds(half, half)
    expert = 2 * r + lax.rem(f // 2, 2)
    step_cols = 256

    load_w = pltpu.make_async_copy(w_ref, wbuf, sem_w.at[0])
    load_w.start()

    def load(step):
        slot = lax.rem(step, 2)
        k = pick(step, ORDER)

        @pl.when(k == 0)
        def _():
            pltpu.make_async_copy(v_ref, xbuf.at[slot], sem_x.at[slot]).start()
            pltpu.make_async_copy(g_ref, gbuf.at[slot], sem_g.at[slot]).start()

        for table, src_x, src_g in (
            ((1, 2, 3), xs, g_all), ((4,), x_late, g_all), ((5, 6, 7), x_late, g_late)
        ):

            @pl.when((k >= table[0]) & (k <= table[-1]))
            def _():
                pltpu.make_async_copy(src_x.at[k], xbuf.at[slot], sem_x.at[slot]).start()
                pltpu.make_async_copy(src_g.at[k], gbuf.at[slot], sem_g.at[slot]).start()

    load(jnp.int32(0))
    wire.meet(PARTNERS_GROUP)
    late_x = {4: wire.send(v_ref, x_late.at[4], 0, 2)}
    far = [
        wire.send(g_all.at[4], g_late.at[6], 2, 0),
        wire.send(xs.at[2, top], x_late.at[6, top], 0, 2),
    ]
    late_g = {5: wire.send(g_all.at[4], g_late.at[5], 1, 0)}
    far.append(wire.plan(x_late.at[4, low], x_late.at[6, low], 2, 0))
    late_x[5] = wire.plan(x_late.at[4], x_late.at[5], 1, 0)
    late_x[7] = wire.plan(x_late.at[6], x_late.at[7], 1, 0)
    late_g[7] = wire.plan(g_late.at[6], g_late.at[7], 1, 0)
    slots = {2: 0, 4: 1, 6: 2, 0: 3}
    to_core = {k: wire.plan(dodd.at[n % 2], rc.at[n], 1, 0) for k, n in slots.items()}
    mix_core = {k: wire.plan(modd.at[n % 2], mrc.at[n], 1, 0) for k, n in slots.items()}
    back = {k: wire.plan(deven.at[k // 2], dx_in.at[k // 2 - 1], *GROUP_AT[k]) for k in (2, 4, 6)}
    acc[...] = jnp.zeros_like(acc)
    lane = lax.broadcasted_iota(jnp.int32, (length, EXTRA), 1)
    load_w.wait()

    def keep_mix(k):
        n = slots[k] % 2
        return pltpu.make_async_copy(meven.at[n], mix_sum.at[k // 2], sem_m.at[n])

    def send_core(k):
        to_core[k].start()
        mix_core[k].start()

    def sent_core(k):
        to_core[k].wait_send()
        mix_core[k].wait_send()

    def complete(k):
        n = slots[k]
        to_core[k].wait_recv()
        deven[k // 2] = (deven[k // 2].astype(f32) + rc[n].astype(f32)).astype(bf16)
        if k in (4, 6):
            back[k].start()
        mix_core[k].wait_recv()
        meven[n % 2] = (meven[n % 2].astype(f32) + mrc[n].astype(f32)).astype(bf16)
        keep_mix(k).start()

    def block(step, carry):
        slot = lax.rem(step, 2)

        @pl.when((step == 0) | (step >= 4) & (step < 7))
        def _():
            load(step + 1)

        pltpu.make_async_copy(v_ref, xbuf.at[slot], sem_x.at[slot]).wait()
        pltpu.make_async_copy(g_ref, gbuf.at[slot], sem_g.at[slot]).wait()
        extra = xbuf[slot, :, width:].astype(f32)
        mine = (lane == expert) | (lane == expert + 8)
        gate = jnp.sum(jnp.where(mine, extra, 0.0), axis=1, keepdims=True)
        here = pl.ds(pl.multiple_of(slot * length, length), length)
        xt[:, here] = xbuf[slot, :, :width].T
        gt_[:, here] = gbuf[slot].T

        def first(c, dgate):
            at = pl.multiple_of(c * step_cols, step_cols)
            u = matmul(xbuf[slot, :, :width], wbuf[:, pl.ds(at, step_cols)])
            up = matmul(xbuf[slot, :, :width], wbuf[:, pl.ds(hidden + at, step_cols)])
            rev = matmul(gbuf[slot], wbuf[:, pl.ds(2 * hidden + at, step_cols)])
            sig = 1.0 / (1.0 + jnp.exp(-u))
            act = u * sig
            hid = act * up
            hidg[here, pl.ds(at, step_cols)] = (gate * hid).astype(bf16)
            dgate = dgate + jnp.sum(rev * hid, axis=1, keepdims=True)
            dhid = gate * rev
            dgu[here, pl.ds(at, step_cols)] = (
                dhid * up * sig * (1.0 + u * (1.0 - sig))
            ).astype(bf16)
            dgu[here, pl.ds(hidden + at, step_cols)] = (dhid * act).astype(bf16)
            return dgate

        dgate = lax.fori_loop(
            0, hidden // step_cols, first, jnp.zeros((length, 1), f32), unroll=UNROLL
        )
        high = dgate.astype(bf16).astype(f32)
        rest = dgate - high
        tail = (
            jnp.where(lane == expert, high, 0.0) + jnp.where(lane == expert + 8, rest, 0.0)
        ).astype(bf16)

        def out_parts(dst_d, n_d, dst_m, n_m):
            def second(c, carry):
                at = pl.multiple_of(c * step_cols, step_cols)
                dst_d[n_d, :, pl.ds(at, step_cols)] = contract_cols(
                    dgu[here, :], wbuf[pl.ds(at, step_cols), pl.ds(0, 2 * hidden)]
                ).astype(bf16)
                dst_m[n_m, :, pl.ds(at, step_cols)] = contract_cols(
                    hidg[here, :], wbuf[pl.ds(at, step_cols), pl.ds(2 * hidden, hidden)]
                ).astype(bf16)
                return carry

            lax.fori_loop(0, width // step_cols, second, 0, unroll=UNROLL)
            dst_d[n_d, :, width:] = tail

        slot_two = pick(step, (0, 0, 1, 1, 0, 0, 1, 1))
        k = pick(step, ORDER)

        @pl.when(step == 4)
        def _():
            sent_core(2)

        @pl.when(step == 6)
        def _():
            sent_core(4)

        @pl.when(step == 5)
        def _():
            keep_mix(2).wait()

        @pl.when(step == 7)
        def _():
            keep_mix(4).wait()

        @pl.when(lax.rem(k, 2) == 1)
        def _():
            out_parts(dodd, slot_two, modd, slot_two)

        @pl.when(lax.rem(k, 2) == 0)
        def _():
            out_parts(deven, k // 2, meven, slot_two)

        def come_5():
            late_x[5].wait_recv()
            late_g[5].wait_recv()
            load(step + 1)

        def come_6():
            for copy in far:
                copy.wait_recv()
            late_x[7].start()
            late_g[7].start()

        for at_step, todo in (
            (0, (lambda: send_core(2),)),
            (1, (lambda: complete(2),)),
            (2, (come_5,)),
            (3, (lambda: send_core(4), come_6)),
            (4, (lambda: complete(4), lambda: send_core(6))),
            (5, (lambda: complete(6),)),
            (6, (lambda: send_core(0),)),
            (7, (lambda: complete(0),)),
        ):

            @pl.when(step == at_step)
            def _():
                for do in todo:
                    do()

        @pl.when(slot == 1)
        def _():
            def third(c, carry):
                at = pl.multiple_of(c * WIDE_COLS, WIDE_COLS)
                acc[:, pl.ds(at, WIDE_COLS)] += matmul(xt[...], dgu[:, pl.ds(at, WIDE_COLS)])
                return carry

            lax.fori_loop(0, 2 * hidden // WIDE_COLS, third, 0, unroll=UNROLL)

            def fourth(c, carry):
                at = pl.multiple_of(c * WIDE_COLS, WIDE_COLS)
                acc[:, pl.ds(2 * hidden + at, WIDE_COLS)] += matmul(
                    gt_[...], hidg[:, pl.ds(at, WIDE_COLS)]
                )
                return carry

            lax.fori_loop(0, hidden // WIDE_COLS, fourth, 0, unroll=UNROLL)

        @pl.when(step == 1)
        def _():
            late_x[4].wait_recv()
            late_x[5].start()
            far[2].start()
            back[2].start()
            load(step + 1)

        @pl.when(step == 3)
        def _():
            late_x[7].wait_recv()
            late_g[7].wait_recv()
            load(step + 1)

        return carry

    lax.fori_loop(0, 8, block, 0)
    keep = pltpu.make_async_copy(deven.at[0], dx_own, sem_w.at[0])
    keep.start()
    parts = 8
    rows = width // parts

    def out(j, slot):
        return pltpu.make_async_copy(
            stage.at[slot], grads.at[pl.ds(j * rows, rows)], sem_s.at[slot]
        )

    for j in range(parts):
        slot = j % 2
        if j >= 2:
            out(j - 2, slot).wait()
        stage[slot] = acc[j * rows : (j + 1) * rows].astype(bf16)
        out(j, slot).start()
    for j in range(parts - 2, parts):
        out(j, j % 2).wait()
    keep.wait()
    keep_mix(6).wait()
    keep_mix(0).wait()
    for k in (2, 4, 6):
        back[k].wait_recv()
        back[k].wait_send()
    sent_core(6)
    sent_core(0)
    for copy in (far[2], late_x[5], late_x[7], late_g[7]):
        copy.wait_send()
    wire.finish()


PARTNERS_GROUP = ((1, 0), (2, 0), (0, 2), (2, 2))
GROUP_SENDS = 8 + 8 + 3


def run_group(v, grad, xs, g_all, w):
    length, width = grad.shape
    wide = v.shape[1]
    cols = w.shape[1]
    hidden = cols // 3
    any_spec = pl.BlockSpec(memory_space=pl.ANY)
    return pl.pallas_call(
        group_kernel,
        out_shape=[
            jax.ShapeDtypeStruct((4, length, width), bf16),
            jax.ShapeDtypeStruct((length, wide), bf16),
            jax.ShapeDtypeStruct((3, length, wide), bf16),
            jax.ShapeDtypeStruct((width, cols), bf16),
            jax.ShapeDtypeStruct((8, length, wide), bf16),
            jax.ShapeDtypeStruct((8, length, width), bf16),
        ],
        in_specs=[any_spec] * 5,
        out_specs=[any_spec] * 6,
        scratch_shapes=[
            pltpu.VMEM((width, cols), bf16),
            pltpu.VMEM((2, length, wide), bf16),
            pltpu.VMEM((2, length, width), bf16),
            pltpu.VMEM((width, 2 * length), bf16),
            pltpu.VMEM((width, 2 * length), bf16),
            pltpu.VMEM((2 * length, hidden), bf16),
            pltpu.VMEM((2 * length, 2 * hidden), bf16),
            pltpu.VMEM((4, length, wide), bf16),
            pltpu.VMEM((2, length, wide), bf16),
            pltpu.VMEM((4, length, wide), bf16),
            pltpu.VMEM((2, length, width), bf16),
            pltpu.VMEM((2, length, width), bf16),
            pltpu.VMEM((4, length, width), bf16),
            pltpu.VMEM((width, cols), f32),
            pltpu.VMEM((2, width // 8, cols), bf16),
            pltpu.SemaphoreType.DMA((1,)),
            pltpu.SemaphoreType.DMA((2,)),
            pltpu.SemaphoreType.DMA((2,)),
            pltpu.SemaphoreType.DMA((2,)),
            pltpu.SemaphoreType.DMA((2,)),
            pltpu.SemaphoreType.DMA((GROUP_SENDS,)),
            pltpu.SemaphoreType.DMA((GROUP_SENDS,)),
        ],
        compiler_params=pltpu.CompilerParams(
            collective_id=2, has_side_effects=True, vmem_limit_bytes=62 * MIB
        ),
        cost_estimate=pl.CostEstimate(
            flops=48 * length * width * cols,
            bytes_accessed=64 * length * width + 4 * width * cols,
            transcendentals=8 * length * hidden,
        ),
        name="group",
    )(v, grad, xs, g_all, w)


PARTNERS_BACK = ((1, 0), (2, 0), (3, 0), (0, 1), (0, 2), (0, 4), (0, 6))
TERMS = 16
BACK_SENDS = 3 + 8 + 6 + 3 + 2 + 3 + 2 * 4 + 2 * 3 + 1 + 6 + 6


def back_kernel(
    dx_own, g_ref, first, table, tiny, v, tokens, qkv, lse, cos, sin, seg_row,
    dx_in, grads, mix_sum, attn, xn, in_all, out_all,
    tokens_grad,
    g_out, mix_in, d_out, xn_core,
    in_v, out_v, mix_v, gl, gy, gz, act_v, aq_v, pq, wo, wi, wyo, wyi, wzo, wzi, wxo, own_d,
    dn, dxn, dl, dattn, dproj, dkv, bias, tbuf,
    local_sem, send_sem, recv_sem,
):
    wire = Wire(send_sem, recv_sem)
    r, f = wire.r, wire.f
    shard = gl.shape[1]
    length, width = tokens.shape
    experts = 8
    low = lax.rem(f // 2, 2)
    cols_p, cols_a = pq.shape[1], aq_v.shape[1]
    scale = HD ** (-0.5)
    used = [0]

    def local(src, dst):
        copy = pltpu.make_async_copy(src, dst, local_sem.at[used[0]])
        copy.start()
        used[0] += 1
        return copy

    def shard_rows(j):
        return pl.ds(pl.multiple_of(flips(f, j) * shard, shard), shard)

    def token_rows(k):
        return pl.ds(k * length, length)

    def part_of(k, cols):
        return pl.ds(pl.multiple_of(flips(r, k) * cols, cols), cols)

    def add(u, w):
        return (u.astype(f32) + w.astype(f32)).astype(bf16)

    half = lax.rem(r, 2)
    side = r // 2

    def half_of(index):
        return pl.ds(pl.multiple_of(index * cols_a, cols_a), cols_a)

    load_dx = [
        local(dx_in.at[n], in_v.at[token_rows(n), pl.ds(0, dx_in.shape[2])]) for n in range(3)
    ]
    load_out = local(out_all, out_v)
    load_g = {j: local(grads.at[shard_rows(j)], gl.at[j // 2]) for j in (4, 6, 2, 0)}
    load_a = local(attn.at[:, half_of(half)], aq_v.at[token_rows(0)])
    load_mix = local(mix_sum.at[2], mix_v.at[0])
    wire.meet(PARTNERS_BACK)
    got_y, got_m = {}, {}
    place_z = f // 2
    inner = (place_z == 1) | (place_z == 2)
    cut = shard // 2
    got_z = {}
    for j in (4, 6, 2, 0):
        for n in (0, 1):
            at = pl.ds(pl.multiple_of(flips(f, j + 1) * shard + n * cut, cut), cut)
            got_y[j, n] = wire.plan(grads.at[at], gy.at[j // 2, pl.ds(n * cut, cut)], 0, 1)
            wire.sent.append(got_y[j, n])
            if j:
                at = pl.ds(n * cut, cut)
                got_z[j, n] = wire.plan(gl.at[j // 2, at], gz.at[j // 2 - 1, at], 0, j)
                wire.sent.append(got_z[j, n])

    def by_place(do, outer_j, inner_j, n):
        @pl.when(inner)
        def _():
            do(inner_j, n)

        @pl.when(jnp.logical_not(inner))
        def _():
            do(outer_j, n)

    def send_y(j, n):
        got_y[j, n].start()

    for outer_j, inner_j in ((4, 2), (6, 4), (2, 6)):
        for n in (0, 1):
            by_place(send_y, outer_j, inner_j, n)
    for n in (0, 1):
        send_y(0, n)
    got_a = wire.send(attn.at[:, half_of(1 - half)], aq_v.at[token_rows(1)], 1, 0)
    got_m[6] = wire.send(mix_sum.at[3], mix_v.at[1], 2, 0)
    got_n = {2: wire.send(xn, act_v.at[token_rows(2)], 2, 0), 1: wire.send(xn, xn_core, 1, 0)}

    spot = lax.broadcasted_iota(jnp.int32, bias.shape, 0)
    keys_at = lax.broadcasted_iota(jnp.int32, bias.shape, 1)
    seg_col = as_columns(seg_row[...])[:, 0:1].astype(jnp.int32)
    bias[...] = jnp.where((spot >= keys_at) & (seg_col == seg_row[...]), 0.0, -1e30)
    tbuf[...] = jnp.zeros_like(tbuf)
    for copy in load_dx:
        copy.wait()

    def sum_dx(c, carry):
        at = pl.ds(pl.multiple_of(c * ROWS, ROWS), ROWS)
        d = dx_own[at, :].astype(f32)
        for n in range(3):
            here = pl.ds(pl.multiple_of(n * length + c * ROWS, ROWS), ROWS)
            d = d + in_v[here, 0 : dx_own.shape[1]].astype(f32)
        dn[at, :] = d[:, :width]
        dgate = d[:, width:]
        dgate = dgate + pltpu.roll(dgate, EXTRA - experts, 1)
        gates = table[at, :]
        mean = jnp.sum(gates * dgate, axis=-1, keepdims=True)
        dl[at, :] = (gates * (dgate - mean)).astype(bf16)
        return carry

    lax.fori_loop(0, length // ROWS, sum_dx, 0)
    load_in = local(in_all, in_v)
    dlt = dl[...].T[0:16]

    def add_router(c, carry):
        at = pl.ds(pl.multiple_of(c * 256, 256), 256)
        row = lax.broadcasted_iota(jnp.int32, (16, 256), 0)
        router = jnp.where(row < experts, tiny[:, at], 0.0).astype(bf16)
        dn[:, at] = dn[:, at] + matmul(dl[:, 0:16], router)
        tbuf[:, at] = matmul(dlt, v[:, at])
        return carry

    lax.fori_loop(0, width // 256, add_router, 0)

    def norm_two(c, gain):
        at = pl.ds(pl.multiple_of(c * ROWS, ROWS), ROWS)
        h = first[at, :]
        r2 = lax.rsqrt(jnp.mean(h * h, axis=-1, keepdims=True) + epsilon)
        unit = h * r2
        d = dn[at, :]
        gain = gain + jnp.sum(d * unit, axis=0, keepdims=True)
        d = d * tiny[experts + 1 : experts + 2, :]
        d = g_ref[at, :].astype(f32) + r2 * (
            d - unit * jnp.mean(d * unit, axis=-1, keepdims=True)
        )
        dn[at, :] = d
        act_v[at, :] = d.astype(bf16)
        return gain

    gain_two = lax.fori_loop(0, length // ROWS, norm_two, jnp.zeros((1, width), f32))
    tbuf[experts + 1 : experts + 2, :] = gain_two
    got_r = wire.send(act_v.at[token_rows(0)], act_v.at[token_rows(1)], 1, 0)
    def pass_y(j, n):
        if n == 0:
            load_g[j].wait()
        got_y[j, n].wait_recv()
        at = pl.ds(n * cut, cut)
        gl[j // 2, at] = add(gl[j // 2, at], gy[j // 2, at])
        got_z[j, n].start()

    def came(got_some, j):
        for n in (0, 1):
            got_some[j, n].wait_recv()

    load_out.wait()

    def to_attn(c, carry):
        at = pl.ds(pl.multiple_of(c * 256, 256), 256)
        dattn[:, at] = matmul(act_v[0:length, :], out_v[:, at]).astype(bf16)
        return carry

    lax.fori_loop(0, WQ // 256, to_attn, 0)
    by_place(pass_y, 4, 2, 0)
    lane = lax.broadcasted_iota(jnp.int32, (length, HD), 1)

    def turn_back(w):
        return w * cos[...] - pltpu.roll(w, HD // 2, 1) * sin[...]

    for group in range(KV):
        k_at = pl.ds(WQ + group * HD, HD)
        v_at = pl.ds(WQ + WK + group * HD, HD)
        dkv[...] = jnp.zeros_like(dkv)

        def head(i, carry):
            h = group * GROUP + i
            at = pl.ds(pl.multiple_of(h * HD, HD), HD)
            s = contract_cols(qkv[:, at], qkv[:, k_at]) * scale + bias[...]
            level = jnp.sum(jnp.where(lane == h, lse[...], 0.0), axis=1, keepdims=True)
            p = jnp.exp(s - level)
            da = dattn[:, at]
            dp = contract_cols(da, qkv[:, v_at])
            delta = jnp.sum(p * dp, axis=-1, keepdims=True)
            ds = (p * (dp - delta)).astype(bf16)
            dkv[1] += contract_rows(p.astype(bf16), da)
            dkv[0] += contract_rows(ds, qkv[:, at])
            dproj[:, at] = turn_back(matmul(ds, qkv[:, k_at]) * scale).astype(bf16)
            return carry

        lax.fori_loop(0, GROUP, head, 0)
        if group == 0:
            by_place(pass_y, 4, 2, 1)
            load_mix.wait()
            got_m[6].wait_recv()
            mix_v[0] = add(mix_v[0], mix_v[1])
            got_m[4] = wire.send(mix_v.at[0], mix_in.at[1], 0, 2)
        dproj[:, k_at] = turn_back(dkv[0] * scale).astype(bf16)
        dproj[:, v_at] = dkv[1].astype(bf16)

    keep_p = local(dproj.at[:, part_of(0, cols_p)], pq.at[token_rows(0)])
    got_p = {}
    for k in (2, 3, 1):
        got_p[k] = wire.send(dproj.at[:, part_of(k, cols_p)], pq.at[token_rows(k)], k, 0)

    got_m[2] = wire.send(mix_sum.at[1], mix_in.at[0], 2, 0)
    by_place(pass_y, 6, 4, 0)

    load_a.wait()
    got_a.wait_recv()
    got_r.wait_recv()

    def dense_out(c, carry):
        at = pl.ds(pl.multiple_of(c * 256, 256), 256)
        wo[at, :] = matmul(act_v[0 : 2 * length, at].T, aq_v[...]).astype(bf16)
        return carry

    lax.fori_loop(0, width // 256, dense_out, 0)
    got_r.wait_send()
    load_x = [local(xn, act_v.at[token_rows(0)])]
    got_n[1].wait_recv()
    load_x.append(local(xn_core, act_v.at[token_rows(1)]))
    got_wo, got_wi, got_wzo, got_wzi = {}, {}, {}, {}
    for j in (4, 6, 2, 0):
        got_wo[j] = wire.send(wo.at[shard_rows(j + 1)], wyo.at[j // 2], 0, 1)

    by_place(pass_y, 6, 4, 1)

    load_in.wait()

    def to_norm(c, carry):
        at = pl.ds(pl.multiple_of(c * 256, 256), 256)
        dxn[:, at] = contract_cols(dproj[...], in_v[at, :])
        return carry

    lax.fori_loop(0, width // 256, to_norm, 0)

    def norm_one(c, gain):
        at = pl.ds(pl.multiple_of(c * ROWS, ROWS), ROWS)
        x = tokens[at, :].astype(f32)
        r1 = lax.rsqrt(jnp.mean(x * x, axis=-1, keepdims=True) + epsilon)
        unit = x * r1
        d = dxn[at, :]
        gain = gain + jnp.sum(d * unit, axis=0, keepdims=True)
        d = d * tiny[experts : experts + 1, :]
        d = dn[at, :] + r1 * (d - unit * jnp.mean(d * unit, axis=-1, keepdims=True))
        tokens_grad[at, :] = d.astype(bf16)
        return gain

    gain_one = lax.fori_loop(0, length // ROWS, norm_one, jnp.zeros((1, width), f32))
    tbuf[experts : experts + 1, :] = gain_one

    by_place(pass_y, 2, 6, 0)
    by_place(pass_y, 2, 6, 1)
    mine, other = 2 * r + low, 2 * r + 1 - low
    load_g[0].wait()
    came(got_y, 0)
    came(got_z, 4)
    gl[0] = (gl[0].astype(f32) + gy[0].astype(f32) + gz[1].astype(f32)).astype(bf16)
    kept = [local(gl.at[0], g_out.at[mine])]
    got_e = {}

    got_n[2].wait_recv()
    got_n[3] = wire.send(act_v.at[token_rows(2)], act_v.at[token_rows(3)], 1, 0)
    keep_p.wait()
    for copy in load_x:
        copy.wait()
    for k in (1, 2, 3):
        got_p[k].wait_recv()
    got_n[3].wait_recv()
    got_e[2, 0] = wire.send(gl.at[0], g_out.at[mine], 2, 0)
    got_e[1, 0] = wire.send(gl.at[0], g_out.at[mine], 1, 0)

    tall = shard + TERMS

    def tall_rows(j):
        return pl.ds(pl.multiple_of(flips(f, j) * tall, TERMS), tall)

    for z in range(4):
        lanes = slice(2 * z * shard, 2 * (z + 1) * shard)
        both = matmul(act_v[:, lanes].T, pq[...]).astype(bf16)
        for y in (0, 1):
            top = (2 * z + y) * tall
            wi[top : top + shard, :] = both[y * shard : (y + 1) * shard]
            wi[top + shard : top + tall, :] = jnp.zeros((TERMS, cols_p), bf16)
            wi[top + shard : top + tall, 0 : 2 * shard] = tbuf[:, lanes].astype(bf16)
    for j in (4, 6, 2, 0):
        got_wi[j] = wire.send(wi.at[tall_rows(j + 1)], wyi.at[j // 2], 0, 1)
    for j in (4, 6, 2):
        got_wo[j].wait_recv()
        wyo[j // 2] = add(wo[shard_rows(j), :], wyo[j // 2])
        got_wzo[j] = wire.send(wyo.at[j // 2], wzo.at[j // 2 - 1], 0, j)

    came(got_z, 2)
    came(got_z, 6)
    gz[0] = add(gz[0], gz[2])
    kept.append(local(gz.at[0], g_out.at[other]))
    got_e[2, 1] = wire.send(gz.at[0], g_out.at[other], 2, 0)
    got_e[1, 1] = wire.send(gz.at[0], g_out.at[other], 1, 0)

    for j in (4, 6, 2):
        got_wi[j].wait_recv()
        wyi[j // 2] = add(wi[tall_rows(j), :], wyi[j // 2])
        got_wzi[j] = wire.send(wyi.at[j // 2], wzi.at[j // 2 - 1], 0, j)

    def own_rows(w, rows, y, z, got_w, got_zs):
        got_w[0].wait_recv()
        total = w[rows, :].astype(f32) + y[0].astype(f32)
        for j in (2, 4, 6):
            got_zs[j].wait_recv()
            total = total + z[j // 2 - 1].astype(f32)
        return total

    wxo[0] = own_rows(wo, shard_rows(0), wyo, wzo, got_wo, got_wzo).astype(bf16)
    quarter = cols_a // 2

    def quarter_of(index):
        return pl.ds(pl.multiple_of(index * quarter, quarter), quarter)

    got_x = wire.send(
        wxo.at[0, :, quarter_of(1 - side)], wxo.at[1, :, pl.ds(0, quarter)], 2, 0
    )
    got_x.wait_recv()
    own_d[shard:, cols_p:] = jnp.zeros((TERMS, quarter), bf16)
    own_d[0:shard, cols_p:] = add(wxo[0, :, quarter_of(side)], wxo[1, :, 0:quarter])
    got_d = {}

    def send_d(n, columns):
        kept.append(local(own_d.at[:, columns], d_out.at[r, :, columns]))
        for k in (2, 1):
            got_d[k, n] = wire.send(own_d.at[:, columns], d_out.at[r, :, columns], k, 0)

    parts_d = (pl.ds(cols_p, quarter), pl.ds(0, cols_p))
    send_d(0, parts_d[0])
    own_d[:, 0:cols_p] = own_rows(wi, tall_rows(0), wyi, wzi, got_wi, got_wzi).astype(bf16)
    send_d(1, parts_d[1])

    far = flips(r, 2)
    for n, e in ((0, 2 * far + low), (1, 2 * far + 1 - low)):
        got_e[2, n].wait_recv()
        got_e[3, n] = wire.send(g_out.at[e], g_out.at[e], 1, 0)
    for n, columns in enumerate(parts_d):
        got_d[2, n].wait_recv()
        at = d_out.at[far, :, columns]
        got_d[3, n] = wire.send(at, at, 1, 0)
    for k in (1, 3):
        for n in (0, 1):
            got_e[k, n].wait_recv()
    for k in (1, 3):
        for n in (0, 1):
            got_d[k, n].wait_recv()
    for k in (2, 4):
        got_m[k].wait_recv()
    for copy in kept:
        copy.wait()
    wire.finish((got_r,))


def run_back(
    dx_own, grad, first, table, tiny, v, tokens, qkv, lse, cos, sin, seg_ids,
    dx_in, grads, mix_sum, attn, xn, in_all, out_all,
):
    any_spec = pl.BlockSpec(memory_space=pl.ANY)
    vmem = pl.BlockSpec(memory_space=pltpu.VMEM)
    length, width = tokens.shape
    shard = width // 8
    cols = grads.shape[1]
    cols_p, cols_a = qkv.shape[1] // 4, attn.shape[1] // 2
    return pl.pallas_call(
        back_kernel,
        out_shape=[
            jax.ShapeDtypeStruct((length, width), bf16),
            jax.ShapeDtypeStruct((8, shard, cols), bf16),
            jax.ShapeDtypeStruct((2, length, width), bf16),
            jax.ShapeDtypeStruct((4, shard + TERMS, cols_p + cols_a // 2), bf16),
            jax.ShapeDtypeStruct((length, width), bf16),
        ],
        in_specs=[vmem] * 12 + [any_spec] * 7,
        out_specs=[vmem] + [any_spec] * 4,
        scratch_shapes=[
            pltpu.VMEM(in_all.shape, bf16),
            pltpu.VMEM(out_all.shape, bf16),
            pltpu.VMEM((2, length, width), bf16),
            pltpu.VMEM((4, shard, cols), bf16),
            pltpu.VMEM((4, shard, cols), bf16),
            pltpu.VMEM((3, shard, cols), bf16),
            pltpu.VMEM((4 * length, width), bf16),
            pltpu.VMEM((2 * length, cols_a), bf16),
            pltpu.VMEM((4 * length, cols_p), bf16),
            pltpu.VMEM((width, cols_a), bf16),
            pltpu.VMEM((width + 8 * TERMS, cols_p), bf16),
            pltpu.VMEM((4, shard, cols_a), bf16),
            pltpu.VMEM((4, shard + TERMS, cols_p), bf16),
            pltpu.VMEM((3, shard, cols_a), bf16),
            pltpu.VMEM((3, shard + TERMS, cols_p), bf16),
            pltpu.VMEM((2, shard, cols_a), bf16),
            pltpu.VMEM((shard + TERMS, cols_p + cols_a // 2), bf16),
            pltpu.VMEM((length, width), f32),
            pltpu.VMEM((length, width), f32),
            pltpu.VMEM((length, EXTRA), bf16),
            pltpu.VMEM((length, WQ), bf16),
            pltpu.VMEM(qkv.shape, bf16),
            pltpu.VMEM((2, length, HD), f32),
            pltpu.VMEM((length, length), f32),
            pltpu.VMEM((TERMS, width), f32),
            pltpu.SemaphoreType.DMA((20,)),
            pltpu.SemaphoreType.DMA((BACK_SENDS,)),
            pltpu.SemaphoreType.DMA((BACK_SENDS,)),
        ],
        compiler_params=pltpu.CompilerParams(
            collective_id=3, has_side_effects=True, vmem_limit_bytes=62 * MIB
        ),
        name="back",
    )(
        dx_own, grad, first, table, tiny, v, tokens, qkv, lse, cos, sin,
        seg_ids,
        dx_in, grads, mix_sum, attn, xn, in_all, out_all,
    )


def finish_kernel(sums, dense, first, own, parts, e_in, e_out, in_grad, out_grad, mixed):
    split = e_in.shape[2]
    for c in range(0, sums.shape[2], 128):
        part = jnp.swapaxes(sums[:, :, c : c + 128].astype(f32), 0, 1)
        if c < split:
            e_in[:, :, c : c + 128] = part
        else:
            e_out[:, :, c - split : c - split + 128] = part
    cut = in_grad.shape[1] // 4
    quarter = out_grad.shape[1] // 4
    for r in range(4):
        in_grad[:, r * cut : (r + 1) * cut] = dense[r, :, :cut].astype(f32)
        place = 2 * (r % 2) + r // 2
        out_grad[:, place * quarter : (place + 1) * quarter] = dense[r, :, cut:].astype(f32)
    total = first[...] + own[0].astype(f32)
    for n in range(parts.shape[0]):
        total = total + parts[n].astype(f32)
    mixed[...] = total.astype(bf16)


def run_finish(expert_sum, dense, first, mix_sum, mix_in, hidden):
    n_experts, shard, cols = expert_sum.shape
    length, width = first.shape
    steps = 6
    rows, tokens = shard // steps, length // steps
    cut = dense.shape[2] - width // 4
    return pl.pallas_call(
        finish_kernel,
        grid=(steps,),
        out_shape=[
            jax.ShapeDtypeStruct((shard, n_experts, 2 * hidden), f32),
            jax.ShapeDtypeStruct((shard, n_experts, hidden), f32),
            jax.ShapeDtypeStruct((shard, 4 * cut), f32),
            jax.ShapeDtypeStruct((shard, width), f32),
            jax.ShapeDtypeStruct((length, width), bf16),
        ],
        in_specs=[
            pl.BlockSpec((n_experts, rows, cols), lambda i: (0, i, 0)),
            pl.BlockSpec((4, rows, dense.shape[2]), lambda i: (0, i, 0)),
            pl.BlockSpec((tokens, width), lambda i: (i, 0)),
            pl.BlockSpec((1, tokens, width), lambda i: (0, i, 0)),
            pl.BlockSpec((mix_in.shape[0], tokens, width), lambda i: (0, i, 0)),
        ],
        out_specs=[
            pl.BlockSpec((rows, n_experts, 2 * hidden), lambda i: (i, 0, 0)),
            pl.BlockSpec((rows, n_experts, hidden), lambda i: (i, 0, 0)),
            pl.BlockSpec((rows, 4 * cut), lambda i: (i, 0)),
            pl.BlockSpec((rows, width), lambda i: (i, 0)),
            pl.BlockSpec((tokens, width), lambda i: (i, 0)),
        ],
        compiler_params=pltpu.CompilerParams(vmem_limit_bytes=62 * MIB),
        name="finish",
    )(expert_sum, dense, first, mix_sum, mix_in)


def near_layer(
    tokens, seg_ids, routes, in_proj, out_proj, router, norm_gains, expert_in, expert_out,
    out_grad,
):
    length, width = tokens.shape
    experts = router.shape[1]
    hidden = expert_out.shape[2]
    shard = router.shape[0]
    f = lax.axis_index("fsdp")
    cosine, sine = [t[:, 0] for t in tables(length)]
    cos = jnp.concatenate([cosine, cosine], axis=1)
    sin = jnp.concatenate([-sine, sine], axis=1)
    tiny = jnp.concatenate(
        [router.T, norm_gains.T, jnp.zeros((16 - experts - 2, shard), bf16)], axis=0
    )
    none = jnp.zeros_like(tiny)
    tiny = jnp.where(
        f % 2 == 0,
        jnp.concatenate([tiny, none], axis=1),
        jnp.concatenate([none, tiny], axis=1),
    )
    qkv, attn, xn, first, lse, table, small, v, in_all, out_all, w_all, g_all, xs = front(
        tokens, seg_ids, routes, cos, sin, in_proj, out_proj, tiny, expert_in, expert_out,
        out_grad,
    )
    mix_sum, dx_own, dx_in, grads, _, _ = run_group(v, out_grad, xs, g_all, w_all)
    tokens_grad, expert_sum, mix_in, dense, _ = run_back(
        dx_own, out_grad, first, table, small, v, tokens, qkv, lse, cos, sin, seg_ids,
        dx_in, grads, mix_sum, attn, xn, in_all, out_all,
    )
    e_in, e_out, in_grad, out_proj_grad, mixed = run_finish(
        expert_sum, dense, first, mix_sum, mix_in, hidden
    )
    terms = jnp.sum(dense[:, shard:, : 2 * shard].astype(f32), axis=0)
    terms = jnp.where(f % 2 == 0, terms[:, :shard], terms[:, shard:]).T
    return (
        mixed,
        tokens_grad,
        in_grad,
        out_proj_grad,
        terms[:, :experts],
        terms[:, experts : experts + 2],
        e_in,
        e_out,
    )


class Wide:
    def __init__(self, n_rep, n_fsdp):
        self.n_rep, self.n_fsdp = n_rep, n_fsdp

    def spread(self, value):
        every = lax.all_gather(value, "replica", axis=0)
        return [every[k] for k in range(self.n_rep)]

    def collect(self, parts):
        return lax.psum_scatter(jnp.stack(parts), "replica", scatter_dimension=0).astype(f32)

    def start(self, in_proj, out_proj, tiny, expert_in, expert_out, grad):
        r = lax.axis_index("replica")
        per = expert_in.shape[1] // self.n_rep
        weights = []
        for i in range(per):
            both = jnp.concatenate(
                [
                    lax.dynamic_index_in_dim(expert_in, per * r + i, 1, keepdims=False),
                    lax.dynamic_index_in_dim(expert_out, per * r + i, 1, keepdims=False),
                ],
                axis=1,
            )
            weights.append(lax.all_gather(both, "fsdp", axis=0, tiled=True))
        return (
            lax.all_gather(in_proj, "fsdp", axis=0, tiled=True),
            lax.all_gather(out_proj, "fsdp", axis=0, tiled=True),
            lax.all_gather(tiny, "fsdp", axis=1, tiled=True),
            (weights, self.spread(grad)),
        )

    def experts(self, payload, held):
        weights, gs = held
        xs = self.spread(payload)
        per = len(weights)
        mixes, dxs, grads = None, None, []
        for i, w in enumerate(weights):

            def expert_of(i=i):
                return per * lax.axis_index("replica") + i

            mix, dx, grad = run_expert(xs, gs, [w], expert_of, lambda j: 0)
            mixes = mix if mixes is None else [a + b for a, b in zip(mixes, mix)]
            dxs = dx if dxs is None else [a + b for a, b in zip(dxs, dx)]
            grads.append(grad[0])
        return self.collect(dxs), (mixes, grads)

    def trade(self, value):
        cut = value.reshape(value.shape[0], self.n_rep, -1).transpose(1, 0, 2)
        got = lax.all_to_all(cut, "replica", 0, 0)
        return got.reshape(-1, got.shape[2])

    def end(self, held, first, normed, attn, dres, dproj, terms):
        mixes, grads = held
        mixed = first + self.collect(mixes)
        own = jnp.stack(
            [lax.psum_scatter(g, "fsdp", scatter_dimension=0, tiled=True) for g in grads]
        )
        expert_sum = lax.all_gather(own, "replica", axis=0, tiled=True).transpose(1, 0, 2)
        dense = []
        for left, right in ((normed, dproj), (dres, attn)):
            left = lax.all_gather(left, "replica", axis=0, tiled=True)
            part = contract_rows(left, self.trade(right)).astype(bf16)
            own = lax.psum_scatter(part, "fsdp", scatter_dimension=0, tiled=True)
            dense.append(lax.all_gather(own, "replica", axis=1, tiled=True))
        return mixed, dense[0], dense[1], expert_sum, lax.psum(terms, ("replica", "fsdp"))


def layer(
    net, tokens, seg_ids, routes, in_proj, out_proj, router, norm_gains, expert_in, expert_out,
    out_grad,
):
    length, width = tokens.shape
    experts = router.shape[1]
    hidden = expert_out.shape[2]
    shard = router.shape[0]
    scale = HD ** (-0.5)
    cosine, sine = tables(length)
    segment = seg_ids[0]
    place = jnp.arange(length)
    allowed = ((place[:, None] >= place[None, :]) & (segment[:, None] == segment[None, :]))[
        None, None
    ]
    tiny = jnp.concatenate(
        [router.T, norm_gains.T, jnp.zeros((16 - experts - 2, shard), bf16)], axis=0
    )
    proj_in, proj_out, tiny, held = net.start(
        in_proj, out_proj, tiny, expert_in, expert_out, out_grad
    )
    router_rows = tiny[:experts]
    gain_one = tiny[experts].astype(f32)
    gain_two = tiny[experts + 1].astype(f32)

    inputs = tokens.astype(f32)
    scale_one = rms_scale(inputs)
    unit_one = inputs * scale_one
    normed = (unit_one * gain_one).astype(bf16)
    proj = matmul(normed, proj_in)
    queries = (
        rotate(proj[:, :WQ].reshape(length, HQ, HD), cosine, sine)
        .astype(bf16)
        .reshape(length, KV, GROUP, HD)
    )
    keys = rotate(proj[:, WQ : WQ + WK].reshape(length, KV, HD), cosine, sine).astype(bf16)
    values = proj[:, WQ + WK :].reshape(length, KV, HD).astype(bf16)
    scores = jnp.einsum("qkgd,tkd->kgqt", queries, keys, preferred_element_type=f32) * scale
    masked = jnp.where(allowed, scores, -1e30)
    highest = jnp.max(masked, axis=-1, keepdims=True)
    expo = jnp.exp(masked - highest)
    total = jnp.sum(expo, axis=-1, keepdims=True)
    log_total = highest + jnp.log(total)
    probs_low = (expo / total).astype(bf16)
    attn = jnp.einsum("kgqt,tkd->qkgd", probs_low, values, preferred_element_type=f32)
    attn = attn.astype(bf16).reshape(length, WQ)
    first = inputs + contract_cols(attn, proj_out)
    scale_two = rms_scale(first)
    unit_two = first * scale_two
    normed_two = (unit_two * gain_two).astype(bf16)
    logits = contract_cols(normed_two, router_rows)
    onehot = (routes[:, :, None] == jnp.arange(experts)[None, None, :]).astype(f32)
    chosen = jnp.sum(onehot * logits[:, None, :], axis=-1)
    gates = jax.nn.softmax(chosen, axis=-1)
    table = jnp.sum(gates[:, :, None] * onehot, axis=1)
    high = table.astype(bf16)
    low = (table - high.astype(f32)).astype(bf16)
    payload = jnp.concatenate(
        [normed_two, high, low, jnp.zeros((length, EXTRA - 2 * experts), bf16)], axis=1
    )
    dx, held = net.experts(payload, held)

    grad_out = out_grad.astype(f32)
    dgate_all = dx[:, width : width + experts] + dx[:, width + experts : width + 2 * experts]
    dgate = jnp.sum(onehot * dgate_all[:, None, :], axis=-1)
    dchosen = gates * (dgate - jnp.sum(gates * dgate, axis=-1, keepdims=True))
    dlogits = jnp.sum(dchosen[:, :, None] * onehot, axis=1).astype(bf16)
    dnormed_two = dx[:, :width] + matmul(dlogits, router_rows)
    gain_two_grad = jnp.sum(dnormed_two * unit_two, axis=0)
    dunit_two = dnormed_two * gain_two
    dfirst = grad_out + scale_two * (
        dunit_two - unit_two * jnp.mean(dunit_two * unit_two, axis=-1, keepdims=True)
    )
    dres = dfirst.astype(bf16)
    dattn = matmul(dres, proj_out).astype(bf16).reshape(length, KV, GROUP, HD)
    probs = jnp.exp(masked - log_total)
    probs_again = probs.astype(bf16)
    dprobs = jnp.einsum("qkgd,tkd->kgqt", dattn, values, preferred_element_type=f32)
    dvalues = jnp.einsum("kgqt,qkgd->tkd", probs_again, dattn, preferred_element_type=f32)
    delta = jnp.sum(probs * dprobs, axis=-1, keepdims=True)
    dscores = (probs * (dprobs - delta)).astype(bf16)
    dqueries = jnp.einsum("kgqt,tkd->qkgd", dscores, keys, preferred_element_type=f32) * scale
    dkeys = jnp.einsum("kgqt,qkgd->tkd", dscores, queries, preferred_element_type=f32) * scale
    dqueries = rotate(dqueries.reshape(length, HQ, HD), cosine, -sine).reshape(length, WQ)
    dkeys = rotate(dkeys, cosine, -sine).reshape(length, WK)
    dproj = jnp.concatenate([dqueries, dkeys, dvalues.reshape(length, WK)], axis=1).astype(bf16)
    dnormed = contract_cols(dproj, proj_in)
    gain_one_grad = jnp.sum(dnormed * unit_one, axis=0)
    dunit_one = dnormed * gain_one
    tokens_grad = (
        dfirst
        + scale_one
        * (dunit_one - unit_one * jnp.mean(dunit_one * unit_one, axis=-1, keepdims=True))
    ).astype(bf16)

    terms = jnp.concatenate(
        [
            contract_rows(dlogits, normed_two),
            gain_one_grad[None],
            gain_two_grad[None],
            jnp.zeros((16 - experts - 2, width), f32),
        ],
        axis=0,
    )
    mixed, in_proj_grad, out_proj_grad, expert_sum, terms = net.end(
        held, first, normed, attn, dres, dproj, terms
    )
    terms = lax.dynamic_slice_in_dim(terms, lax.axis_index("fsdp") * shard, shard, 1).T
    return (
        mixed.astype(bf16),
        tokens_grad,
        in_proj_grad.astype(f32),
        out_proj_grad.astype(f32),
        terms[:, :experts],
        terms[:, experts : experts + 2],
        expert_sum[..., : 2 * hidden].astype(f32),
        expert_sum[..., 2 * hidden :].astype(f32),
    )


def solution(mesh):
    n_rep, n_fsdp = mesh.shape["replica"], mesh.shape["fsdp"]
    if (n_rep, n_fsdp) == (4, 8):
        body = near_layer
    else:
        body = functools.partial(layer, Wide(n_rep, n_fsdp))
    both = P(("replica", "fsdp"), None)
    fsdp, deep = P("fsdp", None), P("fsdp", None, None)
    return jax.shard_map(
        body,
        mesh=mesh,
        in_specs=(both, both, both, fsdp, fsdp, fsdp, fsdp, deep, deep, both),
        out_specs=(both, both, fsdp, fsdp, fsdp, fsdp, deep, deep),
        check_vma=False,
    )
```

```python
import functools

import jax
import jax.numpy as jnp
from jax import lax
from jax.experimental import pallas as pl
from jax.experimental.pallas import tpu as pltpu
from jax.sharding import PartitionSpec as P

HQ = 12
KV = 2
HD = 128
GROUP = HQ // KV
WQ = HQ * HD
WK = KV * HD
EXTRA = 128
MIB = 1024 * 1024

epsilon = 1e-06
rope_base = 1000000.0
bf16 = jnp.bfloat16
f32 = jnp.float32


def rms_scale(v):
    return lax.rsqrt(jnp.mean(v * v, axis=-1, keepdims=True) + epsilon)


def tables(length):
    half = HD // 2
    freq = jnp.power(rope_base, -(jnp.arange(half, dtype=f32) * 2.0 / HD))
    angle = jnp.arange(length, dtype=f32)[:, None] * freq[None, :]
    return (jnp.cos(angle)[:, None, :], jnp.sin(angle)[:, None, :])


def rotate(v, cosine, sine):
    half = v.shape[-1] // 2
    first = v[..., :half]
    second = v[..., half:]
    return jnp.concatenate(
        [first * cosine - second * sine, second * cosine + first * sine], axis=-1
    )


def contract_rows(left, right):
    return lax.dot_general(left, right, (((0,), (0,)), ((), ())), preferred_element_type=f32)


def contract_cols(left, right):
    return lax.dot_general(left, right, (((1,), (1,)), ((), ())), preferred_element_type=f32)


def matmul(left, right):
    return lax.dot_general(left, right, (((1,), (0,)), ((), ())), preferred_element_type=f32)


def expert_kernel(nt, nw, length, width, hidden, rows, expert_of, offset_of, *refs):
    xs, gs, ws = refs[:nt], refs[nt : 2 * nt], refs[2 * nt : 2 * nt + nw]
    refs = refs[2 * nt + nw :]
    mixes, dxs, grads = refs[:nt], refs[nt : 2 * nt], refs[2 * nt : 2 * nt + nw]
    (
        wbuf, xbuf, gbuf, xt, gt_, hidg, dgu, mbuf, dbuf, acc, stage,
        sem_w, sem_x, sem_g, sem_m, sem_d, sem_s,
    ) = refs[2 * nt + nw :]
    cols = 3 * hidden
    step_cols = 256

    def load(k, slot):
        for i in range(nt):

            @pl.when(k == i)
            def _():
                pltpu.make_async_copy(xs[i], xbuf.at[slot], sem_x.at[slot]).start()
                pltpu.make_async_copy(gs[i], gbuf.at[slot], sem_g.at[slot]).start()

    def store(k, slot):
        for i in range(nt):

            @pl.when(k == i)
            def _():
                pltpu.make_async_copy(mbuf.at[slot], mixes[i], sem_m.at[slot]).start()
                pltpu.make_async_copy(dbuf.at[slot], dxs[i], sem_d.at[slot]).start()

    def stored(slot):
        pltpu.make_async_copy(mbuf.at[slot], mixes[0], sem_m.at[slot]).wait()
        pltpu.make_async_copy(dbuf.at[slot], dxs[0], sem_d.at[slot]).wait()

    for j in range(nw):
        pltpu.make_async_copy(
            ws[j], wbuf.at[pl.ds(pl.multiple_of(offset_of(j), 8), rows)], sem_w.at[j]
        ).start()
    load(0, 0)
    expert = expert_of()
    acc[...] = jnp.zeros_like(acc)
    lane = lax.broadcasted_iota(jnp.int32, (length, EXTRA), 1)
    for j in range(nw):
        pltpu.make_async_copy(
            ws[j], wbuf.at[pl.ds(pl.multiple_of(offset_of(j), 8), rows)], sem_w.at[j]
        ).wait()

    def block(k, carry):
        slot = lax.rem(k, 2)

        @pl.when(k + 1 < nt)
        def _():
            load(k + 1, 1 - slot)

        pltpu.make_async_copy(xs[0], xbuf.at[slot], sem_x.at[slot]).wait()
        pltpu.make_async_copy(gs[0], gbuf.at[slot], sem_g.at[slot]).wait()

        @pl.when(k >= 2)
        def _():
            stored(slot)

        extra = xbuf[slot, :, width:].astype(f32)
        mine = (lane == expert) | (lane == expert + 8)
        gate = jnp.sum(jnp.where(mine, extra, 0.0), axis=1, keepdims=True)
        xt[...] = xbuf[slot, :, :width].T
        gt_[...] = gbuf[slot].T

        def first(c, dgate):
            at = pl.multiple_of(c * step_cols, step_cols)
            u = matmul(xbuf[slot, :, :width], wbuf[:, pl.ds(at, step_cols)])
            up = matmul(xbuf[slot, :, :width], wbuf[:, pl.ds(hidden + at, step_cols)])
            back = matmul(gbuf[slot], wbuf[:, pl.ds(2 * hidden + at, step_cols)])
            sig = 1.0 / (1.0 + jnp.exp(-u))
            act = u * sig
            hid = act * up
            hidg[:, pl.ds(at, step_cols)] = (gate * hid).astype(bf16)
            dgate = dgate + jnp.sum(back * hid, axis=1, keepdims=True)
            dhid = gate * back
            dgu[:, pl.ds(at, step_cols)] = (
                dhid * up * sig * (1.0 + u * (1.0 - sig))
            ).astype(bf16)
            dgu[:, pl.ds(hidden + at, step_cols)] = (dhid * act).astype(bf16)
            return dgate

        dgate = lax.fori_loop(
            0, hidden // step_cols, first, jnp.zeros((length, 1), f32)
        )

        def second(c, carry):
            at = pl.multiple_of(c * step_cols, step_cols)
            mbuf[slot, :, pl.ds(at, step_cols)] = contract_cols(
                hidg[...], wbuf[pl.ds(at, step_cols), pl.ds(2 * hidden, hidden)]
            ).astype(bf16)
            dbuf[slot, :, pl.ds(at, step_cols)] = contract_cols(
                dgu[...], wbuf[pl.ds(at, step_cols), pl.ds(0, 2 * hidden)]
            ).astype(bf16)
            return carry

        lax.fori_loop(0, width // step_cols, second, 0)
        high = dgate.astype(bf16).astype(f32)
        low = dgate - high
        dbuf[slot, :, width:] = (
            jnp.where(lane == expert, high, 0.0) + jnp.where(lane == expert + 8, low, 0.0)
        ).astype(bf16)
        store(k, slot)

        def third(c, carry):
            at = pl.multiple_of(c * step_cols, step_cols)
            acc[:, pl.ds(at, step_cols)] += matmul(xt[...], dgu[:, pl.ds(at, step_cols)])
            return carry

        lax.fori_loop(0, 2 * hidden // step_cols, third, 0)

        def fourth(c, carry):
            at = pl.multiple_of(c * step_cols, step_cols)
            acc[:, pl.ds(2 * hidden + at, step_cols)] += matmul(
                gt_[...], hidg[:, pl.ds(at, step_cols)]
            )
            return carry

        lax.fori_loop(0, hidden // step_cols, fourth, 0)
        return carry

    lax.fori_loop(0, nt, block, 0)
    stored(0)
    stored(1)
    for j in range(nw):
        slot = j % 2
        if j >= 2:
            pltpu.make_async_copy(stage.at[slot], grads[j - 2], sem_s.at[slot]).wait()
        stage[slot] = acc[pl.ds(pl.multiple_of(offset_of(j), 8), rows)].astype(bf16)
        pltpu.make_async_copy(stage.at[slot], grads[j], sem_s.at[slot]).start()
    for j in range(max(0, nw - 2), nw):
        pltpu.make_async_copy(stage.at[j % 2], grads[j], sem_s.at[j % 2]).wait()


def run_expert(xs, gs, ws, expert_of, offset_of):
    nt, nw = len(xs), len(ws)
    length, width = gs[0].shape
    rows, cols = ws[0].shape
    hidden = cols // 3
    outs = (
        [jax.ShapeDtypeStruct((length, width), bf16)] * nt
        + [jax.ShapeDtypeStruct((length, width + EXTRA), bf16)] * nt
        + [jax.ShapeDtypeStruct((rows, cols), bf16)] * nw
    )
    any_spec = pl.BlockSpec(memory_space=pl.ANY)
    result = pl.pallas_call(
        functools.partial(
            expert_kernel, nt, nw, length, width, hidden, rows, expert_of, offset_of
        ),
        out_shape=outs,
        in_specs=[any_spec] * (2 * nt + nw),
        out_specs=[any_spec] * len(outs),
        scratch_shapes=[
            pltpu.VMEM((width, cols), bf16),
            pltpu.VMEM((2, length, width + EXTRA), bf16),
            pltpu.VMEM((2, length, width), bf16),
            pltpu.VMEM((width, length), bf16),
            pltpu.VMEM((width, length), bf16),
            pltpu.VMEM((length, hidden), bf16),
            pltpu.VMEM((length, 2 * hidden), bf16),
            pltpu.VMEM((2, length, width), bf16),
            pltpu.VMEM((2, length, width + EXTRA), bf16),
            pltpu.VMEM((width, cols), f32),
            pltpu.VMEM((2, rows, cols), bf16),
            pltpu.SemaphoreType.DMA((nw,)),
            pltpu.SemaphoreType.DMA((2,)),
            pltpu.SemaphoreType.DMA((2,)),
            pltpu.SemaphoreType.DMA((2,)),
            pltpu.SemaphoreType.DMA((2,)),
            pltpu.SemaphoreType.DMA((2,)),
        ],
        compiler_params=pltpu.CompilerParams(vmem_limit_bytes=60 * MIB),
        cost_estimate=pl.CostEstimate(
            flops=6 * nt * length * width * cols,
            bytes_accessed=8 * nt * length * width + 4 * width * cols,
            transcendentals=nt * length * hidden,
        ),
        name="expert",
    )(*xs, *gs, *ws)
    return result[:nt], result[nt : 2 * nt], result[2 * nt :]


MESH_ID = pl.DeviceIdType.MESH


def flip(index, bit):
    return index + bit - 2 * bit * lax.rem(index // bit, 2)


def flips(index, mask):
    for bit in (1, 2, 4):
        if mask & bit:
            index = flip(index, bit)
    return index


class Wire:
    def __init__(self, send_sem, recv_sem):
        self.r, self.f = lax.axis_index("replica"), lax.axis_index("fsdp")
        self.send_sem, self.recv_sem = send_sem, recv_sem
        self.used, self.sent = 0, []

    def meet(self, partners):
        barrier = pltpu.get_barrier_semaphore()
        for d_r, d_f in partners:
            pl.semaphore_signal(
                barrier, inc=1, device_id=self.at(d_r, d_f), device_id_type=MESH_ID
            )
        pl.semaphore_wait(barrier, len(partners))

    def at(self, d_r, d_f):
        return (flips(self.r, d_r), flips(self.f, d_f))

    def plan(self, src, dst, d_r, d_f):
        copy = pltpu.make_async_remote_copy(
            src_ref=src,
            dst_ref=dst,
            send_sem=self.send_sem.at[self.used],
            recv_sem=self.recv_sem.at[self.used],
            device_id=self.at(d_r, d_f),
            device_id_type=MESH_ID,
        )
        self.used += 1
        assert self.used <= self.send_sem.shape[0]
        return copy

    def send(self, src, dst, d_r, d_f):
        copy = self.plan(src, dst, d_r, d_f)
        copy.start()
        self.sent.append(copy)
        return copy

    def finish(self, waited=()):
        for copy in self.sent:
            if all(copy is not other for other in waited):
                copy.wait_send()


CUTS = 4
FRONT_SENDS = 2 * 28 + 7 + 7 * CUTS + 4 + 3
PARTNERS = ((1, 0), (2, 0), (0, 1), (0, 2), (0, 4), (0, 6))
ROWS = 64


def as_columns(rows):
    rows = rows.astype(f32)
    rest = jnp.zeros((128 - rows.shape[0], rows.shape[1]), f32)
    return jnp.concatenate([rows, rest], axis=0).T


def turn(v, cosine, sine):
    return v * cosine + pltpu.roll(v, HD // 2, 1) * sine


def front_kernel(
    tokens, seg_row, routes, cos, sin,
    in_ref, out_ref, tiny_ref, e_in_ref, e_out_ref, g_ref,
    qkv_o, attn_o, xn_o, first_o, lse, table, tiny_out, v_o,
    in_all, out_all, w_all, g_all, xs,
    in_v, out_v, tiny_v, rt, bias, e_in, e_out, e_part, mine_ref, other_ref,
    qkv, attn, xn, first, v, local_sem, send_sem, recv_sem,
):
    wire = Wire(send_sem, recv_sem)
    r, f = wire.r, wire.f
    shard = in_ref.shape[0]
    quarter = shard // 4
    length, width = tokens.shape
    experts = 8
    scale = HD ** (-0.5)

    def rows(j, k):
        at = flips(f, j) * shard + flips(r, k) * quarter
        return pl.ds(pl.multiple_of(at, quarter), quarter)

    def shard_rows(j):
        return pl.ds(pl.multiple_of(flips(f, j) * shard, shard), shard)

    def local(n, src, dst):
        copy = pltpu.make_async_copy(src, dst, local_sem.at[n])
        copy.start()
        return copy

    own_in = local(0, in_ref, in_v.at[shard_rows(0)])
    own_out = local(1, out_ref, out_v.at[shard_rows(0)])
    own_tiny = local(2, tiny_ref, tiny_v.at[f])
    own_w = (local(3, e_in_ref, e_in), local(7, e_out_ref, e_out))
    wire.meet(PARTNERS)

    own = pl.ds(pl.multiple_of(r * quarter, quarter), quarter)
    land = {"in": in_v, "out": out_v}
    source = {"in": in_ref, "out": out_ref}
    got, got_t, got_w, got_g, got_x = {}, {}, {}, {}, {}

    for m in (2, 4, 6, 1):
        got_t[m] = wire.send(tiny_ref, tiny_v.at[f], 0, m)

    def own_pieces(name):
        for m in (2, 4, 6, 1):
            got[name, m, 0] = wire.send(
                source[name].at[own], land[name].at[rows(0, 0)], 0, m
            )

    def pass_on(name, j, k, d_r, d_f):
        at = land[name].at[rows(j, k)]
        return wire.send(at, at, d_r, d_f)

    def near_pieces(name):
        for m in (1, 2, 4, 6):
            got[name, m, 0].wait_recv()
            if m != 1:
                got[name, m + 1, 0] = pass_on(name, m, 0, 0, 1)
            got[name, m, 2] = pass_on(name, m, 0, 2, 0)
            got[name, m, 1] = pass_on(name, m, 0, 1, 0)

    def far_pieces(name):
        for m in (3, 5, 7):
            got[name, m, 0].wait_recv()
            got[name, m, 2] = pass_on(name, m, 0, 2, 0)
            got[name, m, 1] = pass_on(name, m, 0, 1, 0)

    def side_pieces(name):
        for m in (1, 2, 4, 6, 3, 5, 7):
            got[name, m, 2].wait_recv()
            got[name, m, 3] = pass_on(name, m, 2, 1, 0)

    def all_pieces(name):
        for m in range(1, 8):
            got[name, m, 1].wait_recv()
            got[name, m, 3].wait_recv()

    own_pieces("in")
    own_pieces("out")

    for m in (2, 4, 6):
        got_t[m].wait_recv()
        at = tiny_v.at[flips(f, m)]
        got_t[m + 1] = wire.send(at, at, 0, 1)
    for m in (1, 3, 5, 7):
        got_t[m].wait_recv()
    own_tiny.wait()
    lanes = tiny_v.shape[2]
    rt[...] = jnp.zeros_like(rt)
    for z in range(4):
        both = tiny_v[2 * z].astype(f32) + tiny_v[2 * z + 1].astype(f32)
        tiny_out[:, z * lanes : (z + 1) * lanes] = both
        row = lax.broadcasted_iota(jnp.int32, both.shape, 0)
        rt[0:16, z * lanes : (z + 1) * lanes] = jnp.where(row < experts, both, 0.0).astype(bf16)

    def norm_one(c, carry):
        at = pl.ds(pl.multiple_of(c * ROWS, ROWS), ROWS)
        x = tokens[at, :].astype(f32)
        unit = x * lax.rsqrt(jnp.mean(x * x, axis=-1, keepdims=True) + epsilon)
        xn[at, :] = (unit * tiny_out[experts : experts + 1, :]).astype(bf16)
        return carry

    lax.fori_loop(0, length // ROWS, norm_one, 0)
    spot = lax.broadcasted_iota(jnp.int32, bias.shape, 0)
    keys_at = lax.broadcasted_iota(jnp.int32, bias.shape, 1)
    seg_col = as_columns(seg_row[...])[:, 0:1].astype(jnp.int32)
    bias[...] = jnp.where((spot >= keys_at) & (seg_col == seg_row[...]), 0.0, -1e30)

    for copy in own_w:
        copy.wait()
    plane = lax.rem(f // 2, 2)
    split = e_in.shape[2]
    for c in range(0, mine_ref.shape[1], 128):
        part = e_in[:, :, c : c + 128] if c < split else e_out[:, :, c - split : c - split + 128]
        e_part[...] = jnp.swapaxes(part.astype(f32), 0, 1)
        mine_ref[:, c : c + 128] = e_part[2 * r + plane].astype(bf16)
        other_ref[:, c : c + 128] = e_part[2 * r + 1 - plane].astype(bf16)
    kept = [local(4, mine_ref, w_all.at[shard_rows(0)])]
    cut = shard // CUTS

    def send_w(n, src, d_f):
        at = pl.ds(n * cut, cut)
        to = pl.ds(pl.multiple_of(f * shard + n * cut, cut), cut)
        return wire.send(src.at[at], w_all.at[to], 0, d_f)

    def pass_w(n, m):
        got_w[m, n].wait_recv()
        at = w_all.at[pl.ds(pl.multiple_of(flips(f, m) * shard + n * cut, cut), cut)]
        got_w[m + 1, n] = wire.send(at, at, 0, 1)

    near_pieces("in")
    for n in range(CUTS):
        for m, src in ((2, other_ref), (4, mine_ref), (6, other_ref)):
            got_w[m, n] = send_w(n, src, m)
    got_g[4] = wire.send(g_ref, g_all.at[4], 0, 2)
    got_g[1] = wire.send(g_ref, g_all.at[1], 1, 0)
    far_pieces("in")
    near_pieces("out")
    far_pieces("out")
    for n in range(CUTS):
        got_w[1, n] = send_w(n, mine_ref, 1)
    got_g[2] = wire.send(g_ref, g_all.at[2], 2, 0)
    side_pieces("in")
    own_in.wait()
    all_pieces("in")

    def project(c, carry):
        at = pl.multiple_of(c * 256, 256)
        t = matmul(xn[...], in_v[:, pl.ds(at, 256)])
        turned = c < 7
        for n in (0, 1):
            part = t[:, n * HD : (n + 1) * HD]
            part = turn(
                part, jnp.where(turned, cos[...], 1.0), jnp.where(turned, sin[...], 0.0)
            )
            qkv[:, pl.ds(at + n * HD, HD)] = part.astype(bf16)
        return carry

    lax.fori_loop(0, 8, project, 0)
    pass_w(0, 2)
    pass_w(0, 4)
    lane = lax.broadcasted_iota(jnp.int32, (length, HD), 1)
    lse[...] = jnp.zeros_like(lse)

    def head(h, carry):
        at = pl.ds(pl.multiple_of(h * HD, HD), HD)
        group = h // GROUP
        k_at = pl.ds(pl.multiple_of(WQ + group * HD, HD), HD)
        v_at = pl.ds(pl.multiple_of(WQ + WK + group * HD, HD), HD)
        s = contract_cols(qkv[:, at], qkv[:, k_at]) * scale + bias[...]
        highest = jnp.max(s, axis=-1, keepdims=True)
        expo = jnp.exp(s - highest)
        total = jnp.sum(expo, axis=-1, keepdims=True)
        p = (expo * (1.0 / total)).astype(bf16)
        attn[:, at] = matmul(p, qkv[:, v_at]).astype(bf16)
        lse[...] = jnp.where(lane == h, highest + jnp.log(total), lse[...])
        return carry

    lax.fori_loop(0, HQ // 2, head, 0)
    side_pieces("out")
    pass_w(0, 6)
    pass_w(1, 2)
    lax.fori_loop(HQ // 2, HQ, head, 0)
    pass_w(1, 4)
    pass_w(1, 6)
    own_out.wait()
    all_pieces("out")
    kept.append(local(5, in_v, in_all))
    kept.append(local(6, out_v, out_all))

    def add_out(c, carry):
        at = pl.ds(pl.multiple_of(c * 256, 256), 256)
        first[:, at] = tokens[:, at].astype(f32) + contract_cols(attn[...], out_v[at, :])
        return carry

    lax.fori_loop(0, width // 256, add_out, 0)

    def norm_two(c, carry):
        at = pl.ds(pl.multiple_of(c * ROWS, ROWS), ROWS)
        h = first[at, :]
        unit = h * lax.rsqrt(jnp.mean(h * h, axis=-1, keepdims=True) + epsilon)
        v[at, 0:width] = (unit * tiny_out[experts + 1 : experts + 2, :]).astype(bf16)
        return carry

    lax.fori_loop(0, length // ROWS, norm_two, 0)
    logits = contract_cols(v[:, 0:width], rt[...])
    named = as_columns(routes[...]).astype(jnp.int32)
    chosen = lane == named[:, 0:1]
    for j in range(1, routes.shape[0]):
        chosen = chosen | (lane == named[:, j : j + 1])
    logits = jnp.where(chosen, logits, -1e30)
    expo = jnp.exp(logits - jnp.max(logits, axis=-1, keepdims=True))
    expo = jnp.where(chosen, expo, 0.0)
    gates = expo / jnp.sum(expo, axis=-1, keepdims=True)
    table[...] = gates
    high = gates.astype(bf16).astype(f32)
    v[:, width:] = (high + pltpu.roll(gates - high, experts, 1)).astype(bf16)

    got_x[2] = wire.send(v, xs.at[2], 2, 0)
    got_x[1] = wire.send(v, xs.at[1], 1, 0)
    for n, (src, dst) in enumerate(
        ((qkv, qkv_o), (attn, attn_o), (xn, xn_o), (first, first_o), (v, v_o))
    ):
        kept.append(local(8 + n, src, dst))
    for n in range(2, CUTS):
        for m in (2, 4, 6):
            pass_w(n, m)
    got_g[2].wait_recv()
    got_g[3] = wire.send(g_all.at[2], g_all.at[3], 1, 0)
    got_x[2].wait_recv()
    got_x[3] = wire.send(xs.at[2], xs.at[3], 1, 0)
    for n in range(CUTS):
        for m in (1, 3, 5, 7):
            got_w[m, n].wait_recv()
    for m in (1, 3, 4):
        got_g[m].wait_recv()
    for m in (1, 3):
        got_x[m].wait_recv()
    for copy in kept:
        copy.wait()
    wire.finish()


def front(
    tokens, seg_ids, routes, cos, sin, in_proj, out_proj, tiny, expert_in, expert_out, grad
):
    any_spec = pl.BlockSpec(memory_space=pl.ANY)
    vmem = pl.BlockSpec(memory_space=pltpu.VMEM)
    length, width = tokens.shape
    shard, cols = in_proj.shape
    whole = 8 * shard
    wide = width + EXTRA
    e_cols = expert_in.shape[2] + expert_out.shape[2]
    return pl.pallas_call(
        front_kernel,
        out_shape=[
            jax.ShapeDtypeStruct((length, cols), bf16),
            jax.ShapeDtypeStruct((length, WQ), bf16),
            jax.ShapeDtypeStruct((length, width), bf16),
            jax.ShapeDtypeStruct((length, width), f32),
            jax.ShapeDtypeStruct((length, HD), f32),
            jax.ShapeDtypeStruct((length, EXTRA), f32),
            jax.ShapeDtypeStruct((16, width), f32),
            jax.ShapeDtypeStruct((length, wide), bf16),
            jax.ShapeDtypeStruct((whole, cols), bf16),
            jax.ShapeDtypeStruct((whole, out_proj.shape[1]), bf16),
            jax.ShapeDtypeStruct((whole, e_cols), bf16),
            jax.ShapeDtypeStruct((5,) + grad.shape, bf16),
            jax.ShapeDtypeStruct((4, length, wide), bf16),
        ],
        in_specs=[vmem] * 5 + [any_spec] * 6,
        out_specs=[any_spec] * 4 + [vmem] * 3 + [any_spec] * 6,
        scratch_shapes=[
            pltpu.VMEM((whole, cols), bf16),
            pltpu.VMEM((whole, out_proj.shape[1]), bf16),
            pltpu.VMEM((8,) + tiny.shape, bf16),
            pltpu.VMEM((EXTRA, width), bf16),
            pltpu.VMEM((length, length), f32),
            pltpu.VMEM(expert_in.shape, bf16),
            pltpu.VMEM(expert_out.shape, bf16),
            pltpu.VMEM((expert_in.shape[1], shard, 128), f32),
            pltpu.VMEM((shard, e_cols), bf16),
            pltpu.VMEM((shard, e_cols), bf16),
            pltpu.VMEM((length, cols), bf16),
            pltpu.VMEM((length, WQ), bf16),
            pltpu.VMEM((length, width), bf16),
            pltpu.VMEM((length, width), f32),
            pltpu.VMEM((length, wide), bf16),
            pltpu.SemaphoreType.DMA((13,)),
            pltpu.SemaphoreType.DMA((FRONT_SENDS,)),
            pltpu.SemaphoreType.DMA((FRONT_SENDS,)),
        ],
        compiler_params=pltpu.CompilerParams(
            collective_id=1, has_side_effects=True, vmem_limit_bytes=56 * MIB
        ),
        name="front",
    )(
        tokens, seg_ids, routes.T, cos, sin,
        in_proj, out_proj, tiny, expert_in, expert_out, grad,
    )


ORDER = (3, 2, 4, 5, 7, 6, 1, 0)
UNROLL = True
WIDE_COLS = 256
GROUP_AT = {2: (2, 0), 4: (0, 2), 6: (2, 2)}


def pick(step, table):
    value = jnp.int32(table[-1])
    for i, item in enumerate(table[:-1]):
        value = jnp.where(step == i, item, value)
    return value


def group_kernel(
    v_ref, g_ref, xs, g_all, w_ref,
    mix_sum, dx_own, dx_in, grads, x_late, g_late,
    wbuf, xbuf, gbuf, xt, gt_, hidg, dgu, deven, dodd, rc, meven, modd, mrc, acc, stage,
    sem_w, sem_x, sem_g, sem_m, sem_s, send_sem, recv_sem,
):
    wire = Wire(send_sem, recv_sem)
    r, f = wire.r, wire.f
    length, width = g_ref.shape
    hidden = w_ref.shape[1] // 3
    half = length // 2
    low, top = pl.ds(0, half), pl.ds(half, half)
    expert = 2 * r + lax.rem(f // 2, 2)
    step_cols = 256

    load_w = pltpu.make_async_copy(w_ref, wbuf, sem_w.at[0])
    load_w.start()

    def load(step):
        slot = lax.rem(step, 2)
        k = pick(step, ORDER)

        @pl.when(k == 0)
        def _():
            pltpu.make_async_copy(v_ref, xbuf.at[slot], sem_x.at[slot]).start()
            pltpu.make_async_copy(g_ref, gbuf.at[slot], sem_g.at[slot]).start()

        for table, src_x, src_g in (
            ((1, 2, 3), xs, g_all), ((4,), x_late, g_all), ((5, 6, 7), x_late, g_late)
        ):

            @pl.when((k >= table[0]) & (k <= table[-1]))
            def _():
                pltpu.make_async_copy(src_x.at[k], xbuf.at[slot], sem_x.at[slot]).start()
                pltpu.make_async_copy(src_g.at[k], gbuf.at[slot], sem_g.at[slot]).start()

    load(jnp.int32(0))
    wire.meet(PARTNERS_GROUP)
    late_x = {4: wire.send(v_ref, x_late.at[4], 0, 2)}
    far = [
        wire.send(g_all.at[4], g_late.at[6], 2, 0),
        wire.send(xs.at[2, top], x_late.at[6, top], 0, 2),
    ]
    late_g = {5: wire.send(g_all.at[4], g_late.at[5], 1, 0)}
    far.append(wire.plan(x_late.at[4, low], x_late.at[6, low], 2, 0))
    late_x[5] = wire.plan(x_late.at[4], x_late.at[5], 1, 0)
    late_x[7] = wire.plan(x_late.at[6], x_late.at[7], 1, 0)
    late_g[7] = wire.plan(g_late.at[6], g_late.at[7], 1, 0)
    slots = {2: 0, 4: 1, 6: 2, 0: 3}
    to_core = {k: wire.plan(dodd.at[n % 2], rc.at[n], 1, 0) for k, n in slots.items()}
    mix_core = {k: wire.plan(modd.at[n % 2], mrc.at[n], 1, 0) for k, n in slots.items()}
    back = {k: wire.plan(deven.at[k // 2], dx_in.at[k // 2 - 1], *GROUP_AT[k]) for k in (2, 4, 6)}
    acc[...] = jnp.zeros_like(acc)
    lane = lax.broadcasted_iota(jnp.int32, (length, EXTRA), 1)
    load_w.wait()

    def keep_mix(k):
        n = slots[k] % 2
        return pltpu.make_async_copy(meven.at[n], mix_sum.at[k // 2], sem_m.at[n])

    def send_core(k):
        to_core[k].start()
        mix_core[k].start()

    def sent_core(k):
        to_core[k].wait_send()
        mix_core[k].wait_send()

    def complete(k):
        n = slots[k]
        to_core[k].wait_recv()
        deven[k // 2] = (deven[k // 2].astype(f32) + rc[n].astype(f32)).astype(bf16)
        if k in (4, 6):
            back[k].start()
        mix_core[k].wait_recv()
        meven[n % 2] = (meven[n % 2].astype(f32) + mrc[n].astype(f32)).astype(bf16)
        keep_mix(k).start()

    def block(step, carry):
        slot = lax.rem(step, 2)

        @pl.when((step == 0) | (step >= 4) & (step < 7))
        def _():
            load(step + 1)

        pltpu.make_async_copy(v_ref, xbuf.at[slot], sem_x.at[slot]).wait()
        pltpu.make_async_copy(g_ref, gbuf.at[slot], sem_g.at[slot]).wait()
        extra = xbuf[slot, :, width:].astype(f32)
        mine = (lane == expert) | (lane == expert + 8)
        gate = jnp.sum(jnp.where(mine, extra, 0.0), axis=1, keepdims=True)
        here = pl.ds(pl.multiple_of(slot * length, length), length)
        xt[:, here] = xbuf[slot, :, :width].T
        gt_[:, here] = gbuf[slot].T

        def first(c, dgate):
            at = pl.multiple_of(c * step_cols, step_cols)
            u = matmul(xbuf[slot, :, :width], wbuf[:, pl.ds(at, step_cols)])
            up = matmul(xbuf[slot, :, :width], wbuf[:, pl.ds(hidden + at, step_cols)])
            rev = matmul(gbuf[slot], wbuf[:, pl.ds(2 * hidden + at, step_cols)])
            sig = 1.0 / (1.0 + jnp.exp(-u))
            act = u * sig
            hid = act * up
            hidg[here, pl.ds(at, step_cols)] = (gate * hid).astype(bf16)
            dgate = dgate + jnp.sum(rev * hid, axis=1, keepdims=True)
            dhid = gate * rev
            dgu[here, pl.ds(at, step_cols)] = (
                dhid * up * sig * (1.0 + u * (1.0 - sig))
            ).astype(bf16)
            dgu[here, pl.ds(hidden + at, step_cols)] = (dhid * act).astype(bf16)
            return dgate

        dgate = lax.fori_loop(
            0, hidden // step_cols, first, jnp.zeros((length, 1), f32), unroll=UNROLL
        )
        high = dgate.astype(bf16).astype(f32)
        rest = dgate - high
        tail = (
            jnp.where(lane == expert, high, 0.0) + jnp.where(lane == expert + 8, rest, 0.0)
        ).astype(bf16)

        def out_parts(dst_d, n_d, dst_m, n_m):
            def second(c, carry):
                at = pl.multiple_of(c * step_cols, step_cols)
                dst_d[n_d, :, pl.ds(at, step_cols)] = contract_cols(
                    dgu[here, :], wbuf[pl.ds(at, step_cols), pl.ds(0, 2 * hidden)]
                ).astype(bf16)
                dst_m[n_m, :, pl.ds(at, step_cols)] = contract_cols(
                    hidg[here, :], wbuf[pl.ds(at, step_cols), pl.ds(2 * hidden, hidden)]
                ).astype(bf16)
                return carry

            lax.fori_loop(0, width // step_cols, second, 0, unroll=UNROLL)
            dst_d[n_d, :, width:] = tail

        slot_two = pick(step, (0, 0, 1, 1, 0, 0, 1, 1))
        k = pick(step, ORDER)

        @pl.when(step == 4)
        def _():
            sent_core(2)

        @pl.when(step == 6)
        def _():
            sent_core(4)

        @pl.when(step == 5)
        def _():
            keep_mix(2).wait()

        @pl.when(step == 7)
        def _():
            keep_mix(4).wait()

        @pl.when(lax.rem(k, 2) == 1)
        def _():
            out_parts(dodd, slot_two, modd, slot_two)

        @pl.when(lax.rem(k, 2) == 0)
        def _():
            out_parts(deven, k // 2, meven, slot_two)

        def come_5():
            late_x[5].wait_recv()
            late_g[5].wait_recv()
            load(step + 1)

        def come_6():
            for copy in far:
                copy.wait_recv()
            late_x[7].start()
            late_g[7].start()

        for at_step, todo in (
            (0, (lambda: send_core(2),)),
            (1, (lambda: complete(2),)),
            (2, (come_5,)),
            (3, (lambda: send_core(4), come_6)),
            (4, (lambda: complete(4), lambda: send_core(6))),
            (5, (lambda: complete(6),)),
            (6, (lambda: send_core(0),)),
            (7, (lambda: complete(0),)),
        ):

            @pl.when(step == at_step)
            def _():
                for do in todo:
                    do()

        @pl.when(slot == 1)
        def _():
            def third(c, carry):
                at = pl.multiple_of(c * WIDE_COLS, WIDE_COLS)
                acc[:, pl.ds(at, WIDE_COLS)] += matmul(xt[...], dgu[:, pl.ds(at, WIDE_COLS)])
                return carry

            lax.fori_loop(0, 2 * hidden // WIDE_COLS, third, 0, unroll=UNROLL)

            def fourth(c, carry):
                at = pl.multiple_of(c * WIDE_COLS, WIDE_COLS)
                acc[:, pl.ds(2 * hidden + at, WIDE_COLS)] += matmul(
                    gt_[...], hidg[:, pl.ds(at, WIDE_COLS)]
                )
                return carry

            lax.fori_loop(0, hidden // WIDE_COLS, fourth, 0, unroll=UNROLL)

        @pl.when(step == 1)
        def _():
            late_x[4].wait_recv()
            late_x[5].start()
            far[2].start()
            back[2].start()
            load(step + 1)

        @pl.when(step == 3)
        def _():
            late_x[7].wait_recv()
            late_g[7].wait_recv()
            load(step + 1)

        return carry

    lax.fori_loop(0, 8, block, 0)
    keep = pltpu.make_async_copy(deven.at[0], dx_own, sem_w.at[0])
    keep.start()
    parts = 8
    rows = width // parts

    def out(j, slot):
        return pltpu.make_async_copy(
            stage.at[slot], grads.at[pl.ds(j * rows, rows)], sem_s.at[slot]
        )

    for j in range(parts):
        slot = j % 2
        if j >= 2:
            out(j - 2, slot).wait()
        stage[slot] = acc[j * rows : (j + 1) * rows].astype(bf16)
        out(j, slot).start()
    for j in range(parts - 2, parts):
        out(j, j % 2).wait()
    keep.wait()
    keep_mix(6).wait()
    keep_mix(0).wait()
    for k in (2, 4, 6):
        back[k].wait_recv()
        back[k].wait_send()
    sent_core(6)
    sent_core(0)
    for copy in (far[2], late_x[5], late_x[7], late_g[7]):
        copy.wait_send()
    wire.finish()


PARTNERS_GROUP = ((1, 0), (2, 0), (0, 2), (2, 2))
GROUP_SENDS = 8 + 8 + 3


def run_group(v, grad, xs, g_all, w):
    length, width = grad.shape
    wide = v.shape[1]
    cols = w.shape[1]
    hidden = cols // 3
    any_spec = pl.BlockSpec(memory_space=pl.ANY)
    return pl.pallas_call(
        group_kernel,
        out_shape=[
            jax.ShapeDtypeStruct((4, length, width), bf16),
            jax.ShapeDtypeStruct((length, wide), bf16),
            jax.ShapeDtypeStruct((3, length, wide), bf16),
            jax.ShapeDtypeStruct((width, cols), bf16),
            jax.ShapeDtypeStruct((8, length, wide), bf16),
            jax.ShapeDtypeStruct((8, length, width), bf16),
        ],
        in_specs=[any_spec] * 5,
        out_specs=[any_spec] * 6,
        scratch_shapes=[
            pltpu.VMEM((width, cols), bf16),
            pltpu.VMEM((2, length, wide), bf16),
            pltpu.VMEM((2, length, width), bf16),
            pltpu.VMEM((width, 2 * length), bf16),
            pltpu.VMEM((width, 2 * length), bf16),
            pltpu.VMEM((2 * length, hidden), bf16),
            pltpu.VMEM((2 * length, 2 * hidden), bf16),
            pltpu.VMEM((4, length, wide), bf16),
            pltpu.VMEM((2, length, wide), bf16),
            pltpu.VMEM((4, length, wide), bf16),
            pltpu.VMEM((2, length, width), bf16),
            pltpu.VMEM((2, length, width), bf16),
            pltpu.VMEM((4, length, width), bf16),
            pltpu.VMEM((width, cols), f32),
            pltpu.VMEM((2, width // 8, cols), bf16),
            pltpu.SemaphoreType.DMA((1,)),
            pltpu.SemaphoreType.DMA((2,)),
            pltpu.SemaphoreType.DMA((2,)),
            pltpu.SemaphoreType.DMA((2,)),
            pltpu.SemaphoreType.DMA((2,)),
            pltpu.SemaphoreType.DMA((GROUP_SENDS,)),
            pltpu.SemaphoreType.DMA((GROUP_SENDS,)),
        ],
        compiler_params=pltpu.CompilerParams(
            collective_id=2, has_side_effects=True, vmem_limit_bytes=62 * MIB
        ),
        cost_estimate=pl.CostEstimate(
            flops=48 * length * width * cols,
            bytes_accessed=64 * length * width + 4 * width * cols,
            transcendentals=8 * length * hidden,
        ),
        name="group",
    )(v, grad, xs, g_all, w)


PARTNERS_BACK = ((1, 0), (2, 0), (3, 0), (0, 1), (0, 2), (0, 4), (0, 6))
TERMS = 16
BACK_SENDS = 3 + 8 + 6 + 3 + 2 + 3 + 2 * 4 + 2 * 3 + 1 + 6 + 6


def back_kernel(
    dx_h, g_h, first_h, table, tiny, v_h, tokens_h, qkv_h, lse, cos, sin, seg_row,
    dx_in, grads, mix_sum, attn, xn, in_all, out_all,
    tokens_grad,
    g_out, mix_in, d_out, xn_core,
    in_v, out_v, mix_v, gl, gy, gz, act_v, aq_v, pq, wo, wi, wyo, wyi, wzo, wzi, wxo, own_d,
    dn, dxn, dl, dattn, dproj, dkv, bias, tbuf,
    dx_own, g_ref, first, v, tokens, qkv,
    local_sem, send_sem, recv_sem,
):
    wire = Wire(send_sem, recv_sem)
    r, f = wire.r, wire.f
    shard = gl.shape[1]
    length, width = tokens_h.shape
    experts = 8
    low = lax.rem(f // 2, 2)
    cols_p, cols_a = pq.shape[1], aq_v.shape[1]
    scale = HD ** (-0.5)
    used = [0]

    def local(src, dst):
        copy = pltpu.make_async_copy(src, dst, local_sem.at[used[0]])
        copy.start()
        used[0] += 1
        return copy

    def shard_rows(j):
        return pl.ds(pl.multiple_of(flips(f, j) * shard, shard), shard)

    def token_rows(k):
        return pl.ds(k * length, length)

    def part_of(k, cols):
        return pl.ds(pl.multiple_of(flips(r, k) * cols, cols), cols)

    def add(u, w):
        return (u.astype(f32) + w.astype(f32)).astype(bf16)

    half = lax.rem(r, 2)
    side = r // 2

    def half_of(index):
        return pl.ds(pl.multiple_of(index * cols_a, cols_a), cols_a)

    load_dx = [
        local(dx_in.at[n], in_v.at[token_rows(n), pl.ds(0, dx_in.shape[2])]) for n in range(3)
    ]
    load_dx += [
        local(dx_h, dx_own), local(v_h, v), local(first_h, first), local(g_h, g_ref),
        local(qkv_h, qkv), local(tokens_h, tokens),
    ]
    load_out = local(out_all, out_v)
    load_g = {j: local(grads.at[shard_rows(j)], gl.at[j // 2]) for j in (4, 6, 2, 0)}
    load_a = local(attn.at[:, half_of(half)], aq_v.at[token_rows(0)])
    load_mix = local(mix_sum.at[2], mix_v.at[0])
    wire.meet(PARTNERS_BACK)
    got_y, got_m = {}, {}
    place_z = f // 2
    inner = (place_z == 1) | (place_z == 2)
    cut = shard // 2
    got_z = {}
    for j in (4, 6, 2, 0):
        for n in (0, 1):
            at = pl.ds(pl.multiple_of(flips(f, j + 1) * shard + n * cut, cut), cut)
            got_y[j, n] = wire.plan(grads.at[at], gy.at[j // 2, pl.ds(n * cut, cut)], 0, 1)
            wire.sent.append(got_y[j, n])
            if j:
                at = pl.ds(n * cut, cut)
                got_z[j, n] = wire.plan(gl.at[j // 2, at], gz.at[j // 2 - 1, at], 0, j)
                wire.sent.append(got_z[j, n])

    def by_place(do, outer_j, inner_j, n):
        @pl.when(inner)
        def _():
            do(inner_j, n)

        @pl.when(jnp.logical_not(inner))
        def _():
            do(outer_j, n)

    def send_y(j, n):
        got_y[j, n].start()

    for outer_j, inner_j in ((4, 2), (6, 4), (2, 6)):
        for n in (0, 1):
            by_place(send_y, outer_j, inner_j, n)
    for n in (0, 1):
        send_y(0, n)
    got_a = wire.send(attn.at[:, half_of(1 - half)], aq_v.at[token_rows(1)], 1, 0)
    got_m[6] = wire.send(mix_sum.at[3], mix_v.at[1], 2, 0)
    got_n = {2: wire.send(xn, act_v.at[token_rows(2)], 2, 0), 1: wire.send(xn, xn_core, 1, 0)}

    spot = lax.broadcasted_iota(jnp.int32, bias.shape, 0)
    keys_at = lax.broadcasted_iota(jnp.int32, bias.shape, 1)
    seg_col = as_columns(seg_row[...])[:, 0:1].astype(jnp.int32)
    bias[...] = jnp.where((spot >= keys_at) & (seg_col == seg_row[...]), 0.0, -1e30)
    tbuf[...] = jnp.zeros_like(tbuf)
    for copy in load_dx:
        copy.wait()

    def sum_dx(c, carry):
        at = pl.ds(pl.multiple_of(c * ROWS, ROWS), ROWS)
        d = dx_own[at, :].astype(f32)
        for n in range(3):
            here = pl.ds(pl.multiple_of(n * length + c * ROWS, ROWS), ROWS)
            d = d + in_v[here, 0 : dx_own.shape[1]].astype(f32)
        dn[at, :] = d[:, :width]
        dgate = d[:, width:]
        dgate = dgate + pltpu.roll(dgate, EXTRA - experts, 1)
        gates = table[at, :]
        mean = jnp.sum(gates * dgate, axis=-1, keepdims=True)
        dl[at, :] = (gates * (dgate - mean)).astype(bf16)
        return carry

    lax.fori_loop(0, length // ROWS, sum_dx, 0)
    load_in = local(in_all, in_v)
    dlt = dl[...].T[0:16]

    def add_router(c, carry):
        at = pl.ds(pl.multiple_of(c * 256, 256), 256)
        row = lax.broadcasted_iota(jnp.int32, (16, 256), 0)
        router = jnp.where(row < experts, tiny[:, at], 0.0).astype(bf16)
        dn[:, at] = dn[:, at] + matmul(dl[:, 0:16], router)
        tbuf[:, at] = matmul(dlt, v[:, at])
        return carry

    lax.fori_loop(0, width // 256, add_router, 0)

    def norm_two(c, gain):
        at = pl.ds(pl.multiple_of(c * ROWS, ROWS), ROWS)
        h = first[at, :]
        r2 = lax.rsqrt(jnp.mean(h * h, axis=-1, keepdims=True) + epsilon)
        unit = h * r2
        d = dn[at, :]
        gain = gain + jnp.sum(d * unit, axis=0, keepdims=True)
        d = d * tiny[experts + 1 : experts + 2, :]
        d = g_ref[at, :].astype(f32) + r2 * (
            d - unit * jnp.mean(d * unit, axis=-1, keepdims=True)
        )
        dn[at, :] = d
        act_v[at, :] = d.astype(bf16)
        return gain

    gain_two = lax.fori_loop(0, length // ROWS, norm_two, jnp.zeros((1, width), f32))
    tbuf[experts + 1 : experts + 2, :] = gain_two
    got_r = wire.send(act_v.at[token_rows(0)], act_v.at[token_rows(1)], 1, 0)
    def pass_y(j, n):
        if n == 0:
            load_g[j].wait()
        got_y[j, n].wait_recv()
        at = pl.ds(n * cut, cut)
        gl[j // 2, at] = add(gl[j // 2, at], gy[j // 2, at])
        got_z[j, n].start()

    def came(got_some, j):
        for n in (0, 1):
            got_some[j, n].wait_recv()

    load_out.wait()

    def to_attn(c, carry):
        at = pl.ds(pl.multiple_of(c * 256, 256), 256)
        dattn[:, at] = matmul(act_v[0:length, :], out_v[:, at]).astype(bf16)
        return carry

    lax.fori_loop(0, WQ // 256, to_attn, 0)
    by_place(pass_y, 4, 2, 0)
    lane = lax.broadcasted_iota(jnp.int32, (length, HD), 1)

    def turn_back(w):
        return w * cos[...] - pltpu.roll(w, HD // 2, 1) * sin[...]

    for group in range(KV):
        k_at = pl.ds(WQ + group * HD, HD)
        v_at = pl.ds(WQ + WK + group * HD, HD)
        dkv[...] = jnp.zeros_like(dkv)

        def head(i, carry):
            h = group * GROUP + i
            at = pl.ds(pl.multiple_of(h * HD, HD), HD)
            s = contract_cols(qkv[:, at], qkv[:, k_at]) * scale + bias[...]
            level = jnp.sum(jnp.where(lane == h, lse[...], 0.0), axis=1, keepdims=True)
            p = jnp.exp(s - level)
            da = dattn[:, at]
            dp = contract_cols(da, qkv[:, v_at])
            delta = jnp.sum(p * dp, axis=-1, keepdims=True)
            ds = (p * (dp - delta)).astype(bf16)
            dkv[1] += contract_rows(p.astype(bf16), da)
            dkv[0] += contract_rows(ds, qkv[:, at])
            dproj[:, at] = turn_back(matmul(ds, qkv[:, k_at]) * scale).astype(bf16)
            return carry

        lax.fori_loop(0, GROUP, head, 0)
        if group == 0:
            by_place(pass_y, 4, 2, 1)
            load_mix.wait()
            got_m[6].wait_recv()
            mix_v[0] = add(mix_v[0], mix_v[1])
            got_m[4] = wire.send(mix_v.at[0], mix_in.at[1], 0, 2)
        dproj[:, k_at] = turn_back(dkv[0] * scale).astype(bf16)
        dproj[:, v_at] = dkv[1].astype(bf16)

    keep_p = local(dproj.at[:, part_of(0, cols_p)], pq.at[token_rows(0)])
    got_p = {}
    for k in (2, 3, 1):
        got_p[k] = wire.send(dproj.at[:, part_of(k, cols_p)], pq.at[token_rows(k)], k, 0)

    got_m[2] = wire.send(mix_sum.at[1], mix_in.at[0], 2, 0)
    by_place(pass_y, 6, 4, 0)

    load_a.wait()
    got_a.wait_recv()
    got_r.wait_recv()

    def dense_out(c, carry):
        at = pl.ds(pl.multiple_of(c * 256, 256), 256)
        wo[at, :] = matmul(act_v[0 : 2 * length, at].T, aq_v[...]).astype(bf16)
        return carry

    lax.fori_loop(0, width // 256, dense_out, 0)
    got_r.wait_send()
    load_x = [local(xn, act_v.at[token_rows(0)])]
    got_n[1].wait_recv()
    load_x.append(local(xn_core, act_v.at[token_rows(1)]))
    got_wo, got_wi, got_wzo, got_wzi = {}, {}, {}, {}
    for j in (4, 6, 2, 0):
        got_wo[j] = wire.send(wo.at[shard_rows(j + 1)], wyo.at[j // 2], 0, 1)

    by_place(pass_y, 6, 4, 1)

    load_in.wait()

    def to_norm(c, carry):
        at = pl.ds(pl.multiple_of(c * 256, 256), 256)
        dxn[:, at] = contract_cols(dproj[...], in_v[at, :])
        return carry

    lax.fori_loop(0, width // 256, to_norm, 0)

    def norm_one(c, gain):
        at = pl.ds(pl.multiple_of(c * ROWS, ROWS), ROWS)
        x = tokens[at, :].astype(f32)
        r1 = lax.rsqrt(jnp.mean(x * x, axis=-1, keepdims=True) + epsilon)
        unit = x * r1
        d = dxn[at, :]
        gain = gain + jnp.sum(d * unit, axis=0, keepdims=True)
        d = d * tiny[experts : experts + 1, :]
        d = dn[at, :] + r1 * (d - unit * jnp.mean(d * unit, axis=-1, keepdims=True))
        tokens_grad[at, :] = d.astype(bf16)
        return gain

    gain_one = lax.fori_loop(0, length // ROWS, norm_one, jnp.zeros((1, width), f32))
    tbuf[experts : experts + 1, :] = gain_one

    by_place(pass_y, 2, 6, 0)
    by_place(pass_y, 2, 6, 1)
    mine, other = 2 * r + low, 2 * r + 1 - low
    load_g[0].wait()
    came(got_y, 0)
    came(got_z, 4)
    gl[0] = (gl[0].astype(f32) + gy[0].astype(f32) + gz[1].astype(f32)).astype(bf16)
    kept = [local(gl.at[0], g_out.at[mine])]
    got_e = {}

    got_n[2].wait_recv()
    got_n[3] = wire.send(act_v.at[token_rows(2)], act_v.at[token_rows(3)], 1, 0)
    keep_p.wait()
    for copy in load_x:
        copy.wait()
    for k in (1, 2, 3):
        got_p[k].wait_recv()
    got_n[3].wait_recv()
    got_e[2, 0] = wire.send(gl.at[0], g_out.at[mine], 2, 0)
    got_e[1, 0] = wire.send(gl.at[0], g_out.at[mine], 1, 0)

    tall = shard + TERMS

    def tall_rows(j):
        return pl.ds(pl.multiple_of(flips(f, j) * tall, TERMS), tall)

    for z in range(4):
        lanes = slice(2 * z * shard, 2 * (z + 1) * shard)
        both = matmul(act_v[:, lanes].T, pq[...]).astype(bf16)
        for y in (0, 1):
            top = (2 * z + y) * tall
            wi[top : top + shard, :] = both[y * shard : (y + 1) * shard]
            wi[top + shard : top + tall, :] = jnp.zeros((TERMS, cols_p), bf16)
            wi[top + shard : top + tall, 0 : 2 * shard] = tbuf[:, lanes].astype(bf16)
    for j in (4, 6, 2, 0):
        got_wi[j] = wire.send(wi.at[tall_rows(j + 1)], wyi.at[j // 2], 0, 1)
    for j in (4, 6, 2):
        got_wo[j].wait_recv()
        wyo[j // 2] = add(wo[shard_rows(j), :], wyo[j // 2])
        got_wzo[j] = wire.send(wyo.at[j // 2], wzo.at[j // 2 - 1], 0, j)

    came(got_z, 2)
    came(got_z, 6)
    gz[0] = add(gz[0], gz[2])
    kept.append(local(gz.at[0], g_out.at[other]))
    got_e[2, 1] = wire.send(gz.at[0], g_out.at[other], 2, 0)
    got_e[1, 1] = wire.send(gz.at[0], g_out.at[other], 1, 0)

    for j in (4, 6, 2):
        got_wi[j].wait_recv()
        wyi[j // 2] = add(wi[tall_rows(j), :], wyi[j // 2])
        got_wzi[j] = wire.send(wyi.at[j // 2], wzi.at[j // 2 - 1], 0, j)

    def own_rows(w, rows, y, z, got_w, got_zs):
        got_w[0].wait_recv()
        total = w[rows, :].astype(f32) + y[0].astype(f32)
        for j in (2, 4, 6):
            got_zs[j].wait_recv()
            total = total + z[j // 2 - 1].astype(f32)
        return total

    wxo[0] = own_rows(wo, shard_rows(0), wyo, wzo, got_wo, got_wzo).astype(bf16)
    quarter = cols_a // 2

    def quarter_of(index):
        return pl.ds(pl.multiple_of(index * quarter, quarter), quarter)

    got_x = wire.send(
        wxo.at[0, :, quarter_of(1 - side)], wxo.at[1, :, pl.ds(0, quarter)], 2, 0
    )
    got_x.wait_recv()
    own_d[shard:, cols_p:] = jnp.zeros((TERMS, quarter), bf16)
    own_d[0:shard, cols_p:] = add(wxo[0, :, quarter_of(side)], wxo[1, :, 0:quarter])
    got_d = {}

    def send_d(n, columns):
        kept.append(local(own_d.at[:, columns], d_out.at[r, :, columns]))
        for k in (2, 1):
            got_d[k, n] = wire.send(own_d.at[:, columns], d_out.at[r, :, columns], k, 0)

    parts_d = (pl.ds(cols_p, quarter), pl.ds(0, cols_p))
    send_d(0, parts_d[0])
    own_d[:, 0:cols_p] = own_rows(wi, tall_rows(0), wyi, wzi, got_wi, got_wzi).astype(bf16)
    send_d(1, parts_d[1])

    far = flips(r, 2)
    for n, e in ((0, 2 * far + low), (1, 2 * far + 1 - low)):
        got_e[2, n].wait_recv()
        got_e[3, n] = wire.send(g_out.at[e], g_out.at[e], 1, 0)
    for n, columns in enumerate(parts_d):
        got_d[2, n].wait_recv()
        at = d_out.at[far, :, columns]
        got_d[3, n] = wire.send(at, at, 1, 0)
    for k in (1, 3):
        for n in (0, 1):
            got_e[k, n].wait_recv()
    for k in (1, 3):
        for n in (0, 1):
            got_d[k, n].wait_recv()
    for k in (2, 4):
        got_m[k].wait_recv()
    for copy in kept:
        copy.wait()
    wire.finish((got_r,))


def run_back(
    dx_own, grad, first, table, tiny, v, tokens, qkv, lse, cos, sin, seg_ids,
    dx_in, grads, mix_sum, attn, xn, in_all, out_all,
):
    any_spec = pl.BlockSpec(memory_space=pl.ANY)
    vmem = pl.BlockSpec(memory_space=pltpu.VMEM)
    length, width = tokens.shape
    shard = width // 8
    cols = grads.shape[1]
    cols_p, cols_a = qkv.shape[1] // 4, attn.shape[1] // 2
    return pl.pallas_call(
        back_kernel,
        out_shape=[
            jax.ShapeDtypeStruct((length, width), bf16),
            jax.ShapeDtypeStruct((8, shard, cols), bf16),
            jax.ShapeDtypeStruct((2, length, width), bf16),
            jax.ShapeDtypeStruct((4, shard + TERMS, cols_p + cols_a // 2), bf16),
            jax.ShapeDtypeStruct((length, width), bf16),
        ],
        in_specs=[any_spec] * 3 + [vmem] * 2 + [any_spec] * 3 + [vmem] * 4 + [any_spec] * 7,
        out_specs=[vmem] + [any_spec] * 4,
        scratch_shapes=[
            pltpu.VMEM(in_all.shape, bf16),
            pltpu.VMEM(out_all.shape, bf16),
            pltpu.VMEM((2, length, width), bf16),
            pltpu.VMEM((4, shard, cols), bf16),
            pltpu.VMEM((4, shard, cols), bf16),
            pltpu.VMEM((3, shard, cols), bf16),
            pltpu.VMEM((4 * length, width), bf16),
            pltpu.VMEM((2 * length, cols_a), bf16),
            pltpu.VMEM((4 * length, cols_p), bf16),
            pltpu.VMEM((width, cols_a), bf16),
            pltpu.VMEM((width + 8 * TERMS, cols_p), bf16),
            pltpu.VMEM((4, shard, cols_a), bf16),
            pltpu.VMEM((4, shard + TERMS, cols_p), bf16),
            pltpu.VMEM((3, shard, cols_a), bf16),
            pltpu.VMEM((3, shard + TERMS, cols_p), bf16),
            pltpu.VMEM((2, shard, cols_a), bf16),
            pltpu.VMEM((shard + TERMS, cols_p + cols_a // 2), bf16),
            pltpu.VMEM((length, width), f32),
            pltpu.VMEM((length, width), f32),
            pltpu.VMEM((length, EXTRA), bf16),
            pltpu.VMEM((length, WQ), bf16),
            pltpu.VMEM(qkv.shape, bf16),
            pltpu.VMEM((2, length, HD), f32),
            pltpu.VMEM((length, length), f32),
            pltpu.VMEM((TERMS, width), f32),
            pltpu.VMEM(dx_own.shape, bf16),
            pltpu.VMEM(grad.shape, bf16),
            pltpu.VMEM(first.shape, f32),
            pltpu.VMEM(v.shape, bf16),
            pltpu.VMEM(tokens.shape, bf16),
            pltpu.VMEM(qkv.shape, bf16),
            pltpu.SemaphoreType.DMA((26,)),
            pltpu.SemaphoreType.DMA((BACK_SENDS,)),
            pltpu.SemaphoreType.DMA((BACK_SENDS,)),
        ],
        compiler_params=pltpu.CompilerParams(
            collective_id=3, has_side_effects=True, vmem_limit_bytes=62 * MIB
        ),
        name="back",
    )(
        dx_own, grad, first, table, tiny, v, tokens, qkv, lse, cos, sin,
        seg_ids,
        dx_in, grads, mix_sum, attn, xn, in_all, out_all,
    )


def finish_kernel(sums, dense, first, own, parts, e_in, e_out, in_grad, out_grad, mixed):
    split = e_in.shape[2]
    for c in range(0, sums.shape[2], 128):
        part = jnp.swapaxes(sums[:, :, c : c + 128].astype(f32), 0, 1)
        if c < split:
            e_in[:, :, c : c + 128] = part
        else:
            e_out[:, :, c - split : c - split + 128] = part
    cut = in_grad.shape[1] // 4
    quarter = out_grad.shape[1] // 4
    for r in range(4):
        in_grad[:, r * cut : (r + 1) * cut] = dense[r, :, :cut].astype(f32)
        place = 2 * (r % 2) + r // 2
        out_grad[:, place * quarter : (place + 1) * quarter] = dense[r, :, cut:].astype(f32)
    total = first[...] + own[0].astype(f32)
    for n in range(parts.shape[0]):
        total = total + parts[n].astype(f32)
    mixed[...] = total.astype(bf16)


def run_finish(expert_sum, dense, first, mix_sum, mix_in, hidden):
    n_experts, shard, cols = expert_sum.shape
    length, width = first.shape
    steps = 6
    rows, tokens = shard // steps, length // steps
    cut = dense.shape[2] - width // 4
    return pl.pallas_call(
        finish_kernel,
        grid=(steps,),
        out_shape=[
            jax.ShapeDtypeStruct((shard, n_experts, 2 * hidden), f32),
            jax.ShapeDtypeStruct((shard, n_experts, hidden), f32),
            jax.ShapeDtypeStruct((shard, 4 * cut), f32),
            jax.ShapeDtypeStruct((shard, width), f32),
            jax.ShapeDtypeStruct((length, width), bf16),
        ],
        in_specs=[
            pl.BlockSpec((n_experts, rows, cols), lambda i: (0, i, 0)),
            pl.BlockSpec((4, rows, dense.shape[2]), lambda i: (0, i, 0)),
            pl.BlockSpec((tokens, width), lambda i: (i, 0)),
            pl.BlockSpec((1, tokens, width), lambda i: (0, i, 0)),
            pl.BlockSpec((mix_in.shape[0], tokens, width), lambda i: (0, i, 0)),
        ],
        out_specs=[
            pl.BlockSpec((rows, n_experts, 2 * hidden), lambda i: (i, 0, 0)),
            pl.BlockSpec((rows, n_experts, hidden), lambda i: (i, 0, 0)),
            pl.BlockSpec((rows, 4 * cut), lambda i: (i, 0)),
            pl.BlockSpec((rows, width), lambda i: (i, 0)),
            pl.BlockSpec((tokens, width), lambda i: (i, 0)),
        ],
        compiler_params=pltpu.CompilerParams(vmem_limit_bytes=62 * MIB),
        name="finish",
    )(expert_sum, dense, first, mix_sum, mix_in)


def near_layer(
    tokens, seg_ids, routes, in_proj, out_proj, router, norm_gains, expert_in, expert_out,
    out_grad,
):
    length, width = tokens.shape
    experts = router.shape[1]
    hidden = expert_out.shape[2]
    shard = router.shape[0]
    f = lax.axis_index("fsdp")
    cosine, sine = [t[:, 0] for t in tables(length)]
    cos = jnp.concatenate([cosine, cosine], axis=1)
    sin = jnp.concatenate([-sine, sine], axis=1)
    tiny = jnp.concatenate(
        [router.T, norm_gains.T, jnp.zeros((16 - experts - 2, shard), bf16)], axis=0
    )
    none = jnp.zeros_like(tiny)
    tiny = jnp.where(
        f % 2 == 0,
        jnp.concatenate([tiny, none], axis=1),
        jnp.concatenate([none, tiny], axis=1),
    )
    qkv, attn, xn, first, lse, table, small, v, in_all, out_all, w_all, g_all, xs = front(
        tokens, seg_ids, routes, cos, sin, in_proj, out_proj, tiny, expert_in, expert_out,
        out_grad,
    )
    mix_sum, dx_own, dx_in, grads, _, _ = run_group(v, out_grad, xs, g_all, w_all)
    tokens_grad, expert_sum, mix_in, dense, _ = run_back(
        dx_own, out_grad, first, table, small, v, tokens, qkv, lse, cos, sin, seg_ids,
        dx_in, grads, mix_sum, attn, xn, in_all, out_all,
    )
    e_in, e_out, in_grad, out_proj_grad, mixed = run_finish(
        expert_sum, dense, first, mix_sum, mix_in, hidden
    )
    terms = jnp.sum(dense[:, shard:, : 2 * shard].astype(f32), axis=0)
    terms = jnp.where(f % 2 == 0, terms[:, :shard], terms[:, shard:]).T
    return (
        mixed,
        tokens_grad,
        in_grad,
        out_proj_grad,
        terms[:, :experts],
        terms[:, experts : experts + 2],
        e_in,
        e_out,
    )


class Wide:
    def __init__(self, n_rep, n_fsdp):
        self.n_rep, self.n_fsdp = n_rep, n_fsdp

    def spread(self, value):
        every = lax.all_gather(value, "replica", axis=0)
        return [every[k] for k in range(self.n_rep)]

    def collect(self, parts):
        return lax.psum_scatter(jnp.stack(parts), "replica", scatter_dimension=0).astype(f32)

    def start(self, in_proj, out_proj, tiny, expert_in, expert_out, grad):
        r = lax.axis_index("replica")
        per = expert_in.shape[1] // self.n_rep
        weights = []
        for i in range(per):
            both = jnp.concatenate(
                [
                    lax.dynamic_index_in_dim(expert_in, per * r + i, 1, keepdims=False),
                    lax.dynamic_index_in_dim(expert_out, per * r + i, 1, keepdims=False),
                ],
                axis=1,
            )
            weights.append(lax.all_gather(both, "fsdp", axis=0, tiled=True))
        return (
            lax.all_gather(in_proj, "fsdp", axis=0, tiled=True),
            lax.all_gather(out_proj, "fsdp", axis=0, tiled=True),
            lax.all_gather(tiny, "fsdp", axis=1, tiled=True),
            (weights, self.spread(grad)),
        )

    def experts(self, payload, held):
        weights, gs = held
        xs = self.spread(payload)
        per = len(weights)
        mixes, dxs, grads = None, None, []
        for i, w in enumerate(weights):

            def expert_of(i=i):
                return per * lax.axis_index("replica") + i

            mix, dx, grad = run_expert(xs, gs, [w], expert_of, lambda j: 0)
            mixes = mix if mixes is None else [a + b for a, b in zip(mixes, mix)]
            dxs = dx if dxs is None else [a + b for a, b in zip(dxs, dx)]
            grads.append(grad[0])
        return self.collect(dxs), (mixes, grads)

    def trade(self, value):
        cut = value.reshape(value.shape[0], self.n_rep, -1).transpose(1, 0, 2)
        got = lax.all_to_all(cut, "replica", 0, 0)
        return got.reshape(-1, got.shape[2])

    def end(self, held, first, normed, attn, dres, dproj, terms):
        mixes, grads = held
        mixed = first + self.collect(mixes)
        own = jnp.stack(
            [lax.psum_scatter(g, "fsdp", scatter_dimension=0, tiled=True) for g in grads]
        )
        expert_sum = lax.all_gather(own, "replica", axis=0, tiled=True).transpose(1, 0, 2)
        dense = []
        for left, right in ((normed, dproj), (dres, attn)):
            left = lax.all_gather(left, "replica", axis=0, tiled=True)
            part = contract_rows(left, self.trade(right)).astype(bf16)
            own = lax.psum_scatter(part, "fsdp", scatter_dimension=0, tiled=True)
            dense.append(lax.all_gather(own, "replica", axis=1, tiled=True))
        return mixed, dense[0], dense[1], expert_sum, lax.psum(terms, ("replica", "fsdp"))


def layer(
    net, tokens, seg_ids, routes, in_proj, out_proj, router, norm_gains, expert_in, expert_out,
    out_grad,
):
    length, width = tokens.shape
    experts = router.shape[1]
    hidden = expert_out.shape[2]
    shard = router.shape[0]
    scale = HD ** (-0.5)
    cosine, sine = tables(length)
    segment = seg_ids[0]
    place = jnp.arange(length)
    allowed = ((place[:, None] >= place[None, :]) & (segment[:, None] == segment[None, :]))[
        None, None
    ]
    tiny = jnp.concatenate(
        [router.T, norm_gains.T, jnp.zeros((16 - experts - 2, shard), bf16)], axis=0
    )
    proj_in, proj_out, tiny, held = net.start(
        in_proj, out_proj, tiny, expert_in, expert_out, out_grad
    )
    router_rows = tiny[:experts]
    gain_one = tiny[experts].astype(f32)
    gain_two = tiny[experts + 1].astype(f32)

    inputs = tokens.astype(f32)
    scale_one = rms_scale(inputs)
    unit_one = inputs * scale_one
    normed = (unit_one * gain_one).astype(bf16)
    proj = matmul(normed, proj_in)
    queries = (
        rotate(proj[:, :WQ].reshape(length, HQ, HD), cosine, sine)
        .astype(bf16)
        .reshape(length, KV, GROUP, HD)
    )
    keys = rotate(proj[:, WQ : WQ + WK].reshape(length, KV, HD), cosine, sine).astype(bf16)
    values = proj[:, WQ + WK :].reshape(length, KV, HD).astype(bf16)
    scores = jnp.einsum("qkgd,tkd->kgqt", queries, keys, preferred_element_type=f32) * scale
    masked = jnp.where(allowed, scores, -1e30)
    highest = jnp.max(masked, axis=-1, keepdims=True)
    expo = jnp.exp(masked - highest)
    total = jnp.sum(expo, axis=-1, keepdims=True)
    log_total = highest + jnp.log(total)
    probs_low = (expo / total).astype(bf16)
    attn = jnp.einsum("kgqt,tkd->qkgd", probs_low, values, preferred_element_type=f32)
    attn = attn.astype(bf16).reshape(length, WQ)
    first = inputs + contract_cols(attn, proj_out)
    scale_two = rms_scale(first)
    unit_two = first * scale_two
    normed_two = (unit_two * gain_two).astype(bf16)
    logits = contract_cols(normed_two, router_rows)
    onehot = (routes[:, :, None] == jnp.arange(experts)[None, None, :]).astype(f32)
    chosen = jnp.sum(onehot * logits[:, None, :], axis=-1)
    gates = jax.nn.softmax(chosen, axis=-1)
    table = jnp.sum(gates[:, :, None] * onehot, axis=1)
    high = table.astype(bf16)
    low = (table - high.astype(f32)).astype(bf16)
    payload = jnp.concatenate(
        [normed_two, high, low, jnp.zeros((length, EXTRA - 2 * experts), bf16)], axis=1
    )
    dx, held = net.experts(payload, held)

    grad_out = out_grad.astype(f32)
    dgate_all = dx[:, width : width + experts] + dx[:, width + experts : width + 2 * experts]
    dgate = jnp.sum(onehot * dgate_all[:, None, :], axis=-1)
    dchosen = gates * (dgate - jnp.sum(gates * dgate, axis=-1, keepdims=True))
    dlogits = jnp.sum(dchosen[:, :, None] * onehot, axis=1).astype(bf16)
    dnormed_two = dx[:, :width] + matmul(dlogits, router_rows)
    gain_two_grad = jnp.sum(dnormed_two * unit_two, axis=0)
    dunit_two = dnormed_two * gain_two
    dfirst = grad_out + scale_two * (
        dunit_two - unit_two * jnp.mean(dunit_two * unit_two, axis=-1, keepdims=True)
    )
    dres = dfirst.astype(bf16)
    dattn = matmul(dres, proj_out).astype(bf16).reshape(length, KV, GROUP, HD)
    probs = jnp.exp(masked - log_total)
    probs_again = probs.astype(bf16)
    dprobs = jnp.einsum("qkgd,tkd->kgqt", dattn, values, preferred_element_type=f32)
    dvalues = jnp.einsum("kgqt,qkgd->tkd", probs_again, dattn, preferred_element_type=f32)
    delta = jnp.sum(probs * dprobs, axis=-1, keepdims=True)
    dscores = (probs * (dprobs - delta)).astype(bf16)
    dqueries = jnp.einsum("kgqt,tkd->qkgd", dscores, keys, preferred_element_type=f32) * scale
    dkeys = jnp.einsum("kgqt,qkgd->tkd", dscores, queries, preferred_element_type=f32) * scale
    dqueries = rotate(dqueries.reshape(length, HQ, HD), cosine, -sine).reshape(length, WQ)
    dkeys = rotate(dkeys, cosine, -sine).reshape(length, WK)
    dproj = jnp.concatenate([dqueries, dkeys, dvalues.reshape(length, WK)], axis=1).astype(bf16)
    dnormed = contract_cols(dproj, proj_in)
    gain_one_grad = jnp.sum(dnormed * unit_one, axis=0)
    dunit_one = dnormed * gain_one
    tokens_grad = (
        dfirst
        + scale_one
        * (dunit_one - unit_one * jnp.mean(dunit_one * unit_one, axis=-1, keepdims=True))
    ).astype(bf16)

    terms = jnp.concatenate(
        [
            contract_rows(dlogits, normed_two),
            gain_one_grad[None],
            gain_two_grad[None],
            jnp.zeros((16 - experts - 2, width), f32),
        ],
        axis=0,
    )
    mixed, in_proj_grad, out_proj_grad, expert_sum, terms = net.end(
        held, first, normed, attn, dres, dproj, terms
    )
    terms = lax.dynamic_slice_in_dim(terms, lax.axis_index("fsdp") * shard, shard, 1).T
    return (
        mixed.astype(bf16),
        tokens_grad,
        in_proj_grad.astype(f32),
        out_proj_grad.astype(f32),
        terms[:, :experts],
        terms[:, experts : experts + 2],
        expert_sum[..., : 2 * hidden].astype(f32),
        expert_sum[..., 2 * hidden :].astype(f32),
    )


def solution(mesh):
    n_rep, n_fsdp = mesh.shape["replica"], mesh.shape["fsdp"]
    if (n_rep, n_fsdp) == (4, 8):
        body = near_layer
    else:
        body = functools.partial(layer, Wide(n_rep, n_fsdp))
    both = P(("replica", "fsdp"), None)
    fsdp, deep = P("fsdp", None), P("fsdp", None, None)
    return jax.shard_map(
        body,
        mesh=mesh,
        in_specs=(both, both, both, fsdp, fsdp, fsdp, fsdp, deep, deep, both),
        out_specs=(both, both, fsdp, fsdp, fsdp, fsdp, deep, deep),
        check_vma=False,
    )
```

```python
import functools

import jax
import jax.numpy as jnp
from jax import lax
from jax.experimental import pallas as pl
from jax.experimental.pallas import tpu as pltpu
from jax.sharding import PartitionSpec as P

HQ = 12
KV = 2
HD = 128
GROUP = HQ // KV
WQ = HQ * HD
WK = KV * HD
EXTRA = 128
MIB = 1024 * 1024

epsilon = 1e-06
rope_base = 1000000.0
bf16 = jnp.bfloat16
f32 = jnp.float32


def rms_scale(v):
    return lax.rsqrt(jnp.mean(v * v, axis=-1, keepdims=True) + epsilon)


def tables(length):
    half = HD // 2
    freq = jnp.power(rope_base, -(jnp.arange(half, dtype=f32) * 2.0 / HD))
    angle = jnp.arange(length, dtype=f32)[:, None] * freq[None, :]
    return (jnp.cos(angle)[:, None, :], jnp.sin(angle)[:, None, :])


def rotate(v, cosine, sine):
    half = v.shape[-1] // 2
    first = v[..., :half]
    second = v[..., half:]
    return jnp.concatenate(
        [first * cosine - second * sine, second * cosine + first * sine], axis=-1
    )


def contract_rows(left, right):
    return lax.dot_general(left, right, (((0,), (0,)), ((), ())), preferred_element_type=f32)


def contract_cols(left, right):
    return lax.dot_general(left, right, (((1,), (1,)), ((), ())), preferred_element_type=f32)


def matmul(left, right):
    return lax.dot_general(left, right, (((1,), (0,)), ((), ())), preferred_element_type=f32)


def expert_kernel(nt, nw, length, width, hidden, rows, expert_of, offset_of, *refs):
    xs, gs, ws = refs[:nt], refs[nt : 2 * nt], refs[2 * nt : 2 * nt + nw]
    refs = refs[2 * nt + nw :]
    mixes, dxs, grads = refs[:nt], refs[nt : 2 * nt], refs[2 * nt : 2 * nt + nw]
    (
        wbuf, xbuf, gbuf, xt, gt_, hidg, dgu, mbuf, dbuf, acc, stage,
        sem_w, sem_x, sem_g, sem_m, sem_d, sem_s,
    ) = refs[2 * nt + nw :]
    cols = 3 * hidden
    step_cols = 256

    def load(k, slot):
        for i in range(nt):

            @pl.when(k == i)
            def _():
                pltpu.make_async_copy(xs[i], xbuf.at[slot], sem_x.at[slot]).start()
                pltpu.make_async_copy(gs[i], gbuf.at[slot], sem_g.at[slot]).start()

    def store(k, slot):
        for i in range(nt):

            @pl.when(k == i)
            def _():
                pltpu.make_async_copy(mbuf.at[slot], mixes[i], sem_m.at[slot]).start()
                pltpu.make_async_copy(dbuf.at[slot], dxs[i], sem_d.at[slot]).start()

    def stored(slot):
        pltpu.make_async_copy(mbuf.at[slot], mixes[0], sem_m.at[slot]).wait()
        pltpu.make_async_copy(dbuf.at[slot], dxs[0], sem_d.at[slot]).wait()

    for j in range(nw):
        pltpu.make_async_copy(
            ws[j], wbuf.at[pl.ds(pl.multiple_of(offset_of(j), 8), rows)], sem_w.at[j]
        ).start()
    load(0, 0)
    expert = expert_of()
    acc[...] = jnp.zeros_like(acc)
    lane = lax.broadcasted_iota(jnp.int32, (length, EXTRA), 1)
    for j in range(nw):
        pltpu.make_async_copy(
            ws[j], wbuf.at[pl.ds(pl.multiple_of(offset_of(j), 8), rows)], sem_w.at[j]
        ).wait()

    def block(k, carry):
        slot = lax.rem(k, 2)

        @pl.when(k + 1 < nt)
        def _():
            load(k + 1, 1 - slot)

        pltpu.make_async_copy(xs[0], xbuf.at[slot], sem_x.at[slot]).wait()
        pltpu.make_async_copy(gs[0], gbuf.at[slot], sem_g.at[slot]).wait()

        @pl.when(k >= 2)
        def _():
            stored(slot)

        extra = xbuf[slot, :, width:].astype(f32)
        mine = (lane == expert) | (lane == expert + 8)
        gate = jnp.sum(jnp.where(mine, extra, 0.0), axis=1, keepdims=True)
        xt[...] = xbuf[slot, :, :width].T
        gt_[...] = gbuf[slot].T

        def first(c, dgate):
            at = pl.multiple_of(c * step_cols, step_cols)
            u = matmul(xbuf[slot, :, :width], wbuf[:, pl.ds(at, step_cols)])
            up = matmul(xbuf[slot, :, :width], wbuf[:, pl.ds(hidden + at, step_cols)])
            back = matmul(gbuf[slot], wbuf[:, pl.ds(2 * hidden + at, step_cols)])
            sig = 1.0 / (1.0 + jnp.exp(-u))
            act = u * sig
            hid = act * up
            hidg[:, pl.ds(at, step_cols)] = (gate * hid).astype(bf16)
            dgate = dgate + jnp.sum(back * hid, axis=1, keepdims=True)
            dhid = gate * back
            dgu[:, pl.ds(at, step_cols)] = (
                dhid * up * sig * (1.0 + u * (1.0 - sig))
            ).astype(bf16)
            dgu[:, pl.ds(hidden + at, step_cols)] = (dhid * act).astype(bf16)
            return dgate

        dgate = lax.fori_loop(
            0, hidden // step_cols, first, jnp.zeros((length, 1), f32)
        )

        def second(c, carry):
            at = pl.multiple_of(c * step_cols, step_cols)
            mbuf[slot, :, pl.ds(at, step_cols)] = contract_cols(
                hidg[...], wbuf[pl.ds(at, step_cols), pl.ds(2 * hidden, hidden)]
            ).astype(bf16)
            dbuf[slot, :, pl.ds(at, step_cols)] = contract_cols(
                dgu[...], wbuf[pl.ds(at, step_cols), pl.ds(0, 2 * hidden)]
            ).astype(bf16)
            return carry

        lax.fori_loop(0, width // step_cols, second, 0)
        high = dgate.astype(bf16).astype(f32)
        low = dgate - high
        dbuf[slot, :, width:] = (
            jnp.where(lane == expert, high, 0.0) + jnp.where(lane == expert + 8, low, 0.0)
        ).astype(bf16)
        store(k, slot)

        def third(c, carry):
            at = pl.multiple_of(c * step_cols, step_cols)
            acc[:, pl.ds(at, step_cols)] += matmul(xt[...], dgu[:, pl.ds(at, step_cols)])
            return carry

        lax.fori_loop(0, 2 * hidden // step_cols, third, 0)

        def fourth(c, carry):
            at = pl.multiple_of(c * step_cols, step_cols)
            acc[:, pl.ds(2 * hidden + at, step_cols)] += matmul(
                gt_[...], hidg[:, pl.ds(at, step_cols)]
            )
            return carry

        lax.fori_loop(0, hidden // step_cols, fourth, 0)
        return carry

    lax.fori_loop(0, nt, block, 0)
    stored(0)
    stored(1)
    for j in range(nw):
        slot = j % 2
        if j >= 2:
            pltpu.make_async_copy(stage.at[slot], grads[j - 2], sem_s.at[slot]).wait()
        stage[slot] = acc[pl.ds(pl.multiple_of(offset_of(j), 8), rows)].astype(bf16)
        pltpu.make_async_copy(stage.at[slot], grads[j], sem_s.at[slot]).start()
    for j in range(max(0, nw - 2), nw):
        pltpu.make_async_copy(stage.at[j % 2], grads[j], sem_s.at[j % 2]).wait()


def run_expert(xs, gs, ws, expert_of, offset_of):
    nt, nw = len(xs), len(ws)
    length, width = gs[0].shape
    rows, cols = ws[0].shape
    hidden = cols // 3
    outs = (
        [jax.ShapeDtypeStruct((length, width), bf16)] * nt
        + [jax.ShapeDtypeStruct((length, width + EXTRA), bf16)] * nt
        + [jax.ShapeDtypeStruct((rows, cols), bf16)] * nw
    )
    any_spec = pl.BlockSpec(memory_space=pl.ANY)
    result = pl.pallas_call(
        functools.partial(
            expert_kernel, nt, nw, length, width, hidden, rows, expert_of, offset_of
        ),
        out_shape=outs,
        in_specs=[any_spec] * (2 * nt + nw),
        out_specs=[any_spec] * len(outs),
        scratch_shapes=[
            pltpu.VMEM((width, cols), bf16),
            pltpu.VMEM((2, length, width + EXTRA), bf16),
            pltpu.VMEM((2, length, width), bf16),
            pltpu.VMEM((width, length), bf16),
            pltpu.VMEM((width, length), bf16),
            pltpu.VMEM((length, hidden), bf16),
            pltpu.VMEM((length, 2 * hidden), bf16),
            pltpu.VMEM((2, length, width), bf16),
            pltpu.VMEM((2, length, width + EXTRA), bf16),
            pltpu.VMEM((width, cols), f32),
            pltpu.VMEM((2, rows, cols), bf16),
            pltpu.SemaphoreType.DMA((nw,)),
            pltpu.SemaphoreType.DMA((2,)),
            pltpu.SemaphoreType.DMA((2,)),
            pltpu.SemaphoreType.DMA((2,)),
            pltpu.SemaphoreType.DMA((2,)),
            pltpu.SemaphoreType.DMA((2,)),
        ],
        compiler_params=pltpu.CompilerParams(vmem_limit_bytes=60 * MIB),
        cost_estimate=pl.CostEstimate(
            flops=6 * nt * length * width * cols,
            bytes_accessed=8 * nt * length * width + 4 * width * cols,
            transcendentals=nt * length * hidden,
        ),
        name="expert",
    )(*xs, *gs, *ws)
    return result[:nt], result[nt : 2 * nt], result[2 * nt :]


MESH_ID = pl.DeviceIdType.MESH


def flip(index, bit):
    return index + bit - 2 * bit * lax.rem(index // bit, 2)


def flips(index, mask):
    for bit in (1, 2, 4):
        if mask & bit:
            index = flip(index, bit)
    return index


class Wire:
    def __init__(self, send_sem, recv_sem):
        self.r, self.f = lax.axis_index("replica"), lax.axis_index("fsdp")
        self.send_sem, self.recv_sem = send_sem, recv_sem
        self.used, self.sent = 0, []

    def meet(self, partners):
        barrier = pltpu.get_barrier_semaphore()
        for d_r, d_f in partners:
            pl.semaphore_signal(
                barrier, inc=1, device_id=self.at(d_r, d_f), device_id_type=MESH_ID
            )
        pl.semaphore_wait(barrier, len(partners))

    def at(self, d_r, d_f):
        return (flips(self.r, d_r), flips(self.f, d_f))

    def plan(self, src, dst, d_r, d_f):
        copy = pltpu.make_async_remote_copy(
            src_ref=src,
            dst_ref=dst,
            send_sem=self.send_sem.at[self.used],
            recv_sem=self.recv_sem.at[self.used],
            device_id=self.at(d_r, d_f),
            device_id_type=MESH_ID,
        )
        self.used += 1
        assert self.used <= self.send_sem.shape[0]
        return copy

    def send(self, src, dst, d_r, d_f):
        copy = self.plan(src, dst, d_r, d_f)
        copy.start()
        self.sent.append(copy)
        return copy

    def finish(self, waited=()):
        for copy in self.sent:
            if all(copy is not other for other in waited):
                copy.wait_send()


CUTS = 4
FRONT_SENDS = 2 * 28 + 7 + 7 * CUTS + 4 + 3
PARTNERS = ((1, 0), (2, 0), (0, 1), (0, 2), (0, 4), (0, 6))
ROWS = 64


def as_columns(rows):
    rows = rows.astype(f32)
    rest = jnp.zeros((128 - rows.shape[0], rows.shape[1]), f32)
    return jnp.concatenate([rows, rest], axis=0).T


def turn(v, cosine, sine):
    return v * cosine + pltpu.roll(v, HD // 2, 1) * sine


def front_kernel(
    tokens, seg_row, routes, cos, sin,
    in_ref, out_ref, tiny_ref, e_in_ref, e_out_ref, g_ref,
    qkv_o, attn_o, xn_o, first_o, lse, table, tiny_out, v_o,
    in_all, out_all, w_all, g_all, xs,
    in_v, out_v, tiny_v, rt, bias, e_in, e_out, e_part, mine_ref, other_ref,
    qkv, attn, xn, first, v, local_sem, send_sem, recv_sem,
):
    wire = Wire(send_sem, recv_sem)
    r, f = wire.r, wire.f
    shard = in_ref.shape[0]
    quarter = shard // 4
    length, width = tokens.shape
    experts = 8
    scale = HD ** (-0.5)

    def rows(j, k):
        at = flips(f, j) * shard + flips(r, k) * quarter
        return pl.ds(pl.multiple_of(at, quarter), quarter)

    def shard_rows(j):
        return pl.ds(pl.multiple_of(flips(f, j) * shard, shard), shard)

    def local(n, src, dst):
        copy = pltpu.make_async_copy(src, dst, local_sem.at[n])
        copy.start()
        return copy

    own_in = local(0, in_ref, in_v.at[shard_rows(0)])
    own_out = local(1, out_ref, out_v.at[shard_rows(0)])
    own_tiny = local(2, tiny_ref, tiny_v.at[f])
    own_w = (local(3, e_in_ref, e_in), local(7, e_out_ref, e_out))
    wire.meet(PARTNERS)

    own = pl.ds(pl.multiple_of(r * quarter, quarter), quarter)
    land = {"in": in_v, "out": out_v}
    source = {"in": in_ref, "out": out_ref}
    got, got_t, got_w, got_g, got_x = {}, {}, {}, {}, {}

    for m in (2, 4, 6, 1):
        got_t[m] = wire.send(tiny_ref, tiny_v.at[f], 0, m)

    def own_pieces(name):
        for m in (2, 4, 6, 1):
            got[name, m, 0] = wire.send(
                source[name].at[own], land[name].at[rows(0, 0)], 0, m
            )

    def pass_on(name, j, k, d_r, d_f):
        at = land[name].at[rows(j, k)]
        return wire.send(at, at, d_r, d_f)

    def near_pieces(name):
        for m in (1, 2, 4, 6):
            got[name, m, 0].wait_recv()
            if m != 1:
                got[name, m + 1, 0] = pass_on(name, m, 0, 0, 1)
            got[name, m, 2] = pass_on(name, m, 0, 2, 0)
            got[name, m, 1] = pass_on(name, m, 0, 1, 0)

    def far_pieces(name):
        for m in (3, 5, 7):
            got[name, m, 0].wait_recv()
            got[name, m, 2] = pass_on(name, m, 0, 2, 0)
            got[name, m, 1] = pass_on(name, m, 0, 1, 0)

    def side_pieces(name):
        for m in (1, 2, 4, 6, 3, 5, 7):
            got[name, m, 2].wait_recv()
            got[name, m, 3] = pass_on(name, m, 2, 1, 0)

    def all_pieces(name):
        for m in range(1, 8):
            got[name, m, 1].wait_recv()
            got[name, m, 3].wait_recv()

    own_pieces("in")
    own_pieces("out")

    for m in (2, 4, 6):
        got_t[m].wait_recv()
        at = tiny_v.at[flips(f, m)]
        got_t[m + 1] = wire.send(at, at, 0, 1)
    for m in (1, 3, 5, 7):
        got_t[m].wait_recv()
    own_tiny.wait()
    lanes = tiny_v.shape[2]
    rt[...] = jnp.zeros_like(rt)
    for z in range(4):
        both = tiny_v[2 * z].astype(f32) + tiny_v[2 * z + 1].astype(f32)
        tiny_out[:, z * lanes : (z + 1) * lanes] = both
        row = lax.broadcasted_iota(jnp.int32, both.shape, 0)
        rt[0:16, z * lanes : (z + 1) * lanes] = jnp.where(row < experts, both, 0.0).astype(bf16)

    def norm_one(c, carry):
        at = pl.ds(pl.multiple_of(c * ROWS, ROWS), ROWS)
        x = tokens[at, :].astype(f32)
        unit = x * lax.rsqrt(jnp.mean(x * x, axis=-1, keepdims=True) + epsilon)
        xn[at, :] = (unit * tiny_out[experts : experts + 1, :]).astype(bf16)
        return carry

    lax.fori_loop(0, length // ROWS, norm_one, 0)
    spot = lax.broadcasted_iota(jnp.int32, bias.shape, 0)
    keys_at = lax.broadcasted_iota(jnp.int32, bias.shape, 1)
    seg_col = as_columns(seg_row[...])[:, 0:1].astype(jnp.int32)
    bias[...] = jnp.where((spot >= keys_at) & (seg_col == seg_row[...]), 0.0, -1e30)

    for copy in own_w:
        copy.wait()
    plane = lax.rem(f // 2, 2)
    split = e_in.shape[2]
    for c in range(0, mine_ref.shape[1], 128):
        part = e_in[:, :, c : c + 128] if c < split else e_out[:, :, c - split : c - split + 128]
        e_part[...] = jnp.swapaxes(part.astype(f32), 0, 1)
        mine_ref[:, c : c + 128] = e_part[2 * r + plane].astype(bf16)
        other_ref[:, c : c + 128] = e_part[2 * r + 1 - plane].astype(bf16)
    kept = [local(4, mine_ref, w_all.at[shard_rows(0)])]
    cut = shard // CUTS

    def send_w(n, src, d_f):
        at = pl.ds(n * cut, cut)
        to = pl.ds(pl.multiple_of(f * shard + n * cut, cut), cut)
        return wire.send(src.at[at], w_all.at[to], 0, d_f)

    def pass_w(n, m):
        got_w[m, n].wait_recv()
        at = w_all.at[pl.ds(pl.multiple_of(flips(f, m) * shard + n * cut, cut), cut)]
        got_w[m + 1, n] = wire.send(at, at, 0, 1)

    near_pieces("in")
    for n in range(CUTS):
        for m, src in ((2, other_ref), (4, mine_ref), (6, other_ref)):
            got_w[m, n] = send_w(n, src, m)
    got_g[4] = wire.send(g_ref, g_all.at[4], 0, 2)
    got_g[1] = wire.send(g_ref, g_all.at[1], 1, 0)
    far_pieces("in")
    near_pieces("out")
    far_pieces("out")
    for n in range(CUTS):
        got_w[1, n] = send_w(n, mine_ref, 1)
    got_g[2] = wire.send(g_ref, g_all.at[2], 2, 0)
    side_pieces("in")
    own_in.wait()
    all_pieces("in")

    def project(c, carry):
        at = pl.multiple_of(c * 256, 256)
        t = matmul(xn[...], in_v[:, pl.ds(at, 256)])
        turned = c < 7
        for n in (0, 1):
            part = t[:, n * HD : (n + 1) * HD]
            part = turn(
                part, jnp.where(turned, cos[...], 1.0), jnp.where(turned, sin[...], 0.0)
            )
            qkv[:, pl.ds(at + n * HD, HD)] = part.astype(bf16)
        return carry

    lax.fori_loop(0, 8, project, 0)
    pass_w(0, 2)
    pass_w(0, 4)
    lane = lax.broadcasted_iota(jnp.int32, (length, HD), 1)
    lse[...] = jnp.zeros_like(lse)

    def head(h, carry):
        at = pl.ds(pl.multiple_of(h * HD, HD), HD)
        group = h // GROUP
        k_at = pl.ds(pl.multiple_of(WQ + group * HD, HD), HD)
        v_at = pl.ds(pl.multiple_of(WQ + WK + group * HD, HD), HD)
        s = contract_cols(qkv[:, at], qkv[:, k_at]) * scale + bias[...]
        highest = jnp.max(s, axis=-1, keepdims=True)
        expo = jnp.exp(s - highest)
        total = jnp.sum(expo, axis=-1, keepdims=True)
        p = (expo * (1.0 / total)).astype(bf16)
        attn[:, at] = matmul(p, qkv[:, v_at]).astype(bf16)
        lse[...] = jnp.where(lane == h, highest + jnp.log(total), lse[...])
        return carry

    lax.fori_loop(0, HQ // 2, head, 0)
    side_pieces("out")
    pass_w(0, 6)
    pass_w(1, 2)
    lax.fori_loop(HQ // 2, HQ, head, 0)
    pass_w(1, 4)
    pass_w(1, 6)
    own_out.wait()
    all_pieces("out")
    kept.append(local(5, in_v, in_all))
    kept.append(local(6, out_v, out_all))

    def add_out(c, carry):
        at = pl.ds(pl.multiple_of(c * 256, 256), 256)
        first[:, at] = tokens[:, at].astype(f32) + contract_cols(attn[...], out_v[at, :])
        return carry

    lax.fori_loop(0, width // 256, add_out, 0)

    def norm_two(c, carry):
        at = pl.ds(pl.multiple_of(c * ROWS, ROWS), ROWS)
        h = first[at, :]
        unit = h * lax.rsqrt(jnp.mean(h * h, axis=-1, keepdims=True) + epsilon)
        v[at, 0:width] = (unit * tiny_out[experts + 1 : experts + 2, :]).astype(bf16)
        return carry

    lax.fori_loop(0, length // ROWS, norm_two, 0)
    logits = contract_cols(v[:, 0:width], rt[...])
    named = as_columns(routes[...]).astype(jnp.int32)
    chosen = lane == named[:, 0:1]
    for j in range(1, routes.shape[0]):
        chosen = chosen | (lane == named[:, j : j + 1])
    logits = jnp.where(chosen, logits, -1e30)
    expo = jnp.exp(logits - jnp.max(logits, axis=-1, keepdims=True))
    expo = jnp.where(chosen, expo, 0.0)
    gates = expo / jnp.sum(expo, axis=-1, keepdims=True)
    table[...] = gates
    high = gates.astype(bf16).astype(f32)
    v[:, width:] = (high + pltpu.roll(gates - high, experts, 1)).astype(bf16)

    got_x[2] = wire.send(v, xs.at[2], 2, 0)
    got_x[1] = wire.send(v, xs.at[1], 1, 0)
    for n, (src, dst) in enumerate(
        ((qkv, qkv_o), (attn, attn_o), (xn, xn_o), (first, first_o), (v, v_o))
    ):
        kept.append(local(8 + n, src, dst))
    for n in range(2, CUTS):
        for m in (2, 4, 6):
            pass_w(n, m)
    got_g[2].wait_recv()
    got_g[3] = wire.send(g_all.at[2], g_all.at[3], 1, 0)
    got_x[2].wait_recv()
    got_x[3] = wire.send(xs.at[2], xs.at[3], 1, 0)
    for n in range(CUTS):
        for m in (1, 3, 5, 7):
            got_w[m, n].wait_recv()
    for m in (1, 3, 4):
        got_g[m].wait_recv()
    for m in (1, 3):
        got_x[m].wait_recv()
    for copy in kept:
        copy.wait()
    wire.finish()


def front(
    tokens, seg_ids, routes, cos, sin, in_proj, out_proj, tiny, expert_in, expert_out, grad
):
    any_spec = pl.BlockSpec(memory_space=pl.ANY)
    vmem = pl.BlockSpec(memory_space=pltpu.VMEM)
    length, width = tokens.shape
    shard, cols = in_proj.shape
    whole = 8 * shard
    wide = width + EXTRA
    e_cols = expert_in.shape[2] + expert_out.shape[2]
    return pl.pallas_call(
        front_kernel,
        out_shape=[
            jax.ShapeDtypeStruct((length, cols), bf16),
            jax.ShapeDtypeStruct((length, WQ), bf16),
            jax.ShapeDtypeStruct((length, width), bf16),
            jax.ShapeDtypeStruct((length, width), f32),
            jax.ShapeDtypeStruct((length, HD), f32),
            jax.ShapeDtypeStruct((length, EXTRA), f32),
            jax.ShapeDtypeStruct((16, width), f32),
            jax.ShapeDtypeStruct((length, wide), bf16),
            jax.ShapeDtypeStruct((whole, cols), bf16),
            jax.ShapeDtypeStruct((whole, out_proj.shape[1]), bf16),
            jax.ShapeDtypeStruct((whole, e_cols), bf16),
            jax.ShapeDtypeStruct((5,) + grad.shape, bf16),
            jax.ShapeDtypeStruct((4, length, wide), bf16),
        ],
        in_specs=[vmem] * 5 + [any_spec] * 6,
        out_specs=[any_spec] * 4 + [vmem] * 3 + [any_spec] * 6,
        scratch_shapes=[
            pltpu.VMEM((whole, cols), bf16),
            pltpu.VMEM((whole, out_proj.shape[1]), bf16),
            pltpu.VMEM((8,) + tiny.shape, bf16),
            pltpu.VMEM((EXTRA, width), bf16),
            pltpu.VMEM((length, length), f32),
            pltpu.VMEM(expert_in.shape, bf16),
            pltpu.VMEM(expert_out.shape, bf16),
            pltpu.VMEM((expert_in.shape[1], shard, 128), f32),
            pltpu.VMEM((shard, e_cols), bf16),
            pltpu.VMEM((shard, e_cols), bf16),
            pltpu.VMEM((length, cols), bf16),
            pltpu.VMEM((length, WQ), bf16),
            pltpu.VMEM((length, width), bf16),
            pltpu.VMEM((length, width), f32),
            pltpu.VMEM((length, wide), bf16),
            pltpu.SemaphoreType.DMA((13,)),
            pltpu.SemaphoreType.DMA((FRONT_SENDS,)),
            pltpu.SemaphoreType.DMA((FRONT_SENDS,)),
        ],
        compiler_params=pltpu.CompilerParams(
            collective_id=1, has_side_effects=True, vmem_limit_bytes=56 * MIB
        ),
        name="front",
    )(
        tokens, seg_ids, routes.T, cos, sin,
        in_proj, out_proj, tiny, expert_in, expert_out, grad,
    )


ORDER = (3, 2, 4, 5, 7, 6, 1, 0)
UNROLL = True
WIDE_COLS = 256
GROUP_AT = {2: (2, 0), 4: (0, 2), 6: (2, 2)}


def pick(step, table):
    value = jnp.int32(table[-1])
    for i, item in enumerate(table[:-1]):
        value = jnp.where(step == i, item, value)
    return value


def group_kernel(
    v_ref, g_ref, xs, g_all, w_ref,
    mix_sum, dx_own, dx_in, grads, x_late, g_late,
    wbuf, xbuf, gbuf, xt, gt_, hidg, dgu, deven, dodd, rc, meven, modd, mrc, acc, stage,
    sem_w, sem_x, sem_g, sem_m, sem_s, send_sem, recv_sem,
):
    wire = Wire(send_sem, recv_sem)
    r, f = wire.r, wire.f
    length, width = g_ref.shape
    hidden = w_ref.shape[1] // 3
    half = length // 2
    low, top = pl.ds(0, half), pl.ds(half, half)
    expert = 2 * r + lax.rem(f // 2, 2)
    step_cols = 256

    load_w = pltpu.make_async_copy(w_ref, wbuf, sem_w.at[0])
    load_w.start()

    def load(step):
        slot = lax.rem(step, 2)
        k = pick(step, ORDER)

        @pl.when(k == 0)
        def _():
            pltpu.make_async_copy(v_ref, xbuf.at[slot], sem_x.at[slot]).start()
            pltpu.make_async_copy(g_ref, gbuf.at[slot], sem_g.at[slot]).start()

        for table, src_x, src_g in (
            ((1, 2, 3), xs, g_all), ((4,), x_late, g_all), ((5, 6, 7), x_late, g_late)
        ):

            @pl.when((k >= table[0]) & (k <= table[-1]))
            def _():
                pltpu.make_async_copy(src_x.at[k], xbuf.at[slot], sem_x.at[slot]).start()
                pltpu.make_async_copy(src_g.at[k], gbuf.at[slot], sem_g.at[slot]).start()

    load(jnp.int32(0))
    wire.meet(PARTNERS_GROUP)
    late_x = {4: wire.send(v_ref, x_late.at[4], 0, 2)}
    far = [
        wire.send(g_all.at[4], g_late.at[6], 2, 0),
        wire.send(xs.at[2, top], x_late.at[6, top], 0, 2),
    ]
    late_g = {5: wire.send(g_all.at[4], g_late.at[5], 1, 0)}
    far.append(wire.plan(x_late.at[4, low], x_late.at[6, low], 2, 0))
    late_x[5] = wire.plan(x_late.at[4], x_late.at[5], 1, 0)
    late_x[7] = wire.plan(x_late.at[6], x_late.at[7], 1, 0)
    late_g[7] = wire.plan(g_late.at[6], g_late.at[7], 1, 0)
    slots = {2: 0, 4: 1, 6: 2, 0: 3}
    to_core = {k: wire.plan(dodd.at[n % 2], rc.at[n], 1, 0) for k, n in slots.items()}
    mix_core = {k: wire.plan(modd.at[n % 2], mrc.at[n], 1, 0) for k, n in slots.items()}
    back = {k: wire.plan(deven.at[k // 2], dx_in.at[k // 2 - 1], *GROUP_AT[k]) for k in (2, 4, 6)}
    acc[...] = jnp.zeros_like(acc)
    lane = lax.broadcasted_iota(jnp.int32, (length, EXTRA), 1)
    load_w.wait()

    def keep_mix(k):
        n = slots[k] % 2
        return pltpu.make_async_copy(meven.at[n], mix_sum.at[k // 2], sem_m.at[n])

    def send_core(k):
        to_core[k].start()
        mix_core[k].start()

    def sent_core(k):
        to_core[k].wait_send()
        mix_core[k].wait_send()

    def complete(k):
        n = slots[k]
        to_core[k].wait_recv()
        deven[k // 2] = (deven[k // 2].astype(f32) + rc[n].astype(f32)).astype(bf16)
        if k in (4, 6):
            back[k].start()
        mix_core[k].wait_recv()
        meven[n % 2] = (meven[n % 2].astype(f32) + mrc[n].astype(f32)).astype(bf16)
        keep_mix(k).start()

    def block(step, carry):
        slot = lax.rem(step, 2)

        @pl.when((step == 0) | (step >= 4) & (step < 7))
        def _():
            load(step + 1)

        pltpu.make_async_copy(v_ref, xbuf.at[slot], sem_x.at[slot]).wait()
        pltpu.make_async_copy(g_ref, gbuf.at[slot], sem_g.at[slot]).wait()
        extra = xbuf[slot, :, width:].astype(f32)
        mine = (lane == expert) | (lane == expert + 8)
        gate = jnp.sum(jnp.where(mine, extra, 0.0), axis=1, keepdims=True)
        here = pl.ds(pl.multiple_of(slot * length, length), length)
        xt[:, here] = xbuf[slot, :, :width].T
        gt_[:, here] = gbuf[slot].T

        def first(c, dgate):
            at = pl.multiple_of(c * step_cols, step_cols)
            u = matmul(xbuf[slot, :, :width], wbuf[:, pl.ds(at, step_cols)])
            up = matmul(xbuf[slot, :, :width], wbuf[:, pl.ds(hidden + at, step_cols)])
            rev = matmul(gbuf[slot], wbuf[:, pl.ds(2 * hidden + at, step_cols)])
            sig = 1.0 / (1.0 + jnp.exp(-u))
            act = u * sig
            hid = act * up
            hidg[here, pl.ds(at, step_cols)] = (gate * hid).astype(bf16)
            dgate = dgate + jnp.sum(rev * hid, axis=1, keepdims=True)
            dhid = gate * rev
            dgu[here, pl.ds(at, step_cols)] = (
                dhid * up * sig * (1.0 + u * (1.0 - sig))
            ).astype(bf16)
            dgu[here, pl.ds(hidden + at, step_cols)] = (dhid * act).astype(bf16)
            return dgate

        dgate = lax.fori_loop(
            0, hidden // step_cols, first, jnp.zeros((length, 1), f32), unroll=UNROLL
        )
        high = dgate.astype(bf16).astype(f32)
        rest = dgate - high
        tail = (
            jnp.where(lane == expert, high, 0.0) + jnp.where(lane == expert + 8, rest, 0.0)
        ).astype(bf16)

        def out_parts(dst_d, n_d, dst_m, n_m):
            def second(c, carry):
                at = pl.multiple_of(c * step_cols, step_cols)
                dst_d[n_d, :, pl.ds(at, step_cols)] = contract_cols(
                    dgu[here, :], wbuf[pl.ds(at, step_cols), pl.ds(0, 2 * hidden)]
                ).astype(bf16)
                dst_m[n_m, :, pl.ds(at, step_cols)] = contract_cols(
                    hidg[here, :], wbuf[pl.ds(at, step_cols), pl.ds(2 * hidden, hidden)]
                ).astype(bf16)
                return carry

            lax.fori_loop(0, width // step_cols, second, 0, unroll=UNROLL)
            dst_d[n_d, :, width:] = tail

        slot_two = pick(step, (0, 0, 1, 1, 0, 0, 1, 1))
        k = pick(step, ORDER)

        @pl.when(step == 4)
        def _():
            sent_core(2)

        @pl.when(step == 6)
        def _():
            sent_core(4)

        @pl.when(step == 5)
        def _():
            keep_mix(2).wait()

        @pl.when(step == 7)
        def _():
            keep_mix(4).wait()

        @pl.when(lax.rem(k, 2) == 1)
        def _():
            out_parts(dodd, slot_two, modd, slot_two)

        @pl.when(lax.rem(k, 2) == 0)
        def _():
            out_parts(deven, k // 2, meven, slot_two)

        def come_5():
            late_x[5].wait_recv()
            late_g[5].wait_recv()
            load(step + 1)

        def come_6():
            for copy in far:
                copy.wait_recv()
            late_x[7].start()
            late_g[7].start()

        for at_step, todo in (
            (0, (lambda: send_core(2),)),
            (1, (lambda: complete(2),)),
            (2, (come_5,)),
            (3, (lambda: send_core(4), come_6)),
            (4, (lambda: complete(4), lambda: send_core(6))),
            (5, (lambda: complete(6),)),
            (6, (lambda: send_core(0),)),
            (7, (lambda: complete(0),)),
        ):

            @pl.when(step == at_step)
            def _():
                for do in todo:
                    do()

        @pl.when(slot == 1)
        def _():
            def third(c, carry):
                at = pl.multiple_of(c * WIDE_COLS, WIDE_COLS)
                acc[:, pl.ds(at, WIDE_COLS)] += matmul(xt[...], dgu[:, pl.ds(at, WIDE_COLS)])
                return carry

            lax.fori_loop(0, 2 * hidden // WIDE_COLS, third, 0, unroll=UNROLL)

            def fourth(c, carry):
                at = pl.multiple_of(c * WIDE_COLS, WIDE_COLS)
                acc[:, pl.ds(2 * hidden + at, WIDE_COLS)] += matmul(
                    gt_[...], hidg[:, pl.ds(at, WIDE_COLS)]
                )
                return carry

            lax.fori_loop(0, hidden // WIDE_COLS, fourth, 0, unroll=UNROLL)

        @pl.when(step == 1)
        def _():
            late_x[4].wait_recv()
            late_x[5].start()
            far[2].start()
            back[2].start()
            load(step + 1)

        @pl.when(step == 3)
        def _():
            late_x[7].wait_recv()
            late_g[7].wait_recv()
            load(step + 1)

        return carry

    lax.fori_loop(0, 8, block, 0)
    keep = pltpu.make_async_copy(deven.at[0], dx_own, sem_w.at[0])
    keep.start()
    parts = 8
    rows = width // parts

    def out(j, slot):
        return pltpu.make_async_copy(
            stage.at[slot], grads.at[pl.ds(j * rows, rows)], sem_s.at[slot]
        )

    for j in range(parts):
        slot = j % 2
        if j >= 2:
            out(j - 2, slot).wait()
        stage[slot] = acc[j * rows : (j + 1) * rows].astype(bf16)
        out(j, slot).start()
    for j in range(parts - 2, parts):
        out(j, j % 2).wait()
    keep.wait()
    keep_mix(6).wait()
    keep_mix(0).wait()
    for k in (2, 4, 6):
        back[k].wait_recv()
        back[k].wait_send()
    sent_core(6)
    sent_core(0)
    for copy in (far[2], late_x[5], late_x[7], late_g[7]):
        copy.wait_send()
    wire.finish()


PARTNERS_GROUP = ((1, 0), (2, 0), (0, 2), (2, 2))
GROUP_SENDS = 8 + 8 + 3


def run_group(v, grad, xs, g_all, w):
    length, width = grad.shape
    wide = v.shape[1]
    cols = w.shape[1]
    hidden = cols // 3
    any_spec = pl.BlockSpec(memory_space=pl.ANY)
    return pl.pallas_call(
        group_kernel,
        out_shape=[
            jax.ShapeDtypeStruct((4, length, width), bf16),
            jax.ShapeDtypeStruct((length, wide), bf16),
            jax.ShapeDtypeStruct((3, length, wide), bf16),
            jax.ShapeDtypeStruct((width, cols), bf16),
            jax.ShapeDtypeStruct((8, length, wide), bf16),
            jax.ShapeDtypeStruct((8, length, width), bf16),
        ],
        in_specs=[any_spec] * 5,
        out_specs=[any_spec] * 6,
        scratch_shapes=[
            pltpu.VMEM((width, cols), bf16),
            pltpu.VMEM((2, length, wide), bf16),
            pltpu.VMEM((2, length, width), bf16),
            pltpu.VMEM((width, 2 * length), bf16),
            pltpu.VMEM((width, 2 * length), bf16),
            pltpu.VMEM((2 * length, hidden), bf16),
            pltpu.VMEM((2 * length, 2 * hidden), bf16),
            pltpu.VMEM((4, length, wide), bf16),
            pltpu.VMEM((2, length, wide), bf16),
            pltpu.VMEM((4, length, wide), bf16),
            pltpu.VMEM((2, length, width), bf16),
            pltpu.VMEM((2, length, width), bf16),
            pltpu.VMEM((4, length, width), bf16),
            pltpu.VMEM((width, cols), f32),
            pltpu.VMEM((2, width // 8, cols), bf16),
            pltpu.SemaphoreType.DMA((1,)),
            pltpu.SemaphoreType.DMA((2,)),
            pltpu.SemaphoreType.DMA((2,)),
            pltpu.SemaphoreType.DMA((2,)),
            pltpu.SemaphoreType.DMA((2,)),
            pltpu.SemaphoreType.DMA((GROUP_SENDS,)),
            pltpu.SemaphoreType.DMA((GROUP_SENDS,)),
        ],
        compiler_params=pltpu.CompilerParams(
            collective_id=2, has_side_effects=True, vmem_limit_bytes=62 * MIB
        ),
        cost_estimate=pl.CostEstimate(
            flops=48 * length * width * cols,
            bytes_accessed=64 * length * width + 4 * width * cols,
            transcendentals=8 * length * hidden,
        ),
        name="group",
    )(v, grad, xs, g_all, w)


PARTNERS_BACK = ((1, 0), (2, 0), (3, 0), (0, 1), (0, 2), (0, 4), (0, 6))
TERMS = 16
BACK_SENDS = 3 + 8 + 6 + 3 + 2 + 3 + 2 * 4 + 2 * 3 + 1 + 6 + 6


def back_kernel(
    dx_h, g_h, first_h, table, tiny, v_h, tokens_h, qkv_h, lse, cos, sin, seg_row,
    dx_in, grads, mix_sum, attn, xn, in_all, out_all,
    tokens_grad,
    g_out, mix_in, d_out, xn_core,
    in_v, out_v, mix_v, gl, gy, gz, act_v, aq_v, pq, wo, wi, wyo, wyi, wzo, wzi, wxo, own_d,
    dn, dxn, dl, dattn, dproj, dkv, bias, tbuf,
    dx_own, g_ref, first, v, tokens, qkv,
    local_sem, send_sem, recv_sem,
):
    wire = Wire(send_sem, recv_sem)
    r, f = wire.r, wire.f
    shard = gl.shape[1]
    length, width = tokens_h.shape
    experts = 8
    low = lax.rem(f // 2, 2)
    cols_p, cols_a = pq.shape[1], aq_v.shape[1]
    scale = HD ** (-0.5)
    used = [0]

    def local(src, dst):
        copy = pltpu.make_async_copy(src, dst, local_sem.at[used[0]])
        copy.start()
        used[0] += 1
        return copy

    def shard_rows(j):
        return pl.ds(pl.multiple_of(flips(f, j) * shard, shard), shard)

    def token_rows(k):
        return pl.ds(k * length, length)

    def part_of(k, cols):
        return pl.ds(pl.multiple_of(flips(r, k) * cols, cols), cols)

    def add(u, w):
        return (u.astype(f32) + w.astype(f32)).astype(bf16)

    half = lax.rem(r, 2)
    side = r // 2

    def half_of(index):
        return pl.ds(pl.multiple_of(index * cols_a, cols_a), cols_a)

    load_dx = [
        local(dx_in.at[n], in_v.at[token_rows(n), pl.ds(0, dx_in.shape[2])]) for n in range(3)
    ]
    load_dx += [
        local(dx_h, dx_own), local(v_h, v), local(first_h, first), local(g_h, g_ref),
        local(qkv_h, qkv), local(tokens_h, tokens),
    ]
    load_out = local(out_all, out_v)
    load_g = {j: local(grads.at[shard_rows(j)], gl.at[j // 2]) for j in (4, 6, 2, 0)}
    load_a = local(attn.at[:, half_of(half)], aq_v.at[token_rows(0)])
    load_mix = local(mix_sum.at[2], mix_v.at[0])
    wire.meet(PARTNERS_BACK)
    got_y, got_m = {}, {}
    place_z = f // 2
    inner = (place_z == 1) | (place_z == 2)
    cut = shard // 2
    got_z = {}
    for j in (4, 6, 2, 0):
        for n in (0, 1):
            at = pl.ds(pl.multiple_of(flips(f, j + 1) * shard + n * cut, cut), cut)
            got_y[j, n] = wire.plan(grads.at[at], gy.at[j // 2, pl.ds(n * cut, cut)], 0, 1)
            wire.sent.append(got_y[j, n])
            if j:
                at = pl.ds(n * cut, cut)
                got_z[j, n] = wire.plan(gl.at[j // 2, at], gz.at[j // 2 - 1, at], 0, j)
                wire.sent.append(got_z[j, n])

    def by_place(do, outer_j, inner_j, n):
        @pl.when(inner)
        def _():
            do(inner_j, n)

        @pl.when(jnp.logical_not(inner))
        def _():
            do(outer_j, n)

    def send_y(j, n):
        got_y[j, n].start()

    for outer_j, inner_j in ((4, 2), (6, 4), (2, 6)):
        for n in (0, 1):
            by_place(send_y, outer_j, inner_j, n)
    for n in (0, 1):
        send_y(0, n)
    got_a = wire.send(attn.at[:, half_of(1 - half)], aq_v.at[token_rows(1)], 1, 0)
    got_m[6] = wire.send(mix_sum.at[3], mix_v.at[1], 2, 0)
    got_n = {2: wire.send(xn, act_v.at[token_rows(2)], 2, 0), 1: wire.send(xn, xn_core, 1, 0)}

    spot = lax.broadcasted_iota(jnp.int32, bias.shape, 0)
    keys_at = lax.broadcasted_iota(jnp.int32, bias.shape, 1)
    seg_col = as_columns(seg_row[...])[:, 0:1].astype(jnp.int32)
    bias[...] = jnp.where((spot >= keys_at) & (seg_col == seg_row[...]), 0.0, -1e30)
    tbuf[...] = jnp.zeros_like(tbuf)
    for copy in load_dx:
        copy.wait()

    def sum_dx(c, carry):
        at = pl.ds(pl.multiple_of(c * ROWS, ROWS), ROWS)
        d = dx_own[at, :].astype(f32)
        for n in range(3):
            here = pl.ds(pl.multiple_of(n * length + c * ROWS, ROWS), ROWS)
            d = d + in_v[here, 0 : dx_own.shape[1]].astype(f32)
        dn[at, :] = d[:, :width]
        dgate = d[:, width:]
        dgate = dgate + pltpu.roll(dgate, EXTRA - experts, 1)
        gates = table[at, :]
        mean = jnp.sum(gates * dgate, axis=-1, keepdims=True)
        dl[at, :] = (gates * (dgate - mean)).astype(bf16)
        return carry

    lax.fori_loop(0, length // ROWS, sum_dx, 0)
    load_in = local(in_all, in_v)
    dlt = dl[...].T[0:16]

    def add_router(c, carry):
        at = pl.ds(pl.multiple_of(c * 256, 256), 256)
        row = lax.broadcasted_iota(jnp.int32, (16, 256), 0)
        router = jnp.where(row < experts, tiny[:, at], 0.0).astype(bf16)
        dn[:, at] = dn[:, at] + matmul(dl[:, 0:16], router)
        tbuf[:, at] = matmul(dlt, v[:, at])
        return carry

    lax.fori_loop(0, width // 256, add_router, 0)

    def norm_two(c, gain):
        at = pl.ds(pl.multiple_of(c * ROWS, ROWS), ROWS)
        h = first[at, :]
        r2 = lax.rsqrt(jnp.mean(h * h, axis=-1, keepdims=True) + epsilon)
        unit = h * r2
        d = dn[at, :]
        gain = gain + jnp.sum(d * unit, axis=0, keepdims=True)
        d = d * tiny[experts + 1 : experts + 2, :]
        d = g_ref[at, :].astype(f32) + r2 * (
            d - unit * jnp.mean(d * unit, axis=-1, keepdims=True)
        )
        dn[at, :] = d
        act_v[at, :] = d.astype(bf16)
        return gain

    gain_two = lax.fori_loop(0, length // ROWS, norm_two, jnp.zeros((1, width), f32))
    tbuf[experts + 1 : experts + 2, :] = gain_two
    got_r = wire.send(act_v.at[token_rows(0)], act_v.at[token_rows(1)], 1, 0)
    def pass_y(j, n):
        if n == 0:
            load_g[j].wait()
        got_y[j, n].wait_recv()
        at = pl.ds(n * cut, cut)
        gl[j // 2, at] = add(gl[j // 2, at], gy[j // 2, at])
        got_z[j, n].start()

    def came(got_some, j):
        for n in (0, 1):
            got_some[j, n].wait_recv()

    load_out.wait()

    def to_attn(c, carry):
        at = pl.ds(pl.multiple_of(c * 256, 256), 256)
        dattn[:, at] = matmul(act_v[0:length, :], out_v[:, at]).astype(bf16)
        return carry

    lax.fori_loop(0, WQ // 256, to_attn, 0)
    by_place(pass_y, 4, 2, 0)
    lane = lax.broadcasted_iota(jnp.int32, (length, HD), 1)

    def turn_back(w):
        return w * cos[...] - pltpu.roll(w, HD // 2, 1) * sin[...]

    for group in range(KV):
        k_at = pl.ds(WQ + group * HD, HD)
        v_at = pl.ds(WQ + WK + group * HD, HD)
        dkv[...] = jnp.zeros_like(dkv)

        def head(i, carry):
            h = group * GROUP + i
            at = pl.ds(pl.multiple_of(h * HD, HD), HD)
            s = contract_cols(qkv[:, at], qkv[:, k_at]) * scale + bias[...]
            level = jnp.sum(jnp.where(lane == h, lse[...], 0.0), axis=1, keepdims=True)
            p = jnp.exp(s - level)
            da = dattn[:, at]
            dp = contract_cols(da, qkv[:, v_at])
            delta = jnp.sum(p * dp, axis=-1, keepdims=True)
            ds = (p * (dp - delta)).astype(bf16)
            dkv[1] += contract_rows(p.astype(bf16), da)
            dkv[0] += contract_rows(ds, qkv[:, at])
            dproj[:, at] = turn_back(matmul(ds, qkv[:, k_at]) * scale).astype(bf16)
            return carry

        lax.fori_loop(0, GROUP, head, 0)
        if group == 0:
            by_place(pass_y, 4, 2, 1)
            load_mix.wait()
            got_m[6].wait_recv()
            mix_v[0] = add(mix_v[0], mix_v[1])
            got_m[4] = wire.send(mix_v.at[0], mix_in.at[1], 0, 2)
        dproj[:, k_at] = turn_back(dkv[0] * scale).astype(bf16)
        dproj[:, v_at] = dkv[1].astype(bf16)

    keep_p = local(dproj.at[:, part_of(0, cols_p)], pq.at[token_rows(0)])
    got_p = {}
    for k in (2, 3, 1):
        got_p[k] = wire.send(dproj.at[:, part_of(k, cols_p)], pq.at[token_rows(k)], k, 0)

    got_m[2] = wire.send(mix_sum.at[1], mix_in.at[0], 2, 0)
    by_place(pass_y, 6, 4, 0)

    load_a.wait()
    got_a.wait_recv()
    got_r.wait_recv()

    def dense_out(c, carry):
        at = pl.ds(pl.multiple_of(c * 256, 256), 256)
        wo[at, :] = matmul(act_v[0 : 2 * length, at].T, aq_v[...]).astype(bf16)
        return carry

    lax.fori_loop(0, width // 256, dense_out, 0)
    got_r.wait_send()
    load_x = [local(xn, act_v.at[token_rows(0)])]
    got_n[1].wait_recv()
    load_x.append(local(xn_core, act_v.at[token_rows(1)]))
    got_wo, got_wi, got_wzo, got_wzi = {}, {}, {}, {}
    for j in (4, 6, 2, 0):
        got_wo[j] = wire.send(wo.at[shard_rows(j + 1)], wyo.at[j // 2], 0, 1)

    by_place(pass_y, 6, 4, 1)

    load_in.wait()

    def to_norm(c, carry):
        at = pl.ds(pl.multiple_of(c * 256, 256), 256)
        dxn[:, at] = contract_cols(dproj[...], in_v[at, :])
        return carry

    lax.fori_loop(0, width // 256, to_norm, 0)

    def norm_one(c, gain):
        at = pl.ds(pl.multiple_of(c * ROWS, ROWS), ROWS)
        x = tokens[at, :].astype(f32)
        r1 = lax.rsqrt(jnp.mean(x * x, axis=-1, keepdims=True) + epsilon)
        unit = x * r1
        d = dxn[at, :]
        gain = gain + jnp.sum(d * unit, axis=0, keepdims=True)
        d = d * tiny[experts : experts + 1, :]
        d = dn[at, :] + r1 * (d - unit * jnp.mean(d * unit, axis=-1, keepdims=True))
        tokens_grad[at, :] = d.astype(bf16)
        return gain

    gain_one = lax.fori_loop(0, length // ROWS, norm_one, jnp.zeros((1, width), f32))
    tbuf[experts : experts + 1, :] = gain_one

    by_place(pass_y, 2, 6, 0)
    by_place(pass_y, 2, 6, 1)
    mine, other = 2 * r + low, 2 * r + 1 - low
    load_g[0].wait()
    came(got_y, 0)
    came(got_z, 4)
    gl[0] = (gl[0].astype(f32) + gy[0].astype(f32) + gz[1].astype(f32)).astype(bf16)
    kept = [local(gl.at[0], g_out.at[mine])]
    got_e = {}

    got_n[2].wait_recv()
    got_n[3] = wire.send(act_v.at[token_rows(2)], act_v.at[token_rows(3)], 1, 0)
    keep_p.wait()
    for copy in load_x:
        copy.wait()
    for k in (1, 2, 3):
        got_p[k].wait_recv()
    got_n[3].wait_recv()
    got_e[2, 0] = wire.send(gl.at[0], g_out.at[mine], 2, 0)
    got_e[1, 0] = wire.send(gl.at[0], g_out.at[mine], 1, 0)

    tall = shard + TERMS

    def tall_rows(j):
        return pl.ds(pl.multiple_of(flips(f, j) * tall, TERMS), tall)

    for z in range(4):
        lanes = slice(2 * z * shard, 2 * (z + 1) * shard)
        both = matmul(act_v[:, lanes].T, pq[...]).astype(bf16)
        for y in (0, 1):
            top = (2 * z + y) * tall
            wi[top : top + shard, :] = both[y * shard : (y + 1) * shard]
            wi[top + shard : top + tall, :] = jnp.zeros((TERMS, cols_p), bf16)
            wi[top + shard : top + tall, 0 : 2 * shard] = tbuf[:, lanes].astype(bf16)
    for j in (4, 6, 2, 0):
        got_wi[j] = wire.send(wi.at[tall_rows(j + 1)], wyi.at[j // 2], 0, 1)
    for j in (4, 6, 2):
        got_wo[j].wait_recv()
        wyo[j // 2] = add(wo[shard_rows(j), :], wyo[j // 2])
        got_wzo[j] = wire.send(wyo.at[j // 2], wzo.at[j // 2 - 1], 0, j)

    came(got_z, 2)
    came(got_z, 6)
    gz[0] = add(gz[0], gz[2])
    kept.append(local(gz.at[0], g_out.at[other]))
    got_e[2, 1] = wire.send(gz.at[0], g_out.at[other], 2, 0)
    got_e[1, 1] = wire.send(gz.at[0], g_out.at[other], 1, 0)

    for j in (4, 6, 2):
        got_wi[j].wait_recv()
        wyi[j // 2] = add(wi[tall_rows(j), :], wyi[j // 2])
        got_wzi[j] = wire.send(wyi.at[j // 2], wzi.at[j // 2 - 1], 0, j)

    def own_rows(w, rows, y, z, got_w, got_zs):
        got_w[0].wait_recv()
        total = w[rows, :].astype(f32) + y[0].astype(f32)
        for j in (2, 4, 6):
            got_zs[j].wait_recv()
            total = total + z[j // 2 - 1].astype(f32)
        return total

    wxo[0] = own_rows(wo, shard_rows(0), wyo, wzo, got_wo, got_wzo).astype(bf16)
    quarter = cols_a // 2

    def quarter_of(index):
        return pl.ds(pl.multiple_of(index * quarter, quarter), quarter)

    got_x = wire.send(
        wxo.at[0, :, quarter_of(1 - side)], wxo.at[1, :, pl.ds(0, quarter)], 2, 0
    )
    got_x.wait_recv()
    own_d[shard:, cols_p:] = jnp.zeros((TERMS, quarter), bf16)
    own_d[0:shard, cols_p:] = add(wxo[0, :, quarter_of(side)], wxo[1, :, 0:quarter])
    got_d = {}

    def send_d(n, columns):
        kept.append(local(own_d.at[:, columns], d_out.at[r, :, columns]))
        for k in (2, 1):
            got_d[k, n] = wire.send(own_d.at[:, columns], d_out.at[r, :, columns], k, 0)

    parts_d = (pl.ds(cols_p, quarter), pl.ds(0, cols_p))
    send_d(0, parts_d[0])
    own_d[:, 0:cols_p] = own_rows(wi, tall_rows(0), wyi, wzi, got_wi, got_wzi).astype(bf16)
    send_d(1, parts_d[1])

    far = flips(r, 2)
    for n, e in ((0, 2 * far + low), (1, 2 * far + 1 - low)):
        got_e[2, n].wait_recv()
        got_e[3, n] = wire.send(g_out.at[e], g_out.at[e], 1, 0)
    for n, columns in enumerate(parts_d):
        got_d[2, n].wait_recv()
        at = d_out.at[far, :, columns]
        got_d[3, n] = wire.send(at, at, 1, 0)
    for k in (1, 3):
        for n in (0, 1):
            got_e[k, n].wait_recv()
    for k in (1, 3):
        for n in (0, 1):
            got_d[k, n].wait_recv()
    for k in (2, 4):
        got_m[k].wait_recv()
    for copy in kept:
        copy.wait()
    wire.finish((got_r,))


def run_back(
    dx_own, grad, first, table, tiny, v, tokens, qkv, lse, cos, sin, seg_ids,
    dx_in, grads, mix_sum, attn, xn, in_all, out_all,
):
    any_spec = pl.BlockSpec(memory_space=pl.ANY)
    vmem = pl.BlockSpec(memory_space=pltpu.VMEM)
    length, width = tokens.shape
    shard = width // 8
    cols = grads.shape[1]
    cols_p, cols_a = qkv.shape[1] // 4, attn.shape[1] // 2
    return pl.pallas_call(
        back_kernel,
        out_shape=[
            jax.ShapeDtypeStruct((length, width), bf16),
            jax.ShapeDtypeStruct((8, shard, cols), bf16),
            jax.ShapeDtypeStruct((2, length, width), bf16),
            jax.ShapeDtypeStruct((4, shard + TERMS, cols_p + cols_a // 2), bf16),
            jax.ShapeDtypeStruct((length, width), bf16),
        ],
        in_specs=[any_spec] * 3 + [vmem] * 2 + [any_spec] * 3 + [vmem] * 4 + [any_spec] * 7,
        out_specs=[vmem] + [any_spec] * 4,
        scratch_shapes=[
            pltpu.VMEM(in_all.shape, bf16),
            pltpu.VMEM(out_all.shape, bf16),
            pltpu.VMEM((2, length, width), bf16),
            pltpu.VMEM((4, shard, cols), bf16),
            pltpu.VMEM((4, shard, cols), bf16),
            pltpu.VMEM((3, shard, cols), bf16),
            pltpu.VMEM((4 * length, width), bf16),
            pltpu.VMEM((2 * length, cols_a), bf16),
            pltpu.VMEM((4 * length, cols_p), bf16),
            pltpu.VMEM((width, cols_a), bf16),
            pltpu.VMEM((width + 8 * TERMS, cols_p), bf16),
            pltpu.VMEM((4, shard, cols_a), bf16),
            pltpu.VMEM((4, shard + TERMS, cols_p), bf16),
            pltpu.VMEM((3, shard, cols_a), bf16),
            pltpu.VMEM((3, shard + TERMS, cols_p), bf16),
            pltpu.VMEM((2, shard, cols_a), bf16),
            pltpu.VMEM((shard + TERMS, cols_p + cols_a // 2), bf16),
            pltpu.VMEM((length, width), f32),
            pltpu.VMEM((length, width), f32),
            pltpu.VMEM((length, EXTRA), bf16),
            pltpu.VMEM((length, WQ), bf16),
            pltpu.VMEM(qkv.shape, bf16),
            pltpu.VMEM((2, length, HD), f32),
            pltpu.VMEM((length, length), f32),
            pltpu.VMEM((TERMS, width), f32),
            pltpu.VMEM(dx_own.shape, bf16),
            pltpu.VMEM(grad.shape, bf16),
            pltpu.VMEM(first.shape, f32),
            pltpu.VMEM(v.shape, bf16),
            pltpu.VMEM(tokens.shape, bf16),
            pltpu.VMEM(qkv.shape, bf16),
            pltpu.SemaphoreType.DMA((26,)),
            pltpu.SemaphoreType.DMA((BACK_SENDS,)),
            pltpu.SemaphoreType.DMA((BACK_SENDS,)),
        ],
        compiler_params=pltpu.CompilerParams(
            collective_id=3, has_side_effects=True, vmem_limit_bytes=62 * MIB
        ),
        name="back",
    )(
        dx_own, grad, first, table, tiny, v, tokens, qkv, lse, cos, sin,
        seg_ids,
        dx_in, grads, mix_sum, attn, xn, in_all, out_all,
    )


def finish_kernel(sums, dense, first, own, parts, e_in, e_out, in_grad, out_grad, mixed):
    split = e_in.shape[2]
    for c in range(0, sums.shape[2], 128):
        part = jnp.swapaxes(sums[:, :, c : c + 128].astype(f32), 0, 1)
        if c < split:
            e_in[:, :, c : c + 128] = part
        else:
            e_out[:, :, c - split : c - split + 128] = part
    cut = in_grad.shape[1] // 4
    quarter = out_grad.shape[1] // 4
    for r in range(4):
        in_grad[:, r * cut : (r + 1) * cut] = dense[r, :, :cut].astype(f32)
        place = 2 * (r % 2) + r // 2
        out_grad[:, place * quarter : (place + 1) * quarter] = dense[r, :, cut:].astype(f32)
    total = first[...] + own[0].astype(f32)
    for n in range(parts.shape[0]):
        total = total + parts[n].astype(f32)
    mixed[...] = total.astype(bf16)


def run_finish(expert_sum, dense, first, mix_sum, mix_in, hidden):
    n_experts, shard, cols = expert_sum.shape
    length, width = first.shape
    steps = 12
    rows, tokens = shard // steps, length // steps
    cut = dense.shape[2] - width // 4
    return pl.pallas_call(
        finish_kernel,
        grid=(steps,),
        out_shape=[
            jax.ShapeDtypeStruct((shard, n_experts, 2 * hidden), f32),
            jax.ShapeDtypeStruct((shard, n_experts, hidden), f32),
            jax.ShapeDtypeStruct((shard, 4 * cut), f32),
            jax.ShapeDtypeStruct((shard, width), f32),
            jax.ShapeDtypeStruct((length, width), bf16),
        ],
        in_specs=[
            pl.BlockSpec((n_experts, rows, cols), lambda i: (0, i, 0)),
            pl.BlockSpec((4, rows, dense.shape[2]), lambda i: (0, i, 0)),
            pl.BlockSpec((tokens, width), lambda i: (i, 0)),
            pl.BlockSpec((1, tokens, width), lambda i: (0, i, 0)),
            pl.BlockSpec((mix_in.shape[0], tokens, width), lambda i: (0, i, 0)),
        ],
        out_specs=[
            pl.BlockSpec((rows, n_experts, 2 * hidden), lambda i: (i, 0, 0)),
            pl.BlockSpec((rows, n_experts, hidden), lambda i: (i, 0, 0)),
            pl.BlockSpec((rows, 4 * cut), lambda i: (i, 0)),
            pl.BlockSpec((rows, width), lambda i: (i, 0)),
            pl.BlockSpec((tokens, width), lambda i: (i, 0)),
        ],
        compiler_params=pltpu.CompilerParams(vmem_limit_bytes=62 * MIB),
        name="finish",
    )(expert_sum, dense, first, mix_sum, mix_in)


def near_layer(
    tokens, seg_ids, routes, in_proj, out_proj, router, norm_gains, expert_in, expert_out,
    out_grad,
):
    length, width = tokens.shape
    experts = router.shape[1]
    hidden = expert_out.shape[2]
    shard = router.shape[0]
    f = lax.axis_index("fsdp")
    cosine, sine = [t[:, 0] for t in tables(length)]
    cos = jnp.concatenate([cosine, cosine], axis=1)
    sin = jnp.concatenate([-sine, sine], axis=1)
    tiny = jnp.concatenate(
        [router.T, norm_gains.T, jnp.zeros((16 - experts - 2, shard), bf16)], axis=0
    )
    none = jnp.zeros_like(tiny)
    tiny = jnp.where(
        f % 2 == 0,
        jnp.concatenate([tiny, none], axis=1),
        jnp.concatenate([none, tiny], axis=1),
    )
    qkv, attn, xn, first, lse, table, small, v, in_all, out_all, w_all, g_all, xs = front(
        tokens, seg_ids, routes, cos, sin, in_proj, out_proj, tiny, expert_in, expert_out,
        out_grad,
    )
    mix_sum, dx_own, dx_in, grads, _, _ = run_group(v, out_grad, xs, g_all, w_all)
    tokens_grad, expert_sum, mix_in, dense, _ = run_back(
        dx_own, out_grad, first, table, small, v, tokens, qkv, lse, cos, sin, seg_ids,
        dx_in, grads, mix_sum, attn, xn, in_all, out_all,
    )
    e_in, e_out, in_grad, out_proj_grad, mixed = run_finish(
        expert_sum, dense, first, mix_sum, mix_in, hidden
    )
    terms = jnp.sum(dense[:, shard:, : 2 * shard].astype(f32), axis=0)
    terms = jnp.where(f % 2 == 0, terms[:, :shard], terms[:, shard:]).T
    return (
        mixed,
        tokens_grad,
        in_grad,
        out_proj_grad,
        terms[:, :experts],
        terms[:, experts : experts + 2],
        e_in,
        e_out,
    )


class Wide:
    def __init__(self, n_rep, n_fsdp):
        self.n_rep, self.n_fsdp = n_rep, n_fsdp

    def spread(self, value):
        every = lax.all_gather(value, "replica", axis=0)
        return [every[k] for k in range(self.n_rep)]

    def collect(self, parts):
        return lax.psum_scatter(jnp.stack(parts), "replica", scatter_dimension=0).astype(f32)

    def start(self, in_proj, out_proj, tiny, expert_in, expert_out, grad):
        r = lax.axis_index("replica")
        per = expert_in.shape[1] // self.n_rep
        weights = []
        for i in range(per):
            both = jnp.concatenate(
                [
                    lax.dynamic_index_in_dim(expert_in, per * r + i, 1, keepdims=False),
                    lax.dynamic_index_in_dim(expert_out, per * r + i, 1, keepdims=False),
                ],
                axis=1,
            )
            weights.append(lax.all_gather(both, "fsdp", axis=0, tiled=True))
        return (
            lax.all_gather(in_proj, "fsdp", axis=0, tiled=True),
            lax.all_gather(out_proj, "fsdp", axis=0, tiled=True),
            lax.all_gather(tiny, "fsdp", axis=1, tiled=True),
            (weights, self.spread(grad)),
        )

    def experts(self, payload, held):
        weights, gs = held
        xs = self.spread(payload)
        per = len(weights)
        mixes, dxs, grads = None, None, []
        for i, w in enumerate(weights):

            def expert_of(i=i):
                return per * lax.axis_index("replica") + i

            mix, dx, grad = run_expert(xs, gs, [w], expert_of, lambda j: 0)
            mixes = mix if mixes is None else [a + b for a, b in zip(mixes, mix)]
            dxs = dx if dxs is None else [a + b for a, b in zip(dxs, dx)]
            grads.append(grad[0])
        return self.collect(dxs), (mixes, grads)

    def trade(self, value):
        cut = value.reshape(value.shape[0], self.n_rep, -1).transpose(1, 0, 2)
        got = lax.all_to_all(cut, "replica", 0, 0)
        return got.reshape(-1, got.shape[2])

    def end(self, held, first, normed, attn, dres, dproj, terms):
        mixes, grads = held
        mixed = first + self.collect(mixes)
        own = jnp.stack(
            [lax.psum_scatter(g, "fsdp", scatter_dimension=0, tiled=True) for g in grads]
        )
        expert_sum = lax.all_gather(own, "replica", axis=0, tiled=True).transpose(1, 0, 2)
        dense = []
        for left, right in ((normed, dproj), (dres, attn)):
            left = lax.all_gather(left, "replica", axis=0, tiled=True)
            part = contract_rows(left, self.trade(right)).astype(bf16)
            own = lax.psum_scatter(part, "fsdp", scatter_dimension=0, tiled=True)
            dense.append(lax.all_gather(own, "replica", axis=1, tiled=True))
        return mixed, dense[0], dense[1], expert_sum, lax.psum(terms, ("replica", "fsdp"))


def layer(
    net, tokens, seg_ids, routes, in_proj, out_proj, router, norm_gains, expert_in, expert_out,
    out_grad,
):
    length, width = tokens.shape
    experts = router.shape[1]
    hidden = expert_out.shape[2]
    shard = router.shape[0]
    scale = HD ** (-0.5)
    cosine, sine = tables(length)
    segment = seg_ids[0]
    place = jnp.arange(length)
    allowed = ((place[:, None] >= place[None, :]) & (segment[:, None] == segment[None, :]))[
        None, None
    ]
    tiny = jnp.concatenate(
        [router.T, norm_gains.T, jnp.zeros((16 - experts - 2, shard), bf16)], axis=0
    )
    proj_in, proj_out, tiny, held = net.start(
        in_proj, out_proj, tiny, expert_in, expert_out, out_grad
    )
    router_rows = tiny[:experts]
    gain_one = tiny[experts].astype(f32)
    gain_two = tiny[experts + 1].astype(f32)

    inputs = tokens.astype(f32)
    scale_one = rms_scale(inputs)
    unit_one = inputs * scale_one
    normed = (unit_one * gain_one).astype(bf16)
    proj = matmul(normed, proj_in)
    queries = (
        rotate(proj[:, :WQ].reshape(length, HQ, HD), cosine, sine)
        .astype(bf16)
        .reshape(length, KV, GROUP, HD)
    )
    keys = rotate(proj[:, WQ : WQ + WK].reshape(length, KV, HD), cosine, sine).astype(bf16)
    values = proj[:, WQ + WK :].reshape(length, KV, HD).astype(bf16)
    scores = jnp.einsum("qkgd,tkd->kgqt", queries, keys, preferred_element_type=f32) * scale
    masked = jnp.where(allowed, scores, -1e30)
    highest = jnp.max(masked, axis=-1, keepdims=True)
    expo = jnp.exp(masked - highest)
    total = jnp.sum(expo, axis=-1, keepdims=True)
    log_total = highest + jnp.log(total)
    probs_low = (expo / total).astype(bf16)
    attn = jnp.einsum("kgqt,tkd->qkgd", probs_low, values, preferred_element_type=f32)
    attn = attn.astype(bf16).reshape(length, WQ)
    first = inputs + contract_cols(attn, proj_out)
    scale_two = rms_scale(first)
    unit_two = first * scale_two
    normed_two = (unit_two * gain_two).astype(bf16)
    logits = contract_cols(normed_two, router_rows)
    onehot = (routes[:, :, None] == jnp.arange(experts)[None, None, :]).astype(f32)
    chosen = jnp.sum(onehot * logits[:, None, :], axis=-1)
    gates = jax.nn.softmax(chosen, axis=-1)
    table = jnp.sum(gates[:, :, None] * onehot, axis=1)
    high = table.astype(bf16)
    low = (table - high.astype(f32)).astype(bf16)
    payload = jnp.concatenate(
        [normed_two, high, low, jnp.zeros((length, EXTRA - 2 * experts), bf16)], axis=1
    )
    dx, held = net.experts(payload, held)

    grad_out = out_grad.astype(f32)
    dgate_all = dx[:, width : width + experts] + dx[:, width + experts : width + 2 * experts]
    dgate = jnp.sum(onehot * dgate_all[:, None, :], axis=-1)
    dchosen = gates * (dgate - jnp.sum(gates * dgate, axis=-1, keepdims=True))
    dlogits = jnp.sum(dchosen[:, :, None] * onehot, axis=1).astype(bf16)
    dnormed_two = dx[:, :width] + matmul(dlogits, router_rows)
    gain_two_grad = jnp.sum(dnormed_two * unit_two, axis=0)
    dunit_two = dnormed_two * gain_two
    dfirst = grad_out + scale_two * (
        dunit_two - unit_two * jnp.mean(dunit_two * unit_two, axis=-1, keepdims=True)
    )
    dres = dfirst.astype(bf16)
    dattn = matmul(dres, proj_out).astype(bf16).reshape(length, KV, GROUP, HD)
    probs = jnp.exp(masked - log_total)
    probs_again = probs.astype(bf16)
    dprobs = jnp.einsum("qkgd,tkd->kgqt", dattn, values, preferred_element_type=f32)
    dvalues = jnp.einsum("kgqt,qkgd->tkd", probs_again, dattn, preferred_element_type=f32)
    delta = jnp.sum(probs * dprobs, axis=-1, keepdims=True)
    dscores = (probs * (dprobs - delta)).astype(bf16)
    dqueries = jnp.einsum("kgqt,tkd->qkgd", dscores, keys, preferred_element_type=f32) * scale
    dkeys = jnp.einsum("kgqt,qkgd->tkd", dscores, queries, preferred_element_type=f32) * scale
    dqueries = rotate(dqueries.reshape(length, HQ, HD), cosine, -sine).reshape(length, WQ)
    dkeys = rotate(dkeys, cosine, -sine).reshape(length, WK)
    dproj = jnp.concatenate([dqueries, dkeys, dvalues.reshape(length, WK)], axis=1).astype(bf16)
    dnormed = contract_cols(dproj, proj_in)
    gain_one_grad = jnp.sum(dnormed * unit_one, axis=0)
    dunit_one = dnormed * gain_one
    tokens_grad = (
        dfirst
        + scale_one
        * (dunit_one - unit_one * jnp.mean(dunit_one * unit_one, axis=-1, keepdims=True))
    ).astype(bf16)

    terms = jnp.concatenate(
        [
            contract_rows(dlogits, normed_two),
            gain_one_grad[None],
            gain_two_grad[None],
            jnp.zeros((16 - experts - 2, width), f32),
        ],
        axis=0,
    )
    mixed, in_proj_grad, out_proj_grad, expert_sum, terms = net.end(
        held, first, normed, attn, dres, dproj, terms
    )
    terms = lax.dynamic_slice_in_dim(terms, lax.axis_index("fsdp") * shard, shard, 1).T
    return (
        mixed.astype(bf16),
        tokens_grad,
        in_proj_grad.astype(f32),
        out_proj_grad.astype(f32),
        terms[:, :experts],
        terms[:, experts : experts + 2],
        expert_sum[..., : 2 * hidden].astype(f32),
        expert_sum[..., 2 * hidden :].astype(f32),
    )


def solution(mesh):
    n_rep, n_fsdp = mesh.shape["replica"], mesh.shape["fsdp"]
    if (n_rep, n_fsdp) == (4, 8):
        body = near_layer
    else:
        body = functools.partial(layer, Wide(n_rep, n_fsdp))
    both = P(("replica", "fsdp"), None)
    fsdp, deep = P("fsdp", None), P("fsdp", None, None)
    return jax.shard_map(
        body,
        mesh=mesh,
        in_specs=(both, both, both, fsdp, fsdp, fsdp, fsdp, deep, deep, both),
        out_specs=(both, both, fsdp, fsdp, fsdp, fsdp, deep, deep),
        check_vma=False,
    )
```
